512 devices in a mesh: tile: 32 (over z, x_lo, core), src: 16 (over x_hi, y).
Axes of the slice: x: 4 (x_hi: 2, x_lo: 2; x = x_hi * 2 + x_lo), y: 8, z: 8, core: 2. Of those that a mesh axis runs over, the one named last changes fastest.
Arguments:
- mask: float32 [256, 8192], P('src', 'tile'), may hold values from 0 to 1
- target: int32 [256, 8192], P(None, 'tile'), may hold values 0 or 1
- shifts: int32 [128, 2], P('src'), may hold values from -12 to 12
- weights: float32 [128], P('src'), may hold values from 0.5 to 2
Outputs:
- resist: float32 [256, 8192], P('src', 'tile')
- mask_grad: float32 [256, 8192], P('src', 'tile')
- source_grad: float32 [128], P('src')
The draws below stay inside these ranges and needn't reach their ends.
All inputs are finite; a program needn't handle non-finite values. No bound on the sum of `target` on one device may be relied on, other than what follows from the above.
Results may differ from the reference program's by a relative error of at most 0.0003.
Values sent between devices are 32-bit elements; how exact they have to be, the bound alone decides.
A program may use at most 64 MiB of HBM per device.

```python
import math
import jax
import jax.numpy as jnp
from jax import lax

TILE = 256
MARGIN = 32
BAND = 64
RAD = 16
SHIFT = 12
EXT = 320
SRC = 128
TILES = 32
N_TILE = 32


def plant(entries, own_key, low, high):
    spot = [jax.random.randint(jax.random.fold_in(own_key, axis), (), 0, length) for axis, length in enumerate(entries.shape)]
    main_axis = entries.shape.index(max(entries.shape))
    next_to = spot[:main_axis] + [(spot[main_axis] + 1) % entries.shape[main_axis]] + spot[main_axis + 1:]
    return entries.at[tuple(spot)].set(low).at[tuple(next_to)].set(high)


def level_of(own_key, shape, pieces, smallest, high):
    def one(position, blocks):
        steps = jax.random.uniform(jax.random.fold_in(jax.random.fold_in(own_key, 6), position), (blocks,), jnp.float32, smallest / len(pieces), high / len(pieces))
        return jnp.repeat(jnp.exp(steps), shape[position] // blocks).reshape((-1,) + (1,) * (len(shape) - position - 1))

    factor_of = one(*pieces[0])
    for cut in pieces[1:]:
        factor_of = factor_of * one(*cut)
    return factor_of


def setup_inputs(seed: int = 0) -> dict:
    arg_keys = jax.random.split(jax.random.key(seed), 5)
    return {
        "mask": jnp.clip(1.0 * jax.random.uniform(arg_keys[0], (TILE, TILES * TILE), jnp.float32) ** level_of(arg_keys[0], (TILE, TILES * TILE), ((0, 16), (1, 32)), -0.2, 0.2), 0.0, 1.0),
        "target": plant((jax.random.randint(arg_keys[1], (TILE, TILES * TILE), 0, 2) < 1).astype(jnp.int32), jax.random.fold_in(arg_keys[1], 1), 0, 1),
        "shifts": plant(jax.random.randint(arg_keys[2], (SRC, 2), -SHIFT, SHIFT + 1), jax.random.fold_in(arg_keys[2], 1), -SHIFT, SHIFT).astype(jnp.int32),
        "weights": jnp.clip(jnp.exp(math.log(2.0) - 1.3862944 * jax.random.uniform(arg_keys[3], (SRC,), jnp.float32) ** level_of(arg_keys[3], (SRC,), ((0, 16),), -0.2, 0.2)), 0.5, 2.0),
    }


STEEP = 8.0
THRESH = 0.25
LOSS_SCALE = 2.0

def product(left, right):
    return jnp.matmul(left, right, precision=lax.Precision.HIGHEST)

def tables():
    freq = jnp.arange(BAND, dtype=jnp.int32) - BAND // 2
    place = jnp.arange(EXT, dtype=jnp.int32)
    phase = (freq[:, None] * place[None, :] % EXT).astype(jnp.float32) * (2.0 * jnp.pi / EXT)
    fwd_real = jnp.cos(phase) / EXT
    fwd_imag = -jnp.sin(phase) / EXT
    inner = place[MARGIN:MARGIN + TILE]
    phase_back = (inner[:, None] * freq[None, :] % EXT).astype(jnp.float32) * (2.0 * jnp.pi / EXT)
    return (fwd_real, fwd_imag, jnp.cos(phase_back), jnp.sin(phase_back), freq)

def pupils(shifts, freq):
    rows_off = freq[None, :, None] + shifts[:, 0][:, None, None]
    cols_off = freq[None, None, :] + shifts[:, 1][:, None, None]
    return (rows_off * rows_off + cols_off * cols_off <= RAD * RAD).astype(jnp.float32)

def forward(ext_tile, weights, pupil, goal):
    fwd_real, fwd_imag, inv_real, inv_imag, freq = tables()
    rows_real = fwd_real[:, MARGIN:MARGIN + TILE]
    rows_imag = fwd_imag[:, MARGIN:MARGIN + TILE]
    half_real = product(rows_real, ext_tile)
    half_imag = product(rows_imag, ext_tile)
    spec_real = product(half_real, fwd_real.T) - product(half_imag, fwd_imag.T)
    spec_imag = product(half_real, fwd_imag.T) + product(half_imag, fwd_real.T)

    def one_source(image, item):
        mask_band, weight = item
        band_real = mask_band * spec_real
        band_imag = mask_band * spec_imag
        left_real = product(inv_real, band_real) - product(inv_imag, band_imag)
        left_imag = product(inv_real, band_imag) + product(inv_imag, band_real)
        field_real = product(left_real, inv_real.T) - product(left_imag, inv_imag.T)
        field_imag = product(left_real, inv_imag.T) + product(left_imag, inv_real.T)
        return (image + weight * (field_real * field_real + field_imag * field_imag), None)
    start = jnp.zeros((TILE, TILE), jnp.float32)
    image, unused = lax.scan(one_source, start, (pupil, weights))
    image = image / SRC
    printed = jax.nn.sigmoid(STEEP * (image - THRESH))
    loss = LOSS_SCALE * jnp.sum((printed - goal) ** 2)
    return (loss, printed)

def reference(mask, target, shifts, weights):
    freq = jnp.arange(BAND, dtype=jnp.int32) - BAND // 2
    pupil = pupils(shifts, freq)
    tiles = mask.reshape(TILE, N_TILE, TILE).transpose(1, 0, 2)
    blank = jnp.zeros((1, TILE, MARGIN), jnp.float32)
    left = jnp.concatenate([blank, tiles[:-1, :, TILE - MARGIN:]], axis=0)
    right = jnp.concatenate([tiles[1:, :, :MARGIN], blank], axis=0)
    ext = jnp.concatenate([left, tiles, right], axis=2)
    goals = target.reshape(TILE, N_TILE, TILE).transpose(1, 0, 2).astype(jnp.float32)

    def per_tile(item):
        ext_tile, goal = item
        loss, pull, printed = jax.vjp(lambda e, w: forward(e, w, pupil, goal), ext_tile, weights, has_aux=True)
        grad_ext, grad_weight = pull(jnp.ones_like(loss))
        return (printed, grad_ext[:, MARGIN:MARGIN + TILE], grad_weight)
    printed, grads, weight_grads = lax.map(per_tile, (ext, goals))
    resist = printed.transpose(1, 0, 2).reshape(TILE, N_TILE * TILE)
    mask_grad = grads.transpose(1, 0, 2).reshape(TILE, N_TILE * TILE)
    source_grad = lax.optimization_barrier(jnp.sum(weight_grads, axis=0)) / (N_TILE * TILE * TILE)
    return (resist, mask_grad, source_grad)
```

```python
import functools

import jax
import jax.numpy as jnp
import ml_dtypes
import numpy as np
from jax import lax
from jax.experimental import pallas as pl
from jax.experimental.pallas import tpu as pltpu
from jax.sharding import PartitionSpec as P

TILE = 256
MARGIN = 32
BAND = 64
RAD = 16
EXT = 320
STEEP = 8.0
THRESH = 0.25
LOSS_SCALE = 2.0

N_SRC = 16
N_TILE = 32
PER_DEV = 8
SOURCES = 128
ROWS = 16
HALF = 32
ROWS_C = 80
COLS_C = 128
QUAD = 4
GROUP = 4
DEPTH = 8

MESH = pl.DeviceIdType.MESH
BF16 = ml_dtypes.bfloat16


def halves(table):
    high = table.astype(BF16)
    low = (table - high.astype(np.float64)).astype(BF16)
    return high, low


def column_slots():
    plus = np.arange(HALF)
    return np.concatenate([plus, -plus]), np.concatenate([np.ones(HALF), [0.0], np.ones(HALF - 1)])


def waves(freq, place, period):
    phase = 2.0 * np.pi * ((freq[:, None] * place[None, :]) % period) / period
    return np.cos(phase), np.sin(phase)


def interpolation(points):
    order = np.arange(-2 * RAD, 2 * RAD + 1)
    place = np.arange(TILE) + MARGIN
    offset = place[:, None] / EXT - np.arange(points)[None, :] / points
    return np.cos(2.0 * np.pi * order[None, None, :] * offset[:, :, None]).sum(axis=2) / points


def build_tables():
    slots, used = column_slots()
    row_freq = np.arange(BAND) - BAND // 2
    pixels = np.arange(TILE) + MARGIN
    parts = {}

    real, imag = waves(np.arange(HALF), np.arange(EXT), EXT)
    fwd = np.concatenate([real, -imag], axis=0).T / EXT
    wide = np.zeros((2 * TILE, 2 * HALF))
    wide[:TILE] = fwd[MARGIN : MARGIN + TILE]
    wide[TILE + 96 : TILE + 128] = fwd[:MARGIN]
    wide[TILE + 128 : TILE + 160] = fwd[MARGIN + TILE :]
    high, low = halves(np.concatenate([wide, wide], axis=1))
    parts["enter"] = np.concatenate([high, low], axis=1)

    rows = np.arange(TILE).reshape(N_SRC, 2, 8)
    first, second = rows[:, 0].reshape(-1), rows[:, 1].reshape(-1)
    real, imag = waves(row_freq, pixels, EXT)
    real, imag = real / EXT, -imag / EXT
    both = np.concatenate([real, imag], axis=0)
    high, low = halves(np.concatenate([both[:, first], both[:, second]], axis=0))
    parts["spec"] = np.concatenate([high, high], axis=1)
    spec_low = low

    inter_rows, inter_cols = 2.0 * interpolation(ROWS_C), interpolation(COLS_C)
    even, odd = np.arange(0, COLS_C, 2), np.arange(1, COLS_C, 2)
    for name, order in (("even", np.concatenate([even, odd])), ("odd", np.concatenate([odd, even]))):
        real, imag = waves(slots, order, COLS_C)
        real, imag = real * used[:, None], imag * used[:, None]
        cols = np.concatenate(
            [np.concatenate([real, imag], axis=1), np.concatenate([-imag, real], axis=1)], axis=0
        )
        high, low = halves(cols)
        parts["cols_" + name] = np.concatenate([high, high], axis=0)
        parts["cols_low_" + name] = low
        high, low = halves(np.concatenate([cols[:, :COLS_C].T, cols[:, COLS_C:].T], axis=0))
        parts["cols_back_" + name] = np.concatenate([high, low], axis=1)

    lows = []
    for name, start in (("even", 0), ("odd", 1)):
        real, imag = waves(row_freq, np.arange(start, ROWS_C, 2), ROWS_C)
        real, imag = real.T, imag.T
        high, low = halves(
            np.concatenate(
                [np.concatenate([real, -imag], axis=1), np.concatenate([imag, real], axis=1)], axis=0
            )
        )
        parts["rows_" + name] = np.concatenate([high, high], axis=1)
        lows.append(low)
        pad = np.zeros((2 * BAND, TILE - 3 * ROWS_C), BF16)
        parts["rows_back_" + name] = np.concatenate([high.T, high.T, low.T, pad], axis=1)
    rows_low = np.concatenate(lows, axis=0)

    mixed = np.concatenate([np.arange(0, ROWS_C, 2), np.arange(1, ROWS_C, 2)])
    inter_rows, inter_cols = inter_rows[:, mixed], inter_cols[:, np.concatenate([even, odd])]
    high, low = halves(inter_rows)
    pad = np.zeros((TILE, TILE - 3 * ROWS_C), BF16)
    parts["fine_rows"] = np.concatenate([high, high, low, pad], axis=1)
    high, low = halves(inter_cols.T)
    parts["fine_cols"] = np.concatenate([high, high], axis=0)
    parts["fine_cols_low"] = low
    parts["coarse_cols"] = np.concatenate([high.T, low.T], axis=1)
    high, low = halves(inter_rows.T)
    parts["coarse_rows"] = high
    parts["coarse_rows_low"] = low

    high, low = halves(np.concatenate([both[:, first], both[:, second]], axis=1).T)
    parts["leave"] = np.concatenate([high, high], axis=1)
    leave_low = low
    last = fwd[MARGIN : MARGIN + TILE].T
    high, low = halves(np.concatenate([last, last], axis=0))
    parts["last"] = high
    parts["last_low"] = low

    parts["lows_a"] = np.concatenate([spec_low, np.zeros((TILE, 128), BF16)], axis=1)
    rows_low = np.concatenate([rows_low, np.zeros((TILE - 2 * ROWS_C, 128), BF16)], axis=0)
    parts["lows_b"] = np.concatenate([leave_low, rows_low], axis=1)

    order = [
        "enter",
        "spec", "lows_a", "cols_even", "cols_low_even", "cols_odd", "cols_low_odd", "rows_even", "rows_odd", "lows_b",
        "fine_rows", "fine_cols", "fine_cols_low", "coarse_cols", "coarse_rows", "coarse_rows_low",
        "rows_back_even", "rows_back_odd", "cols_back_even", "cols_back_odd", "leave", "last", "last_low",
    ]
    places, start = {}, 0
    for name in order:
        places[name] = (start, parts[name].shape[0])
        start += parts[name].shape[0]
    return np.concatenate([parts[name] for name in order], axis=0), places


TABLE, PLACES = build_tables()
CUTS = (0, PLACES["spec"][0], PLACES["fine_rows"][0], TABLE.shape[0])


def dot(left, right):
    return jnp.dot(left, right, preferred_element_type=jnp.float32)


def cut(value):
    high = value.astype(jnp.bfloat16)
    low = (value - high.astype(jnp.float32)).astype(jnp.bfloat16)
    return high, low


def lanes(shape):
    return lax.broadcasted_iota(jnp.int32, shape, 1)


def enter(value, table):
    high, low = cut(value)
    both = dot(high, table)
    return both[:, :128] + both[:, 128:] + dot(low, table[:, :128])


def pack(first, second):
    return jnp.where(lanes(first.shape) < 64, first, second)


def spectrum(gathered, table, low_table, roll):
    high, low = cut(gathered)
    out = dot(table, jnp.concatenate([high, low], axis=0)) + dot(low_table, high)
    both = pack(out[:128], out[128:])
    both = both + roll(both, 64, 1)
    turned = roll(both, 32, 1)
    quarter = lanes((BAND, 128)) >> 5
    outer = (quarter == 0) | (quarter == 3)
    even = jnp.where(outer, both[:BAND], turned[:BAND])
    odd = jnp.where(outer, turned[BAND:], both[BAND:])
    return jnp.where(quarter == 3, -even, even) + jnp.where(quarter == 0, -odd, odd)


def pupil_of(row_shift, col_shift):
    shape = (BAND, 128)
    row = lax.broadcasted_iota(jnp.int32, shape, 0) - BAND // 2 + row_shift
    slot = lanes(shape) & 63
    col = jnp.where(slot < HALF, slot, HALF - slot) + col_shift
    inside = (row * row + col * col <= RAD * RAD) & (slot != HALF)
    return inside.astype(jnp.float32)


def swap(first, second):
    return pack(first, second), pack(second, first)


def coarse_fields(spec, pupils, cols, rows):
    high, low = cut(spec)
    mids = []
    for which in range(2):
        band_high = jnp.concatenate([high * pupil for pupil in pupils[which::2]], axis=0)
        band_low = jnp.concatenate([low * pupil for pupil in pupils[which::2]], axis=0)
        table, low_table = cols[which]
        mids.append(
            dot(jnp.concatenate([band_high, band_low], axis=1), table) + dot(band_high, low_table)
        )
    fields = []
    for group in range(2):
        stacks = ([], [])
        for pair in (2 * group, 2 * group + 1):
            at = slice(BAND * pair, BAND * pair + BAND)
            real = swap(mids[0][at, :128], mids[1][at, :128])
            imag = swap(mids[0][at, 128:], mids[1][at, 128:])
            for parity in range(2):
                stacks[parity].append(jnp.concatenate([real[parity], imag[parity]], axis=0))
        both = []
        for parity in range(2):
            upper, lower = cut(jnp.concatenate(stacks[parity], axis=1))
            table, low_table = rows[parity]
            both.append(dot(table, jnp.concatenate([upper, lower], axis=0)) + dot(low_table, upper))
        fields.append(both)
    return fields


def power_of(field):
    half = ROWS_C // 2
    return field[:half] * field[:half] + field[half:] * field[half:]


def join_image(even, odd, roll):
    return pack(even + roll(even, 64, 1), odd + roll(odd, 64, 1))


def pixels_of(coarse, fine_rows, fine_cols, fine_cols_low):
    first = lanes(coarse.shape) < 64
    coarse = jnp.concatenate([jnp.where(first, coarse, 0.0), jnp.where(first, 0.0, coarse)], axis=0)
    high, low = cut(coarse)
    mid = dot(jnp.concatenate([high, low], axis=1), fine_cols) + dot(high, fine_cols_low)
    return dot(fine_rows, three(mid))


def three(value):
    high, low = cut(value)
    pad = jnp.zeros((TILE - 3 * value.shape[0], value.shape[1]), jnp.bfloat16)
    return jnp.concatenate([high, low, high, pad], axis=0)


def coarse_of(slope, coarse_rows, coarse_rows_low, coarse_cols):
    high, low = cut(slope)
    mid = dot(coarse_rows, high) + dot(coarse_rows, low) + dot(coarse_rows_low, high)
    high, low = cut(mid)
    both = dot(high, coarse_cols)
    return both[:, :128] + both[:, 128:] + dot(low, coarse_cols[:, :128])


def twice(coarse, roll):
    half = ROWS_C // 2
    even, odd = coarse[:half], coarse[half:]
    return pack(even, roll(even, 64, 1)), pack(roll(odd, 64, 1), odd)


def band_grad(total, adjoints, pupils, rows_back, cols_back):
    sides = ([], [])
    for group in range(2):
        even, odd = [dot(rows_back[parity], three(adjoints[group][parity])) for parity in range(2)]
        for pair in range(2):
            at = slice(128 * pair, 128 * pair + 128)
            real = swap(even[:BAND, at], odd[:BAND, at])
            imag = swap(even[BAND:, at], odd[BAND:, at])
            for which in range(2):
                sides[which].append(jnp.concatenate([real[which], imag[which]], axis=1))
    for which in range(2):
        high, low = cut(jnp.concatenate(sides[which], axis=0))
        both = dot(high, cols_back[which])
        term = both[:, :128] + both[:, 128:] + dot(low, cols_back[which][:, :128])
        for k in range(PER_DEV // 2):
            total = total + term[BAND * k : BAND * k + BAND] * pupils[2 * k + which]
    return total


def fold(grad, roll):
    r32, r64, r96 = roll(grad, 32, 1), roll(grad, 64, 1), roll(grad, 96, 1)
    quarter = lanes(grad.shape) >> 5
    upper = jnp.where(
        quarter == 0, grad + r96, jnp.where(quarter == 1, r96 - r64, jnp.where(quarter == 2, r64 + r32, r32 - grad))
    )
    lower = jnp.where(
        quarter == 0, r64 + r32, jnp.where(quarter == 1, grad - r32, jnp.where(quarter == 2, grad + r96, r64 - r96))
    )
    return jnp.concatenate([upper, lower], axis=0)


def row_grads(grad, leave, leave_low, roll):
    high, low = cut(fold(grad, roll))
    out = dot(leave, jnp.concatenate([high, low], axis=0)) + dot(leave_low, high)
    half = out.shape[0] // 2
    return pack(out[:half], out[half:])


def last_step(total, last, last_low):
    first = lanes(total.shape) < 64
    value = jnp.concatenate([jnp.where(first, total, 0.0), jnp.where(first, 0.0, total)], axis=0)
    high, low = cut(value)
    return dot(high, last) + dot(low, last) + dot(high, last_low)


def rank_of(side, along):
    step = jnp.where(along <= DEPTH // 2, 2 * along - 1, 2 * (DEPTH - along))
    return 2 * jnp.maximum(step, 0) + side


def src_of(rank):
    step, side = rank // 2, rank % 2
    half = (step + 1) // 2
    return side * DEPTH + jnp.where(step % 2 == 1, half, (DEPTH - half) % DEPTH)


def repeat(first, last, body):
    def step(k, carry):
        body(k)
        return carry

    lax.fori_loop(first, last, step, 0)


def everything(mask, target, shifts, weights, table, resist, mask_grad, source_grad, *scratch):
    (
        mask_v, target_v, shifts_v, weights_v, table_v,
        left_v, right_v, spec_v, pupil_v, scale_v, image_v, term_v, field_v, power_v,
        printed_v, grad_v, part_v, sums_v, local_sem, send_sem, recv_sem, sums_sem, ready_sem,
    ) = scratch
    tile, src = lax.axis_index("tile"), lax.axis_index("src")
    n_tile = lax.axis_size("tile")
    left, right = tile - 1, tile + 1
    has_left, has_right = tile > 0, tile < n_tile - 1
    side, along = src // DEPTH, src % DEPTH
    rank = rank_of(side, along)
    quad = along // QUAD
    partners = [
        (side + across) % 2 * DEPTH + (along + step) % DEPTH for across, step in ((0, QUAD), (1, 0), (1, QUAD))
    ]
    members = [side * DEPTH + quad * QUAD + (along + k) % QUAD for k in range(1, QUAD)]
    layer = tile // GROUP
    layer_first, layer_last = layer * GROUP, layer * GROUP + GROUP

    def get(name, start=None, stop=None):
        at, size = PLACES[name]
        if start is None:
            return table_v[at : at + size, :]
        return table_v[at : at + size, start:stop]

    def signal(sem, device):
        pl.semaphore_signal(sem, inc=1, device_id=device, device_id_type=MESH)

    def send(source, target_ref, number, device):
        copy = pltpu.make_async_remote_copy(
            src_ref=source,
            dst_ref=target_ref,
            send_sem=send_sem.at[number],
            recv_sem=recv_sem.at[number],
            device_id=device,
            device_id_type=MESH,
        )
        copy.start()

    def wait(ref, sem):
        pltpu.make_async_copy(ref, ref, sem).wait()

    barrier = pltpu.get_barrier_semaphore()

    @pl.when(has_left)
    def _():
        signal(barrier, {"tile": left})

    @pl.when(has_right)
    def _():
        signal(barrier, {"tile": right})

    repeat(rank + 1, N_SRC, lambda k: signal(barrier, {"src": src_of(k)}))
    local = [
        pltpu.make_async_copy(mask, mask_v, local_sem.at[0]),
        pltpu.make_async_copy(shifts, shifts_v, local_sem.at[1]),
        pltpu.make_async_copy(weights, weights_v, local_sem.at[2]),
    ]
    for k in range(3):
        rows = pl.ds(CUTS[k], CUTS[k + 1] - CUTS[k])
        local.append(pltpu.make_async_copy(table.at[rows], table_v.at[rows], local_sem.at[3 + k]))
    local.append(pltpu.make_async_copy(target, target_v, local_sem.at[6]))
    for copy in local:
        copy.start()
    repeat(layer_first, tile, lambda k: signal(barrier, {"tile": k}))
    repeat(tile + 1, n_tile, lambda k: signal(barrier, {"tile": k}))

    ends = has_left.astype(jnp.int32) + has_right.astype(jnp.int32)
    pl.semaphore_wait(barrier, rank + ends + layer_last - 1)

    @pl.when(has_right)
    def _():
        send(mask.at[:, pl.ds(128, 128)], left_v, 0, {"tile": right})

    @pl.when(has_left)
    def _():
        send(mask.at[:, pl.ds(0, 128)], right_v, 1, {"tile": left})

    repeat(0, rank, lambda k: signal(ready_sem.at[rank], {"src": src_of(k)}))

    @pl.when(jnp.logical_not(has_left))
    def _():
        left_v[...] = jnp.zeros_like(left_v)

    @pl.when(jnp.logical_not(has_right))
    def _():
        right_v[...] = jnp.zeros_like(right_v)

    local[1].wait()
    local[2].wait()
    spec_v[src, 8:16, :] = jnp.zeros((8, 128), jnp.float32)
    spec_v[src, 8:10, 0:PER_DEV] = shifts_v[...].astype(jnp.float32)
    spec_v[src, 10:11, 0:PER_DEV] = weights_v[...]
    local[0].wait()
    local[3].wait()
    at = PLACES["enter"][0]
    own = enter(mask_v[...], table_v[at : at + TILE, :])

    @pl.when(has_left)
    def _():
        wait(left_v, recv_sem.at[0])

    @pl.when(has_right)
    def _():
        wait(right_v, recv_sem.at[1])

    margins = jnp.concatenate([left_v[...], right_v[...]], axis=1)
    own = own + enter(margins, table_v[at + TILE : at + 2 * TILE, :])
    spec_v[src, 0:8, :] = pack(own[:8], own[8:])
    piece = pl.ds(0, 11)

    def send_piece(k):
        send(spec_v.at[src, piece], spec_v.at[src, piece], 2, {"src": src_of(k)})

    def answer_piece(k):
        pl.semaphore_wait(ready_sem.at[k], 1)
        send_piece(k)

    repeat(0, rank, send_piece)
    repeat(rank + 1, N_SRC, answer_piece)
    local[4].wait()
    wait(spec_v.at[pl.ds(0, N_SRC - 1), piece], recv_sem.at[2])

    gathered = spec_v[:, 0:8, :].reshape(128, 128)
    spec = spectrum(gathered, get("spec"), get("lows_a", 0, 128), pltpu.roll)
    at = PLACES["lows_b"][0]
    cols = [(get("cols_" + name), get("cols_low_" + name)) for name in ("even", "odd")]
    rows = [
        (get("rows_even"), table_v[at : at + ROWS_C, 128:256]),
        (get("rows_odd"), table_v[at + ROWS_C : at + 2 * ROWS_C, 128:256]),
    ]

    def add_fields(part, images):
        owner = src
        for k, peer in enumerate(partners):
            owner = jnp.where(part == k + 1, peer, owner)
        extra = spec_v[owner, 8:16, :]
        shift = extra[0:2, :].astype(jnp.int32)
        for s in range(PER_DEV):
            pupil_v[part, s] = pupil_of(shift[0:1, s : s + 1], shift[1:2, s : s + 1])
        for pair in range(PER_DEV // 2):
            first, second = [
                jnp.broadcast_to(extra[2:3, s : s + 1], (8, 128)) for s in (2 * pair, 2 * pair + 1)
            ]
            at = slice(128 * (pair % 2), 128 * (pair % 2) + 128)
            for parity, scale in enumerate(swap(first, second)):
                scale_v[part, pair // 2, parity, :, at] = scale
        fields = coarse_fields(
            spec, [pupil_v[part, s].astype(jnp.bfloat16) for s in range(PER_DEV)], cols, rows
        )
        images = list(images)
        for group in range(2):
            for parity in range(2):
                field_v[part, group, parity] = fields[group][parity]
                power = power_of(fields[group][parity])
                power_v[part, group, parity] = power
                power = power * scale_v[part, group, parity, 0:1, :]
                images[parity] = images[parity] + power[:, :128] + power[:, 128:]
        return tuple(images)

    none = jnp.zeros((ROWS_C // 2, 128), jnp.float32)
    image_v[...] = join_image(*lax.fori_loop(0, QUAD, add_fields, (none, none)), pltpu.roll)
    for k, peer in enumerate(members):
        send(image_v, term_v.at[k], 3, {"src": peer})
    local[5].wait()
    local[6].wait()
    wait(term_v, recv_sem.at[3])

    image = pixels_of(
        image_v[...] + term_v[0] + term_v[1] + term_v[2],
        get("fine_rows"),
        get("fine_cols"),
        get("fine_cols_low"),
    )
    printed = jax.nn.sigmoid(STEEP * (image * (1.0 / SOURCES) - THRESH))
    printed_v[...] = printed
    resist[...] = printed_v[pl.ds(pl.multiple_of(src * ROWS, ROWS), ROWS), :]
    goal = target_v[...].astype(jnp.float32)
    slope = (LOSS_SCALE * 2.0 * STEEP) * (printed - goal) * printed * (1.0 - printed)
    coarse = coarse_of(slope, get("coarse_rows"), get("coarse_rows_low"), get("coarse_cols"))

    slopes = twice(coarse, pltpu.roll)
    sums = []
    for pair in range(PER_DEV // 2):
        at = slice(128 * (pair % 2), 128 * (pair % 2) + 128)
        terms = [
            jnp.sum(slopes[parity] * power_v[0, pair // 2, parity, :, at], axis=0, keepdims=True) for parity in range(2)
        ]
        sums.extend(swap(*terms))
    sums = jnp.sum(jnp.concatenate(sums, axis=0), axis=1, keepdims=True)
    spot = (PER_DEV, 128)
    sums = jnp.where(lanes(spot) == lax.broadcasted_iota(jnp.int32, spot, 0), sums, 0.0)
    sums_v[tile] = jnp.sum(sums, axis=0, keepdims=True)

    def send_sums(k):
        pltpu.make_async_remote_copy(
            src_ref=sums_v.at[tile],
            dst_ref=sums_v.at[tile],
            send_sem=send_sem.at[5],
            recv_sem=sums_sem.at[layer],
            device_id={"tile": k},
            device_id_type=MESH,
        ).start()

    repeat(0, tile, send_sums)
    repeat(tile + 1, layer_last, send_sums)

    wide = [jnp.concatenate([slope, slope], axis=1) * (2.0 / SOURCES) for slope in slopes]
    rows_back = [get("rows_back_even"), get("rows_back_odd")]
    cols_back = [get("cols_back_even"), get("cols_back_odd")]

    def add_part(part, total):
        adjoints = []
        for group in range(2):
            adjoints.append([])
            for parity in range(2):
                scaled = wide[parity] * scale_v[part, group, parity, 0:1, :]
                adjoints[group].append(field_v[part, group, parity] * jnp.concatenate([scaled, scaled], axis=0))
        return band_grad(total, adjoints, [pupil_v[part, s] for s in range(PER_DEV)], rows_back, cols_back)

    grad = lax.fori_loop(0, QUAD, add_part, jnp.zeros((BAND, 128), jnp.float32))
    first = PLACES["leave"][0] + 8 * QUAD * (src // QUAD)
    low_first = PLACES["lows_b"][0] + 8 * QUAD * (src // QUAD)

    def halves_of(start, stop, begin):
        begin = pl.multiple_of(begin, 32)
        then = pl.multiple_of(begin + 128, 32)
        return jnp.concatenate(
            [table_v[pl.ds(begin, 8 * QUAD), start:stop], table_v[pl.ds(then, 8 * QUAD), start:stop]], axis=0
        )

    rows = row_grads(grad, halves_of(0, 256, first), halves_of(0, 128, low_first), pltpu.roll)
    grad_v[...] = rows.reshape(QUAD, 8, 128)
    for k, peer in enumerate(members):
        send(grad_v.at[peer % QUAD], part_v.at[k], 4, {"src": peer})

    def finish():
        wait(part_v, recv_sem.at[4])
        total = grad_v[along % QUAD] + part_v[0] + part_v[1] + part_v[2]
        mask_grad[...] = last_step(total, get("last"), get("last_low"))

    def answer_sums(k):
        wait(sums_v.at[pl.ds(k * GROUP, GROUP)], sums_sem.at[k])
        repeat(k * GROUP, k * GROUP + GROUP, send_sums)

    pl.when(layer == 0)(finish)
    repeat(layer + 1, n_tile // GROUP, answer_sums)
    pl.when(layer > 0)(finish)
    wait(sums_v.at[pl.ds(0, GROUP - 1)], sums_sem.at[layer])
    repeat(0, layer, lambda k: wait(sums_v.at[pl.ds(k * GROUP, GROUP)], sums_sem.at[k]))
    source_grad[...] = jnp.sum(sums_v[...], axis=0) * (1.0 / (SOURCES * n_tile * TILE * TILE))

    @pl.when(has_right)
    def _():
        wait(left_v, send_sem.at[0])

    @pl.when(has_left)
    def _():
        wait(right_v, send_sem.at[1])

    wait(spec_v.at[pl.ds(0, N_SRC - 1), piece], send_sem.at[2])
    wait(term_v, send_sem.at[3])
    wait(part_v, send_sem.at[4])
    wait(sums_v.at[pl.ds(0, n_tile - 1)], send_sem.at[5])


def hand_over(resist, mask_grad, source_grad, resist_out, mask_grad_out, source_grad_out, sem):
    copies = [
        pltpu.make_async_copy(resist, resist_out, sem.at[0]),
        pltpu.make_async_copy(mask_grad, mask_grad_out, sem.at[1]),
    ]
    for copy in copies:
        copy.start()
    source_grad_out[...] = source_grad[0, :PER_DEV]
    for copy in copies:
        copy.wait()


def local(mask, target, shifts, weights):
    f32 = jnp.float32
    anywhere = pl.BlockSpec(memory_space=pl.ANY)
    inside = pl.BlockSpec(memory_space=pltpu.VMEM)
    results = pl.pallas_call(
        everything,
        out_shape=(
            pltpu.VMEM((ROWS, TILE), f32),
            pltpu.VMEM((ROWS, TILE), f32),
            pltpu.VMEM((1, 128), f32),
        ),
        in_specs=[anywhere] * 5,
        out_specs=(inside, inside, inside),
        scratch_shapes=[
            pltpu.VMEM((ROWS, TILE), f32),
            pltpu.VMEM((TILE, TILE), jnp.int32),
            pltpu.VMEM((2, PER_DEV), jnp.int32),
            pltpu.VMEM((1, PER_DEV), f32),
            pltpu.VMEM(TABLE.shape, jnp.bfloat16),
            pltpu.VMEM((ROWS, 128), f32),
            pltpu.VMEM((ROWS, 128), f32),
            pltpu.VMEM((N_SRC, 16, 128), f32),
            pltpu.VMEM((QUAD, PER_DEV, BAND, 128), f32),
            pltpu.VMEM((QUAD, 2, 2, 8, 256), f32),
            pltpu.VMEM((ROWS_C // 2, 128), f32),
            pltpu.VMEM((QUAD - 1, ROWS_C // 2, 128), f32),
            pltpu.VMEM((QUAD, 2, 2, ROWS_C, 256), f32),
            pltpu.VMEM((QUAD, 2, 2, ROWS_C // 2, 256), f32),
            pltpu.VMEM((TILE, TILE), f32),
            pltpu.VMEM((QUAD, 8, 128), f32),
            pltpu.VMEM((QUAD - 1, 8, 128), f32),
            pltpu.VMEM((N_TILE, 1, 128), f32),
            pltpu.SemaphoreType.DMA((7,)),
            pltpu.SemaphoreType.DMA((6,)),
            pltpu.SemaphoreType.DMA((5,)),
            pltpu.SemaphoreType.DMA((DEPTH,)),
            pltpu.SemaphoreType.REGULAR((N_SRC,)),
        ],
        compiler_params=pltpu.CompilerParams(
            collective_id=0, has_side_effects=True, vmem_limit_bytes=60 * 1024 * 1024
        ),
    )(mask, target, shifts.T, weights.reshape(1, PER_DEV), jnp.asarray(TABLE))
    return pl.pallas_call(
        hand_over,
        out_shape=(
            jax.ShapeDtypeStruct((ROWS, TILE), f32),
            jax.ShapeDtypeStruct((ROWS, TILE), f32),
            jax.ShapeDtypeStruct((PER_DEV,), f32),
        ),
        in_specs=[inside] * 3,
        out_specs=(anywhere, anywhere, inside),
        scratch_shapes=[pltpu.SemaphoreType.DMA((2,))],
    )(*[pltpu.with_memory_space_constraint(result, pltpu.VMEM) for result in results])


def solution(mesh):
    placed = (P("src", "tile"), P(None, "tile"), P("src", None), P("src"))
    return jax.shard_map(
        local,
        mesh=mesh,
        in_specs=placed,
        out_specs=(P("src", "tile"), P("src", "tile"), P("src")),
        check_vma=False,
    )
```

```python
import functools

import jax
import jax.numpy as jnp
import ml_dtypes
import numpy as np
from jax import lax
from jax.experimental import pallas as pl
from jax.experimental.pallas import tpu as pltpu
from jax.sharding import PartitionSpec as P

TILE = 256
MARGIN = 32
BAND = 64
RAD = 16
EXT = 320
STEEP = 8.0
THRESH = 0.25
LOSS_SCALE = 2.0

N_SRC = 16
N_TILE = 32
PER_DEV = 8
SOURCES = 128
ROWS = 16
HALF = 32
ROWS_C = 80
COLS_C = 128
QUAD = 4
GROUP = 4
DEPTH = 8
HUB = 2 * GROUP

MESH = pl.DeviceIdType.MESH
BF16 = ml_dtypes.bfloat16


def halves(table):
    high = table.astype(BF16)
    low = (table - high.astype(np.float64)).astype(BF16)
    return high, low


def column_slots():
    plus = np.arange(HALF)
    return np.concatenate([plus, -plus]), np.concatenate([np.ones(HALF), [0.0], np.ones(HALF - 1)])


def waves(freq, place, period):
    phase = 2.0 * np.pi * ((freq[:, None] * place[None, :]) % period) / period
    return np.cos(phase), np.sin(phase)


def interpolation(points):
    order = np.arange(-2 * RAD, 2 * RAD + 1)
    place = np.arange(TILE) + MARGIN
    offset = place[:, None] / EXT - np.arange(points)[None, :] / points
    return np.cos(2.0 * np.pi * order[None, None, :] * offset[:, :, None]).sum(axis=2) / points


def build_tables():
    slots, used = column_slots()
    row_freq = np.arange(BAND) - BAND // 2
    pixels = np.arange(TILE) + MARGIN
    parts = {}

    real, imag = waves(np.arange(HALF), np.arange(EXT), EXT)
    fwd = np.concatenate([real, -imag], axis=0).T / EXT
    wide = np.zeros((2 * TILE, 2 * HALF))
    wide[:TILE] = fwd[MARGIN : MARGIN + TILE]
    wide[TILE + 96 : TILE + 128] = fwd[:MARGIN]
    wide[TILE + 128 : TILE + 160] = fwd[MARGIN + TILE :]
    high, low = halves(np.concatenate([wide, wide], axis=1))
    parts["enter"] = np.concatenate([high, low], axis=1)

    rows = np.arange(TILE).reshape(N_SRC, 2, 8)
    first, second = rows[:, 0].reshape(-1), rows[:, 1].reshape(-1)
    real, imag = waves(row_freq, pixels, EXT)
    real, imag = real / EXT, -imag / EXT
    both = np.concatenate([real, imag], axis=0)
    high, low = halves(np.concatenate([both[:, first], both[:, second]], axis=0))
    parts["spec"] = np.concatenate([high, high], axis=1)
    spec_low = low

    inter_rows, inter_cols = 2.0 * interpolation(ROWS_C), interpolation(COLS_C)
    even, odd = np.arange(0, COLS_C, 2), np.arange(1, COLS_C, 2)
    for name, order in (("even", np.concatenate([even, odd])), ("odd", np.concatenate([odd, even]))):
        real, imag = waves(slots, order, COLS_C)
        real, imag = real * used[:, None], imag * used[:, None]
        cols = np.concatenate(
            [np.concatenate([real, imag], axis=1), np.concatenate([-imag, real], axis=1)], axis=0
        )
        high, low = halves(cols)
        parts["cols_" + name] = np.concatenate([high, high], axis=0)
        parts["cols_low_" + name] = low
        high, low = halves(np.concatenate([cols[:, :COLS_C].T, cols[:, COLS_C:].T], axis=0))
        parts["cols_back_" + name] = np.concatenate([high, low], axis=1)

    lows = []
    for name, start in (("even", 0), ("odd", 1)):
        real, imag = waves(row_freq, np.arange(start, ROWS_C, 2), ROWS_C)
        real, imag = real.T, imag.T
        high, low = halves(
            np.concatenate(
                [np.concatenate([real, -imag], axis=1), np.concatenate([imag, real], axis=1)], axis=0
            )
        )
        parts["rows_" + name] = np.concatenate([high, high], axis=1)
        lows.append(low)
        pad = np.zeros((2 * BAND, TILE - 3 * ROWS_C), BF16)
        parts["rows_back_" + name] = np.concatenate([high.T, high.T, low.T, pad], axis=1)
    rows_low = np.concatenate(lows, axis=0)

    mixed = np.concatenate([np.arange(0, ROWS_C, 2), np.arange(1, ROWS_C, 2)])
    inter_rows, inter_cols = inter_rows[:, mixed], inter_cols[:, np.concatenate([even, odd])]
    high, low = halves(inter_rows)
    pad = np.zeros((TILE, TILE - 3 * ROWS_C), BF16)
    parts["fine_rows"] = np.concatenate([high, high, low, pad], axis=1)
    high, low = halves(inter_cols.T)
    parts["fine_cols"] = np.concatenate([high, high], axis=0)
    parts["fine_cols_low"] = low
    parts["coarse_cols"] = np.concatenate([high.T, low.T], axis=1)
    high, low = halves(inter_rows.T)
    parts["coarse_rows"] = high
    parts["coarse_rows_low"] = low

    high, low = halves(np.concatenate([both[:, first], both[:, second]], axis=1).T)
    parts["leave"] = np.concatenate([high, high], axis=1)
    leave_low = low
    last = fwd[MARGIN : MARGIN + TILE].T
    high, low = halves(np.concatenate([last, last], axis=0))
    parts["last"] = high
    parts["last_low"] = low

    parts["lows_a"] = np.concatenate([spec_low, np.zeros((TILE, 128), BF16)], axis=1)
    rows_low = np.concatenate([rows_low, np.zeros((TILE - 2 * ROWS_C, 128), BF16)], axis=0)
    parts["lows_b"] = np.concatenate([leave_low, rows_low], axis=1)

    order = [
        "enter",
        "spec", "lows_a", "cols_even", "cols_low_even", "cols_odd", "cols_low_odd", "rows_even", "rows_odd", "lows_b",
        "fine_rows", "fine_cols", "fine_cols_low", "coarse_cols", "coarse_rows", "coarse_rows_low",
        "rows_back_even", "rows_back_odd", "cols_back_even", "cols_back_odd", "leave", "last", "last_low",
    ]
    places, start = {}, 0
    for name in order:
        places[name] = (start, parts[name].shape[0])
        start += parts[name].shape[0]
    return np.concatenate([parts[name] for name in order], axis=0), places


TABLE, PLACES = build_tables()
CUTS = (0, PLACES["spec"][0], PLACES["fine_rows"][0], TABLE.shape[0])


def dot(left, right):
    return jnp.dot(left, right, preferred_element_type=jnp.float32)


def cut(value):
    high = value.astype(jnp.bfloat16)
    low = (value - high.astype(jnp.float32)).astype(jnp.bfloat16)
    return high, low


def lanes(shape):
    return lax.broadcasted_iota(jnp.int32, shape, 1)


def enter(value, table):
    high, low = cut(value)
    both = dot(high, table)
    return both[:, :128] + both[:, 128:] + dot(low, table[:, :128])


def pack(first, second):
    return jnp.where(lanes(first.shape) < 64, first, second)


def spectrum(gathered, table, low_table, roll):
    high, low = cut(gathered)
    out = dot(table, jnp.concatenate([high, low], axis=0)) + dot(low_table, high)
    both = pack(out[:128], out[128:])
    both = both + roll(both, 64, 1)
    turned = roll(both, 32, 1)
    quarter = lanes((BAND, 128)) >> 5
    outer = (quarter == 0) | (quarter == 3)
    even = jnp.where(outer, both[:BAND], turned[:BAND])
    odd = jnp.where(outer, turned[BAND:], both[BAND:])
    return jnp.where(quarter == 3, -even, even) + jnp.where(quarter == 0, -odd, odd)


def pupil_of(row_shift, col_shift):
    shape = (BAND, 128)
    row = lax.broadcasted_iota(jnp.int32, shape, 0) - BAND // 2 + row_shift
    slot = lanes(shape) & 63
    col = jnp.where(slot < HALF, slot, HALF - slot) + col_shift
    inside = (row * row + col * col <= RAD * RAD) & (slot != HALF)
    return inside.astype(jnp.float32)


def swap(first, second):
    return pack(first, second), pack(second, first)


def coarse_fields(spec, pupils, cols, rows):
    high, low = cut(spec)
    mids = []
    for which in range(2):
        band_high = jnp.concatenate([high * pupil for pupil in pupils[which::2]], axis=0)
        band_low = jnp.concatenate([low * pupil for pupil in pupils[which::2]], axis=0)
        table, low_table = cols[which]
        mids.append(
            dot(jnp.concatenate([band_high, band_low], axis=1), table) + dot(band_high, low_table)
        )
    fields = []
    for group in range(2):
        stacks = ([], [])
        for pair in (2 * group, 2 * group + 1):
            at = slice(BAND * pair, BAND * pair + BAND)
            real = swap(mids[0][at, :128], mids[1][at, :128])
            imag = swap(mids[0][at, 128:], mids[1][at, 128:])
            for parity in range(2):
                stacks[parity].append(jnp.concatenate([real[parity], imag[parity]], axis=0))
        both = []
        for parity in range(2):
            upper, lower = cut(jnp.concatenate(stacks[parity], axis=1))
            table, low_table = rows[parity]
            both.append(dot(table, jnp.concatenate([upper, lower], axis=0)) + dot(low_table, upper))
        fields.append(both)
    return fields


def power_of(field):
    half = ROWS_C // 2
    return field[:half] * field[:half] + field[half:] * field[half:]


def join_image(even, odd, roll):
    return pack(even + roll(even, 64, 1), odd + roll(odd, 64, 1))


def pixels_of(coarse, fine_rows, fine_cols, fine_cols_low):
    first = lanes(coarse.shape) < 64
    coarse = jnp.concatenate([jnp.where(first, coarse, 0.0), jnp.where(first, 0.0, coarse)], axis=0)
    high, low = cut(coarse)
    mid = dot(jnp.concatenate([high, low], axis=1), fine_cols) + dot(high, fine_cols_low)
    return dot(fine_rows, three(mid))


def three(value):
    high, low = cut(value)
    pad = jnp.zeros((TILE - 3 * value.shape[0], value.shape[1]), jnp.bfloat16)
    return jnp.concatenate([high, low, high, pad], axis=0)


def coarse_of(slope, coarse_rows, coarse_rows_low, coarse_cols):
    high, low = cut(slope)
    mid = dot(coarse_rows, high) + dot(coarse_rows, low) + dot(coarse_rows_low, high)
    high, low = cut(mid)
    both = dot(high, coarse_cols)
    return both[:, :128] + both[:, 128:] + dot(low, coarse_cols[:, :128])


def twice(coarse, roll):
    half = ROWS_C // 2
    even, odd = coarse[:half], coarse[half:]
    return pack(even, roll(even, 64, 1)), pack(roll(odd, 64, 1), odd)


def band_grad(total, adjoints, pupils, rows_back, cols_back):
    sides = ([], [])
    for group in range(2):
        even, odd = [dot(rows_back[parity], three(adjoints[group][parity])) for parity in range(2)]
        for pair in range(2):
            at = slice(128 * pair, 128 * pair + 128)
            real = swap(even[:BAND, at], odd[:BAND, at])
            imag = swap(even[BAND:, at], odd[BAND:, at])
            for which in range(2):
                sides[which].append(jnp.concatenate([real[which], imag[which]], axis=1))
    for which in range(2):
        high, low = cut(jnp.concatenate(sides[which], axis=0))
        both = dot(high, cols_back[which])
        term = both[:, :128] + both[:, 128:] + dot(low, cols_back[which][:, :128])
        for k in range(PER_DEV // 2):
            total = total + term[BAND * k : BAND * k + BAND] * pupils[2 * k + which]
    return total


def fold(grad, roll):
    r32, r64, r96 = roll(grad, 32, 1), roll(grad, 64, 1), roll(grad, 96, 1)
    quarter = lanes(grad.shape) >> 5
    upper = jnp.where(
        quarter == 0, grad + r96, jnp.where(quarter == 1, r96 - r64, jnp.where(quarter == 2, r64 + r32, r32 - grad))
    )
    lower = jnp.where(
        quarter == 0, r64 + r32, jnp.where(quarter == 1, grad - r32, jnp.where(quarter == 2, grad + r96, r64 - r96))
    )
    return jnp.concatenate([upper, lower], axis=0)


def row_grads(grad, leave, leave_low, roll):
    high, low = cut(fold(grad, roll))
    out = dot(leave, jnp.concatenate([high, low], axis=0)) + dot(leave_low, high)
    half = out.shape[0] // 2
    return pack(out[:half], out[half:])


def last_step(total, last, last_low):
    first = lanes(total.shape) < 64
    value = jnp.concatenate([jnp.where(first, total, 0.0), jnp.where(first, 0.0, total)], axis=0)
    high, low = cut(value)
    return dot(high, last) + dot(low, last) + dot(high, last_low)


def rank_of(side, along):
    step = jnp.where(along <= DEPTH // 2, 2 * along - 1, 2 * (DEPTH - along))
    return 2 * jnp.maximum(step, 0) + side


def src_of(rank):
    step, side = rank // 2, rank % 2
    half = (step + 1) // 2
    return side * DEPTH + jnp.where(step % 2 == 1, half, (DEPTH - half) % DEPTH)


def repeat(first, last, body):
    def step(k, carry):
        body(k)
        return carry

    lax.fori_loop(first, last, step, 0)


def everything(mask, target, shifts, weights, table, resist, mask_grad, source_grad, *scratch):
    (
        mask_v, target_v, shifts_v, weights_v, table_v,
        left_v, right_v, spec_v, pupil_v, scale_v, image_v, term_v, field_v, power_v,
        printed_v, grad_v, part_v, sums_v, total_v, local_sem, send_sem, recv_sem, ready_sem, hub_sem,
    ) = scratch
    tile, src = lax.axis_index("tile"), lax.axis_index("src")
    n_tile = lax.axis_size("tile")
    left, right = tile - 1, tile + 1
    has_left, has_right = tile > 0, tile < n_tile - 1
    side, along = src // DEPTH, src % DEPTH
    rank = rank_of(side, along)
    quad = along // QUAD
    partners = [
        (side + across) % 2 * DEPTH + (along + step) % DEPTH for across, step in ((0, QUAD), (1, 0), (1, QUAD))
    ]
    members = [side * DEPTH + quad * QUAD + (along + k) % QUAD for k in range(1, QUAD)]
    layer = tile // GROUP
    place = tile % GROUP
    is_hub, is_teller = tile < HUB, layer == 1

    def get(name, start=None, stop=None):
        at, size = PLACES[name]
        if start is None:
            return table_v[at : at + size, :]
        return table_v[at : at + size, start:stop]

    def signal(sem, device):
        pl.semaphore_signal(sem, inc=1, device_id=device, device_id_type=MESH)

    def send(source, target_ref, number, device):
        copy = pltpu.make_async_remote_copy(
            src_ref=source,
            dst_ref=target_ref,
            send_sem=send_sem.at[number],
            recv_sem=recv_sem.at[number],
            device_id=device,
            device_id_type=MESH,
        )
        copy.start()

    def wait(ref, sem):
        pltpu.make_async_copy(ref, ref, sem).wait()

    barrier = pltpu.get_barrier_semaphore()

    @pl.when(has_left)
    def _():
        signal(barrier, {"tile": left})

    @pl.when(has_right)
    def _():
        signal(barrier, {"tile": right})

    repeat(rank + 1, N_SRC, lambda k: signal(barrier, {"src": src_of(k)}))
    local = [
        pltpu.make_async_copy(mask, mask_v, local_sem.at[0]),
        pltpu.make_async_copy(shifts, shifts_v, local_sem.at[1]),
        pltpu.make_async_copy(weights, weights_v, local_sem.at[2]),
    ]
    for k in range(3):
        rows = pl.ds(CUTS[k], CUTS[k + 1] - CUTS[k])
        local.append(pltpu.make_async_copy(table.at[rows], table_v.at[rows], local_sem.at[3 + k]))
    local.append(pltpu.make_async_copy(target, target_v, local_sem.at[6]))
    for copy in local:
        copy.start()
    repeat(jnp.where(is_hub, tile + 1, n_tile), n_tile, lambda k: signal(barrier, {"tile": k}))

    ends = has_left.astype(jnp.int32) + has_right.astype(jnp.int32)
    pl.semaphore_wait(barrier, rank + ends + jnp.minimum(tile, HUB))

    @pl.when(has_right)
    def _():
        send(mask.at[:, pl.ds(128, 128)], left_v, 0, {"tile": right})

    @pl.when(has_left)
    def _():
        send(mask.at[:, pl.ds(0, 128)], right_v, 1, {"tile": left})

    repeat(0, rank, lambda k: signal(ready_sem.at[rank], {"src": src_of(k)}))

    @pl.when(jnp.logical_not(has_left))
    def _():
        left_v[...] = jnp.zeros_like(left_v)

    @pl.when(jnp.logical_not(has_right))
    def _():
        right_v[...] = jnp.zeros_like(right_v)

    local[1].wait()
    local[2].wait()
    spec_v[src, 8:16, :] = jnp.zeros((8, 128), jnp.float32)
    spec_v[src, 8:10, 0:PER_DEV] = shifts_v[...].astype(jnp.float32)
    spec_v[src, 10:11, 0:PER_DEV] = weights_v[...]
    local[0].wait()
    local[3].wait()
    at = PLACES["enter"][0]
    own = enter(mask_v[...], table_v[at : at + TILE, :])

    @pl.when(has_left)
    def _():
        wait(left_v, recv_sem.at[0])

    @pl.when(has_right)
    def _():
        wait(right_v, recv_sem.at[1])

    margins = jnp.concatenate([left_v[...], right_v[...]], axis=1)
    own = own + enter(margins, table_v[at + TILE : at + 2 * TILE, :])
    spec_v[src, 0:8, :] = pack(own[:8], own[8:])
    piece = pl.ds(0, 11)

    def send_piece(k):
        send(spec_v.at[src, piece], spec_v.at[src, piece], 2, {"src": src_of(k)})

    def answer_piece(k):
        pl.semaphore_wait(ready_sem.at[k], 1)
        send_piece(k)

    repeat(0, rank, send_piece)
    repeat(rank + 1, N_SRC, answer_piece)
    repeat(0, jnp.where(is_hub, tile, 0), lambda k: signal(hub_sem.at[0], {"tile": k}))

    @pl.when(jnp.logical_not(is_hub))
    def _():
        signal(hub_sem.at[1], {"tile": GROUP + place})

    local[4].wait()
    wait(spec_v.at[pl.ds(0, N_SRC - 1), piece], recv_sem.at[2])

    gathered = spec_v[:, 0:8, :].reshape(128, 128)
    spec = spectrum(gathered, get("spec"), get("lows_a", 0, 128), pltpu.roll)
    at = PLACES["lows_b"][0]
    cols = [(get("cols_" + name), get("cols_low_" + name)) for name in ("even", "odd")]
    rows = [
        (get("rows_even"), table_v[at : at + ROWS_C, 128:256]),
        (get("rows_odd"), table_v[at + ROWS_C : at + 2 * ROWS_C, 128:256]),
    ]

    def add_fields(part, images):
        owner = src
        for k, peer in enumerate(partners):
            owner = jnp.where(part == k + 1, peer, owner)
        extra = spec_v[owner, 8:16, :]
        shift = extra[0:2, :].astype(jnp.int32)
        for s in range(PER_DEV):
            pupil_v[part, s] = pupil_of(shift[0:1, s : s + 1], shift[1:2, s : s + 1])
        for pair in range(PER_DEV // 2):
            first, second = [
                jnp.broadcast_to(extra[2:3, s : s + 1], (8, 128)) for s in (2 * pair, 2 * pair + 1)
            ]
            at = slice(128 * (pair % 2), 128 * (pair % 2) + 128)
            for parity, scale in enumerate(swap(first, second)):
                scale_v[part, pair // 2, parity, :, at] = scale
        fields = coarse_fields(
            spec, [pupil_v[part, s].astype(jnp.bfloat16) for s in range(PER_DEV)], cols, rows
        )
        images = list(images)
        for group in range(2):
            for parity in range(2):
                field_v[part, group, parity] = fields[group][parity]
                power = power_of(fields[group][parity])
                power_v[part, group, parity] = power
                power = power * scale_v[part, group, parity, 0:1, :]
                images[parity] = images[parity] + power[:, :128] + power[:, 128:]
        return tuple(images)

    none = jnp.zeros((ROWS_C // 2, 128), jnp.float32)
    image_v[...] = join_image(*lax.fori_loop(0, QUAD, add_fields, (none, none)), pltpu.roll)
    for k, peer in enumerate(members):
        send(image_v, term_v.at[k], 3, {"src": peer})
    local[5].wait()
    local[6].wait()
    wait(term_v, recv_sem.at[3])

    image = pixels_of(
        image_v[...] + term_v[0] + term_v[1] + term_v[2],
        get("fine_rows"),
        get("fine_cols"),
        get("fine_cols_low"),
    )
    printed = jax.nn.sigmoid(STEEP * (image * (1.0 / SOURCES) - THRESH))
    printed_v[...] = printed
    resist[...] = printed_v[pl.ds(pl.multiple_of(src * ROWS, ROWS), ROWS), :]
    goal = target_v[...].astype(jnp.float32)
    slope = (LOSS_SCALE * 2.0 * STEEP) * (printed - goal) * printed * (1.0 - printed)
    coarse = coarse_of(slope, get("coarse_rows"), get("coarse_rows_low"), get("coarse_cols"))

    slopes = twice(coarse, pltpu.roll)
    sums = []
    for pair in range(PER_DEV // 2):
        at = slice(128 * (pair % 2), 128 * (pair % 2) + 128)
        terms = [
            jnp.sum(slopes[parity] * power_v[0, pair // 2, parity, :, at], axis=0, keepdims=True) for parity in range(2)
        ]
        sums.extend(swap(*terms))
    sums = jnp.sum(jnp.concatenate(sums, axis=0), axis=1, keepdims=True)
    spot = (PER_DEV, 128)
    sums = jnp.where(lanes(spot) == lax.broadcasted_iota(jnp.int32, spot, 0), sums, 0.0)
    sums_v[tile] = jnp.sum(sums, axis=0, keepdims=True)

    def send_sums(k):
        pltpu.make_async_remote_copy(
            src_ref=sums_v.at[tile],
            dst_ref=sums_v.at[tile],
            send_sem=send_sem.at[5],
            recv_sem=recv_sem.at[5],
            device_id={"tile": k},
            device_id_type=MESH,
        ).start()

    repeat(0, jnp.minimum(tile, HUB), send_sums)

    wide = [jnp.concatenate([slope, slope], axis=1) * (2.0 / SOURCES) for slope in slopes]
    rows_back = [get("rows_back_even"), get("rows_back_odd")]
    cols_back = [get("cols_back_even"), get("cols_back_odd")]

    def add_part(part, total):
        adjoints = []
        for group in range(2):
            adjoints.append([])
            for parity in range(2):
                scaled = wide[parity] * scale_v[part, group, parity, 0:1, :]
                adjoints[group].append(field_v[part, group, parity] * jnp.concatenate([scaled, scaled], axis=0))
        return band_grad(total, adjoints, [pupil_v[part, s] for s in range(PER_DEV)], rows_back, cols_back)

    grad = lax.fori_loop(0, QUAD, add_part, jnp.zeros((BAND, 128), jnp.float32))
    first = PLACES["leave"][0] + 8 * QUAD * (src // QUAD)
    low_first = PLACES["lows_b"][0] + 8 * QUAD * (src // QUAD)

    def halves_of(start, stop, begin):
        begin = pl.multiple_of(begin, 32)
        then = pl.multiple_of(begin + 128, 32)
        return jnp.concatenate(
            [table_v[pl.ds(begin, 8 * QUAD), start:stop], table_v[pl.ds(then, 8 * QUAD), start:stop]], axis=0
        )

    rows = row_grads(grad, halves_of(0, 256, first), halves_of(0, 128, low_first), pltpu.roll)
    grad_v[...] = rows.reshape(QUAD, 8, 128)
    for k, peer in enumerate(members):
        send(grad_v.at[peer % QUAD], part_v.at[k], 4, {"src": peer})


    @pl.when(tile < HUB - 1)
    def _():
        pl.semaphore_wait(hub_sem.at[0], HUB - 1 - tile)
        repeat(tile + 1, HUB, send_sums)

    wait(part_v, recv_sem.at[4])
    total = grad_v[along % QUAD] + part_v[0] + part_v[1] + part_v[2]
    mask_grad[...] = last_step(total, get("last"), get("last_low"))

    @pl.when(is_hub)
    def _():
        wait(sums_v.at[pl.ds(0, n_tile - 1)], recv_sem.at[5])
        total_v[...] = jnp.sum(sums_v[...], axis=0) * (1.0 / (SOURCES * n_tile * TILE * TILE))

    def tell(k):
        send(total_v, total_v, 6, {"tile": k * GROUP + place})

    @pl.when(is_teller)
    def _():
        pl.semaphore_wait(hub_sem.at[1], n_tile // GROUP - 2)
        repeat(2, n_tile // GROUP, tell)

    @pl.when(jnp.logical_not(is_hub))
    def _():
        wait(total_v, recv_sem.at[6])

    source_grad[...] = total_v[...]

    @pl.when(is_teller)
    def _():
        wait(sums_v.at[pl.ds(0, n_tile // GROUP - 2)], send_sem.at[6])

    @pl.when(is_hub)
    def _():
        wait(sums_v.at[pl.ds(0, HUB - 1)], send_sem.at[5])

    @pl.when(jnp.logical_not(is_hub))
    def _():
        wait(sums_v.at[pl.ds(0, HUB)], send_sem.at[5])


    @pl.when(has_right)
    def _():
        wait(left_v, send_sem.at[0])

    @pl.when(has_left)
    def _():
        wait(right_v, send_sem.at[1])

    wait(spec_v.at[pl.ds(0, N_SRC - 1), piece], send_sem.at[2])
    wait(term_v, send_sem.at[3])
    wait(part_v, send_sem.at[4])


def hand_over(resist, mask_grad, source_grad, resist_out, mask_grad_out, source_grad_out, sem):
    copies = [
        pltpu.make_async_copy(resist, resist_out, sem.at[0]),
        pltpu.make_async_copy(mask_grad, mask_grad_out, sem.at[1]),
    ]
    for copy in copies:
        copy.start()
    source_grad_out[...] = source_grad[0, :PER_DEV]
    for copy in copies:
        copy.wait()


def local(mask, target, shifts, weights):
    f32 = jnp.float32
    anywhere = pl.BlockSpec(memory_space=pl.ANY)
    inside = pl.BlockSpec(memory_space=pltpu.VMEM)
    results = pl.pallas_call(
        everything,
        out_shape=(
            pltpu.VMEM((ROWS, TILE), f32),
            pltpu.VMEM((ROWS, TILE), f32),
            pltpu.VMEM((1, 128), f32),
        ),
        in_specs=[anywhere] * 5,
        out_specs=(inside, inside, inside),
        scratch_shapes=[
            pltpu.VMEM((ROWS, TILE), f32),
            pltpu.VMEM((TILE, TILE), jnp.int32),
            pltpu.VMEM((2, PER_DEV), jnp.int32),
            pltpu.VMEM((1, PER_DEV), f32),
            pltpu.VMEM(TABLE.shape, jnp.bfloat16),
            pltpu.VMEM((ROWS, 128), f32),
            pltpu.VMEM((ROWS, 128), f32),
            pltpu.VMEM((N_SRC, 16, 128), f32),
            pltpu.VMEM((QUAD, PER_DEV, BAND, 128), f32),
            pltpu.VMEM((QUAD, 2, 2, 8, 256), f32),
            pltpu.VMEM((ROWS_C // 2, 128), f32),
            pltpu.VMEM((QUAD - 1, ROWS_C // 2, 128), f32),
            pltpu.VMEM((QUAD, 2, 2, ROWS_C, 256), f32),
            pltpu.VMEM((QUAD, 2, 2, ROWS_C // 2, 256), f32),
            pltpu.VMEM((TILE, TILE), f32),
            pltpu.VMEM((QUAD, 8, 128), f32),
            pltpu.VMEM((QUAD - 1, 8, 128), f32),
            pltpu.VMEM((N_TILE, 1, 128), f32),
            pltpu.VMEM((1, 128), f32),
            pltpu.SemaphoreType.DMA((7,)),
            pltpu.SemaphoreType.DMA((7,)),
            pltpu.SemaphoreType.DMA((7,)),
            pltpu.SemaphoreType.REGULAR((N_SRC,)),
            pltpu.SemaphoreType.REGULAR((2,)),
        ],
        compiler_params=pltpu.CompilerParams(
            collective_id=0, has_side_effects=True, vmem_limit_bytes=60 * 1024 * 1024
        ),
    )(mask, target, shifts.T, weights.reshape(1, PER_DEV), jnp.asarray(TABLE))
    return pl.pallas_call(
        hand_over,
        out_shape=(
            jax.ShapeDtypeStruct((ROWS, TILE), f32),
            jax.ShapeDtypeStruct((ROWS, TILE), f32),
            jax.ShapeDtypeStruct((PER_DEV,), f32),
        ),
        in_specs=[inside] * 3,
        out_specs=(anywhere, anywhere, inside),
        scratch_shapes=[pltpu.SemaphoreType.DMA((2,))],
    )(*[pltpu.with_memory_space_constraint(result, pltpu.VMEM) for result in results])


def solution(mesh):
    placed = (P("src", "tile"), P(None, "tile"), P("src", None), P("src"))
    return jax.shard_map(
        local,
        mesh=mesh,
        in_specs=placed,
        out_specs=(P("src", "tile"), P("src", "tile"), P("src")),
        check_vma=False,
    )
```

```python
import functools

import jax
import jax.numpy as jnp
import ml_dtypes
import numpy as np
from jax import lax
from jax.experimental import pallas as pl
from jax.experimental.pallas import tpu as pltpu
from jax.sharding import PartitionSpec as P

TILE = 256
MARGIN = 32
BAND = 64
RAD = 16
EXT = 320
STEEP = 8.0
THRESH = 0.25
LOSS_SCALE = 2.0

N_SRC = 16
N_TILE = 32
PER_DEV = 8
SOURCES = 128
ROWS = 16
HALF = 32
ROWS_C = 80
COLS_C = 128
QUAD = 4
GROUP = 4
DEPTH = 8
HUB = 2 * GROUP

MESH = pl.DeviceIdType.MESH
BF16 = ml_dtypes.bfloat16


def halves(table):
    high = table.astype(BF16)
    low = (table - high.astype(np.float64)).astype(BF16)
    return high, low


def column_slots():
    plus = np.arange(HALF)
    return np.concatenate([plus, -plus]), np.concatenate([np.ones(HALF), [0.0], np.ones(HALF - 1)])


def waves(freq, place, period):
    phase = 2.0 * np.pi * ((freq[:, None] * place[None, :]) % period) / period
    return np.cos(phase), np.sin(phase)


def interpolation(points):
    order = np.arange(-2 * RAD, 2 * RAD + 1)
    place = np.arange(TILE) + MARGIN
    offset = place[:, None] / EXT - np.arange(points)[None, :] / points
    return np.cos(2.0 * np.pi * order[None, None, :] * offset[:, :, None]).sum(axis=2) / points


def build_tables():
    slots, used = column_slots()
    row_freq = np.arange(BAND) - BAND // 2
    pixels = np.arange(TILE) + MARGIN
    parts = {}

    real, imag = waves(np.arange(HALF), np.arange(EXT), EXT)
    fwd = np.concatenate([real, -imag], axis=0).T / EXT
    wide = np.zeros((2 * TILE, 2 * HALF))
    wide[:TILE] = fwd[MARGIN : MARGIN + TILE]
    wide[TILE + 96 : TILE + 128] = fwd[:MARGIN]
    wide[TILE + 128 : TILE + 160] = fwd[MARGIN + TILE :]
    high, low = halves(np.concatenate([wide, wide], axis=1))
    parts["enter"] = np.concatenate([high, low], axis=1)

    rows = np.arange(TILE).reshape(N_SRC, 2, 8)
    first, second = rows[:, 0].reshape(-1), rows[:, 1].reshape(-1)
    real, imag = waves(row_freq, pixels, EXT)
    real, imag = real / EXT, -imag / EXT
    both = np.concatenate([real, imag], axis=0)
    high, low = halves(np.concatenate([both[:, first], both[:, second]], axis=0))
    parts["spec"] = np.concatenate([high, high], axis=1)
    spec_low = low

    inter_rows, inter_cols = 2.0 * interpolation(ROWS_C), interpolation(COLS_C)
    even, odd = np.arange(0, COLS_C, 2), np.arange(1, COLS_C, 2)
    for name, order in (("even", np.concatenate([even, odd])), ("odd", np.concatenate([odd, even]))):
        real, imag = waves(slots, order, COLS_C)
        real, imag = real * used[:, None], imag * used[:, None]
        cols = np.concatenate(
            [np.concatenate([real, imag], axis=1), np.concatenate([-imag, real], axis=1)], axis=0
        )
        high, low = halves(cols)
        parts["cols_" + name] = np.concatenate([high, high], axis=0)
        parts["cols_low_" + name] = low
        high, low = halves(np.concatenate([cols[:, :COLS_C].T, cols[:, COLS_C:].T], axis=0))
        parts["cols_back_" + name] = np.concatenate([high, low], axis=1)

    lows = []
    for name, start in (("even", 0), ("odd", 1)):
        real, imag = waves(row_freq, np.arange(start, ROWS_C, 2), ROWS_C)
        real, imag = real.T, imag.T
        high, low = halves(
            np.concatenate(
                [np.concatenate([real, -imag], axis=1), np.concatenate([imag, real], axis=1)], axis=0
            )
        )
        parts["rows_" + name] = np.concatenate([high, high], axis=1)
        lows.append(low)
        pad = np.zeros((2 * BAND, TILE - 3 * ROWS_C), BF16)
        parts["rows_back_" + name] = np.concatenate([high.T, high.T, low.T, pad], axis=1)
    rows_low = np.concatenate(lows, axis=0)

    mixed = np.concatenate([np.arange(0, ROWS_C, 2), np.arange(1, ROWS_C, 2)])
    inter_rows, inter_cols = inter_rows[:, mixed], inter_cols[:, np.concatenate([even, odd])]
    high, low = halves(inter_rows)
    pad = np.zeros((TILE, TILE - 3 * ROWS_C), BF16)
    parts["fine_rows"] = np.concatenate([high, high, low, pad], axis=1)
    high, low = halves(inter_cols.T)
    parts["fine_cols"] = np.concatenate([high, high], axis=0)
    parts["fine_cols_low"] = low
    parts["coarse_cols"] = np.concatenate([high.T, low.T], axis=1)
    high, low = halves(inter_rows.T)
    parts["coarse_rows"] = high
    parts["coarse_rows_low"] = low

    high, low = halves(np.concatenate([both[:, first], both[:, second]], axis=1).T)
    parts["leave"] = np.concatenate([high, high], axis=1)
    leave_low = low
    last = fwd[MARGIN : MARGIN + TILE].T
    high, low = halves(np.concatenate([last, last], axis=0))
    parts["last"] = high
    parts["last_low"] = low

    parts["lows_a"] = np.concatenate([spec_low, np.zeros((TILE, 128), BF16)], axis=1)
    rows_low = np.concatenate([rows_low, np.zeros((TILE - 2 * ROWS_C, 128), BF16)], axis=0)
    parts["lows_b"] = np.concatenate([leave_low, rows_low], axis=1)

    order = [
        "enter",
        "spec", "lows_a", "cols_even", "cols_low_even", "cols_odd", "cols_low_odd", "rows_even", "rows_odd", "lows_b",
        "fine_rows", "fine_cols", "fine_cols_low", "coarse_cols", "coarse_rows", "coarse_rows_low",
        "rows_back_even", "rows_back_odd", "cols_back_even", "cols_back_odd", "leave", "last", "last_low",
    ]
    places, start = {}, 0
    for name in order:
        places[name] = (start, parts[name].shape[0])
        start += parts[name].shape[0]
    return np.concatenate([parts[name] for name in order], axis=0), places


TABLE, PLACES = build_tables()
CUTS = (0, PLACES["spec"][0], PLACES["fine_rows"][0], TABLE.shape[0])


def dot(left, right):
    return jnp.dot(left, right, preferred_element_type=jnp.float32)


def cut(value):
    high = value.astype(jnp.bfloat16)
    low = (value - high.astype(jnp.float32)).astype(jnp.bfloat16)
    return high, low


def lanes(shape):
    return lax.broadcasted_iota(jnp.int32, shape, 1)


def enter(value, table):
    high, low = cut(value)
    both = dot(high, table)
    return both[:, :128] + both[:, 128:] + dot(low, table[:, :128])


def pack(first, second):
    return jnp.where(lanes(first.shape) < 64, first, second)


def spectrum(gathered, table, low_table, roll):
    high, low = cut(gathered)
    out = dot(table, jnp.concatenate([high, low], axis=0)) + dot(low_table, high)
    both = pack(out[:128], out[128:])
    both = both + roll(both, 64, 1)
    turned = roll(both, 32, 1)
    quarter = lanes((BAND, 128)) >> 5
    outer = (quarter == 0) | (quarter == 3)
    even = jnp.where(outer, both[:BAND], turned[:BAND])
    odd = jnp.where(outer, turned[BAND:], both[BAND:])
    return jnp.where(quarter == 3, -even, even) + jnp.where(quarter == 0, -odd, odd)


def pupil_of(row_shift, col_shift):
    shape = (BAND, 128)
    row = lax.broadcasted_iota(jnp.int32, shape, 0) - BAND // 2 + row_shift
    slot = lanes(shape) & 63
    col = jnp.where(slot < HALF, slot, HALF - slot) + col_shift
    inside = (row * row + col * col <= RAD * RAD) & (slot != HALF)
    return inside.astype(jnp.float32)


def swap(first, second):
    return pack(first, second), pack(second, first)


def coarse_fields(spec, pupils, cols, rows):
    high, low = cut(spec)
    mids = []
    for which in range(2):
        band_high = jnp.concatenate([high * pupil for pupil in pupils[which::2]], axis=0)
        band_low = jnp.concatenate([low * pupil for pupil in pupils[which::2]], axis=0)
        table, low_table = cols[which]
        mids.append(
            dot(jnp.concatenate([band_high, band_low], axis=1), table) + dot(band_high, low_table)
        )
    fields = []
    for group in range(2):
        stacks = ([], [])
        for pair in (2 * group, 2 * group + 1):
            at = slice(BAND * pair, BAND * pair + BAND)
            real = swap(mids[0][at, :128], mids[1][at, :128])
            imag = swap(mids[0][at, 128:], mids[1][at, 128:])
            for parity in range(2):
                stacks[parity].append(jnp.concatenate([real[parity], imag[parity]], axis=0))
        both = []
        for parity in range(2):
            upper, lower = cut(jnp.concatenate(stacks[parity], axis=1))
            table, low_table = rows[parity]
            both.append(dot(table, jnp.concatenate([upper, lower], axis=0)) + dot(low_table, upper))
        fields.append(both)
    return fields


def power_of(field):
    half = ROWS_C // 2
    return field[:half] * field[:half] + field[half:] * field[half:]


def join_image(even, odd, roll):
    return pack(even + roll(even, 64, 1), odd + roll(odd, 64, 1))


def pixels_of(coarse, fine_rows, fine_cols, fine_cols_low):
    first = lanes(coarse.shape) < 64
    coarse = jnp.concatenate([jnp.where(first, coarse, 0.0), jnp.where(first, 0.0, coarse)], axis=0)
    high, low = cut(coarse)
    mid = dot(jnp.concatenate([high, low], axis=1), fine_cols) + dot(high, fine_cols_low)
    return dot(fine_rows, three(mid))


def three(value):
    high, low = cut(value)
    pad = jnp.zeros((TILE - 3 * value.shape[0], value.shape[1]), jnp.bfloat16)
    return jnp.concatenate([high, low, high, pad], axis=0)


def coarse_of(slope, coarse_rows, coarse_rows_low, coarse_cols):
    high, low = cut(slope)
    mid = dot(coarse_rows, high) + dot(coarse_rows, low) + dot(coarse_rows_low, high)
    high, low = cut(mid)
    both = dot(high, coarse_cols)
    return both[:, :128] + both[:, 128:] + dot(low, coarse_cols[:, :128])


def twice(coarse, roll):
    half = ROWS_C // 2
    even, odd = coarse[:half], coarse[half:]
    return pack(even, roll(even, 64, 1)), pack(roll(odd, 64, 1), odd)


def band_grad(total, adjoints, pupils, rows_back, cols_back):
    sides = ([], [])
    for group in range(2):
        even, odd = [dot(rows_back[parity], three(adjoints[group][parity])) for parity in range(2)]
        for pair in range(2):
            at = slice(128 * pair, 128 * pair + 128)
            real = swap(even[:BAND, at], odd[:BAND, at])
            imag = swap(even[BAND:, at], odd[BAND:, at])
            for which in range(2):
                sides[which].append(jnp.concatenate([real[which], imag[which]], axis=1))
    for which in range(2):
        high, low = cut(jnp.concatenate(sides[which], axis=0))
        both = dot(high, cols_back[which])
        term = both[:, :128] + both[:, 128:] + dot(low, cols_back[which][:, :128])
        for k in range(PER_DEV // 2):
            total = total + term[BAND * k : BAND * k + BAND] * pupils[2 * k + which]
    return total


def fold(grad, roll):
    r32, r64, r96 = roll(grad, 32, 1), roll(grad, 64, 1), roll(grad, 96, 1)
    quarter = lanes(grad.shape) >> 5
    upper = jnp.where(
        quarter == 0, grad + r96, jnp.where(quarter == 1, r96 - r64, jnp.where(quarter == 2, r64 + r32, r32 - grad))
    )
    lower = jnp.where(
        quarter == 0, r64 + r32, jnp.where(quarter == 1, grad - r32, jnp.where(quarter == 2, grad + r96, r64 - r96))
    )
    return jnp.concatenate([upper, lower], axis=0)


def row_grads(grad, leave, leave_low, roll):
    high, low = cut(fold(grad, roll))
    out = dot(leave, jnp.concatenate([high, low], axis=0)) + dot(leave_low, high)
    half = out.shape[0] // 2
    return pack(out[:half], out[half:])


def last_step(total, last, last_low):
    first = lanes(total.shape) < 64
    value = jnp.concatenate([jnp.where(first, total, 0.0), jnp.where(first, 0.0, total)], axis=0)
    high, low = cut(value)
    return dot(high, last) + dot(low, last) + dot(high, last_low)


def rank_of(side, along):
    step = jnp.where(along <= DEPTH // 2, 2 * along - 1, 2 * (DEPTH - along))
    return 2 * jnp.maximum(step, 0) + side


def src_of(rank):
    step, side = rank // 2, rank % 2
    half = (step + 1) // 2
    return side * DEPTH + jnp.where(step % 2 == 1, half, (DEPTH - half) % DEPTH)


def repeat(first, last, body):
    def step(k, carry):
        body(k)
        return carry

    lax.fori_loop(first, last, step, 0)


def everything(mask, target, shifts, weights, table, resist, mask_grad, source_grad, *scratch):
    (
        mask_v, target_v, shifts_v, weights_v, table_v,
        left_v, right_v, spec_v, pupil_v, scale_v, image_v, term_v, field_v, power_v,
        printed_v, grad_v, part_v, sums_v, total_v, local_sem, send_sem, recv_sem, ready_sem, hub_sem,
    ) = scratch
    tile, src = lax.axis_index("tile"), lax.axis_index("src")
    n_tile = lax.axis_size("tile")
    left, right = tile - 1, tile + 1
    has_left, has_right = tile > 0, tile < n_tile - 1
    side, along = src // DEPTH, src % DEPTH
    rank = rank_of(side, along)
    quad = along // QUAD
    partners = [
        (side + across) % 2 * DEPTH + (along + step) % DEPTH for across, step in ((0, QUAD), (1, 0), (1, QUAD))
    ]
    members = [side * DEPTH + quad * QUAD + (along + k) % QUAD for k in range(1, QUAD)]
    layer = tile // GROUP
    place = tile % GROUP
    is_hub, is_teller = tile < HUB, layer == 1

    def get(name, start=None, stop=None):
        at, size = PLACES[name]
        if start is None:
            return table_v[at : at + size, :]
        return table_v[at : at + size, start:stop]

    def signal(sem, device):
        pl.semaphore_signal(sem, inc=1, device_id=device, device_id_type=MESH)

    def send(source, target_ref, number, device):
        copy = pltpu.make_async_remote_copy(
            src_ref=source,
            dst_ref=target_ref,
            send_sem=send_sem.at[number],
            recv_sem=recv_sem.at[number],
            device_id=device,
            device_id_type=MESH,
        )
        copy.start()

    def wait(ref, sem):
        pltpu.make_async_copy(ref, ref, sem).wait()

    barrier = pltpu.get_barrier_semaphore()

    @pl.when(has_left)
    def _():
        signal(barrier, {"tile": left})

    @pl.when(has_right)
    def _():
        signal(barrier, {"tile": right})

    repeat(rank + 1, N_SRC, lambda k: signal(barrier, {"src": src_of(k)}))
    local = [
        pltpu.make_async_copy(mask, mask_v, local_sem.at[0]),
        pltpu.make_async_copy(shifts, shifts_v, local_sem.at[1]),
        pltpu.make_async_copy(weights, weights_v, local_sem.at[2]),
    ]
    for k in range(3):
        rows = pl.ds(CUTS[k], CUTS[k + 1] - CUTS[k])
        local.append(pltpu.make_async_copy(table.at[rows], table_v.at[rows], local_sem.at[3 + k]))
    local.append(pltpu.make_async_copy(target, target_v, local_sem.at[6]))
    for copy in local:
        copy.start()
    repeat(jnp.where(is_hub, tile + 1, n_tile), n_tile, lambda k: signal(barrier, {"tile": k}))

    ends = has_left.astype(jnp.int32) + has_right.astype(jnp.int32)
    pl.semaphore_wait(barrier, rank + ends + jnp.minimum(tile, HUB))

    @pl.when(has_right)
    def _():
        send(mask.at[:, pl.ds(128, 128)], left_v, 0, {"tile": right})

    @pl.when(has_left)
    def _():
        send(mask.at[:, pl.ds(0, 128)], right_v, 1, {"tile": left})

    repeat(0, rank, lambda k: signal(ready_sem.at[rank], {"src": src_of(k)}))

    @pl.when(jnp.logical_not(has_left))
    def _():
        left_v[...] = jnp.zeros_like(left_v)

    @pl.when(jnp.logical_not(has_right))
    def _():
        right_v[...] = jnp.zeros_like(right_v)

    local[1].wait()
    local[2].wait()
    spec_v[src, 8:16, :] = jnp.zeros((8, 128), jnp.float32)
    spec_v[src, 8:10, 0:PER_DEV] = shifts_v[...].astype(jnp.float32)
    spec_v[src, 10:11, 0:PER_DEV] = weights_v[...]
    local[0].wait()
    local[3].wait()
    at = PLACES["enter"][0]
    own = enter(mask_v[...], table_v[at : at + TILE, :])

    @pl.when(has_left)
    def _():
        wait(left_v, recv_sem.at[0])

    @pl.when(has_right)
    def _():
        wait(right_v, recv_sem.at[1])

    margins = jnp.concatenate([left_v[...], right_v[...]], axis=1)
    own = own + enter(margins, table_v[at + TILE : at + 2 * TILE, :])
    spec_v[src, 0:8, :] = pack(own[:8], own[8:])
    piece = pl.ds(0, 11)

    def send_piece(k):
        send(spec_v.at[src, piece], spec_v.at[src, piece], 2, {"src": src_of(k)})

    def answer_piece(k):
        pl.semaphore_wait(ready_sem.at[k], 1)
        send_piece(k)

    repeat(0, rank, send_piece)
    repeat(rank + 1, N_SRC, answer_piece)
    repeat(0, jnp.where(is_hub, tile, 0), lambda k: signal(hub_sem.at[0], {"tile": k}))

    @pl.when(jnp.logical_not(is_hub))
    def _():
        signal(hub_sem.at[1], {"tile": GROUP + place})

    local[4].wait()
    wait(spec_v.at[pl.ds(0, N_SRC - 1), piece], recv_sem.at[2])

    gathered = spec_v[:, 0:8, :].reshape(128, 128)
    spec = spectrum(gathered, get("spec"), get("lows_a", 0, 128), pltpu.roll)
    at = PLACES["lows_b"][0]
    cols = [(get("cols_" + name), get("cols_low_" + name)) for name in ("even", "odd")]
    rows = [
        (get("rows_even"), table_v[at : at + ROWS_C, 128:256]),
        (get("rows_odd"), table_v[at + ROWS_C : at + 2 * ROWS_C, 128:256]),
    ]

    def add_fields(part, images):
        owner = src
        for k, peer in enumerate(partners):
            owner = jnp.where(part == k + 1, peer, owner)
        extra = spec_v[owner, 8:16, :]
        shift = extra[0:2, :].astype(jnp.int32)
        for s in range(PER_DEV):
            pupil_v[part, s] = pupil_of(shift[0:1, s : s + 1], shift[1:2, s : s + 1])
        for pair in range(PER_DEV // 2):
            first, second = [
                jnp.broadcast_to(extra[2:3, s : s + 1], (8, 128)) for s in (2 * pair, 2 * pair + 1)
            ]
            at = slice(128 * (pair % 2), 128 * (pair % 2) + 128)
            for parity, scale in enumerate(swap(first, second)):
                scale_v[part, pair // 2, parity, :, at] = scale
        fields = coarse_fields(
            spec, [pupil_v[part, s].astype(jnp.bfloat16) for s in range(PER_DEV)], cols, rows
        )
        images = list(images)
        for group in range(2):
            for parity in range(2):
                field_v[part, group, parity] = fields[group][parity]
                power = power_of(fields[group][parity])
                power_v[part, group, parity] = power
                power = power * scale_v[part, group, parity, 0:1, :]
                images[parity] = images[parity] + power[:, :128] + power[:, 128:]
        return tuple(images)

    none = jnp.zeros((ROWS_C // 2, 128), jnp.float32)
    image_v[...] = join_image(*lax.fori_loop(0, QUAD, add_fields, (none, none), unroll=True), pltpu.roll)
    for k, peer in enumerate(members):
        send(image_v, term_v.at[k], 3, {"src": peer})
    local[5].wait()
    local[6].wait()
    wait(term_v, recv_sem.at[3])

    image = pixels_of(
        image_v[...] + term_v[0] + term_v[1] + term_v[2],
        get("fine_rows"),
        get("fine_cols"),
        get("fine_cols_low"),
    )
    printed = jax.nn.sigmoid(STEEP * (image * (1.0 / SOURCES) - THRESH))
    printed_v[...] = printed
    resist[...] = printed_v[pl.ds(pl.multiple_of(src * ROWS, ROWS), ROWS), :]
    goal = target_v[...].astype(jnp.float32)
    slope = (LOSS_SCALE * 2.0 * STEEP) * (printed - goal) * printed * (1.0 - printed)
    coarse = coarse_of(slope, get("coarse_rows"), get("coarse_rows_low"), get("coarse_cols"))

    slopes = twice(coarse, pltpu.roll)
    sums = []
    for pair in range(PER_DEV // 2):
        at = slice(128 * (pair % 2), 128 * (pair % 2) + 128)
        terms = [
            jnp.sum(slopes[parity] * power_v[0, pair // 2, parity, :, at], axis=0, keepdims=True) for parity in range(2)
        ]
        sums.extend(swap(*terms))
    sums = jnp.sum(jnp.concatenate(sums, axis=0), axis=1, keepdims=True)
    spot = (PER_DEV, 128)
    sums = jnp.where(lanes(spot) == lax.broadcasted_iota(jnp.int32, spot, 0), sums, 0.0)
    sums_v[tile] = jnp.sum(sums, axis=0, keepdims=True)

    def send_sums(k):
        pltpu.make_async_remote_copy(
            src_ref=sums_v.at[tile],
            dst_ref=sums_v.at[tile],
            send_sem=send_sem.at[5],
            recv_sem=recv_sem.at[5],
            device_id={"tile": k},
            device_id_type=MESH,
        ).start()

    repeat(0, jnp.minimum(tile, HUB), send_sums)

    wide = [jnp.concatenate([slope, slope], axis=1) * (2.0 / SOURCES) for slope in slopes]
    rows_back = [get("rows_back_even"), get("rows_back_odd")]
    cols_back = [get("cols_back_even"), get("cols_back_odd")]

    def add_part(part, total):
        adjoints = []
        for group in range(2):
            adjoints.append([])
            for parity in range(2):
                scaled = wide[parity] * scale_v[part, group, parity, 0:1, :]
                adjoints[group].append(field_v[part, group, parity] * jnp.concatenate([scaled, scaled], axis=0))
        return band_grad(total, adjoints, [pupil_v[part, s] for s in range(PER_DEV)], rows_back, cols_back)

    grad = lax.fori_loop(0, QUAD, add_part, jnp.zeros((BAND, 128), jnp.float32))
    first = PLACES["leave"][0] + 8 * QUAD * (src // QUAD)
    low_first = PLACES["lows_b"][0] + 8 * QUAD * (src // QUAD)

    def halves_of(start, stop, begin):
        begin = pl.multiple_of(begin, 32)
        then = pl.multiple_of(begin + 128, 32)
        return jnp.concatenate(
            [table_v[pl.ds(begin, 8 * QUAD), start:stop], table_v[pl.ds(then, 8 * QUAD), start:stop]], axis=0
        )

    rows = row_grads(grad, halves_of(0, 256, first), halves_of(0, 128, low_first), pltpu.roll)
    grad_v[...] = rows.reshape(QUAD, 8, 128)
    for k, peer in enumerate(members):
        send(grad_v.at[peer % QUAD], part_v.at[k], 4, {"src": peer})


    @pl.when(tile < HUB - 1)
    def _():
        pl.semaphore_wait(hub_sem.at[0], HUB - 1 - tile)
        repeat(tile + 1, HUB, send_sums)

    wait(part_v, recv_sem.at[4])
    total = grad_v[along % QUAD] + part_v[0] + part_v[1] + part_v[2]
    mask_grad[...] = last_step(total, get("last"), get("last_low"))

    @pl.when(is_hub)
    def _():
        wait(sums_v.at[pl.ds(0, n_tile - 1)], recv_sem.at[5])
        total_v[...] = jnp.sum(sums_v[...], axis=0) * (1.0 / (SOURCES * n_tile * TILE * TILE))

    def tell(k):
        send(total_v, total_v, 6, {"tile": k * GROUP + place})

    @pl.when(is_teller)
    def _():
        pl.semaphore_wait(hub_sem.at[1], n_tile // GROUP - 2)
        repeat(2, n_tile // GROUP, tell)

    @pl.when(jnp.logical_not(is_hub))
    def _():
        wait(total_v, recv_sem.at[6])

    source_grad[...] = total_v[...]

    @pl.when(is_teller)
    def _():
        wait(sums_v.at[pl.ds(0, n_tile // GROUP - 2)], send_sem.at[6])

    @pl.when(is_hub)
    def _():
        wait(sums_v.at[pl.ds(0, HUB - 1)], send_sem.at[5])

    @pl.when(jnp.logical_not(is_hub))
    def _():
        wait(sums_v.at[pl.ds(0, HUB)], send_sem.at[5])


    @pl.when(has_right)
    def _():
        wait(left_v, send_sem.at[0])

    @pl.when(has_left)
    def _():
        wait(right_v, send_sem.at[1])

    wait(spec_v.at[pl.ds(0, N_SRC - 1), piece], send_sem.at[2])
    wait(term_v, send_sem.at[3])
    wait(part_v, send_sem.at[4])


def hand_over(resist, mask_grad, source_grad, resist_out, mask_grad_out, source_grad_out, sem):
    copies = [
        pltpu.make_async_copy(resist, resist_out, sem.at[0]),
        pltpu.make_async_copy(mask_grad, mask_grad_out, sem.at[1]),
    ]
    for copy in copies:
        copy.start()
    source_grad_out[...] = source_grad[0, :PER_DEV]
    for copy in copies:
        copy.wait()


def local(mask, target, shifts, weights):
    f32 = jnp.float32
    anywhere = pl.BlockSpec(memory_space=pl.ANY)
    inside = pl.BlockSpec(memory_space=pltpu.VMEM)
    results = pl.pallas_call(
        everything,
        out_shape=(
            pltpu.VMEM((ROWS, TILE), f32),
            pltpu.VMEM((ROWS, TILE), f32),
            pltpu.VMEM((1, 128), f32),
        ),
        in_specs=[anywhere] * 5,
        out_specs=(inside, inside, inside),
        scratch_shapes=[
            pltpu.VMEM((ROWS, TILE), f32),
            pltpu.VMEM((TILE, TILE), jnp.int32),
            pltpu.VMEM((2, PER_DEV), jnp.int32),
            pltpu.VMEM((1, PER_DEV), f32),
            pltpu.VMEM(TABLE.shape, jnp.bfloat16),
            pltpu.VMEM((ROWS, 128), f32),
            pltpu.VMEM((ROWS, 128), f32),
            pltpu.VMEM((N_SRC, 16, 128), f32),
            pltpu.VMEM((QUAD, PER_DEV, BAND, 128), f32),
            pltpu.VMEM((QUAD, 2, 2, 8, 256), f32),
            pltpu.VMEM((ROWS_C // 2, 128), f32),
            pltpu.VMEM((QUAD - 1, ROWS_C // 2, 128), f32),
            pltpu.VMEM((QUAD, 2, 2, ROWS_C, 256), f32),
            pltpu.VMEM((QUAD, 2, 2, ROWS_C // 2, 256), f32),
            pltpu.VMEM((TILE, TILE), f32),
            pltpu.VMEM((QUAD, 8, 128), f32),
            pltpu.VMEM((QUAD - 1, 8, 128), f32),
            pltpu.VMEM((N_TILE, 1, 128), f32),
            pltpu.VMEM((1, 128), f32),
            pltpu.SemaphoreType.DMA((7,)),
            pltpu.SemaphoreType.DMA((7,)),
            pltpu.SemaphoreType.DMA((7,)),
            pltpu.SemaphoreType.REGULAR((N_SRC,)),
            pltpu.SemaphoreType.REGULAR((2,)),
        ],
        compiler_params=pltpu.CompilerParams(
            collective_id=0, has_side_effects=True, vmem_limit_bytes=60 * 1024 * 1024
        ),
    )(mask, target, shifts.T, weights.reshape(1, PER_DEV), jnp.asarray(TABLE))
    return pl.pallas_call(
        hand_over,
        out_shape=(
            jax.ShapeDtypeStruct((ROWS, TILE), f32),
            jax.ShapeDtypeStruct((ROWS, TILE), f32),
            jax.ShapeDtypeStruct((PER_DEV,), f32),
        ),
        in_specs=[inside] * 3,
        out_specs=(anywhere, anywhere, inside),
        scratch_shapes=[pltpu.SemaphoreType.DMA((2,))],
    )(*[pltpu.with_memory_space_constraint(result, pltpu.VMEM) for result in results])


def solution(mesh):
    placed = (P("src", "tile"), P(None, "tile"), P("src", None), P("src"))
    return jax.shard_map(
        local,
        mesh=mesh,
        in_specs=placed,
        out_specs=(P("src", "tile"), P("src", "tile"), P("src")),
        check_vma=False,
    )
```

```python
import functools

import jax
import jax.numpy as jnp
import ml_dtypes
import numpy as np
from jax import lax
from jax.experimental import pallas as pl
from jax.experimental.pallas import tpu as pltpu
from jax.sharding import PartitionSpec as P

TILE = 256
MARGIN = 32
BAND = 64
RAD = 16
EXT = 320
STEEP = 8.0
THRESH = 0.25
LOSS_SCALE = 2.0

N_SRC = 16
N_TILE = 32
PER_DEV = 8
SOURCES = 128
ROWS = 16
HALF = 32
POINTS_R = 66
ROWS_C = 80
COLS_C = 128
QUAD = 4
GROUP = 4
DEPTH = 8
HUB = 2 * GROUP

MESH = pl.DeviceIdType.MESH
BF16 = ml_dtypes.bfloat16


def halves(table):
    high = table.astype(BF16)
    low = (table - high.astype(np.float64)).astype(BF16)
    return high, low


def column_slots():
    plus = np.arange(HALF)
    return np.concatenate([plus, -plus]), np.concatenate([np.ones(HALF), [0.0], np.ones(HALF - 1)])


def waves(freq, place, period):
    phase = 2.0 * np.pi * ((freq[:, None] * place[None, :]) % period) / period
    return np.cos(phase), np.sin(phase)


def interpolation(points):
    order = np.arange(-2 * RAD, 2 * RAD + 1)
    place = np.arange(TILE) + MARGIN
    offset = place[:, None] / EXT - np.arange(points)[None, :] / points
    return np.cos(2.0 * np.pi * order[None, None, :] * offset[:, :, None]).sum(axis=2) / points


def padded(rows):
    return np.concatenate([rows, np.zeros((ROWS_C // 2 - rows.shape[0], rows.shape[1]))], axis=0)


def build_tables():
    slots, used = column_slots()
    row_freq = np.arange(BAND) - BAND // 2
    pixels = np.arange(TILE) + MARGIN
    parts = {}

    real, imag = waves(np.arange(HALF), np.arange(EXT), EXT)
    fwd = np.concatenate([real, -imag], axis=0).T / EXT
    wide = np.zeros((2 * TILE, 2 * HALF))
    wide[:TILE] = fwd[MARGIN : MARGIN + TILE]
    wide[TILE + 96 : TILE + 128] = fwd[:MARGIN]
    wide[TILE + 128 : TILE + 160] = fwd[MARGIN + TILE :]
    high, low = halves(np.concatenate([wide, wide], axis=1))
    parts["enter"] = np.concatenate([high, low], axis=1)

    rows = np.arange(TILE).reshape(N_SRC, 2, 8)
    first, second = rows[:, 0].reshape(-1), rows[:, 1].reshape(-1)
    real, imag = waves(row_freq, pixels, EXT)
    real, imag = real / EXT, -imag / EXT
    both = np.concatenate([real, imag], axis=0)
    high, low = halves(np.concatenate([both[:, first], both[:, second]], axis=0))
    parts["spec"] = np.concatenate([high, high], axis=1)
    spec_low = low

    inter_rows, inter_cols = 2.0 * interpolation(POINTS_R), interpolation(COLS_C)
    even, odd = np.arange(0, COLS_C, 2), np.arange(1, COLS_C, 2)
    for name, order in (("even", np.concatenate([even, odd])), ("odd", np.concatenate([odd, even]))):
        real, imag = waves(slots, order, COLS_C)
        real, imag = real * used[:, None], imag * used[:, None]
        cols = np.concatenate(
            [np.concatenate([real, imag], axis=1), np.concatenate([-imag, real], axis=1)], axis=0
        )
        high, low = halves(cols)
        parts["cols_" + name] = np.concatenate([high, high], axis=0)
        parts["cols_low_" + name] = low
        high, low = halves(np.concatenate([cols[:, :COLS_C].T, cols[:, COLS_C:].T], axis=0))
        parts["cols_back_" + name] = np.concatenate([high, low], axis=1)

    lows = []
    for name, start in (("even", 0), ("odd", 1)):
        real, imag = waves(row_freq, np.arange(start, POINTS_R, 2), POINTS_R)
        real, imag = padded(real.T), padded(imag.T)
        high, low = halves(
            np.concatenate(
                [np.concatenate([real, -imag], axis=1), np.concatenate([imag, real], axis=1)], axis=0
            )
        )
        parts["rows_" + name] = np.concatenate([high, high], axis=1)
        lows.append(low)
        pad = np.zeros((2 * BAND, TILE - 3 * ROWS_C), BF16)
        parts["rows_back_" + name] = np.concatenate([high.T, high.T, low.T, pad], axis=1)
    rows_low = np.concatenate(lows, axis=0)

    inter_rows = np.concatenate([padded(inter_rows[:, 0::2].T), padded(inter_rows[:, 1::2].T)], axis=0).T
    inter_cols = inter_cols[:, np.concatenate([even, odd])]
    high, low = halves(inter_rows)
    pad = np.zeros((TILE, TILE - 3 * ROWS_C), BF16)
    parts["fine_rows"] = np.concatenate([high, high, low, pad], axis=1)
    high, low = halves(inter_cols.T)
    parts["fine_cols"] = np.concatenate([high, high], axis=0)
    parts["fine_cols_low"] = low
    parts["coarse_cols"] = np.concatenate([high.T, low.T], axis=1)
    high, low = halves(inter_rows.T)
    parts["coarse_rows"] = high
    parts["coarse_rows_low"] = low

    high, low = halves(np.concatenate([both[:, first], both[:, second]], axis=1).T)
    parts["leave"] = np.concatenate([high, high], axis=1)
    leave_low = low
    last = fwd[MARGIN : MARGIN + TILE].T
    high, low = halves(np.concatenate([last, last], axis=0))
    parts["last"] = high
    parts["last_low"] = low

    parts["lows_a"] = np.concatenate([spec_low, np.zeros((TILE, 128), BF16)], axis=1)
    rows_low = np.concatenate([rows_low, np.zeros((TILE - 2 * ROWS_C, 128), BF16)], axis=0)
    parts["lows_b"] = np.concatenate([leave_low, rows_low], axis=1)

    order = [
        "enter",
        "spec", "lows_a", "cols_even", "cols_low_even", "cols_odd", "cols_low_odd", "rows_even", "rows_odd", "lows_b",
        "fine_rows", "fine_cols", "fine_cols_low", "coarse_cols", "coarse_rows", "coarse_rows_low",
        "rows_back_even", "rows_back_odd", "cols_back_even", "cols_back_odd", "leave", "last", "last_low",
    ]
    places, start = {}, 0
    for name in order:
        places[name] = (start, parts[name].shape[0])
        start += parts[name].shape[0]
    return np.concatenate([parts[name] for name in order], axis=0), places


TABLE, PLACES = build_tables()
CUTS = (0, PLACES["spec"][0], PLACES["fine_rows"][0], TABLE.shape[0])


def dot(left, right):
    return jnp.dot(left, right, preferred_element_type=jnp.float32)


def cut(value):
    high = value.astype(jnp.bfloat16)
    low = (value - high.astype(jnp.float32)).astype(jnp.bfloat16)
    return high, low


def lanes(shape):
    return lax.broadcasted_iota(jnp.int32, shape, 1)


def enter(value, table):
    high, low = cut(value)
    both = dot(high, table)
    return both[:, :128] + both[:, 128:] + dot(low, table[:, :128])


def pack(first, second):
    return jnp.where(lanes(first.shape) < 64, first, second)


def spectrum(gathered, table, low_table, roll):
    high, low = cut(gathered)
    out = dot(table, jnp.concatenate([high, low], axis=0)) + dot(low_table, high)
    both = pack(out[:128], out[128:])
    both = both + roll(both, 64, 1)
    turned = roll(both, 32, 1)
    quarter = lanes((BAND, 128)) >> 5
    outer = (quarter == 0) | (quarter == 3)
    even = jnp.where(outer, both[:BAND], turned[:BAND])
    odd = jnp.where(outer, turned[BAND:], both[BAND:])
    return jnp.where(quarter == 3, -even, even) + jnp.where(quarter == 0, -odd, odd)


def pupil_of(row_shift, col_shift):
    row = lax.broadcasted_iota(jnp.int32, (BAND, 128), 0) - BAND // 2 + row_shift
    slot = lanes((1, 128)) & 63
    col = jnp.where(slot < HALF, slot, HALF - slot) + col_shift
    room = jnp.where(slot == HALF, -1, RAD * RAD - col * col)
    return jnp.where(row * row <= room, 1.0, 0.0)


def swap(first, second):
    return pack(first, second), pack(second, first)


def coarse_fields(spec, pupils, cols, rows):
    high, low = cut(spec)
    mids = []
    for which in range(2):
        band_high = jnp.concatenate([high * pupil for pupil in pupils[which::2]], axis=0)
        band_low = jnp.concatenate([low * pupil for pupil in pupils[which::2]], axis=0)
        table, low_table = cols[which]
        mids.append(
            dot(jnp.concatenate([band_high, band_low], axis=1), table) + dot(band_high, low_table)
        )
    fields = []
    for group in range(2):
        stacks = ([], [])
        for pair in (2 * group, 2 * group + 1):
            at = slice(BAND * pair, BAND * pair + BAND)
            real = swap(mids[0][at, :128], mids[1][at, :128])
            imag = swap(mids[0][at, 128:], mids[1][at, 128:])
            for parity in range(2):
                stacks[parity].append(jnp.concatenate([real[parity], imag[parity]], axis=0))
        both = []
        for parity in range(2):
            upper, lower = cut(jnp.concatenate(stacks[parity], axis=1))
            table, low_table = rows[parity]
            both.append(dot(table, jnp.concatenate([upper, lower], axis=0)) + dot(low_table, upper))
        fields.append(both)
    return fields


def power_of(field):
    half = ROWS_C // 2
    return field[:half] * field[:half] + field[half:] * field[half:]


def join_image(even, odd, roll):
    return pack(even + roll(even, 64, 1), odd + roll(odd, 64, 1))


def pixels_of(coarse, fine_rows, fine_cols, fine_cols_low):
    first = lanes(coarse.shape) < 64
    coarse = jnp.concatenate([jnp.where(first, coarse, 0.0), jnp.where(first, 0.0, coarse)], axis=0)
    high, low = cut(coarse)
    mid = dot(jnp.concatenate([high, low], axis=1), fine_cols) + dot(high, fine_cols_low)
    return dot(fine_rows, three(mid))


def three(value):
    high, low = cut(value)
    pad = jnp.zeros((TILE - 3 * value.shape[0], value.shape[1]), jnp.bfloat16)
    return jnp.concatenate([high, low, high, pad], axis=0)


def coarse_of(slope, coarse_rows, coarse_rows_low, coarse_cols):
    high, low = cut(slope)
    mid = dot(coarse_rows, high) + dot(coarse_rows, low) + dot(coarse_rows_low, high)
    high, low = cut(mid)
    both = dot(high, coarse_cols)
    return both[:, :128] + both[:, 128:] + dot(low, coarse_cols[:, :128])


def twice(coarse, roll):
    half = ROWS_C // 2
    even, odd = coarse[:half], coarse[half:]
    return pack(even, roll(even, 64, 1)), pack(roll(odd, 64, 1), odd)


def band_grad(total, adjoints, pupils, rows_back, cols_back):
    sides = ([], [])
    for group in range(2):
        even, odd = [dot(rows_back[parity], three(adjoints[group][parity])) for parity in range(2)]
        for pair in range(2):
            at = slice(128 * pair, 128 * pair + 128)
            real = swap(even[:BAND, at], odd[:BAND, at])
            imag = swap(even[BAND:, at], odd[BAND:, at])
            for which in range(2):
                sides[which].append(jnp.concatenate([real[which], imag[which]], axis=1))
    for which in range(2):
        high, low = cut(jnp.concatenate(sides[which], axis=0))
        both = dot(high, cols_back[which])
        term = both[:, :128] + both[:, 128:] + dot(low, cols_back[which][:, :128])
        for k in range(PER_DEV // 2):
            total = total + term[BAND * k : BAND * k + BAND] * pupils[2 * k + which]
    return total


def fold(grad, roll):
    r32, r64, r96 = roll(grad, 32, 1), roll(grad, 64, 1), roll(grad, 96, 1)
    quarter = lanes(grad.shape) >> 5
    upper = jnp.where(
        quarter == 0, grad + r96, jnp.where(quarter == 1, r96 - r64, jnp.where(quarter == 2, r64 + r32, r32 - grad))
    )
    lower = jnp.where(
        quarter == 0, r64 + r32, jnp.where(quarter == 1, grad - r32, jnp.where(quarter == 2, grad + r96, r64 - r96))
    )
    return jnp.concatenate([upper, lower], axis=0)


def row_grads(grad, leave, leave_low, roll):
    high, low = cut(fold(grad, roll))
    out = dot(leave, jnp.concatenate([high, low], axis=0)) + dot(leave_low, high)
    half = out.shape[0] // 2
    return pack(out[:half], out[half:])


def last_step(total, last, last_low):
    first = lanes(total.shape) < 64
    value = jnp.concatenate([jnp.where(first, total, 0.0), jnp.where(first, 0.0, total)], axis=0)
    high, low = cut(value)
    return dot(high, last) + dot(low, last) + dot(high, last_low)


def rank_of(side, along):
    return 2 * jnp.where(along < DEPTH // 2, along, DEPTH + DEPTH // 2 - 1 - along) + side


def src_of(rank):
    step, side = rank // 2, rank % 2
    return side * DEPTH + jnp.where(step < DEPTH // 2, step, DEPTH + DEPTH // 2 - 1 - step)


def repeat(first, last, body):
    def step(k, carry):
        body(k)
        return carry

    lax.fori_loop(first, last, step, 0)


def everything(mask, target, shifts, weights, table, resist, mask_grad, source_grad, *scratch):
    (
        mask_v, target_v, shifts_v, weights_v, table_v,
        left_v, right_v, spec_v, pupil_v, scale_v, image_v, term_v, field_v, power_v,
        printed_v, grad_v, part_v, sums_v, total_v, local_sem, send_sem, recv_sem, ready_sem, hub_sem,
    ) = scratch
    tile, src = lax.axis_index("tile"), lax.axis_index("src")
    n_tile = lax.axis_size("tile")
    left, right = tile - 1, tile + 1
    has_left, has_right = tile > 0, tile < n_tile - 1
    side, along = src // DEPTH, src % DEPTH
    rank = rank_of(side, along)
    quad = along // QUAD
    partners = [
        (side + across) % 2 * DEPTH + (along + step) % DEPTH for across, step in ((0, QUAD), (1, 0), (1, QUAD))
    ]
    members = [side * DEPTH + quad * QUAD + (along + k) % QUAD for k in range(1, QUAD)]
    layer = tile // GROUP
    place = tile % GROUP
    is_hub, is_teller = tile < HUB, layer == 1

    def get(name, start=None, stop=None):
        at, size = PLACES[name]
        if start is None:
            return table_v[at : at + size, :]
        return table_v[at : at + size, start:stop]

    def signal(sem, device):
        pl.semaphore_signal(sem, inc=1, device_id=device, device_id_type=MESH)

    def send(source, target_ref, number, device):
        copy = pltpu.make_async_remote_copy(
            src_ref=source,
            dst_ref=target_ref,
            send_sem=send_sem.at[number],
            recv_sem=recv_sem.at[number],
            device_id=device,
            device_id_type=MESH,
        )
        copy.start()

    def wait(ref, sem):
        pltpu.make_async_copy(ref, ref, sem).wait()

    barrier = pltpu.get_barrier_semaphore()

    @pl.when(has_left)
    def _():
        signal(barrier, {"tile": left})

    @pl.when(has_right)
    def _():
        signal(barrier, {"tile": right})

    repeat(rank + 1, N_SRC, lambda k: signal(barrier, {"src": src_of(k)}))
    local = [
        pltpu.make_async_copy(mask, mask_v, local_sem.at[0]),
        pltpu.make_async_copy(shifts, shifts_v, local_sem.at[1]),
        pltpu.make_async_copy(weights, weights_v, local_sem.at[2]),
    ]
    for k in range(3):
        rows = pl.ds(CUTS[k], CUTS[k + 1] - CUTS[k])
        local.append(pltpu.make_async_copy(table.at[rows], table_v.at[rows], local_sem.at[3 + k]))
    local.append(pltpu.make_async_copy(target, target_v, local_sem.at[6]))
    local[0].start()
    local[3].start()
    repeat(jnp.where(is_hub, tile + 1, n_tile), n_tile, lambda k: signal(barrier, {"tile": k}))

    ends = has_left.astype(jnp.int32) + has_right.astype(jnp.int32)
    pl.semaphore_wait(barrier, rank + ends + jnp.minimum(tile, HUB))

    @pl.when(has_right)
    def _():
        send(mask.at[:, pl.ds(128, 128)], left_v, 0, {"tile": right})

    @pl.when(has_left)
    def _():
        send(mask.at[:, pl.ds(0, 128)], right_v, 1, {"tile": left})

    for k in (1, 2, 4, 5, 6):
        local[k].start()
    repeat(0, rank, lambda k: signal(ready_sem.at[rank], {"src": src_of(k)}))
    term_v[:, POINTS_R // 2 :, :] = jnp.zeros((QUAD - 1, (ROWS_C - POINTS_R) // 2, 128), jnp.float32)

    @pl.when(jnp.logical_not(has_left))
    def _():
        left_v[...] = jnp.zeros_like(left_v)

    @pl.when(jnp.logical_not(has_right))
    def _():
        right_v[...] = jnp.zeros_like(right_v)

    local[1].wait()
    local[2].wait()
    spec_v[src, 8:16, :] = jnp.zeros((8, 128), jnp.float32)
    spec_v[src, 8:10, 0:PER_DEV] = shifts_v[...].astype(jnp.float32)
    spec_v[src, 10:11, 0:PER_DEV] = weights_v[...]
    local[0].wait()
    local[3].wait()
    at = PLACES["enter"][0]
    own = enter(mask_v[...], table_v[at : at + TILE, :])

    @pl.when(has_left)
    def _():
        wait(left_v, recv_sem.at[0])

    @pl.when(has_right)
    def _():
        wait(right_v, recv_sem.at[1])

    margins = jnp.concatenate([left_v[...], right_v[...]], axis=1)
    own = own + enter(margins, table_v[at + TILE : at + 2 * TILE, :])
    spec_v[src, 0:8, :] = pack(own[:8], own[8:])
    piece = pl.ds(0, 11)

    def send_piece(k):
        send(spec_v.at[src, piece], spec_v.at[src, piece], 2, {"src": src_of(k)})

    def answer_piece(k):
        pl.semaphore_wait(ready_sem.at[k], 1)
        send_piece(k)

    repeat(0, (rank + 1) // 2, lambda k: send_piece(2 * k))
    repeat(0, rank // 2, lambda k: send_piece(2 * k + 1))
    repeat(rank + 1, N_SRC, answer_piece)
    repeat(0, jnp.where(is_hub, tile, 0), lambda k: signal(hub_sem.at[0], {"tile": k}))

    @pl.when(jnp.logical_not(is_hub))
    def _():
        signal(hub_sem.at[1], {"tile": GROUP + place})

    local[4].wait()
    wait(spec_v.at[pl.ds(0, N_SRC - 1), piece], recv_sem.at[2])

    gathered = spec_v[:, 0:8, :].reshape(128, 128)
    spec = spectrum(gathered, get("spec"), get("lows_a", 0, 128), pltpu.roll)
    at = PLACES["lows_b"][0]
    cols = [(get("cols_" + name), get("cols_low_" + name)) for name in ("even", "odd")]
    rows = [
        (get("rows_even"), table_v[at : at + ROWS_C, 128:256]),
        (get("rows_odd"), table_v[at + ROWS_C : at + 2 * ROWS_C, 128:256]),
    ]

    def add_fields(part, images):
        owner = src
        for k, peer in enumerate(partners):
            owner = jnp.where(part == k + 1, peer, owner)
        extra = spec_v[owner, 8:16, :]
        shift = extra[0:2, :].astype(jnp.int32)
        for s in range(PER_DEV):
            pupil_v[part, s] = pupil_of(shift[0:1, s : s + 1], shift[1:2, s : s + 1])
        for pair in range(PER_DEV // 2):
            first, second = [
                jnp.broadcast_to(extra[2:3, s : s + 1], (8, 128)) for s in (2 * pair, 2 * pair + 1)
            ]
            at = slice(128 * (pair % 2), 128 * (pair % 2) + 128)
            for parity, scale in enumerate(swap(first, second)):
                scale_v[part, pair // 2, parity, :, at] = scale
        fields = coarse_fields(
            spec, [pupil_v[part, s].astype(jnp.bfloat16) for s in range(PER_DEV)], cols, rows
        )
        images = list(images)
        for group in range(2):
            for parity in range(2):
                field_v[part, group, parity] = fields[group][parity]
                power = power_of(fields[group][parity])
                power_v[part, group, parity] = power
                power = power * scale_v[part, group, parity, 0:1, :]
                images[parity] = images[parity] + power[:, :128] + power[:, 128:]
        return tuple(images)

    none = jnp.zeros((ROWS_C // 2, 128), jnp.float32)
    image_v[...] = join_image(*lax.fori_loop(0, QUAD, add_fields, (none, none), unroll=True), pltpu.roll)
    image_rows = pl.ds(0, POINTS_R // 2)
    for k, peer in enumerate(members):
        send(image_v.at[image_rows], term_v.at[k, image_rows], 3, {"src": peer})
    local[5].wait()
    local[6].wait()
    wait(term_v.at[:, image_rows], recv_sem.at[3])

    image = pixels_of(
        image_v[...] + term_v[0] + term_v[1] + term_v[2],
        get("fine_rows"),
        get("fine_cols"),
        get("fine_cols_low"),
    )
    printed = jax.nn.sigmoid(STEEP * (image * (1.0 / SOURCES) - THRESH))
    printed_v[...] = printed
    resist[...] = printed_v[pl.ds(pl.multiple_of(src * ROWS, ROWS), ROWS), :]
    goal = target_v[...].astype(jnp.float32)
    slope = (LOSS_SCALE * 2.0 * STEEP) * (printed - goal) * printed * (1.0 - printed)
    coarse = coarse_of(slope, get("coarse_rows"), get("coarse_rows_low"), get("coarse_cols"))

    slopes = twice(coarse, pltpu.roll)
    sums = []
    for pair in range(PER_DEV // 2):
        at = slice(128 * (pair % 2), 128 * (pair % 2) + 128)
        terms = [
            jnp.sum(slopes[parity] * power_v[0, pair // 2, parity, :, at], axis=0, keepdims=True) for parity in range(2)
        ]
        sums.extend(swap(*terms))
    sums = jnp.sum(jnp.concatenate(sums, axis=0), axis=1, keepdims=True)
    spot = (PER_DEV, 128)
    sums = jnp.where(lanes(spot) == lax.broadcasted_iota(jnp.int32, spot, 0), sums, 0.0)
    sums_v[tile] = jnp.sum(sums, axis=0, keepdims=True)

    def send_sums(k):
        pltpu.make_async_remote_copy(
            src_ref=sums_v.at[tile],
            dst_ref=sums_v.at[tile],
            send_sem=send_sem.at[5],
            recv_sem=recv_sem.at[5],
            device_id={"tile": k},
            device_id_type=MESH,
        ).start()

    repeat(0, jnp.minimum(tile, HUB), send_sums)

    wide = [jnp.concatenate([slope, slope], axis=1) * (2.0 / SOURCES) for slope in slopes]
    rows_back = [get("rows_back_even"), get("rows_back_odd")]
    cols_back = [get("cols_back_even"), get("cols_back_odd")]

    def add_part(part, total):
        adjoints = []
        for group in range(2):
            adjoints.append([])
            for parity in range(2):
                scaled = wide[parity] * scale_v[part, group, parity, 0:1, :]
                adjoints[group].append(field_v[part, group, parity] * jnp.concatenate([scaled, scaled], axis=0))
        return band_grad(total, adjoints, [pupil_v[part, s] for s in range(PER_DEV)], rows_back, cols_back)

    grad = lax.fori_loop(0, QUAD, add_part, jnp.zeros((BAND, 128), jnp.float32))
    first = PLACES["leave"][0] + 8 * QUAD * (src // QUAD)
    low_first = PLACES["lows_b"][0] + 8 * QUAD * (src // QUAD)

    def halves_of(start, stop, begin):
        begin = pl.multiple_of(begin, 32)
        then = pl.multiple_of(begin + 128, 32)
        return jnp.concatenate(
            [table_v[pl.ds(begin, 8 * QUAD), start:stop], table_v[pl.ds(then, 8 * QUAD), start:stop]], axis=0
        )

    rows = row_grads(grad, halves_of(0, 256, first), halves_of(0, 128, low_first), pltpu.roll)
    grad_v[...] = rows.reshape(QUAD, 8, 128)
    for k, peer in enumerate(members):
        send(grad_v.at[peer % QUAD], part_v.at[k], 4, {"src": peer})


    @pl.when(tile < HUB - 1)
    def _():
        pl.semaphore_wait(hub_sem.at[0], HUB - 1 - tile)
        repeat(tile + 1, HUB, send_sums)

    wait(part_v, recv_sem.at[4])
    total = grad_v[along % QUAD] + part_v[0] + part_v[1] + part_v[2]
    mask_grad[...] = last_step(total, get("last"), get("last_low"))

    @pl.when(is_hub)
    def _():
        wait(sums_v.at[pl.ds(0, n_tile - 1)], recv_sem.at[5])
        total_v[...] = jnp.sum(sums_v[...], axis=0) * (1.0 / (SOURCES * n_tile * TILE * TILE))

    def tell(k):
        send(total_v, total_v, 6, {"tile": k * GROUP + place})

    @pl.when(is_teller)
    def _():
        pl.semaphore_wait(hub_sem.at[1], n_tile // GROUP - 2)
        repeat(2, n_tile // GROUP, tell)

    @pl.when(jnp.logical_not(is_hub))
    def _():
        wait(total_v, recv_sem.at[6])

    source_grad[...] = total_v[...]

    @pl.when(is_teller)
    def _():
        wait(sums_v.at[pl.ds(0, n_tile // GROUP - 2)], send_sem.at[6])

    @pl.when(is_hub)
    def _():
        wait(sums_v.at[pl.ds(0, HUB - 1)], send_sem.at[5])

    @pl.when(jnp.logical_not(is_hub))
    def _():
        wait(sums_v.at[pl.ds(0, HUB)], send_sem.at[5])


    @pl.when(has_right)
    def _():
        wait(left_v, send_sem.at[0])

    @pl.when(has_left)
    def _():
        wait(right_v, send_sem.at[1])

    wait(spec_v.at[pl.ds(0, N_SRC - 1), piece], send_sem.at[2])
    wait(term_v.at[:, image_rows], send_sem.at[3])
    wait(part_v, send_sem.at[4])


def hand_over(resist, mask_grad, source_grad, resist_out, mask_grad_out, source_grad_out, sem):
    copies = [
        pltpu.make_async_copy(resist, resist_out, sem.at[0]),
        pltpu.make_async_copy(mask_grad, mask_grad_out, sem.at[1]),
    ]
    for copy in copies:
        copy.start()
    source_grad_out[...] = source_grad[0, :PER_DEV]
    for copy in copies:
        copy.wait()


def local(mask, target, shifts, weights):
    f32 = jnp.float32
    anywhere = pl.BlockSpec(memory_space=pl.ANY)
    inside = pl.BlockSpec(memory_space=pltpu.VMEM)
    results = pl.pallas_call(
        everything,
        out_shape=(
            pltpu.VMEM((ROWS, TILE), f32),
            pltpu.VMEM((ROWS, TILE), f32),
            pltpu.VMEM((1, 128), f32),
        ),
        in_specs=[anywhere] * 5,
        out_specs=(inside, inside, inside),
        scratch_shapes=[
            pltpu.VMEM((ROWS, TILE), f32),
            pltpu.VMEM((TILE, TILE), jnp.int32),
            pltpu.VMEM((2, PER_DEV), jnp.int32),
            pltpu.VMEM((1, PER_DEV), f32),
            pltpu.VMEM(TABLE.shape, jnp.bfloat16),
            pltpu.VMEM((ROWS, 128), f32),
            pltpu.VMEM((ROWS, 128), f32),
            pltpu.VMEM((N_SRC, 16, 128), f32),
            pltpu.VMEM((QUAD, PER_DEV, BAND, 128), f32),
            pltpu.VMEM((QUAD, 2, 2, 8, 256), f32),
            pltpu.VMEM((ROWS_C // 2, 128), f32),
            pltpu.VMEM((QUAD - 1, ROWS_C // 2, 128), f32),
            pltpu.VMEM((QUAD, 2, 2, ROWS_C, 256), f32),
            pltpu.VMEM((QUAD, 2, 2, ROWS_C // 2, 256), f32),
            pltpu.VMEM((TILE, TILE), f32),
            pltpu.VMEM((QUAD, 8, 128), f32),
            pltpu.VMEM((QUAD - 1, 8, 128), f32),
            pltpu.VMEM((N_TILE, 1, 128), f32),
            pltpu.VMEM((1, 128), f32),
            pltpu.SemaphoreType.DMA((7,)),
            pltpu.SemaphoreType.DMA((7,)),
            pltpu.SemaphoreType.DMA((7,)),
            pltpu.SemaphoreType.REGULAR((N_SRC,)),
            pltpu.SemaphoreType.REGULAR((2,)),
        ],
        compiler_params=pltpu.CompilerParams(
            collective_id=0, has_side_effects=True, vmem_limit_bytes=60 * 1024 * 1024
        ),
    )(mask, target, shifts.T, weights.reshape(1, PER_DEV), jnp.asarray(TABLE))
    return pl.pallas_call(
        hand_over,
        out_shape=(
            jax.ShapeDtypeStruct((ROWS, TILE), f32),
            jax.ShapeDtypeStruct((ROWS, TILE), f32),
            jax.ShapeDtypeStruct((PER_DEV,), f32),
        ),
        in_specs=[inside] * 3,
        out_specs=(anywhere, anywhere, inside),
        scratch_shapes=[pltpu.SemaphoreType.DMA((2,))],
    )(*[pltpu.with_memory_space_constraint(result, pltpu.VMEM) for result in results])


def solution(mesh):
    placed = (P("src", "tile"), P(None, "tile"), P("src", None), P("src"))
    return jax.shard_map(
        local,
        mesh=mesh,
        in_specs=placed,
        out_specs=(P("src", "tile"), P("src", "tile"), P("src")),
        check_vma=False,
    )
```

```python
import functools

import jax
import jax.numpy as jnp
import ml_dtypes
import numpy as np
from jax import lax
from jax.experimental import pallas as pl
from jax.experimental.pallas import tpu as pltpu
from jax.sharding import PartitionSpec as P

TILE = 256
MARGIN = 32
BAND = 64
RAD = 16
EXT = 320
STEEP = 8.0
THRESH = 0.25
LOSS_SCALE = 2.0

N_SRC = 16
N_TILE = 32
PER_DEV = 8
SOURCES = 128
ROWS = 16
HALF = 32
POINTS_R = 66
ROWS_C = 80
COLS_C = 128
QUAD = 4
GROUP = 4
DEPTH = 8
HUB = 2 * GROUP

MESH = pl.DeviceIdType.MESH
BF16 = ml_dtypes.bfloat16


def halves(table):
    high = table.astype(BF16)
    low = (table - high.astype(np.float64)).astype(BF16)
    return high, low


def column_slots():
    plus = np.arange(HALF)
    return np.concatenate([plus, -plus]), np.concatenate([np.ones(HALF), [0.0], np.ones(HALF - 1)])


def waves(freq, place, period):
    phase = 2.0 * np.pi * ((freq[:, None] * place[None, :]) % period) / period
    return np.cos(phase), np.sin(phase)


def interpolation(points):
    order = np.arange(-2 * RAD, 2 * RAD + 1)
    place = np.arange(TILE) + MARGIN
    offset = place[:, None] / EXT - np.arange(points)[None, :] / points
    return np.cos(2.0 * np.pi * order[None, None, :] * offset[:, :, None]).sum(axis=2) / points


def padded(rows):
    return np.concatenate([rows, np.zeros((ROWS_C // 2 - rows.shape[0], rows.shape[1]))], axis=0)


def build_tables():
    slots, used = column_slots()
    row_freq = np.arange(BAND) - BAND // 2
    pixels = np.arange(TILE) + MARGIN
    parts = {}

    real, imag = waves(np.arange(HALF), np.arange(EXT), EXT)
    fwd = np.concatenate([real, -imag], axis=0).T / EXT
    wide = np.zeros((2 * TILE, 2 * HALF))
    wide[:TILE] = fwd[MARGIN : MARGIN + TILE]
    wide[TILE + 96 : TILE + 128] = fwd[:MARGIN]
    wide[TILE + 128 : TILE + 160] = fwd[MARGIN + TILE :]
    high, low = halves(np.concatenate([wide, wide], axis=1))
    parts["enter"] = np.concatenate([high, low], axis=1)

    rows = np.arange(TILE).reshape(N_SRC, 2, 8)
    first, second = rows[:, 0].reshape(-1), rows[:, 1].reshape(-1)
    real, imag = waves(row_freq, pixels, EXT)
    real, imag = real / EXT, -imag / EXT
    both = np.concatenate([real, imag], axis=0)
    high, low = halves(np.concatenate([both[:, first], both[:, second]], axis=0))
    parts["spec"] = np.concatenate([high, high], axis=1)
    spec_low = low

    inter_rows, inter_cols = 2.0 * interpolation(POINTS_R), interpolation(COLS_C)
    even, odd = np.arange(0, COLS_C, 2), np.arange(1, COLS_C, 2)
    for name, order in (("even", np.concatenate([even, odd])), ("odd", np.concatenate([odd, even]))):
        real, imag = waves(slots, order, COLS_C)
        real, imag = real * used[:, None], imag * used[:, None]
        cols = np.concatenate(
            [np.concatenate([real, imag], axis=1), np.concatenate([-imag, real], axis=1)], axis=0
        )
        high, low = halves(cols)
        parts["cols_" + name] = np.concatenate([high, high], axis=0)
        parts["cols_low_" + name] = low
        high, low = halves(np.concatenate([cols[:, :COLS_C].T, cols[:, COLS_C:].T], axis=0))
        parts["cols_back_" + name] = np.concatenate([high, low], axis=1)

    lows = []
    for name, start in (("even", 0), ("odd", 1)):
        real, imag = waves(row_freq, np.arange(start, POINTS_R, 2), POINTS_R)
        real, imag = padded(real.T), padded(imag.T)
        high, low = halves(
            np.concatenate(
                [np.concatenate([real, -imag], axis=1), np.concatenate([imag, real], axis=1)], axis=0
            )
        )
        parts["rows_" + name] = np.concatenate([high, high], axis=1)
        lows.append(low)
        pad = np.zeros((2 * BAND, TILE - 3 * ROWS_C), BF16)
        parts["rows_back_" + name] = np.concatenate([high.T, high.T, low.T, pad], axis=1)
    rows_low = np.concatenate(lows, axis=0)

    inter_rows = np.concatenate([padded(inter_rows[:, 0::2].T), padded(inter_rows[:, 1::2].T)], axis=0).T
    inter_cols = inter_cols[:, np.concatenate([even, odd])]
    high, low = halves(inter_rows)
    pad = np.zeros((TILE, TILE - 3 * ROWS_C), BF16)
    parts["fine_rows"] = np.concatenate([high, high, low, pad], axis=1)
    high, low = halves(inter_cols.T)
    parts["fine_cols"] = np.concatenate([high, high], axis=0)
    parts["fine_cols_low"] = low
    parts["coarse_cols"] = np.concatenate([high.T, low.T], axis=1)
    high, low = halves(inter_rows.T)
    parts["coarse_rows"] = high
    parts["coarse_rows_low"] = low

    high, low = halves(np.concatenate([both[:, first], both[:, second]], axis=1).T)
    parts["leave"] = np.concatenate([high, high], axis=1)
    leave_low = low
    last = fwd[MARGIN : MARGIN + TILE].T
    high, low = halves(np.concatenate([last, last], axis=0))
    parts["last"] = high
    parts["last_low"] = low

    parts["lows_a"] = np.concatenate([spec_low, np.zeros((TILE, 128), BF16)], axis=1)
    rows_low = np.concatenate([rows_low, np.zeros((TILE - 2 * ROWS_C, 128), BF16)], axis=0)
    parts["lows_b"] = np.concatenate([leave_low, rows_low], axis=1)

    order = [
        "enter",
        "spec", "lows_a", "cols_even", "cols_low_even", "cols_odd", "cols_low_odd", "rows_even", "rows_odd", "lows_b",
        "fine_rows", "fine_cols", "fine_cols_low", "coarse_cols", "coarse_rows", "coarse_rows_low",
        "rows_back_even", "rows_back_odd", "cols_back_even", "cols_back_odd", "leave", "last", "last_low",
    ]
    places, start = {}, 0
    for name in order:
        places[name] = (start, parts[name].shape[0])
        start += parts[name].shape[0]
    return np.concatenate([parts[name] for name in order], axis=0), places


TABLE, PLACES = build_tables()
CUTS = (0, PLACES["spec"][0], PLACES["fine_rows"][0], TABLE.shape[0])


def dot(left, right):
    return jnp.dot(left, right, preferred_element_type=jnp.float32)


def cut(value):
    high = value.astype(jnp.bfloat16)
    low = (value - high.astype(jnp.float32)).astype(jnp.bfloat16)
    return high, low


def lanes(shape):
    return lax.broadcasted_iota(jnp.int32, shape, 1)


def enter(value, table):
    high, low = cut(value)
    both = dot(high, table)
    return both[:, :128] + both[:, 128:] + dot(low, table[:, :128])


def pack(first, second):
    return jnp.where(lanes(first.shape) < 64, first, second)


def spectrum(gathered, table, low_table, roll):
    high, low = cut(gathered)
    out = dot(table, jnp.concatenate([high, low], axis=0)) + dot(low_table, high)
    both = pack(out[:128], out[128:])
    both = both + roll(both, 64, 1)
    turned = roll(both, 32, 1)
    quarter = lanes((BAND, 128)) >> 5
    outer = (quarter == 0) | (quarter == 3)
    even = jnp.where(outer, both[:BAND], turned[:BAND])
    odd = jnp.where(outer, turned[BAND:], both[BAND:])
    return jnp.where(quarter == 3, -even, even) + jnp.where(quarter == 0, -odd, odd)


def pupil_of(row_shift, col_shift):
    row = lax.broadcasted_iota(jnp.int32, (BAND, 128), 0) - BAND // 2 + row_shift
    slot = lanes((1, 128)) & 63
    col = jnp.where(slot < HALF, slot, HALF - slot) + col_shift
    room = jnp.where(slot == HALF, -1, RAD * RAD - col * col)
    return jnp.where(row * row <= room, 1.0, 0.0)


def swap(first, second):
    return pack(first, second), pack(second, first)


def coarse_fields(spec, pupils, cols, rows):
    high, low = cut(spec)
    mids = []
    for which in range(2):
        band_high = jnp.concatenate([high * pupil for pupil in pupils[which::2]], axis=0)
        band_low = jnp.concatenate([low * pupil for pupil in pupils[which::2]], axis=0)
        table, low_table = cols[which]
        mids.append(
            dot(jnp.concatenate([band_high, band_low], axis=1), table) + dot(band_high, low_table)
        )
    fields = []
    for group in range(2):
        stacks = ([], [])
        for pair in (2 * group, 2 * group + 1):
            at = slice(BAND * pair, BAND * pair + BAND)
            real = swap(mids[0][at, :128], mids[1][at, :128])
            imag = swap(mids[0][at, 128:], mids[1][at, 128:])
            for parity in range(2):
                stacks[parity].append(jnp.concatenate([real[parity], imag[parity]], axis=0))
        both = []
        for parity in range(2):
            upper, lower = cut(jnp.concatenate(stacks[parity], axis=1))
            table, low_table = rows[parity]
            both.append(dot(table, jnp.concatenate([upper, lower], axis=0)) + dot(low_table, upper))
        fields.append(both)
    return fields


def power_of(field):
    half = ROWS_C // 2
    return field[:half] * field[:half] + field[half:] * field[half:]


def join_image(even, odd, roll):
    return pack(even + roll(even, 64, 1), odd + roll(odd, 64, 1))


def pixels_of(coarse, fine_rows, fine_cols, fine_cols_low):
    first = lanes(coarse.shape) < 64
    coarse = jnp.concatenate([jnp.where(first, coarse, 0.0), jnp.where(first, 0.0, coarse)], axis=0)
    high, low = cut(coarse)
    mid = dot(jnp.concatenate([high, low], axis=1), fine_cols) + dot(high, fine_cols_low)
    return dot(fine_rows, three(mid))


def three(value):
    high, low = cut(value)
    pad = jnp.zeros((TILE - 3 * value.shape[0], value.shape[1]), jnp.bfloat16)
    return jnp.concatenate([high, low, high, pad], axis=0)


def coarse_of(slope, coarse_rows, coarse_rows_low, coarse_cols):
    high, low = cut(slope)
    mid = dot(coarse_rows, high) + dot(coarse_rows, low) + dot(coarse_rows_low, high)
    high, low = cut(mid)
    both = dot(high, coarse_cols)
    return both[:, :128] + both[:, 128:] + dot(low, coarse_cols[:, :128])


def twice(coarse, roll):
    half = ROWS_C // 2
    even, odd = coarse[:half], coarse[half:]
    return pack(even, roll(even, 64, 1)), pack(roll(odd, 64, 1), odd)


def band_grad(total, adjoints, pupils, rows_back, cols_back):
    sides = ([], [])
    for group in range(2):
        even, odd = [dot(rows_back[parity], three(adjoints[group][parity])) for parity in range(2)]
        for pair in range(2):
            at = slice(128 * pair, 128 * pair + 128)
            real = swap(even[:BAND, at], odd[:BAND, at])
            imag = swap(even[BAND:, at], odd[BAND:, at])
            for which in range(2):
                sides[which].append(jnp.concatenate([real[which], imag[which]], axis=1))
    for which in range(2):
        high, low = cut(jnp.concatenate(sides[which], axis=0))
        both = dot(high, cols_back[which])
        term = both[:, :128] + both[:, 128:] + dot(low, cols_back[which][:, :128])
        for k in range(PER_DEV // 2):
            total = total + term[BAND * k : BAND * k + BAND] * pupils[2 * k + which]
    return total


def fold(grad, roll):
    r32, r64, r96 = roll(grad, 32, 1), roll(grad, 64, 1), roll(grad, 96, 1)
    quarter = lanes(grad.shape) >> 5
    upper = jnp.where(
        quarter == 0, grad + r96, jnp.where(quarter == 1, r96 - r64, jnp.where(quarter == 2, r64 + r32, r32 - grad))
    )
    lower = jnp.where(
        quarter == 0, r64 + r32, jnp.where(quarter == 1, grad - r32, jnp.where(quarter == 2, grad + r96, r64 - r96))
    )
    return jnp.concatenate([upper, lower], axis=0)


def row_grads(grad, leave, leave_low, roll):
    high, low = cut(fold(grad, roll))
    out = dot(leave, jnp.concatenate([high, low], axis=0)) + dot(leave_low, high)
    half = out.shape[0] // 2
    return pack(out[:half], out[half:])


def last_step(total, last, last_low):
    first = lanes(total.shape) < 64
    value = jnp.concatenate([jnp.where(first, total, 0.0), jnp.where(first, 0.0, total)], axis=0)
    high, low = cut(value)
    return dot(high, last) + dot(low, last) + dot(high, last_low)


def rank_of(side, along):
    return 2 * jnp.where(along < DEPTH // 2, along, DEPTH + DEPTH // 2 - 1 - along) + side


def src_of(rank):
    step, side = rank // 2, rank % 2
    return side * DEPTH + jnp.where(step < DEPTH // 2, step, DEPTH + DEPTH // 2 - 1 - step)


RANKED = tuple(side * DEPTH + along for along in (0, 1, 2, 3, 7, 6, 5, 4) for side in range(2))
SERVED = tuple(range(0, N_SRC, 2)) + tuple(range(1, N_SRC, 2))


def repeat(first, last, body):
    def step(k, carry):
        body(k)
        return carry

    lax.fori_loop(first, last, step, 0)


def everything(mask, target, shifts, weights, table, resist, mask_grad, source_grad, *scratch):
    (
        mask_v, target_v, shifts_v, weights_v, table_v,
        left_v, right_v, spec_v, pupil_v, scale_v, term_v, field_v, power_v,
        printed_v, grad_v, part_v, sums_v, total_v, local_sem, send_sem, recv_sem, ready_sem, hub_sem,
    ) = scratch
    tile, src = lax.axis_index("tile"), lax.axis_index("src")
    n_tile = lax.axis_size("tile")
    left, right = tile - 1, tile + 1
    has_left, has_right = tile > 0, tile < n_tile - 1
    side, along = src // DEPTH, src % DEPTH
    rank = rank_of(side, along)
    quad = along // QUAD
    partners = [
        (side + across) % 2 * DEPTH + (along + step) % DEPTH for across, step in ((0, QUAD), (1, 0), (1, QUAD))
    ]
    members = [side * DEPTH + quad * QUAD + (along + k) % QUAD for k in range(1, QUAD)]
    layer = tile // GROUP
    place = tile % GROUP
    is_hub, is_teller = tile < HUB, layer == 1

    def get(name, start=None, stop=None):
        at, size = PLACES[name]
        if start is None:
            return table_v[at : at + size, :]
        return table_v[at : at + size, start:stop]

    def signal(sem, device):
        pl.semaphore_signal(sem, inc=1, device_id=device, device_id_type=MESH)

    def send(source, target_ref, number, device):
        copy = pltpu.make_async_remote_copy(
            src_ref=source,
            dst_ref=target_ref,
            send_sem=send_sem.at[number],
            recv_sem=recv_sem.at[number],
            device_id=device,
            device_id_type=MESH,
        )
        copy.start()

    def wait(ref, sem):
        pltpu.make_async_copy(ref, ref, sem).wait()

    barrier = pltpu.get_barrier_semaphore()

    @pl.when(has_left)
    def _():
        signal(barrier, {"tile": left})

    @pl.when(has_right)
    def _():
        signal(barrier, {"tile": right})

    repeat(rank + 1, N_SRC, lambda k: signal(barrier, {"src": src_of(k)}))
    local = [
        pltpu.make_async_copy(mask, mask_v, local_sem.at[0]),
        pltpu.make_async_copy(shifts, shifts_v, local_sem.at[1]),
        pltpu.make_async_copy(weights, weights_v, local_sem.at[2]),
    ]
    for k in range(3):
        rows = pl.ds(CUTS[k], CUTS[k + 1] - CUTS[k])
        local.append(pltpu.make_async_copy(table.at[rows], table_v.at[rows], local_sem.at[3 + k]))
    local.append(pltpu.make_async_copy(target, target_v, local_sem.at[6]))
    local[0].start()
    local[3].start()
    repeat(jnp.where(is_hub, tile + 1, n_tile), n_tile, lambda k: signal(barrier, {"tile": k}))

    ends = has_left.astype(jnp.int32) + has_right.astype(jnp.int32)
    pl.semaphore_wait(barrier, rank + ends + jnp.minimum(tile, HUB))

    @pl.when(has_right)
    def _():
        send(mask.at[:, pl.ds(128, 128)], left_v, 0, {"tile": right})

    @pl.when(has_left)
    def _():
        send(mask.at[:, pl.ds(0, 128)], right_v, 1, {"tile": left})

    for k in (1, 2, 4, 5, 6):
        local[k].start()
    term_v[:, POINTS_R // 2 :, :] = jnp.zeros((QUAD, (ROWS_C - POINTS_R) // 2, 128), jnp.float32)

    @pl.when(jnp.logical_not(has_left))
    def _():
        left_v[...] = jnp.zeros_like(left_v)

    @pl.when(jnp.logical_not(has_right))
    def _():
        right_v[...] = jnp.zeros_like(right_v)

    local[1].wait()
    local[2].wait()
    spec_v[src, 8:16, :] = jnp.zeros((8, 128), jnp.float32)
    spec_v[src, 8:10, 0:PER_DEV] = shifts_v[...].astype(jnp.float32)
    spec_v[src, 10:11, 0:PER_DEV] = weights_v[...]
    local[0].wait()
    local[3].wait()
    at = PLACES["enter"][0]
    own = enter(mask_v[...], table_v[at : at + TILE, :])
    for k in SERVED:
        pl.when(k < rank)(functools.partial(signal, ready_sem.at[rank], {"src": RANKED[k]}))

    @pl.when(has_left)
    def _():
        wait(left_v, recv_sem.at[0])

    @pl.when(has_right)
    def _():
        wait(right_v, recv_sem.at[1])

    margins = jnp.concatenate([left_v[...], right_v[...]], axis=1)
    own = own + enter(margins, table_v[at + TILE : at + 2 * TILE, :])
    spec_v[src, 0:8, :] = pack(own[:8], own[8:])
    piece = pl.ds(0, 11)

    def send_piece(k):
        send(spec_v.at[src, piece], spec_v.at[src, piece], 2, {"src": RANKED[k]})

    def answer_piece(k):
        pl.semaphore_wait(ready_sem.at[k], 1)
        send_piece(k)

    for k in SERVED:
        pl.when(k < rank)(functools.partial(send_piece, k))
    for k in range(1, N_SRC):
        pl.when(k > rank)(functools.partial(answer_piece, k))
    repeat(0, jnp.where(is_hub, tile, 0), lambda k: signal(hub_sem.at[0], {"tile": k}))

    @pl.when(jnp.logical_not(is_hub))
    def _():
        signal(hub_sem.at[1], {"tile": GROUP + place})

    local[4].wait()
    wait(spec_v.at[pl.ds(0, N_SRC - 1), piece], recv_sem.at[2])

    gathered = spec_v[:, 0:8, :].reshape(128, 128)
    spec = spectrum(gathered, get("spec"), get("lows_a", 0, 128), pltpu.roll)
    at = PLACES["lows_b"][0]
    cols = [(get("cols_" + name), get("cols_low_" + name)) for name in ("even", "odd")]
    rows = [
        (get("rows_even"), table_v[at : at + ROWS_C, 128:256]),
        (get("rows_odd"), table_v[at + ROWS_C : at + 2 * ROWS_C, 128:256]),
    ]

    def add_fields(part, images):
        owner = src
        for k, peer in enumerate(partners):
            owner = jnp.where(part == k + 1, peer, owner)
        extra = spec_v[owner, 8:16, :]
        shift = extra[0:2, :].astype(jnp.int32)
        for s in range(PER_DEV):
            pupil_v[part, s] = pupil_of(shift[0:1, s : s + 1], shift[1:2, s : s + 1])
        for pair in range(PER_DEV // 2):
            first, second = [
                jnp.broadcast_to(extra[2:3, s : s + 1], (8, 128)) for s in (2 * pair, 2 * pair + 1)
            ]
            at = slice(128 * (pair % 2), 128 * (pair % 2) + 128)
            for parity, scale in enumerate(swap(first, second)):
                scale_v[part, pair // 2, parity, :, at] = scale
        fields = coarse_fields(
            spec, [pupil_v[part, s].astype(jnp.bfloat16) for s in range(PER_DEV)], cols, rows
        )
        images = list(images)
        for group in range(2):
            for parity in range(2):
                field_v[part, group, parity] = fields[group][parity]
                power = power_of(fields[group][parity])
                power_v[part, group, parity] = power
                power = power * scale_v[part, group, parity, 0:1, :]
                images[parity] = images[parity] + power[:, :128] + power[:, 128:]
        return tuple(images)

    none = jnp.zeros((ROWS_C // 2, 128), jnp.float32)
    image = lax.fori_loop(0, QUAD, add_fields, (none, none), unroll=True)
    place_in_quad = along % QUAD
    term_v[place_in_quad] = join_image(*image, pltpu.roll)
    image_rows = pl.ds(0, POINTS_R // 2)
    mine = term_v.at[place_in_quad, image_rows]

    def send_image(k):
        send(mine, mine, 3, {"src": side * DEPTH + quad * QUAD + k})

    for k in range(QUAD):
        pl.when(k != place_in_quad)(functools.partial(send_image, k))
    local[5].wait()
    local[6].wait()
    wait(term_v.at[pl.ds(0, QUAD - 1), image_rows], recv_sem.at[3])

    image = pixels_of(
        term_v[0] + term_v[1] + term_v[2] + term_v[3],
        get("fine_rows"),
        get("fine_cols"),
        get("fine_cols_low"),
    )
    printed = jax.nn.sigmoid(STEEP * (image * (1.0 / SOURCES) - THRESH))
    printed_v[...] = printed
    resist[...] = printed_v[pl.ds(pl.multiple_of(src * ROWS, ROWS), ROWS), :]
    goal = target_v[...].astype(jnp.float32)
    slope = (LOSS_SCALE * 2.0 * STEEP) * (printed - goal) * printed * (1.0 - printed)
    coarse = coarse_of(slope, get("coarse_rows"), get("coarse_rows_low"), get("coarse_cols"))

    slopes = twice(coarse, pltpu.roll)
    sums = []
    for pair in range(PER_DEV // 2):
        at = slice(128 * (pair % 2), 128 * (pair % 2) + 128)
        terms = [
            jnp.sum(slopes[parity] * power_v[0, pair // 2, parity, :, at], axis=0, keepdims=True) for parity in range(2)
        ]
        sums.extend(swap(*terms))
    sums = jnp.sum(jnp.concatenate(sums, axis=0), axis=1, keepdims=True)
    spot = (PER_DEV, 128)
    sums = jnp.where(lanes(spot) == lax.broadcasted_iota(jnp.int32, spot, 0), sums, 0.0)
    sums_v[tile] = jnp.sum(sums, axis=0, keepdims=True)

    def send_sums(k):
        pltpu.make_async_remote_copy(
            src_ref=sums_v.at[tile],
            dst_ref=sums_v.at[tile],
            send_sem=send_sem.at[5],
            recv_sem=recv_sem.at[5],
            device_id={"tile": k},
            device_id_type=MESH,
        ).start()

    for k in range(HUB):
        first = k + 1 - 2 * (k % 2)
        pl.when(first < tile)(functools.partial(send_sums, first))

    wide = [jnp.concatenate([slope, slope], axis=1) * (2.0 / SOURCES) for slope in slopes]
    rows_back = [get("rows_back_even"), get("rows_back_odd")]
    cols_back = [get("cols_back_even"), get("cols_back_odd")]

    def add_part(part, total):
        adjoints = []
        for group in range(2):
            adjoints.append([])
            for parity in range(2):
                scaled = wide[parity] * scale_v[part, group, parity, 0:1, :]
                adjoints[group].append(field_v[part, group, parity] * jnp.concatenate([scaled, scaled], axis=0))
        return band_grad(total, adjoints, [pupil_v[part, s] for s in range(PER_DEV)], rows_back, cols_back)

    grad = lax.fori_loop(0, QUAD, add_part, jnp.zeros((BAND, 128), jnp.float32))
    first = PLACES["leave"][0] + 8 * QUAD * (src // QUAD)
    low_first = PLACES["lows_b"][0] + 8 * QUAD * (src // QUAD)

    def halves_of(start, stop, begin):
        begin = pl.multiple_of(begin, 32)
        then = pl.multiple_of(begin + 128, 32)
        return jnp.concatenate(
            [table_v[pl.ds(begin, 8 * QUAD), start:stop], table_v[pl.ds(then, 8 * QUAD), start:stop]], axis=0
        )

    rows = row_grads(grad, halves_of(0, 256, first), halves_of(0, 128, low_first), pltpu.roll)
    grad_v[...] = rows.reshape(QUAD, 8, 128)
    for k, peer in enumerate(members):
        send(grad_v.at[peer % QUAD], part_v.at[k], 4, {"src": peer})


    @pl.when(tile < HUB - 1)
    def _():
        pl.semaphore_wait(hub_sem.at[0], HUB - 1 - tile)
        repeat(tile + 1, HUB, send_sums)

    wait(part_v, recv_sem.at[4])
    total = grad_v[along % QUAD] + part_v[0] + part_v[1] + part_v[2]
    mask_grad[...] = last_step(total, get("last"), get("last_low"))

    @pl.when(is_hub)
    def _():
        wait(sums_v.at[pl.ds(0, n_tile - 1)], recv_sem.at[5])
        total_v[...] = jnp.sum(sums_v[...], axis=0) * (1.0 / (SOURCES * n_tile * TILE * TILE))

    def tell(k):
        send(total_v, total_v, 6, {"tile": k * GROUP + place})

    @pl.when(is_teller)
    def _():
        pl.semaphore_wait(hub_sem.at[1], n_tile // GROUP - 2)
        repeat(2, n_tile // GROUP, tell)

    @pl.when(jnp.logical_not(is_hub))
    def _():
        wait(total_v, recv_sem.at[6])

    source_grad[...] = total_v[...]

    @pl.when(is_teller)
    def _():
        wait(sums_v.at[pl.ds(0, n_tile // GROUP - 2)], send_sem.at[6])

    @pl.when(is_hub)
    def _():
        wait(sums_v.at[pl.ds(0, HUB - 1)], send_sem.at[5])

    @pl.when(jnp.logical_not(is_hub))
    def _():
        wait(sums_v.at[pl.ds(0, HUB)], send_sem.at[5])


    @pl.when(has_right)
    def _():
        wait(left_v, send_sem.at[0])

    @pl.when(has_left)
    def _():
        wait(right_v, send_sem.at[1])

    wait(spec_v.at[pl.ds(0, N_SRC - 1), piece], send_sem.at[2])
    wait(term_v.at[pl.ds(0, QUAD - 1), image_rows], send_sem.at[3])
    wait(part_v, send_sem.at[4])


def hand_over(resist, mask_grad, source_grad, resist_out, mask_grad_out, source_grad_out, sem):
    copies = [
        pltpu.make_async_copy(resist, resist_out, sem.at[0]),
        pltpu.make_async_copy(mask_grad, mask_grad_out, sem.at[1]),
    ]
    for copy in copies:
        copy.start()
    source_grad_out[...] = source_grad[0, :PER_DEV]
    for copy in copies:
        copy.wait()


def local(mask, target, shifts, weights):
    f32 = jnp.float32
    anywhere = pl.BlockSpec(memory_space=pl.ANY)
    inside = pl.BlockSpec(memory_space=pltpu.VMEM)
    results = pl.pallas_call(
        everything,
        out_shape=(
            pltpu.VMEM((ROWS, TILE), f32),
            pltpu.VMEM((ROWS, TILE), f32),
            pltpu.VMEM((1, 128), f32),
        ),
        in_specs=[anywhere] * 5,
        out_specs=(inside, inside, inside),
        scratch_shapes=[
            pltpu.VMEM((ROWS, TILE), f32),
            pltpu.VMEM((TILE, TILE), jnp.int32),
            pltpu.VMEM((2, PER_DEV), jnp.int32),
            pltpu.VMEM((1, PER_DEV), f32),
            pltpu.VMEM(TABLE.shape, jnp.bfloat16),
            pltpu.VMEM((ROWS, 128), f32),
            pltpu.VMEM((ROWS, 128), f32),
            pltpu.VMEM((N_SRC, 16, 128), f32),
            pltpu.VMEM((QUAD, PER_DEV, BAND, 128), f32),
            pltpu.VMEM((QUAD, 2, 2, 8, 256), f32),
            pltpu.VMEM((QUAD, ROWS_C // 2, 128), f32),
            pltpu.VMEM((QUAD, 2, 2, ROWS_C, 256), f32),
            pltpu.VMEM((QUAD, 2, 2, ROWS_C // 2, 256), f32),
            pltpu.VMEM((TILE, TILE), f32),
            pltpu.VMEM((QUAD, 8, 128), f32),
            pltpu.VMEM((QUAD - 1, 8, 128), f32),
            pltpu.VMEM((N_TILE, 1, 128), f32),
            pltpu.VMEM((1, 128), f32),
            pltpu.SemaphoreType.DMA((7,)),
            pltpu.SemaphoreType.DMA((7,)),
            pltpu.SemaphoreType.DMA((7,)),
            pltpu.SemaphoreType.REGULAR((N_SRC,)),
            pltpu.SemaphoreType.REGULAR((2,)),
        ],
        compiler_params=pltpu.CompilerParams(
            collective_id=0, has_side_effects=True, vmem_limit_bytes=60 * 1024 * 1024
        ),
    )(mask, target, shifts.T, weights.reshape(1, PER_DEV), jnp.asarray(TABLE))
    return pl.pallas_call(
        hand_over,
        out_shape=(
            jax.ShapeDtypeStruct((ROWS, TILE), f32),
            jax.ShapeDtypeStruct((ROWS, TILE), f32),
            jax.ShapeDtypeStruct((PER_DEV,), f32),
        ),
        in_specs=[inside] * 3,
        out_specs=(anywhere, anywhere, inside),
        scratch_shapes=[pltpu.SemaphoreType.DMA((2,))],
    )(*[pltpu.with_memory_space_constraint(result, pltpu.VMEM) for result in results])


def solution(mesh):
    placed = (P("src", "tile"), P(None, "tile"), P("src", None), P("src"))
    return jax.shard_map(
        local,
        mesh=mesh,
        in_specs=placed,
        out_specs=(P("src", "tile"), P("src", "tile"), P("src")),
        check_vma=False,
    )
```

```python
import functools

import jax
import jax.numpy as jnp
import ml_dtypes
import numpy as np
from jax import lax
from jax.experimental import pallas as pl
from jax.experimental.pallas import tpu as pltpu
from jax.sharding import PartitionSpec as P

TILE = 256
MARGIN = 32
BAND = 64
RAD = 16
EXT = 320
STEEP = 8.0
THRESH = 0.25
LOSS_SCALE = 2.0

N_SRC = 16
N_TILE = 32
PER_DEV = 8
SOURCES = 128
ROWS = 16
HALF = 32
POINTS_R = 66
ROWS_C = 80
COLS_C = 128
QUAD = 4
GROUP = 4
DEPTH = 8
HUB = 3 * GROUP
RIDERS = (31, 63, 95)

MESH = pl.DeviceIdType.MESH
BF16 = ml_dtypes.bfloat16


def halves(table):
    high = table.astype(BF16)
    low = (table - high.astype(np.float64)).astype(BF16)
    return high, low


def column_slots():
    plus = np.arange(HALF)
    return np.concatenate([plus, -plus]), np.concatenate([np.ones(HALF), [0.0], np.ones(HALF - 1)])


def waves(freq, place, period):
    phase = 2.0 * np.pi * ((freq[:, None] * place[None, :]) % period) / period
    return np.cos(phase), np.sin(phase)


def interpolation(points):
    order = np.arange(-2 * RAD, 2 * RAD + 1)
    place = np.arange(TILE) + MARGIN
    offset = place[:, None] / EXT - np.arange(points)[None, :] / points
    return np.cos(2.0 * np.pi * order[None, None, :] * offset[:, :, None]).sum(axis=2) / points


def padded(rows):
    return np.concatenate([rows, np.zeros((ROWS_C // 2 - rows.shape[0], rows.shape[1]))], axis=0)


def build_tables():
    slots, used = column_slots()
    row_freq = np.arange(BAND) - BAND // 2
    pixels = np.arange(TILE) + MARGIN
    parts = {}

    real, imag = waves(np.arange(HALF), np.arange(EXT), EXT)
    fwd = np.concatenate([real, -imag], axis=0).T
    wide = np.zeros((2 * TILE, 2 * HALF))
    wide[:TILE] = fwd[MARGIN : MARGIN + TILE]
    wide[TILE + 96 : TILE + 128] = fwd[:MARGIN]
    wide[TILE + 128 : TILE + 160] = fwd[MARGIN + TILE :]
    high, low = halves(np.concatenate([wide, wide], axis=1))
    parts["enter"] = np.concatenate([high, low], axis=1)

    rows = np.arange(TILE).reshape(N_SRC, 2, 8)
    first, second = rows[:, 0].reshape(-1), rows[:, 1].reshape(-1)
    real, imag = waves(row_freq, pixels, EXT)
    both = np.concatenate([real, -imag], axis=0)
    high, low = halves(np.concatenate([both[:, first], both[:, second]], axis=0))
    parts["spec"] = np.concatenate([high, high], axis=1)
    spec_low = low

    inter_rows, inter_cols = 2.0 * interpolation(POINTS_R), interpolation(COLS_C)
    even, odd = np.arange(0, COLS_C, 2), np.arange(1, COLS_C, 2)
    for name, order in (("even", np.concatenate([even, odd])), ("odd", np.concatenate([odd, even]))):
        real, imag = waves(slots, order, COLS_C)
        real, imag = real * used[:, None], imag * used[:, None]
        cols = np.concatenate(
            [np.concatenate([real, imag], axis=1), np.concatenate([-imag, real], axis=1)], axis=0
        )
        high, low = halves(cols)
        parts["cols_" + name] = np.concatenate([high, high], axis=0)
        parts["cols_low_" + name] = np.concatenate([low, high], axis=0)
        high, low = halves(np.concatenate([cols[:, :COLS_C].T, cols[:, COLS_C:].T], axis=0))
        parts["cols_back_" + name] = np.concatenate([high, low], axis=1)

    lows = []
    for name, start in (("even", 0), ("odd", 1)):
        real, imag = waves(row_freq, np.arange(start, POINTS_R, 2), POINTS_R)
        real, imag = padded(real.T), padded(imag.T)
        high, low = halves(
            np.concatenate(
                [np.concatenate([real, -imag], axis=1), np.concatenate([imag, real], axis=1)], axis=0
            )
        )
        parts["rows_" + name] = np.concatenate([high, high], axis=1)
        lows.append(low)
        pad = np.zeros((2 * BAND, TILE - 3 * ROWS_C), BF16)
        parts["rows_back_" + name] = np.concatenate([high.T, high.T, low.T, pad], axis=1)
    rows_low = np.concatenate(lows, axis=0)

    inter_rows = np.concatenate([padded(inter_rows[:, 0::2].T), padded(inter_rows[:, 1::2].T)], axis=0).T
    inter_cols = inter_cols[:, np.concatenate([even, odd])]
    high, low = halves(inter_rows)
    pad = np.zeros((TILE, TILE - 3 * ROWS_C), BF16)
    parts["fine_rows"] = np.concatenate([high, high, low, pad], axis=1)
    high, low = halves(inter_cols.T)
    parts["fine_cols"] = np.concatenate([high, high], axis=0)
    parts["fine_cols_low"] = low
    parts["coarse_cols"] = np.concatenate([high.T, low.T], axis=1)
    high, low = halves(inter_rows.T)
    parts["coarse_rows"] = high
    parts["coarse_rows_low"] = low

    owners = [
        side * DEPTH + (quad * QUAD + k - 1) % DEPTH for side in range(2) for quad in range(2) for k in range(QUAD)
    ]
    first, second = rows[owners, 0].reshape(-1), rows[owners, 1].reshape(-1)
    high, low = halves(np.concatenate([both[:, first], both[:, second]], axis=1).T)
    parts["leave"] = np.concatenate([high, high], axis=1)
    leave_low = low
    last = fwd[MARGIN : MARGIN + TILE].T
    high, low = halves(np.concatenate([last, last], axis=0))
    parts["last"] = high
    parts["last_low"] = low

    parts["lows_a"] = np.concatenate([spec_low, np.zeros((TILE, 128), BF16)], axis=1)
    rows_low = np.concatenate([rows_low, np.zeros((TILE - 2 * ROWS_C, 128), BF16)], axis=0)
    parts["lows_b"] = np.concatenate([leave_low, rows_low], axis=1)

    order = [
        "enter",
        "spec", "lows_a", "cols_even", "cols_low_even", "cols_odd", "cols_low_odd", "rows_even", "rows_odd", "lows_b",
        "fine_rows", "fine_cols", "fine_cols_low", "coarse_cols", "coarse_rows", "coarse_rows_low",
        "rows_back_even", "rows_back_odd", "cols_back_even", "cols_back_odd", "leave", "last", "last_low",
    ]
    places, start = {}, 0
    for name in order:
        places[name] = (start, parts[name].shape[0])
        start += parts[name].shape[0]
    return np.concatenate([parts[name] for name in order], axis=0), places


TABLE, PLACES = build_tables()
CUTS = (0, PLACES["spec"][0], PLACES["fine_rows"][0], TABLE.shape[0])


def dot(left, right):
    return jnp.dot(left, right, preferred_element_type=jnp.float32)


def cut(value):
    high = value.astype(jnp.bfloat16)
    low = (value - high.astype(jnp.float32)).astype(jnp.bfloat16)
    return high, low


def lanes(shape):
    return lax.broadcasted_iota(jnp.int32, shape, 1)


def enter(value, table):
    high, low = cut(value)
    both = dot(high, table)
    return both[:, :128] + both[:, 128:] + dot(low, table[:, :128])


def pack(first, second):
    return jnp.where(lanes(first.shape) < 64, first, second)


def spectrum(gathered, table, low_table, roll):
    high, low = cut(gathered)
    out = dot(table, jnp.concatenate([high, low], axis=0)) + dot(low_table, high)
    both = pack(out[:128], out[128:])
    both = both + roll(both, 64, 1)
    turned = roll(both, 32, 1)
    quarter = lanes((BAND, 128)) >> 5
    outer = (quarter == 0) | (quarter == 3)
    even = jnp.where(outer, both[:BAND], turned[:BAND])
    odd = jnp.where(outer, turned[BAND:], both[BAND:])
    return (jnp.where(quarter == 3, -even, even) + jnp.where(quarter == 0, -odd, odd)) * (1.0 / (EXT * EXT))


def pupil_of(row_shift, col_shift):
    row = (lax.broadcasted_iota(jnp.int32, (BAND, 128), 0) - BAND // 2).astype(jnp.float32) + row_shift
    slot = lanes((1, 128)) & 63
    col = jnp.where(slot < HALF, slot, HALF - slot).astype(jnp.float32) + col_shift
    room = jnp.where(slot == HALF, -1.0, RAD * RAD - col * col)
    return jnp.where(row * row <= room, 1.0, 0.0)


def swap(first, second):
    return pack(first, second), pack(second, first)


def coarse_fields(spec, pupils, cols, rows):
    high = spec.astype(jnp.bfloat16)
    rest = spec - high.astype(jnp.float32)
    low, lowest = cut(rest)
    mids = []
    for which in range(2):
        band_high, band_low, band_lowest = [
            jnp.concatenate([part * pupil for pupil in pupils[which::2]], axis=0) for part in (high, low, lowest)
        ]
        table, low_table = cols[which]
        mids.append(
            dot(jnp.concatenate([band_high, band_low], axis=1), table)
            + dot(jnp.concatenate([band_high, band_lowest], axis=1), low_table)
        )
    fields = []
    for group in range(2):
        stacks = ([], [])
        for pair in (2 * group, 2 * group + 1):
            at = slice(BAND * pair, BAND * pair + BAND)
            real = swap(mids[0][at, :128], mids[1][at, :128])
            imag = swap(mids[0][at, 128:], mids[1][at, 128:])
            for parity in range(2):
                stacks[parity].append(jnp.concatenate([real[parity], imag[parity]], axis=0))
        both = []
        for parity in range(2):
            upper, lower = cut(jnp.concatenate(stacks[parity], axis=1))
            table, low_table = rows[parity]
            both.append(dot(table, jnp.concatenate([upper, lower], axis=0)) + dot(low_table, upper))
        fields.append(both)
    return fields


def power_of(field):
    half = ROWS_C // 2
    return field[:half] * field[:half] + field[half:] * field[half:]


def join_image(even, odd, roll):
    return pack(even + roll(even, 64, 1), odd + roll(odd, 64, 1))


def pixels_of(coarse, fine_rows, fine_cols, fine_cols_low):
    first = lanes(coarse.shape) < 64
    coarse = jnp.concatenate([jnp.where(first, coarse, 0.0), jnp.where(first, 0.0, coarse)], axis=0)
    high, low = cut(coarse)
    mid = dot(jnp.concatenate([high, low], axis=1), fine_cols) + dot(high, fine_cols_low)
    return dot(fine_rows, three(mid))


def three(value):
    high, low = cut(value)
    pad = jnp.zeros((TILE - 3 * value.shape[0], value.shape[1]), jnp.bfloat16)
    return jnp.concatenate([high, low, high, pad], axis=0)


def coarse_of(slope, coarse_rows, coarse_rows_low, coarse_cols):
    high, low = cut(slope)
    mid = dot(coarse_rows, high) + dot(coarse_rows, low) + dot(coarse_rows_low, high)
    high, low = cut(mid)
    both = dot(high, coarse_cols)
    return both[:, :128] + both[:, 128:] + dot(low, coarse_cols[:, :128])


def twice(coarse, roll):
    half = ROWS_C // 2
    even, odd = coarse[:half], coarse[half:]
    return pack(even, roll(even, 64, 1)), pack(roll(odd, 64, 1), odd)


def band_grad(total, adjoints, pupils, rows_back, cols_back):
    sides = ([], [])
    for group in range(2):
        even, odd = [dot(rows_back[parity], three(adjoints[group][parity])) for parity in range(2)]
        for pair in range(2):
            at = slice(128 * pair, 128 * pair + 128)
            real = swap(even[:BAND, at], odd[:BAND, at])
            imag = swap(even[BAND:, at], odd[BAND:, at])
            for which in range(2):
                sides[which].append(jnp.concatenate([real[which], imag[which]], axis=1))
    for which in range(2):
        high, low = cut(jnp.concatenate(sides[which], axis=0))
        both = dot(high, cols_back[which])
        term = both[:, :128] + both[:, 128:] + dot(low, cols_back[which][:, :128])
        for k in range(PER_DEV // 2):
            total = total + term[BAND * k : BAND * k + BAND] * pupils[2 * k + which]
    return total


def fold(grad, roll):
    r32, r64, r96 = roll(grad, 32, 1), roll(grad, 64, 1), roll(grad, 96, 1)
    quarter = lanes(grad.shape) >> 5
    upper = jnp.where(
        quarter == 0, grad + r96, jnp.where(quarter == 1, r96 - r64, jnp.where(quarter == 2, r64 + r32, r32 - grad))
    )
    lower = jnp.where(
        quarter == 0, r64 + r32, jnp.where(quarter == 1, grad - r32, jnp.where(quarter == 2, grad + r96, r64 - r96))
    )
    return jnp.concatenate([upper, lower], axis=0)


def row_grads(grad, leave, leave_low, roll):
    high, low = cut(fold(grad, roll))
    out = dot(leave, jnp.concatenate([high, low], axis=0)) + dot(leave_low, high)
    half = out.shape[0] // 2
    return pack(out[:half], out[half:])


def last_step(total, last, last_low):
    first = lanes(total.shape) < 64
    value = jnp.concatenate([jnp.where(first, total, 0.0), jnp.where(first, 0.0, total)], axis=0)
    high, low = cut(value)
    return (dot(high, last) + dot(low, last) + dot(high, last_low)) * (1.0 / (EXT * EXT))


def rank_of(side, along):
    step = jnp.where(along == 3, 4, jnp.where(along == 7, 3, 11 - along))
    return 2 * jnp.where(along < 3, along, step) + side


def src_of(rank):
    step, side = rank // 2, rank % 2
    along = jnp.where(step == 3, 7, jnp.where(step == 4, 3, 11 - step))
    return side * DEPTH + jnp.where(step < 3, step, along)


def repeat(first, last, body):
    def step(k, carry):
        body(k)
        return carry

    lax.fori_loop(first, last, step, 0)


def everything(mask, target, shifts, weights, table, resist, mask_grad, source_grad, *scratch):
    (
        mask_v, target_v, shifts_v, weights_v, table_v,
        left_v, right_v, spec_v, pupil_v, scale_v, term_v, field_v, power_v,
        printed_v, grad_v, part_v, sums_v, total_v, local_sem, send_sem, recv_sem, ready_sem, hub_sem,
    ) = scratch
    tile, src = lax.axis_index("tile"), lax.axis_index("src")
    n_tile = lax.axis_size("tile")
    left, right = tile - 1, tile + 1
    has_left, has_right = tile > 0, tile < n_tile - 1
    side, along = src // DEPTH, src % DEPTH
    rank = rank_of(side, along)
    place_in_quad = (along + 1) % QUAD
    quad = (along + 1) % DEPTH // QUAD
    partners = [
        (side + across) % 2 * DEPTH + (along + step) % DEPTH for across, step in ((0, QUAD), (1, 0), (1, QUAD))
    ]

    def member(k):
        return side * DEPTH + (quad * QUAD + k + DEPTH - 1) % DEPTH

    layer = tile // GROUP
    place = tile % GROUP
    is_hub, is_teller = tile < HUB, layer == HUB // GROUP - 1

    def get(name, start=None, stop=None):
        at, size = PLACES[name]
        if start is None:
            return table_v[at : at + size, :]
        return table_v[at : at + size, start:stop]

    def signal(sem, device):
        pl.semaphore_signal(sem, inc=1, device_id=device, device_id_type=MESH)

    def send(source, target_ref, number, device):
        copy = pltpu.make_async_remote_copy(
            src_ref=source,
            dst_ref=target_ref,
            send_sem=send_sem.at[number],
            recv_sem=recv_sem.at[number],
            device_id=device,
            device_id_type=MESH,
        )
        copy.start()

    def wait(ref, sem):
        pltpu.make_async_copy(ref, ref, sem).wait()

    barrier = pltpu.get_barrier_semaphore()

    @pl.when(has_left)
    def _():
        signal(barrier, {"tile": left})

    @pl.when(has_right)
    def _():
        signal(barrier, {"tile": right})

    repeat(rank + 1, N_SRC, lambda k: signal(barrier, {"src": src_of(k)}))
    local = [
        pltpu.make_async_copy(mask, mask_v, local_sem.at[0]),
        pltpu.make_async_copy(shifts, shifts_v, local_sem.at[1]),
        pltpu.make_async_copy(weights, weights_v, local_sem.at[2]),
    ]
    for k in range(3):
        rows = pl.ds(CUTS[k], CUTS[k + 1] - CUTS[k])
        local.append(pltpu.make_async_copy(table.at[rows], table_v.at[rows], local_sem.at[3 + k]))
    local.append(pltpu.make_async_copy(target, target_v, local_sem.at[6]))
    local[0].start()
    local[3].start()
    repeat(jnp.where(is_hub, tile + 1, n_tile), n_tile, lambda k: signal(barrier, {"tile": k}))

    ends = has_left.astype(jnp.int32) + has_right.astype(jnp.int32)
    pl.semaphore_wait(barrier, rank + ends + jnp.minimum(tile, HUB))

    @pl.when(has_right)
    def _():
        send(mask.at[:, pl.ds(128, 128)], left_v, 0, {"tile": right})

    @pl.when(has_left)
    def _():
        send(mask.at[:, pl.ds(0, 128)], right_v, 1, {"tile": left})

    for k in (1, 2, 4, 5, 6):
        local[k].start()
    repeat(0, rank, lambda k: signal(ready_sem.at[rank], {"src": src_of(k)}))
    term_v[:, POINTS_R // 2 :, :] = jnp.zeros((QUAD, (ROWS_C - POINTS_R) // 2, 128), jnp.float32)

    @pl.when(jnp.logical_not(has_left))
    def _():
        left_v[...] = jnp.zeros_like(left_v)

    @pl.when(jnp.logical_not(has_right))
    def _():
        right_v[...] = jnp.zeros_like(right_v)

    local[1].wait()
    local[2].wait()
    shape = (PER_DEV, PER_DEV)
    own_place = lanes(shape) == lax.broadcasted_iota(jnp.int32, shape, 0)

    def upright(row):
        return jnp.sum(jnp.where(own_place, row, 0.0), axis=1, keepdims=True)

    own_shifts = shifts_v[...].astype(jnp.float32)
    riders = [upright(own_shifts[0:1, :]), upright(own_shifts[1:2, :]), upright(weights_v[...])]
    local[0].wait()
    local[3].wait()
    at = PLACES["enter"][0]
    own = enter(mask_v[...], table_v[at : at + TILE, :])

    @pl.when(has_left)
    def _():
        wait(left_v, recv_sem.at[0])

    @pl.when(has_right)
    def _():
        wait(right_v, recv_sem.at[1])

    margins = jnp.concatenate([left_v[...], right_v[...]], axis=1)
    own = own + enter(margins, table_v[at + TILE : at + 2 * TILE, :])
    own = pack(own[:8], own[8:])
    for lane, rider in zip(RIDERS, riders):
        own = jnp.where(lanes(own.shape) == lane, rider, own)
    spec_v[src] = own

    def send_piece(k):
        send(spec_v.at[src], spec_v.at[src], 2, {"src": src_of(k)})

    def answer_piece(k):
        pl.semaphore_wait(ready_sem.at[k], 1)
        send_piece(k)

    repeat(0, (rank + 1) // 2, lambda k: send_piece(2 * k))
    repeat(0, rank // 2, lambda k: send_piece(2 * k + 1))
    repeat(rank + 1, N_SRC, answer_piece)
    repeat(0, jnp.where(is_hub, tile, 0), lambda k: signal(hub_sem.at[0], {"tile": k}))

    @pl.when(jnp.logical_not(is_hub))
    def _():
        signal(hub_sem.at[1], {"tile": HUB - GROUP + place})

    local[4].wait()
    wait(spec_v.at[pl.ds(0, N_SRC - 1)], recv_sem.at[2])

    gathered = spec_v[...].reshape(128, 128)
    spec = spectrum(gathered, get("spec"), get("lows_a", 0, 128), pltpu.roll)
    at = PLACES["lows_b"][0]
    cols = [(get("cols_" + name), get("cols_low_" + name)) for name in ("even", "odd")]
    rows = [
        (get("rows_even"), table_v[at : at + ROWS_C, 128:256]),
        (get("rows_odd"), table_v[at + ROWS_C : at + 2 * ROWS_C, 128:256]),
    ]

    def add_fields(part, images):
        owner = src
        for k, peer in enumerate(partners):
            owner = jnp.where(part == k + 1, peer, owner)
        rows_by, cols_by, scales = [spec_v[owner, :, lane : lane + 1] for lane in RIDERS]
        for s in range(PER_DEV):
            pupil_v[part, s] = pupil_of(rows_by[s : s + 1], cols_by[s : s + 1])
        for pair in range(PER_DEV // 2):
            first, second = [jnp.broadcast_to(scales[s : s + 1], (8, 128)) for s in (2 * pair, 2 * pair + 1)]
            at = slice(128 * (pair % 2), 128 * (pair % 2) + 128)
            for parity, scale in enumerate(swap(first, second)):
                scale_v[part, pair // 2, parity, :, at] = scale
        fields = coarse_fields(
            spec, [pupil_v[part, s].astype(jnp.bfloat16) for s in range(PER_DEV)], cols, rows
        )
        images = list(images)
        for group in range(2):
            for parity in range(2):
                field_v[part, group, parity] = fields[group][parity]
                power = power_of(fields[group][parity])
                power_v[part, group, parity] = power
                power = power * scale_v[part, group, parity, 0:1, :]
                images[parity] = images[parity] + power[:, :128] + power[:, 128:]
        return tuple(images)

    none = jnp.zeros((ROWS_C // 2, 128), jnp.float32)
    image = lax.fori_loop(0, QUAD, add_fields, (none, none), unroll=True)
    term_v[place_in_quad] = join_image(*image, pltpu.roll)
    image_rows = pl.ds(0, POINTS_R // 2)
    mine = term_v.at[place_in_quad, image_rows]

    def send_image(k):
        send(mine, mine, 3, {"src": member(k)})

    for k in (1, 0, 2, 3):
        pl.when(k != place_in_quad)(functools.partial(send_image, k))
    local[5].wait()
    local[6].wait()
    wait(term_v.at[pl.ds(0, QUAD - 1), image_rows], recv_sem.at[3])

    image = pixels_of(
        term_v[0] + term_v[1] + term_v[2] + term_v[3],
        get("fine_rows"),
        get("fine_cols"),
        get("fine_cols_low"),
    )
    printed = jax.nn.sigmoid(STEEP * (image * (1.0 / SOURCES) - THRESH))
    printed_v[...] = printed
    resist[...] = printed_v[pl.ds(pl.multiple_of(src * ROWS, ROWS), ROWS), :]
    goal = target_v[...].astype(jnp.float32)
    slope = (LOSS_SCALE * 2.0 * STEEP) * (printed - goal) * printed * (1.0 - printed)
    coarse = coarse_of(slope, get("coarse_rows"), get("coarse_rows_low"), get("coarse_cols"))

    slopes = twice(coarse, pltpu.roll)
    sums = []
    for pair in range(PER_DEV // 2):
        at = slice(128 * (pair % 2), 128 * (pair % 2) + 128)
        terms = [
            jnp.sum(slopes[parity] * power_v[0, pair // 2, parity, :, at], axis=0, keepdims=True) for parity in range(2)
        ]
        sums.extend(swap(*terms))
    sums = jnp.sum(jnp.concatenate(sums, axis=0), axis=1, keepdims=True)
    spot = (PER_DEV, 128)
    sums = jnp.where(lanes(spot) == lax.broadcasted_iota(jnp.int32, spot, 0), sums, 0.0)
    sums_v[tile] = jnp.sum(sums, axis=0, keepdims=True)

    def send_sums(k):
        pltpu.make_async_remote_copy(
            src_ref=sums_v.at[tile],
            dst_ref=sums_v.at[tile],
            send_sem=send_sem.at[5],
            recv_sem=recv_sem.at[5],
            device_id={"tile": k},
            device_id_type=MESH,
        ).start()

    for k in range(HUB):
        first = k + 1 - 2 * (k % 2)
        pl.when(first < tile)(functools.partial(send_sums, first))

    wide = [jnp.concatenate([slope, slope], axis=1) * (2.0 / SOURCES) for slope in slopes]
    rows_back = [get("rows_back_even"), get("rows_back_odd")]
    cols_back = [get("cols_back_even"), get("cols_back_odd")]

    def add_part(part, total):
        adjoints = []
        for group in range(2):
            adjoints.append([])
            for parity in range(2):
                scaled = wide[parity] * scale_v[part, group, parity, 0:1, :]
                adjoints[group].append(field_v[part, group, parity] * jnp.concatenate([scaled, scaled], axis=0))
        return band_grad(total, adjoints, [pupil_v[part, s] for s in range(PER_DEV)], rows_back, cols_back)

    grad = lax.fori_loop(0, QUAD, add_part, jnp.zeros((BAND, 128), jnp.float32))
    first = PLACES["leave"][0] + 8 * QUAD * (2 * side + quad)
    low_first = PLACES["lows_b"][0] + 8 * QUAD * (2 * side + quad)

    def halves_of(start, stop, begin):
        begin = pl.multiple_of(begin, 32)
        then = pl.multiple_of(begin + 128, 32)
        return jnp.concatenate(
            [table_v[pl.ds(begin, 8 * QUAD), start:stop], table_v[pl.ds(then, 8 * QUAD), start:stop]], axis=0
        )

    rows = row_grads(grad, halves_of(0, 256, first), halves_of(0, 128, low_first), pltpu.roll)
    grad_v[...] = rows.reshape(QUAD, 8, 128)
    for k in range(1, QUAD):
        other = (place_in_quad + k) % QUAD
        send(grad_v.at[other], part_v.at[k - 1], 4, {"src": member(other)})

    @pl.when(tile < HUB - 1)
    def _():
        pl.semaphore_wait(hub_sem.at[0], HUB - 1 - tile)
        repeat(tile + 1, HUB, send_sums)

    wait(part_v, recv_sem.at[4])
    total = grad_v[place_in_quad] + part_v[0] + part_v[1] + part_v[2]
    mask_grad[...] = last_step(total, get("last"), get("last_low"))

    @pl.when(is_hub)
    def _():
        wait(sums_v.at[pl.ds(0, n_tile - 1)], recv_sem.at[5])
        total_v[...] = jnp.sum(sums_v[...], axis=0) * (1.0 / (SOURCES * n_tile * TILE * TILE))

    def tell(k):
        send(total_v, total_v, 6, {"tile": k * GROUP + place})

    @pl.when(is_teller)
    def _():
        pl.semaphore_wait(hub_sem.at[1], (n_tile - HUB) // GROUP)
        repeat(HUB // GROUP, n_tile // GROUP, tell)

    @pl.when(jnp.logical_not(is_hub))
    def _():
        wait(total_v, recv_sem.at[6])

    source_grad[...] = total_v[...]

    @pl.when(is_teller)
    def _():
        wait(sums_v.at[pl.ds(0, (n_tile - HUB) // GROUP)], send_sem.at[6])

    @pl.when(is_hub)
    def _():
        wait(sums_v.at[pl.ds(0, HUB - 1)], send_sem.at[5])

    @pl.when(jnp.logical_not(is_hub))
    def _():
        wait(sums_v.at[pl.ds(0, HUB)], send_sem.at[5])


    @pl.when(has_right)
    def _():
        wait(left_v, send_sem.at[0])

    @pl.when(has_left)
    def _():
        wait(right_v, send_sem.at[1])

    wait(spec_v.at[pl.ds(0, N_SRC - 1)], send_sem.at[2])
    wait(term_v.at[pl.ds(0, QUAD - 1), image_rows], send_sem.at[3])
    wait(part_v, send_sem.at[4])


def hand_over(resist, mask_grad, source_grad, resist_out, mask_grad_out, source_grad_out, row, sem):
    row[...] = source_grad[0, :PER_DEV]
    copies = [
        pltpu.make_async_copy(resist, resist_out, sem.at[0]),
        pltpu.make_async_copy(mask_grad, mask_grad_out, sem.at[1]),
        pltpu.make_async_copy(row, source_grad_out, sem.at[2]),
    ]
    for copy in copies:
        copy.start()
    for copy in copies:
        copy.wait()


def local(mask, target, shifts, weights):
    f32 = jnp.float32
    anywhere = pl.BlockSpec(memory_space=pl.ANY)
    inside = pl.BlockSpec(memory_space=pltpu.VMEM)
    results = pl.pallas_call(
        everything,
        out_shape=(
            pltpu.VMEM((ROWS, TILE), f32),
            pltpu.VMEM((ROWS, TILE), f32),
            pltpu.VMEM((1, 128), f32),
        ),
        in_specs=[anywhere] * 5,
        out_specs=(inside, inside, inside),
        scratch_shapes=[
            pltpu.VMEM((ROWS, TILE), f32),
            pltpu.VMEM((TILE, TILE), jnp.int32),
            pltpu.VMEM((2, PER_DEV), jnp.int32),
            pltpu.VMEM((1, PER_DEV), f32),
            pltpu.VMEM(TABLE.shape, jnp.bfloat16),
            pltpu.VMEM((ROWS, 128), f32),
            pltpu.VMEM((ROWS, 128), f32),
            pltpu.VMEM((N_SRC, 8, 128), f32),
            pltpu.VMEM((QUAD, PER_DEV, BAND, 128), f32),
            pltpu.VMEM((QUAD, 2, 2, 8, 256), f32),
            pltpu.VMEM((QUAD, ROWS_C // 2, 128), f32),
            pltpu.VMEM((QUAD, 2, 2, ROWS_C, 256), f32),
            pltpu.VMEM((QUAD, 2, 2, ROWS_C // 2, 256), f32),
            pltpu.VMEM((TILE, TILE), f32),
            pltpu.VMEM((QUAD, 8, 128), f32),
            pltpu.VMEM((QUAD - 1, 8, 128), f32),
            pltpu.VMEM((N_TILE, 1, 128), f32),
            pltpu.VMEM((1, 128), f32),
            pltpu.SemaphoreType.DMA((7,)),
            pltpu.SemaphoreType.DMA((7,)),
            pltpu.SemaphoreType.DMA((7,)),
            pltpu.SemaphoreType.REGULAR((N_SRC,)),
            pltpu.SemaphoreType.REGULAR((2,)),
        ],
        compiler_params=pltpu.CompilerParams(
            collective_id=0, has_side_effects=True, vmem_limit_bytes=60 * 1024 * 1024
        ),
    )(mask, target, shifts.T, weights.reshape(1, PER_DEV), jnp.asarray(TABLE))
    return pl.pallas_call(
        hand_over,
        out_shape=(
            jax.ShapeDtypeStruct((ROWS, TILE), f32),
            jax.ShapeDtypeStruct((ROWS, TILE), f32),
            jax.ShapeDtypeStruct((PER_DEV,), f32),
        ),
        in_specs=[inside] * 3,
        out_specs=(anywhere,) * 3,
        scratch_shapes=[pltpu.VMEM((PER_DEV,), f32), pltpu.SemaphoreType.DMA((3,))],
    )(*[pltpu.with_memory_space_constraint(result, pltpu.VMEM) for result in results])


def solution(mesh):
    placed = (P("src", "tile"), P(None, "tile"), P("src", None), P("src"))
    return jax.shard_map(
        local,
        mesh=mesh,
        in_specs=placed,
        out_specs=(P("src", "tile"), P("src", "tile"), P("src")),
        check_vma=False,
    )
```

```python
import functools

import jax
import jax.numpy as jnp
import ml_dtypes
import numpy as np
from jax import lax
from jax.experimental import pallas as pl
from jax.experimental.pallas import tpu as pltpu
from jax.sharding import PartitionSpec as P

TILE = 256
MARGIN = 32
BAND = 64
RAD = 16
EXT = 320
STEEP = 8.0
THRESH = 0.25
LOSS_SCALE = 2.0

N_SRC = 16
N_TILE = 32
PER_DEV = 8
SOURCES = 128
ROWS = 16
HALF = 32
POINTS_R = 66
ROWS_C = 80
COLS_C = 128
QUAD = 4
GROUP = 4
DEPTH = 8
HUB = 3 * GROUP
RIDERS = (31, 63, 95)

MESH = pl.DeviceIdType.MESH
BF16 = ml_dtypes.bfloat16


def halves(table):
    high = table.astype(BF16)
    low = (table - high.astype(np.float64)).astype(BF16)
    return high, low


def column_slots():
    plus = np.arange(HALF)
    return np.concatenate([plus, -plus]), np.concatenate([np.ones(HALF), [0.0], np.ones(HALF - 1)])


def waves(freq, place, period):
    phase = 2.0 * np.pi * ((freq[:, None] * place[None, :]) % period) / period
    return np.cos(phase), np.sin(phase)


def interpolation(points):
    order = np.arange(-2 * RAD, 2 * RAD + 1)
    place = np.arange(TILE) + MARGIN
    offset = place[:, None] / EXT - np.arange(points)[None, :] / points
    return np.cos(2.0 * np.pi * order[None, None, :] * offset[:, :, None]).sum(axis=2) / points


def padded(rows):
    return np.concatenate([rows, np.zeros((ROWS_C // 2 - rows.shape[0], rows.shape[1]))], axis=0)


def build_tables():
    slots, used = column_slots()
    row_freq = np.arange(BAND) - BAND // 2
    pixels = np.arange(TILE) + MARGIN
    parts = {}

    real, imag = waves(np.arange(HALF), np.arange(EXT), EXT)
    fwd = np.concatenate([real, -imag], axis=0).T
    wide = np.zeros((2 * TILE, 2 * HALF))
    wide[:TILE] = fwd[MARGIN : MARGIN + TILE]
    wide[TILE + 96 : TILE + 128] = fwd[:MARGIN]
    wide[TILE + 128 : TILE + 160] = fwd[MARGIN + TILE :]
    high, low = halves(np.concatenate([wide, wide], axis=1))
    parts["enter"] = np.concatenate([high, low], axis=1)

    rows = np.arange(TILE).reshape(N_SRC, 2, 8)
    first, second = rows[:, 0].reshape(-1), rows[:, 1].reshape(-1)
    real, imag = waves(row_freq, pixels, EXT)
    both = np.concatenate([real, -imag], axis=0)
    high, low = halves(np.concatenate([both[:, first], both[:, second]], axis=0))
    parts["spec"] = np.concatenate([high, high], axis=1)
    spec_low = low

    inter_rows, inter_cols = 2.0 * interpolation(POINTS_R), interpolation(COLS_C)
    even, odd = np.arange(0, COLS_C, 2), np.arange(1, COLS_C, 2)
    for name, order in (("even", np.concatenate([even, odd])), ("odd", np.concatenate([odd, even]))):
        real, imag = waves(slots, order, COLS_C)
        real, imag = real * used[:, None], imag * used[:, None]
        cols = np.concatenate(
            [np.concatenate([real, imag], axis=1), np.concatenate([-imag, real], axis=1)], axis=0
        )
        high, low = halves(cols)
        again = high.copy()
        again[[HALF, 3 * HALF]] = high[[0, 2 * HALF]]
        parts["cols_" + name] = np.concatenate([high, again], axis=0)
        parts["cols_low_" + name] = low
        high, low = halves(np.concatenate([cols[:, :COLS_C].T, cols[:, COLS_C:].T], axis=0))
        parts["cols_back_" + name] = np.concatenate([high, low], axis=1)

    lows = []
    for name, start in (("even", 0), ("odd", 1)):
        real, imag = waves(row_freq, np.arange(start, POINTS_R, 2), POINTS_R)
        real, imag = padded(real.T), padded(imag.T)
        high, low = halves(
            np.concatenate(
                [np.concatenate([real, -imag], axis=1), np.concatenate([imag, real], axis=1)], axis=0
            )
        )
        parts["rows_" + name] = np.concatenate([high, high], axis=1)
        lows.append(low)
        pad = np.zeros((2 * BAND, TILE - 3 * ROWS_C), BF16)
        parts["rows_back_" + name] = np.concatenate([high.T, high.T, low.T, pad], axis=1)
    rows_low = np.concatenate(lows, axis=0)

    inter_rows = np.concatenate([padded(inter_rows[:, 0::2].T), padded(inter_rows[:, 1::2].T)], axis=0).T
    inter_cols = inter_cols[:, np.concatenate([even, odd])]
    high, low = halves(inter_rows)
    pad = np.zeros((TILE, TILE - 3 * ROWS_C), BF16)
    parts["fine_rows"] = np.concatenate([high, high, low, pad], axis=1)
    high, low = halves(inter_cols.T)
    parts["fine_cols"] = np.concatenate([high, high], axis=0)
    parts["fine_cols_low"] = low
    parts["coarse_cols"] = np.concatenate([high.T, low.T], axis=1)
    high, low = halves(inter_rows.T)
    parts["coarse_rows"] = high
    parts["coarse_rows_low"] = low

    owners = [
        side * DEPTH + (quad * QUAD + k - 1) % DEPTH for side in range(2) for quad in range(2) for k in range(QUAD)
    ]
    first, second = rows[owners, 0].reshape(-1), rows[owners, 1].reshape(-1)
    high, low = halves(np.concatenate([both[:, first], both[:, second]], axis=1).T)
    parts["leave"] = np.concatenate([high, high], axis=1)
    leave_low = low
    last = fwd[MARGIN : MARGIN + TILE].T
    high, low = halves(np.concatenate([last, last], axis=0))
    parts["last"] = high
    parts["last_low"] = low

    parts["lows_a"] = np.concatenate([spec_low, np.zeros((TILE, 128), BF16)], axis=1)
    rows_low = np.concatenate([rows_low, np.zeros((TILE - 2 * ROWS_C, 128), BF16)], axis=0)
    parts["lows_b"] = np.concatenate([leave_low, rows_low], axis=1)

    order = [
        "enter",
        "spec", "lows_a", "cols_even", "cols_low_even", "cols_odd", "cols_low_odd", "rows_even", "rows_odd", "lows_b",
        "fine_rows", "fine_cols", "fine_cols_low", "coarse_cols", "coarse_rows", "coarse_rows_low",
        "rows_back_even", "rows_back_odd", "cols_back_even", "cols_back_odd", "leave", "last", "last_low",
    ]
    places, start = {}, 0
    for name in order:
        places[name] = (start, parts[name].shape[0])
        start += parts[name].shape[0]
    return np.concatenate([parts[name] for name in order], axis=0), places


TABLE, PLACES = build_tables()
CUTS = (0, PLACES["spec"][0], PLACES["fine_rows"][0], TABLE.shape[0])


def dot(left, right):
    return jnp.dot(left, right, preferred_element_type=jnp.float32)


def cut(value):
    high = value.astype(jnp.bfloat16)
    low = (value - high.astype(jnp.float32)).astype(jnp.bfloat16)
    return high, low


def lanes(shape):
    return lax.broadcasted_iota(jnp.int32, shape, 1)


def enter(value, table):
    rows = value.shape[0]
    both = dot(jnp.concatenate(cut(value), axis=0), table)
    return both[:rows, :128] + both[:rows, 128:] + both[rows:, :128]


def pack(first, second):
    return jnp.where(lanes(first.shape) < 64, first, second)


def spectrum(gathered, table, low_table, roll):
    high, low = cut(gathered)
    out = dot(table, jnp.concatenate([high, low], axis=0)) + dot(low_table, high)
    both = pack(out[:128], out[128:])
    both = both + roll(both, 64, 1)
    turned = roll(both, 32, 1)
    quarter = lanes((BAND, 128)) >> 5
    outer = (quarter == 0) | (quarter == 3)
    even = jnp.where(outer, both[:BAND], turned[:BAND])
    odd = jnp.where(outer, turned[BAND:], both[BAND:])
    return (jnp.where(quarter == 3, -even, even) + jnp.where(quarter == 0, -odd, odd)) * (1.0 / (EXT * EXT))


def pupil_of(row_shift, col_shift):
    row = (lax.broadcasted_iota(jnp.int32, (BAND, 128), 0) - BAND // 2).astype(jnp.float32) + row_shift
    slot = lanes((1, 128)) & 63
    col = jnp.where(slot < HALF, slot, HALF - slot).astype(jnp.float32) + col_shift
    room = RAD * RAD - col * col
    return jnp.where(row * row <= room, 1.0, 0.0)


def swap(first, second):
    return pack(first, second), pack(second, first)


def split_bands(spec, roll):
    spare = (lanes(spec.shape) & 63) == HALF
    high, low = cut(jnp.where(spare, 0.0, spec))
    left = spec - high.astype(jnp.float32) - low.astype(jnp.float32)
    low = jnp.where(spare, roll(left, HALF, 1), low.astype(jnp.float32)).astype(jnp.bfloat16)
    return high, low


def coarse_fields(bands, pupils, cols, rows):
    high, low = bands
    mids = []
    for which in range(2):
        band_high, band_low = [
            jnp.concatenate([part * pupil for pupil in pupils[which::2]], axis=0) for part in (high, low)
        ]
        table, low_table = cols[which]
        mids.append(
            dot(jnp.concatenate([band_high, band_low], axis=1), table) + dot(band_high, low_table)
        )
    fields = []
    for group in range(2):
        stacks = ([], [])
        for pair in (2 * group, 2 * group + 1):
            at = slice(BAND * pair, BAND * pair + BAND)
            real = swap(mids[0][at, :128], mids[1][at, :128])
            imag = swap(mids[0][at, 128:], mids[1][at, 128:])
            for parity in range(2):
                stacks[parity].append(jnp.concatenate([real[parity], imag[parity]], axis=0))
        both = []
        for parity in range(2):
            upper, lower = cut(jnp.concatenate(stacks[parity], axis=1))
            table, low_table = rows[parity]
            both.append(dot(table, jnp.concatenate([upper, lower], axis=0)) + dot(low_table, upper))
        fields.append(both)
    return fields


def power_of(field):
    half = ROWS_C // 2
    return field[:half] * field[:half] + field[half:] * field[half:]


def join_image(even, odd, roll):
    return pack(even + roll(even, 64, 1), odd + roll(odd, 64, 1))


def pixels_of(coarse, fine_rows, fine_cols, fine_cols_low):
    first = lanes(coarse.shape) < 64
    coarse = jnp.concatenate([jnp.where(first, coarse, 0.0), jnp.where(first, 0.0, coarse)], axis=0)
    high, low = cut(coarse)
    mid = dot(jnp.concatenate([high, low], axis=1), fine_cols) + dot(high, fine_cols_low)
    return dot(fine_rows, three(mid))


def three(value):
    high, low = cut(value)
    pad = jnp.zeros((TILE - 3 * value.shape[0], value.shape[1]), jnp.bfloat16)
    return jnp.concatenate([high, low, high, pad], axis=0)


def coarse_of(slope, coarse_rows, coarse_rows_low, coarse_cols):
    high, low = cut(slope)
    mid = dot(coarse_rows, high) + dot(coarse_rows, low) + dot(coarse_rows_low, high)
    high, low = cut(mid)
    both = dot(high, coarse_cols)
    return both[:, :128] + both[:, 128:] + dot(low, coarse_cols[:, :128])


def twice(coarse, roll):
    half = ROWS_C // 2
    even, odd = coarse[:half], coarse[half:]
    return pack(even, roll(even, 64, 1)), pack(roll(odd, 64, 1), odd)


def band_grad(total, adjoints, pupils, rows_back, cols_back):
    sides = ([], [])
    for group in range(2):
        even, odd = [dot(rows_back[parity], three(adjoints[group][parity])) for parity in range(2)]
        for pair in range(2):
            at = slice(128 * pair, 128 * pair + 128)
            real = swap(even[:BAND, at], odd[:BAND, at])
            imag = swap(even[BAND:, at], odd[BAND:, at])
            for which in range(2):
                sides[which].append(jnp.concatenate([real[which], imag[which]], axis=1))
    for which in range(2):
        high, low = cut(jnp.concatenate(sides[which], axis=0))
        both = dot(high, cols_back[which])
        term = both[:, :128] + both[:, 128:] + dot(low, cols_back[which][:, :128])
        for k in range(PER_DEV // 2):
            total = total + term[BAND * k : BAND * k + BAND] * pupils[2 * k + which]
    return total


def fold(grad, roll):
    r32, r64, r96 = roll(grad, 32, 1), roll(grad, 64, 1), roll(grad, 96, 1)
    quarter = lanes(grad.shape) >> 5
    upper = jnp.where(
        quarter == 0, grad + r96, jnp.where(quarter == 1, r96 - r64, jnp.where(quarter == 2, r64 + r32, r32 - grad))
    )
    lower = jnp.where(
        quarter == 0, r64 + r32, jnp.where(quarter == 1, grad - r32, jnp.where(quarter == 2, grad + r96, r64 - r96))
    )
    return jnp.concatenate([upper, lower], axis=0)


def row_grads(grad, leave, leave_low, roll):
    high, low = cut(fold(grad, roll))
    out = dot(leave, jnp.concatenate([high, low], axis=0)) + dot(leave_low, high)
    half = out.shape[0] // 2
    return pack(out[:half], out[half:])


def last_step(total, last, last_low):
    first = lanes(total.shape) < 64
    value = jnp.concatenate([jnp.where(first, total, 0.0), jnp.where(first, 0.0, total)], axis=0)
    high, low = cut(value)
    return (dot(high, last) + dot(low, last) + dot(high, last_low)) * (1.0 / (EXT * EXT))


def rank_of(side, along):
    step = jnp.where(along == 3, 4, jnp.where(along == 7, 3, 11 - along))
    return 2 * jnp.where(along < 3, along, step) + side


def src_of(rank):
    step, side = rank // 2, rank % 2
    along = jnp.where(step == 3, 7, jnp.where(step == 4, 3, 11 - step))
    return side * DEPTH + jnp.where(step < 3, step, along)


def repeat(first, last, body):
    def step(k, carry):
        body(k)
        return carry

    lax.fori_loop(first, last, step, 0)


def everything(mask, target, shifts, weights, table, resist, mask_grad, source_grad, *scratch):
    (
        mask_v, target_v, shifts_v, weights_v, table_v,
        left_v, right_v, spec_v, pupil_v, scale_v, term_v, field_v, power_v,
        printed_v, grad_v, part_v, sums_v, total_v, local_sem, send_sem, recv_sem, ready_sem, hub_sem,
    ) = scratch
    tile, src = lax.axis_index("tile"), lax.axis_index("src")
    n_tile = lax.axis_size("tile")
    left, right = tile - 1, tile + 1
    has_left, has_right = tile > 0, tile < n_tile - 1
    side, along = src // DEPTH, src % DEPTH
    rank = rank_of(side, along)
    place_in_quad = (along + 1) % QUAD
    quad = (along + 1) % DEPTH // QUAD
    partners = [
        (side + across) % 2 * DEPTH + (along + step) % DEPTH for across, step in ((0, QUAD), (1, 0), (1, QUAD))
    ]

    def member(k):
        return side * DEPTH + (quad * QUAD + k + DEPTH - 1) % DEPTH

    layer = tile // GROUP
    place = tile % GROUP
    is_hub, is_teller = tile < HUB, layer == HUB // GROUP - 1

    def get(name, start=None, stop=None):
        at, size = PLACES[name]
        if start is None:
            return table_v[at : at + size, :]
        return table_v[at : at + size, start:stop]

    def signal(sem, device):
        pl.semaphore_signal(sem, inc=1, device_id=device, device_id_type=MESH)

    def send(source, target_ref, number, device):
        copy = pltpu.make_async_remote_copy(
            src_ref=source,
            dst_ref=target_ref,
            send_sem=send_sem.at[number],
            recv_sem=recv_sem.at[number],
            device_id=device,
            device_id_type=MESH,
        )
        copy.start()

    def wait(ref, sem):
        pltpu.make_async_copy(ref, ref, sem).wait()

    barrier = pltpu.get_barrier_semaphore()

    @pl.when(has_left)
    def _():
        signal(barrier, {"tile": left})

    @pl.when(has_right)
    def _():
        signal(barrier, {"tile": right})

    repeat(rank + 1, N_SRC, lambda k: signal(barrier, {"src": src_of(k)}))
    local = [
        pltpu.make_async_copy(mask, mask_v, local_sem.at[0]),
        pltpu.make_async_copy(shifts, shifts_v, local_sem.at[1]),
        pltpu.make_async_copy(weights, weights_v, local_sem.at[2]),
    ]
    for k in range(3):
        rows = pl.ds(CUTS[k], CUTS[k + 1] - CUTS[k])
        local.append(pltpu.make_async_copy(table.at[rows], table_v.at[rows], local_sem.at[3 + k]))
    local.append(pltpu.make_async_copy(target, target_v, local_sem.at[6]))
    local[0].start()
    local[3].start()
    repeat(jnp.where(is_hub, tile + 1, n_tile), n_tile, lambda k: signal(barrier, {"tile": k}))

    ends = has_left.astype(jnp.int32) + has_right.astype(jnp.int32)
    pl.semaphore_wait(barrier, rank + ends + jnp.minimum(tile, HUB))

    @pl.when(has_right)
    def _():
        send(mask.at[:, pl.ds(128, 128)], left_v, 0, {"tile": right})

    @pl.when(has_left)
    def _():
        send(mask.at[:, pl.ds(0, 128)], right_v, 1, {"tile": left})

    for k in (1, 2, 4, 5, 6):
        local[k].start()
    repeat(0, rank, lambda k: signal(ready_sem.at[rank], {"src": src_of(k)}))
    term_v[:, POINTS_R // 2 :, :] = jnp.zeros((QUAD, (ROWS_C - POINTS_R) // 2, 128), jnp.float32)

    @pl.when(jnp.logical_not(has_left))
    def _():
        left_v[...] = jnp.zeros_like(left_v)

    @pl.when(jnp.logical_not(has_right))
    def _():
        right_v[...] = jnp.zeros_like(right_v)

    local[1].wait()
    local[2].wait()
    shape = (PER_DEV, PER_DEV)
    own_place = lanes(shape) == lax.broadcasted_iota(jnp.int32, shape, 0)

    def upright(row):
        return jnp.sum(jnp.where(own_place, row, 0.0), axis=1, keepdims=True)

    own_shifts = shifts_v[...].astype(jnp.float32)
    riders = [upright(own_shifts[0:1, :]), upright(own_shifts[1:2, :]), upright(weights_v[...])]
    local[0].wait()
    local[3].wait()
    at = PLACES["enter"][0]
    own = enter(mask_v[...], table_v[at : at + TILE, :])

    @pl.when(has_left)
    def _():
        wait(left_v, recv_sem.at[0])

    @pl.when(has_right)
    def _():
        wait(right_v, recv_sem.at[1])

    margins = jnp.concatenate([left_v[...], right_v[...]], axis=1)
    own = own + enter(margins, table_v[at + TILE : at + 2 * TILE, :])
    own = pack(own[:8], own[8:])
    for lane, rider in zip(RIDERS, riders):
        own = jnp.where(lanes(own.shape) == lane, rider, own)
    spec_v[src] = own

    def send_piece(k):
        send(spec_v.at[src], spec_v.at[src], 2, {"src": src_of(k)})

    def answer_piece(k):
        pl.semaphore_wait(ready_sem.at[k], 1)
        send_piece(k)

    repeat(0, (rank + 1) // 2, lambda k: send_piece(2 * k))
    repeat(0, rank // 2, lambda k: send_piece(2 * k + 1))
    repeat(rank + 1, N_SRC, answer_piece)
    repeat(0, jnp.where(is_hub, tile, 0), lambda k: signal(hub_sem.at[0], {"tile": k}))

    @pl.when(jnp.logical_not(is_hub))
    def _():
        signal(hub_sem.at[1], {"tile": HUB - GROUP + place})

    local[4].wait()
    wait(spec_v.at[pl.ds(0, N_SRC - 1)], recv_sem.at[2])

    gathered = spec_v[...].reshape(128, 128)
    spec = spectrum(gathered, get("spec"), get("lows_a", 0, 128), pltpu.roll)
    bands = split_bands(spec, pltpu.roll)
    at = PLACES["lows_b"][0]
    cols = [(get("cols_" + name), get("cols_low_" + name)) for name in ("even", "odd")]
    rows = [
        (get("rows_even"), table_v[at : at + ROWS_C, 128:256]),
        (get("rows_odd"), table_v[at + ROWS_C : at + 2 * ROWS_C, 128:256]),
    ]

    def add_fields(part, images):
        owner = src
        for k, peer in enumerate(partners):
            owner = jnp.where(part == k + 1, peer, owner)
        rows_by, cols_by, scales = [spec_v[owner, :, lane : lane + 1] for lane in RIDERS]
        for s in range(PER_DEV):
            pupil_v[part, s] = pupil_of(rows_by[s : s + 1], cols_by[s : s + 1])
        for pair in range(PER_DEV // 2):
            first, second = [jnp.broadcast_to(scales[s : s + 1], (8, 128)) for s in (2 * pair, 2 * pair + 1)]
            at = slice(128 * (pair % 2), 128 * (pair % 2) + 128)
            for parity, scale in enumerate(swap(first, second)):
                scale_v[part, pair // 2, parity, :, at] = scale
        fields = coarse_fields(
            bands, [pupil_v[part, s].astype(jnp.bfloat16) for s in range(PER_DEV)], cols, rows
        )
        images = list(images)
        for group in range(2):
            for parity in range(2):
                field_v[part, group, parity] = fields[group][parity]
                power = power_of(fields[group][parity])
                power_v[part, group, parity] = power
                power = power * scale_v[part, group, parity, 0:1, :]
                images[parity] = images[parity] + power[:, :128] + power[:, 128:]
        return tuple(images)

    none = jnp.zeros((ROWS_C // 2, 128), jnp.float32)
    image = lax.fori_loop(0, QUAD, add_fields, (none, none), unroll=True)
    term_v[place_in_quad] = join_image(*image, pltpu.roll)
    image_rows = pl.ds(0, POINTS_R // 2)
    mine = term_v.at[place_in_quad, image_rows]

    def send_image(k):
        send(mine, mine, 3, {"src": member(k)})

    for k in (1, 0, 2, 3):
        pl.when(k != place_in_quad)(functools.partial(send_image, k))
    local[5].wait()
    local[6].wait()
    wait(term_v.at[pl.ds(0, QUAD - 1), image_rows], recv_sem.at[3])

    image = pixels_of(
        term_v[0] + term_v[1] + term_v[2] + term_v[3],
        get("fine_rows"),
        get("fine_cols"),
        get("fine_cols_low"),
    )
    printed = jax.nn.sigmoid(STEEP * (image * (1.0 / SOURCES) - THRESH))
    goal = target_v[...].astype(jnp.float32)
    slope = (LOSS_SCALE * 2.0 * STEEP) * (printed - goal) * printed * (1.0 - printed)
    coarse = coarse_of(slope, get("coarse_rows"), get("coarse_rows_low"), get("coarse_cols"))

    slopes = twice(coarse, pltpu.roll)
    sums = []
    for pair in range(PER_DEV // 2):
        at = slice(128 * (pair % 2), 128 * (pair % 2) + 128)
        terms = [
            jnp.sum(slopes[parity] * power_v[0, pair // 2, parity, :, at], axis=0, keepdims=True) for parity in range(2)
        ]
        sums.extend(swap(*terms))
    sums = jnp.sum(jnp.concatenate(sums, axis=0), axis=1, keepdims=True)
    spot = (PER_DEV, 128)
    sums = jnp.where(lanes(spot) == lax.broadcasted_iota(jnp.int32, spot, 0), sums, 0.0)
    sums_v[tile] = jnp.sum(sums, axis=0, keepdims=True)

    def send_sums(k):
        pltpu.make_async_remote_copy(
            src_ref=sums_v.at[tile],
            dst_ref=sums_v.at[tile],
            send_sem=send_sem.at[5],
            recv_sem=recv_sem.at[5],
            device_id={"tile": k},
            device_id_type=MESH,
        ).start()

    for k in range(HUB):
        first = k + 1 - 2 * (k % 2)
        pl.when(first < tile)(functools.partial(send_sums, first))

    printed_v[...] = printed
    resist[...] = printed_v[pl.ds(pl.multiple_of(src * ROWS, ROWS), ROWS), :]

    wide = [jnp.concatenate([slope, slope], axis=1) * (2.0 / SOURCES) for slope in slopes]
    rows_back = [get("rows_back_even"), get("rows_back_odd")]
    cols_back = [get("cols_back_even"), get("cols_back_odd")]

    def add_part(part, total):
        adjoints = []
        for group in range(2):
            adjoints.append([])
            for parity in range(2):
                scaled = wide[parity] * scale_v[part, group, parity, 0:1, :]
                adjoints[group].append(field_v[part, group, parity] * jnp.concatenate([scaled, scaled], axis=0))
        return band_grad(total, adjoints, [pupil_v[part, s] for s in range(PER_DEV)], rows_back, cols_back)

    grad = lax.fori_loop(0, QUAD, add_part, jnp.zeros((BAND, 128), jnp.float32))
    first = PLACES["leave"][0] + 8 * QUAD * (2 * side + quad)
    low_first = PLACES["lows_b"][0] + 8 * QUAD * (2 * side + quad)

    def halves_of(start, stop, begin):
        begin = pl.multiple_of(begin, 32)
        then = pl.multiple_of(begin + 128, 32)
        return jnp.concatenate(
            [table_v[pl.ds(begin, 8 * QUAD), start:stop], table_v[pl.ds(then, 8 * QUAD), start:stop]], axis=0
        )

    rows = row_grads(grad, halves_of(0, 256, first), halves_of(0, 128, low_first), pltpu.roll)
    grad_v[...] = rows.reshape(QUAD, 8, 128)
    for k in range(1, QUAD):
        other = (place_in_quad + k) % QUAD
        send(grad_v.at[other], part_v.at[k - 1], 4, {"src": member(other)})

    @pl.when(tile < HUB - 1)
    def _():
        pl.semaphore_wait(hub_sem.at[0], HUB - 1 - tile)
        repeat(tile + 1, HUB, send_sums)

    wait(part_v, recv_sem.at[4])
    total = grad_v[place_in_quad] + part_v[0] + part_v[1] + part_v[2]
    mask_grad[...] = last_step(total, get("last"), get("last_low"))

    @pl.when(is_hub)
    def _():
        wait(sums_v.at[pl.ds(0, n_tile - 1)], recv_sem.at[5])
        total_v[...] = jnp.sum(sums_v[...], axis=0) * (1.0 / (SOURCES * n_tile * TILE * TILE))

    def tell(k):
        send(total_v, total_v, 6, {"tile": k * GROUP + place})

    @pl.when(is_teller)
    def _():
        pl.semaphore_wait(hub_sem.at[1], (n_tile - HUB) // GROUP)
        repeat(HUB // GROUP, n_tile // GROUP, tell)

    @pl.when(jnp.logical_not(is_hub))
    def _():
        wait(total_v, recv_sem.at[6])

    source_grad[...] = total_v[...]

    @pl.when(is_teller)
    def _():
        wait(sums_v.at[pl.ds(0, (n_tile - HUB) // GROUP)], send_sem.at[6])

    @pl.when(is_hub)
    def _():
        wait(sums_v.at[pl.ds(0, HUB - 1)], send_sem.at[5])

    @pl.when(jnp.logical_not(is_hub))
    def _():
        wait(sums_v.at[pl.ds(0, HUB)], send_sem.at[5])


    @pl.when(has_right)
    def _():
        wait(left_v, send_sem.at[0])

    @pl.when(has_left)
    def _():
        wait(right_v, send_sem.at[1])

    wait(spec_v.at[pl.ds(0, N_SRC - 1)], send_sem.at[2])
    wait(term_v.at[pl.ds(0, QUAD - 1), image_rows], send_sem.at[3])
    wait(part_v, send_sem.at[4])


def hand_over(resist, mask_grad, source_grad, resist_out, mask_grad_out, source_grad_out, row, sem):
    row[...] = source_grad[0, :PER_DEV]
    copies = [
        pltpu.make_async_copy(resist, resist_out, sem.at[0]),
        pltpu.make_async_copy(mask_grad, mask_grad_out, sem.at[1]),
        pltpu.make_async_copy(row, source_grad_out, sem.at[2]),
    ]
    for copy in copies:
        copy.start()
    for copy in copies:
        copy.wait()


def local(mask, target, shifts, weights):
    f32 = jnp.float32
    anywhere = pl.BlockSpec(memory_space=pl.ANY)
    inside = pl.BlockSpec(memory_space=pltpu.VMEM)
    results = pl.pallas_call(
        everything,
        out_shape=(
            pltpu.VMEM((ROWS, TILE), f32),
            pltpu.VMEM((ROWS, TILE), f32),
            pltpu.VMEM((1, 128), f32),
        ),
        in_specs=[anywhere] * 5,
        out_specs=(inside, inside, inside),
        scratch_shapes=[
            pltpu.VMEM((ROWS, TILE), f32),
            pltpu.VMEM((TILE, TILE), jnp.int32),
            pltpu.VMEM((2, PER_DEV), jnp.int32),
            pltpu.VMEM((1, PER_DEV), f32),
            pltpu.VMEM(TABLE.shape, jnp.bfloat16),
            pltpu.VMEM((ROWS, 128), f32),
            pltpu.VMEM((ROWS, 128), f32),
            pltpu.VMEM((N_SRC, 8, 128), f32),
            pltpu.VMEM((QUAD, PER_DEV, BAND, 128), f32),
            pltpu.VMEM((QUAD, 2, 2, 8, 256), f32),
            pltpu.VMEM((QUAD, ROWS_C // 2, 128), f32),
            pltpu.VMEM((QUAD, 2, 2, ROWS_C, 256), f32),
            pltpu.VMEM((QUAD, 2, 2, ROWS_C // 2, 256), f32),
            pltpu.VMEM((TILE, TILE), f32),
            pltpu.VMEM((QUAD, 8, 128), f32),
            pltpu.VMEM((QUAD - 1, 8, 128), f32),
            pltpu.VMEM((N_TILE, 1, 128), f32),
            pltpu.VMEM((1, 128), f32),
            pltpu.SemaphoreType.DMA((7,)),
            pltpu.SemaphoreType.DMA((7,)),
            pltpu.SemaphoreType.DMA((7,)),
            pltpu.SemaphoreType.REGULAR((N_SRC,)),
            pltpu.SemaphoreType.REGULAR((2,)),
        ],
        compiler_params=pltpu.CompilerParams(
            collective_id=0, has_side_effects=True, vmem_limit_bytes=60 * 1024 * 1024
        ),
    )(mask, target, shifts.T, weights.reshape(1, PER_DEV), jnp.asarray(TABLE))
    return pl.pallas_call(
        hand_over,
        out_shape=(
            jax.ShapeDtypeStruct((ROWS, TILE), f32),
            jax.ShapeDtypeStruct((ROWS, TILE), f32),
            jax.ShapeDtypeStruct((PER_DEV,), f32),
        ),
        in_specs=[inside] * 3,
        out_specs=(anywhere,) * 3,
        scratch_shapes=[pltpu.VMEM((PER_DEV,), f32), pltpu.SemaphoreType.DMA((3,))],
    )(*[pltpu.with_memory_space_constraint(result, pltpu.VMEM) for result in results])


def solution(mesh):
    placed = (P("src", "tile"), P(None, "tile"), P("src", None), P("src"))
    return jax.shard_map(
        local,
        mesh=mesh,
        in_specs=placed,
        out_specs=(P("src", "tile"), P("src", "tile"), P("src")),
        check_vma=False,
    )
```

```python
import functools

import jax
import jax.numpy as jnp
import ml_dtypes
import numpy as np
from jax import lax
from jax.experimental import pallas as pl
from jax.experimental.pallas import tpu as pltpu
from jax.sharding import PartitionSpec as P

TILE = 256
MARGIN = 32
BAND = 64
RAD = 16
EXT = 320
STEEP = 8.0
THRESH = 0.25
LOSS_SCALE = 2.0

N_SRC = 16
N_TILE = 32
PER_DEV = 8
SOURCES = 128
ROWS = 16
HALF = 32
POINTS_R = 66
ROWS_C = 80
COLS_C = 128
QUAD = 4
GROUP = 4
DEPTH = 8
HUB = 3 * GROUP
RIDERS = (31, 63, 95)

MESH = pl.DeviceIdType.MESH
BF16 = ml_dtypes.bfloat16


def halves(table):
    high = table.astype(BF16)
    low = (table - high.astype(np.float64)).astype(BF16)
    return high, low


def column_slots():
    plus = np.arange(HALF)
    return np.concatenate([plus, -plus]), np.concatenate([np.ones(HALF), [0.0], np.ones(HALF - 1)])


def waves(freq, place, period):
    phase = 2.0 * np.pi * ((freq[:, None] * place[None, :]) % period) / period
    return np.cos(phase), np.sin(phase)


def interpolation(points):
    order = np.arange(-2 * RAD, 2 * RAD + 1)
    place = np.arange(TILE) + MARGIN
    offset = place[:, None] / EXT - np.arange(points)[None, :] / points
    return np.cos(2.0 * np.pi * order[None, None, :] * offset[:, :, None]).sum(axis=2) / points


def padded(rows):
    return np.concatenate([rows, np.zeros((ROWS_C // 2 - rows.shape[0], rows.shape[1]))], axis=0)


def build_tables():
    slots, used = column_slots()
    row_freq = np.arange(BAND) - BAND // 2
    pixels = np.arange(TILE) + MARGIN
    parts = {}

    real, imag = waves(np.arange(HALF), np.arange(EXT), EXT)
    fwd = np.concatenate([real, -imag], axis=0).T
    wide = np.zeros((2 * TILE, 2 * HALF))
    wide[:TILE] = fwd[MARGIN : MARGIN + TILE]
    wide[TILE + 96 : TILE + 128] = fwd[:MARGIN]
    wide[TILE + 128 : TILE + 160] = fwd[MARGIN + TILE :]
    high, low = halves(np.concatenate([wide, wide], axis=1))
    parts["enter"] = np.concatenate([high, low], axis=1)

    rows = np.arange(TILE).reshape(N_SRC, 2, 8)
    first, second = rows[:, 0].reshape(-1), rows[:, 1].reshape(-1)
    real, imag = waves(row_freq, pixels, EXT)
    both = np.concatenate([real, -imag], axis=0)
    high, low = halves(np.concatenate([both[:, first], both[:, second]], axis=0))
    parts["spec"] = np.concatenate([high, high], axis=1)
    spec_low = low

    inter_rows, inter_cols = 2.0 * interpolation(POINTS_R), interpolation(COLS_C)
    even, odd = np.arange(0, COLS_C, 2), np.arange(1, COLS_C, 2)
    for name, order in (("even", np.concatenate([even, odd])), ("odd", np.concatenate([odd, even]))):
        real, imag = waves(slots, order, COLS_C)
        real, imag = real * used[:, None], imag * used[:, None]
        cols = np.concatenate(
            [np.concatenate([real, imag], axis=1), np.concatenate([-imag, real], axis=1)], axis=0
        )
        high, low = halves(cols)
        again = high.copy()
        again[[HALF, 3 * HALF]] = high[[0, 2 * HALF]]
        parts["cols_" + name] = np.concatenate([high, again], axis=0)
        parts["cols_low_" + name] = low
        high, low = halves(np.concatenate([cols[:, :COLS_C].T, cols[:, COLS_C:].T], axis=0))
        parts["cols_back_" + name] = np.concatenate([high, low], axis=1)

    lows = []
    for name, start in (("even", 0), ("odd", 1)):
        real, imag = waves(row_freq, np.arange(start, POINTS_R, 2), POINTS_R)
        real, imag = padded(real.T), padded(imag.T)
        high, low = halves(
            np.concatenate(
                [np.concatenate([real, -imag], axis=1), np.concatenate([imag, real], axis=1)], axis=0
            )
        )
        parts["rows_" + name] = np.concatenate([high, high], axis=1)
        lows.append(low)
        pad = np.zeros((2 * BAND, TILE - 3 * ROWS_C), BF16)
        parts["rows_back_" + name] = np.concatenate([high.T, high.T, low.T, pad], axis=1)
    rows_low = np.concatenate(lows, axis=0)

    inter_rows = np.concatenate([padded(inter_rows[:, 0::2].T), padded(inter_rows[:, 1::2].T)], axis=0).T
    inter_cols = inter_cols[:, np.concatenate([even, odd])]
    high, low = halves(inter_rows)
    pad = np.zeros((TILE, TILE - 3 * ROWS_C), BF16)
    parts["fine_rows"] = np.concatenate([high, high, low, pad], axis=1)
    high, low = halves(inter_cols.T)
    parts["fine_cols"] = np.concatenate([high, high], axis=0)
    parts["fine_cols_low"] = low
    parts["coarse_cols"] = np.concatenate([high.T, low.T], axis=1)
    high, low = halves(inter_rows.T)
    parts["coarse_rows"] = high
    parts["coarse_rows_low"] = low

    owners = [
        side * DEPTH + (quad * QUAD + k - 1) % DEPTH for side in range(2) for quad in range(2) for k in range(QUAD)
    ]
    first, second = rows[owners, 0].reshape(-1), rows[owners, 1].reshape(-1)
    high, low = halves(np.concatenate([both[:, first], both[:, second]], axis=1).T)
    parts["leave"] = np.concatenate([high, high], axis=1)
    leave_low = low
    last = fwd[MARGIN : MARGIN + TILE].T
    high, low = halves(np.concatenate([last, last], axis=0))
    parts["last"] = high
    parts["last_low"] = low

    parts["lows_a"] = np.concatenate([spec_low, np.zeros((TILE, 128), BF16)], axis=1)
    rows_low = np.concatenate([rows_low, np.zeros((TILE - 2 * ROWS_C, 128), BF16)], axis=0)
    parts["lows_b"] = np.concatenate([leave_low, rows_low], axis=1)

    order = [
        "enter",
        "spec", "lows_a", "cols_even", "cols_low_even", "cols_odd", "cols_low_odd", "rows_even", "rows_odd", "lows_b",
        "fine_rows", "fine_cols", "fine_cols_low", "coarse_cols", "coarse_rows", "coarse_rows_low",
        "rows_back_even", "rows_back_odd", "cols_back_even", "cols_back_odd", "leave", "last", "last_low",
    ]
    places, start = {}, 0
    for name in order:
        places[name] = (start, parts[name].shape[0])
        start += parts[name].shape[0]
    return np.concatenate([parts[name] for name in order], axis=0), places


TABLE, PLACES = build_tables()
CUTS = (0, PLACES["spec"][0], PLACES["fine_rows"][0], TABLE.shape[0])


def dot(left, right):
    return jnp.dot(left, right, preferred_element_type=jnp.float32)


def cut(value):
    high = value.astype(jnp.bfloat16)
    low = (value - high.astype(jnp.float32)).astype(jnp.bfloat16)
    return high, low


def beside(value):
    high, low = cut(value)
    return jnp.concatenate([high, low, high], axis=1)


def below(value):
    high, low = cut(value)
    return jnp.concatenate([high, low, high], axis=0)


def lanes(shape):
    return lax.broadcasted_iota(jnp.int32, shape, 1)


def enter(value, table):
    rows = value.shape[0]
    both = dot(jnp.concatenate(cut(value), axis=0), table)
    return both[:rows, :128] + both[:rows, 128:] + both[rows:, :128]


def pack(first, second):
    return jnp.where(lanes(first.shape) < 64, first, second)


def spectrum(gathered, table, low_table, roll):
    out = dot(jnp.concatenate([table, low_table], axis=1), below(gathered))
    both = pack(out[:128], out[128:])
    both = both + roll(both, 64, 1)
    turned = roll(both, 32, 1)
    quarter = lanes((BAND, 128)) >> 5
    outer = (quarter == 0) | (quarter == 3)
    even = jnp.where(outer, both[:BAND], turned[:BAND])
    odd = jnp.where(outer, turned[BAND:], both[BAND:])
    return (jnp.where(quarter == 3, -even, even) + jnp.where(quarter == 0, -odd, odd)) * (1.0 / (EXT * EXT))


def pupil_of(row_shift, col_shift):
    row = (lax.broadcasted_iota(jnp.int32, (BAND, 128), 0) - BAND // 2).astype(jnp.float32) + row_shift
    slot = lanes((1, 128)) & 63
    col = jnp.where(slot < HALF, slot, HALF - slot).astype(jnp.float32) + col_shift
    room = RAD * RAD - col * col
    return jnp.where(row * row <= room, 1.0, 0.0)


def swap(first, second):
    return pack(first, second), pack(second, first)


def split_bands(spec, roll):
    spare = (lanes(spec.shape) & 63) == HALF
    high, low = cut(jnp.where(spare, 0.0, spec))
    left = spec - high.astype(jnp.float32) - low.astype(jnp.float32)
    low = jnp.where(spare, roll(left, HALF, 1), low.astype(jnp.float32)).astype(jnp.bfloat16)
    return high, low


def coarse_fields(bands, pupils, cols, rows):
    high, low = bands
    mids = []
    for which in range(2):
        band_high, band_low = [
            jnp.concatenate([part * pupil for pupil in pupils[which::2]], axis=0) for part in (high, low)
        ]
        mids.append(dot(jnp.concatenate([band_high, band_low, band_high], axis=1), cols[which]))
    fields = []
    for group in range(2):
        stacks = ([], [])
        for pair in (2 * group, 2 * group + 1):
            at = slice(BAND * pair, BAND * pair + BAND)
            real = swap(mids[0][at, :128], mids[1][at, :128])
            imag = swap(mids[0][at, 128:], mids[1][at, 128:])
            for parity in range(2):
                stacks[parity].append(jnp.concatenate([real[parity], imag[parity]], axis=0))
        both = []
        for parity in range(2):
            both.append(dot(rows[parity], below(jnp.concatenate(stacks[parity], axis=1))))
        fields.append(both)
    return fields


def power_of(field):
    half = ROWS_C // 2
    return field[:half] * field[:half] + field[half:] * field[half:]


def join_image(even, odd, roll):
    return pack(even + roll(even, 64, 1), odd + roll(odd, 64, 1))


def pixels_of(coarse, fine_rows, fine_cols):
    first = lanes(coarse.shape) < 64
    coarse = jnp.concatenate([jnp.where(first, coarse, 0.0), jnp.where(first, 0.0, coarse)], axis=0)
    return dot(fine_rows, three(dot(beside(coarse), fine_cols)))


def three(value):
    high, low = cut(value)
    pad = jnp.zeros((TILE - 3 * value.shape[0], value.shape[1]), jnp.bfloat16)
    return jnp.concatenate([high, low, high, pad], axis=0)


def coarse_of(slope, coarse_rows, coarse_rows_low, coarse_cols):
    mid = dot(jnp.concatenate([coarse_rows, coarse_rows, coarse_rows_low], axis=1), below(slope))
    high, low = cut(mid)
    both = dot(high, coarse_cols)
    return both[:, :128] + both[:, 128:] + dot(low, coarse_cols[:, :128])


def twice(coarse, roll):
    half = ROWS_C // 2
    even, odd = coarse[:half], coarse[half:]
    return pack(even, roll(even, 64, 1)), pack(roll(odd, 64, 1), odd)


def band_grad(total, adjoints, pupils, rows_back, cols_back):
    sides = ([], [])
    for group in range(2):
        even, odd = [dot(rows_back[parity], three(adjoints[group][parity])) for parity in range(2)]
        for pair in range(2):
            at = slice(128 * pair, 128 * pair + 128)
            real = swap(even[:BAND, at], odd[:BAND, at])
            imag = swap(even[BAND:, at], odd[BAND:, at])
            for which in range(2):
                sides[which].append(jnp.concatenate([real[which], imag[which]], axis=1))
    for which in range(2):
        high, low = cut(jnp.concatenate(sides[which], axis=0))
        both = dot(high, cols_back[which])
        term = both[:, :128] + both[:, 128:] + dot(low, cols_back[which][:, :128])
        for k in range(PER_DEV // 2):
            total = total + term[BAND * k : BAND * k + BAND] * pupils[2 * k + which]
    return total


def fold(grad, roll):
    r32, r64, r96 = roll(grad, 32, 1), roll(grad, 64, 1), roll(grad, 96, 1)
    quarter = lanes(grad.shape) >> 5
    upper = jnp.where(
        quarter == 0, grad + r96, jnp.where(quarter == 1, r96 - r64, jnp.where(quarter == 2, r64 + r32, r32 - grad))
    )
    lower = jnp.where(
        quarter == 0, r64 + r32, jnp.where(quarter == 1, grad - r32, jnp.where(quarter == 2, grad + r96, r64 - r96))
    )
    return jnp.concatenate([upper, lower], axis=0)


def row_grads(grad, leave, leave_low, roll):
    out = dot(jnp.concatenate([leave, leave_low], axis=1), below(fold(grad, roll)))
    half = out.shape[0] // 2
    return pack(out[:half], out[half:])


def last_step(total, last, last_low):
    first = lanes(total.shape) < 64
    value = jnp.concatenate([jnp.where(first, total, 0.0), jnp.where(first, 0.0, total)], axis=0)
    high, low = cut(value)
    return (dot(high, last) + dot(low, last) + dot(high, last_low)) * (1.0 / (EXT * EXT))


def rank_of(side, along):
    step = jnp.where(along == 3, 4, jnp.where(along == 7, 3, 11 - along))
    return 2 * jnp.where(along < 3, along, step) + side


def src_of(rank):
    step, side = rank // 2, rank % 2
    along = jnp.where(step == 3, 7, jnp.where(step == 4, 3, 11 - step))
    return side * DEPTH + jnp.where(step < 3, step, along)


def repeat(first, last, body):
    def step(k, carry):
        body(k)
        return carry

    lax.fori_loop(first, last, step, 0)


def everything(mask, target, shifts, weights, table, resist, mask_grad, source_grad, *scratch):
    (
        mask_v, target_v, shifts_v, weights_v, table_v,
        left_v, right_v, spec_v, pupil_v, scale_v, term_v, field_v, power_v,
        printed_v, grad_v, part_v, sums_v, total_v, local_sem, send_sem, recv_sem, ready_sem, hub_sem,
    ) = scratch
    tile, src = lax.axis_index("tile"), lax.axis_index("src")
    n_tile = lax.axis_size("tile")
    left, right = tile - 1, tile + 1
    has_left, has_right = tile > 0, tile < n_tile - 1
    side, along = src // DEPTH, src % DEPTH
    rank = rank_of(side, along)
    place_in_quad = (along + 1) % QUAD
    quad = (along + 1) % DEPTH // QUAD
    partners = [
        (side + across) % 2 * DEPTH + (along + step) % DEPTH for across, step in ((0, QUAD), (1, 0), (1, QUAD))
    ]

    def member(k):
        return side * DEPTH + (quad * QUAD + k + DEPTH - 1) % DEPTH

    layer = tile // GROUP
    place = tile % GROUP
    is_hub, is_teller = tile < HUB, layer == HUB // GROUP - 1

    def get(name, start=None, stop=None):
        at, size = PLACES[name]
        if start is None:
            return table_v[at : at + size, :]
        return table_v[at : at + size, start:stop]

    def joint(name, last):
        start, (at, size) = PLACES[name][0], PLACES[last]
        return table_v[start : at + size, :]

    def signal(sem, device):
        pl.semaphore_signal(sem, inc=1, device_id=device, device_id_type=MESH)

    def send(source, target_ref, number, device):
        copy = pltpu.make_async_remote_copy(
            src_ref=source,
            dst_ref=target_ref,
            send_sem=send_sem.at[number],
            recv_sem=recv_sem.at[number],
            device_id=device,
            device_id_type=MESH,
        )
        copy.start()

    def wait(ref, sem):
        pltpu.make_async_copy(ref, ref, sem).wait()

    barrier = pltpu.get_barrier_semaphore()

    @pl.when(has_left)
    def _():
        signal(barrier, {"tile": left})

    @pl.when(has_right)
    def _():
        signal(barrier, {"tile": right})

    repeat(rank + 1, N_SRC, lambda k: signal(barrier, {"src": src_of(k)}))
    local = [
        pltpu.make_async_copy(mask, mask_v, local_sem.at[0]),
        pltpu.make_async_copy(shifts, shifts_v, local_sem.at[1]),
        pltpu.make_async_copy(weights, weights_v, local_sem.at[2]),
    ]
    for k in range(3):
        rows = pl.ds(CUTS[k], CUTS[k + 1] - CUTS[k])
        local.append(pltpu.make_async_copy(table.at[rows], table_v.at[rows], local_sem.at[3 + k]))
    local.append(pltpu.make_async_copy(target, target_v, local_sem.at[6]))
    local[0].start()
    local[3].start()
    repeat(jnp.where(is_hub, tile + 1, n_tile), n_tile, lambda k: signal(barrier, {"tile": k}))

    ends = has_left.astype(jnp.int32) + has_right.astype(jnp.int32)
    pl.semaphore_wait(barrier, rank + ends + jnp.minimum(tile, HUB))

    @pl.when(has_right)
    def _():
        send(mask.at[:, pl.ds(128, 128)], left_v, 0, {"tile": right})

    @pl.when(has_left)
    def _():
        send(mask.at[:, pl.ds(0, 128)], right_v, 1, {"tile": left})

    for k in (1, 2, 4, 5, 6):
        local[k].start()
    repeat(0, rank, lambda k: signal(ready_sem.at[rank], {"src": src_of(k)}))
    term_v[:, POINTS_R // 2 :, :] = jnp.zeros((QUAD, (ROWS_C - POINTS_R) // 2, 128), jnp.float32)

    @pl.when(jnp.logical_not(has_left))
    def _():
        left_v[...] = jnp.zeros_like(left_v)

    @pl.when(jnp.logical_not(has_right))
    def _():
        right_v[...] = jnp.zeros_like(right_v)

    local[1].wait()
    local[2].wait()
    shape = (PER_DEV, PER_DEV)
    own_place = lanes(shape) == lax.broadcasted_iota(jnp.int32, shape, 0)

    def upright(row):
        return jnp.sum(jnp.where(own_place, row, 0.0), axis=1, keepdims=True)

    own_shifts = shifts_v[...].astype(jnp.float32)
    riders = [upright(own_shifts[0:1, :]), upright(own_shifts[1:2, :]), upright(weights_v[...])]
    local[0].wait()
    local[3].wait()
    at = PLACES["enter"][0]
    own = enter(mask_v[...], table_v[at : at + TILE, :])

    @pl.when(has_left)
    def _():
        wait(left_v, recv_sem.at[0])

    @pl.when(has_right)
    def _():
        wait(right_v, recv_sem.at[1])

    margins = jnp.concatenate([left_v[...], right_v[...]], axis=1)
    own = own + enter(margins, table_v[at + TILE : at + 2 * TILE, :])
    own = pack(own[:8], own[8:])
    for lane, rider in zip(RIDERS, riders):
        own = jnp.where(lanes(own.shape) == lane, rider, own)
    spec_v[src] = own

    def send_piece(k):
        send(spec_v.at[src], spec_v.at[src], 2, {"src": src_of(k)})

    def answer_piece(k):
        pl.semaphore_wait(ready_sem.at[k], 1)
        send_piece(k)

    repeat(0, (rank + 1) // 2, lambda k: send_piece(2 * k))
    repeat(0, rank // 2, lambda k: send_piece(2 * k + 1))
    repeat(rank + 1, N_SRC, answer_piece)
    repeat(0, jnp.where(is_hub, tile, 0), lambda k: signal(hub_sem.at[0], {"tile": k}))

    @pl.when(jnp.logical_not(is_hub))
    def _():
        signal(hub_sem.at[1], {"tile": HUB - GROUP + place})

    local[4].wait()
    wait(spec_v.at[pl.ds(0, N_SRC - 1)], recv_sem.at[2])

    gathered = spec_v[...].reshape(128, 128)
    spec = spectrum(gathered, get("spec"), get("lows_a", 0, 128), pltpu.roll)
    bands = split_bands(spec, pltpu.roll)
    at = PLACES["lows_b"][0]
    cols = [joint("cols_" + name, "cols_low_" + name) for name in ("even", "odd")]
    rows = [
        jnp.concatenate([get("rows_even"), table_v[at : at + ROWS_C, 128:256]], axis=1),
        jnp.concatenate([get("rows_odd"), table_v[at + ROWS_C : at + 2 * ROWS_C, 128:256]], axis=1),
    ]

    def add_fields(part, images):
        owner = src
        for k, peer in enumerate(partners):
            owner = jnp.where(part == k + 1, peer, owner)
        rows_by, cols_by, scales = [spec_v[owner, :, lane : lane + 1] for lane in RIDERS]
        for s in range(PER_DEV):
            pupil_v[part, s] = pupil_of(rows_by[s : s + 1], cols_by[s : s + 1])
        for pair in range(PER_DEV // 2):
            first, second = [jnp.broadcast_to(scales[s : s + 1], (8, 128)) for s in (2 * pair, 2 * pair + 1)]
            at = slice(128 * (pair % 2), 128 * (pair % 2) + 128)
            for parity, scale in enumerate(swap(first, second)):
                scale_v[part, pair // 2, parity, :, at] = scale
        fields = coarse_fields(
            bands, [pupil_v[part, s].astype(jnp.bfloat16) for s in range(PER_DEV)], cols, rows
        )
        images = list(images)
        for group in range(2):
            for parity in range(2):
                field_v[part, group, parity] = fields[group][parity]
                power = power_of(fields[group][parity])
                power_v[part, group, parity] = power
                power = power * scale_v[part, group, parity, 0:1, :]
                images[parity] = images[parity] + power[:, :128] + power[:, 128:]
        return tuple(images)

    none = jnp.zeros((ROWS_C // 2, 128), jnp.float32)
    image = lax.fori_loop(0, QUAD, add_fields, (none, none), unroll=True)
    term_v[place_in_quad] = join_image(*image, pltpu.roll)
    image_rows = pl.ds(0, POINTS_R // 2)
    mine = term_v.at[place_in_quad, image_rows]

    def send_image(k):
        send(mine, mine, 3, {"src": member(k)})

    for k in (1, 0, 2, 3):
        pl.when(k != place_in_quad)(functools.partial(send_image, k))
    local[5].wait()
    local[6].wait()
    wait(term_v.at[pl.ds(0, QUAD - 1), image_rows], recv_sem.at[3])

    image = pixels_of(
        term_v[0] + term_v[1] + term_v[2] + term_v[3],
        get("fine_rows"),
        joint("fine_cols", "fine_cols_low"),
    )
    printed = jax.nn.sigmoid(STEEP * (image * (1.0 / SOURCES) - THRESH))
    goal = target_v[...].astype(jnp.float32)
    slope = (LOSS_SCALE * 2.0 * STEEP) * (printed - goal) * printed * (1.0 - printed)
    coarse = coarse_of(slope, get("coarse_rows"), get("coarse_rows_low"), get("coarse_cols"))

    slopes = twice(coarse, pltpu.roll)
    sums = []
    for pair in range(PER_DEV // 2):
        at = slice(128 * (pair % 2), 128 * (pair % 2) + 128)
        terms = [
            jnp.sum(slopes[parity] * power_v[0, pair // 2, parity, :, at], axis=0, keepdims=True) for parity in range(2)
        ]
        sums.extend(swap(*terms))
    sums = jnp.sum(jnp.concatenate(sums, axis=0), axis=1, keepdims=True)
    spot = (PER_DEV, 128)
    sums = jnp.where(lanes(spot) == lax.broadcasted_iota(jnp.int32, spot, 0), sums, 0.0)
    sums_v[tile] = jnp.sum(sums, axis=0, keepdims=True)

    def send_sums(k):
        pltpu.make_async_remote_copy(
            src_ref=sums_v.at[tile],
            dst_ref=sums_v.at[tile],
            send_sem=send_sem.at[5],
            recv_sem=recv_sem.at[5],
            device_id={"tile": k},
            device_id_type=MESH,
        ).start()

    for k in range(HUB):
        first = k + 1 - 2 * (k % 2)
        pl.when(first < tile)(functools.partial(send_sums, first))

    printed_v[...] = printed
    resist[...] = printed_v[pl.ds(pl.multiple_of(src * ROWS, ROWS), ROWS), :]

    wide = [jnp.concatenate([slope, slope], axis=1) * (2.0 / SOURCES) for slope in slopes]
    rows_back = [get("rows_back_even"), get("rows_back_odd")]
    cols_back = [get("cols_back_even"), get("cols_back_odd")]

    def add_part(part, total):
        adjoints = []
        for group in range(2):
            adjoints.append([])
            for parity in range(2):
                scaled = wide[parity] * scale_v[part, group, parity, 0:1, :]
                adjoints[group].append(field_v[part, group, parity] * jnp.concatenate([scaled, scaled], axis=0))
        return band_grad(total, adjoints, [pupil_v[part, s] for s in range(PER_DEV)], rows_back, cols_back)

    grad = lax.fori_loop(0, QUAD, add_part, jnp.zeros((BAND, 128), jnp.float32))
    first = PLACES["leave"][0] + 8 * QUAD * (2 * side + quad)
    low_first = PLACES["lows_b"][0] + 8 * QUAD * (2 * side + quad)

    def halves_of(start, stop, begin):
        begin = pl.multiple_of(begin, 32)
        then = pl.multiple_of(begin + 128, 32)
        return jnp.concatenate(
            [table_v[pl.ds(begin, 8 * QUAD), start:stop], table_v[pl.ds(then, 8 * QUAD), start:stop]], axis=0
        )

    rows = row_grads(grad, halves_of(0, 256, first), halves_of(0, 128, low_first), pltpu.roll)
    grad_v[...] = rows.reshape(QUAD, 8, 128)
    for k in range(1, QUAD):
        other = (place_in_quad + k) % QUAD
        send(grad_v.at[other], part_v.at[k - 1], 4, {"src": member(other)})

    @pl.when(tile < HUB - 1)
    def _():
        pl.semaphore_wait(hub_sem.at[0], HUB - 1 - tile)
        repeat(tile + 1, HUB, send_sums)

    wait(part_v, recv_sem.at[4])
    total = grad_v[place_in_quad] + part_v[0] + part_v[1] + part_v[2]
    mask_grad[...] = last_step(total, get("last"), get("last_low"))

    @pl.when(is_hub)
    def _():
        wait(sums_v.at[pl.ds(0, n_tile - 1)], recv_sem.at[5])
        total_v[...] = jnp.sum(sums_v[...], axis=0) * (1.0 / (SOURCES * n_tile * TILE * TILE))

    def tell(k):
        send(total_v, total_v, 6, {"tile": k * GROUP + place})

    @pl.when(is_teller)
    def _():
        pl.semaphore_wait(hub_sem.at[1], (n_tile - HUB) // GROUP)
        repeat(HUB // GROUP, n_tile // GROUP, tell)

    @pl.when(jnp.logical_not(is_hub))
    def _():
        wait(total_v, recv_sem.at[6])

    source_grad[...] = total_v[...]

    @pl.when(is_teller)
    def _():
        wait(sums_v.at[pl.ds(0, (n_tile - HUB) // GROUP)], send_sem.at[6])

    @pl.when(is_hub)
    def _():
        wait(sums_v.at[pl.ds(0, HUB - 1)], send_sem.at[5])

    @pl.when(jnp.logical_not(is_hub))
    def _():
        wait(sums_v.at[pl.ds(0, HUB)], send_sem.at[5])


    @pl.when(has_right)
    def _():
        wait(left_v, send_sem.at[0])

    @pl.when(has_left)
    def _():
        wait(right_v, send_sem.at[1])

    wait(spec_v.at[pl.ds(0, N_SRC - 1)], send_sem.at[2])
    wait(term_v.at[pl.ds(0, QUAD - 1), image_rows], send_sem.at[3])
    wait(part_v, send_sem.at[4])


def hand_over(resist, mask_grad, source_grad, resist_out, mask_grad_out, source_grad_out, row, sem):
    row[...] = source_grad[0, :PER_DEV]
    copies = [
        pltpu.make_async_copy(resist, resist_out, sem.at[0]),
        pltpu.make_async_copy(mask_grad, mask_grad_out, sem.at[1]),
        pltpu.make_async_copy(row, source_grad_out, sem.at[2]),
    ]
    for copy in copies:
        copy.start()
    for copy in copies:
        copy.wait()


def local(mask, target, shifts, weights):
    f32 = jnp.float32
    anywhere = pl.BlockSpec(memory_space=pl.ANY)
    inside = pl.BlockSpec(memory_space=pltpu.VMEM)
    results = pl.pallas_call(
        everything,
        out_shape=(
            pltpu.VMEM((ROWS, TILE), f32),
            pltpu.VMEM((ROWS, TILE), f32),
            pltpu.VMEM((1, 128), f32),
        ),
        in_specs=[anywhere] * 5,
        out_specs=(inside, inside, inside),
        scratch_shapes=[
            pltpu.VMEM((ROWS, TILE), f32),
            pltpu.VMEM((TILE, TILE), jnp.int32),
            pltpu.VMEM((2, PER_DEV), jnp.int32),
            pltpu.VMEM((1, PER_DEV), f32),
            pltpu.VMEM(TABLE.shape, jnp.bfloat16),
            pltpu.VMEM((ROWS, 128), f32),
            pltpu.VMEM((ROWS, 128), f32),
            pltpu.VMEM((N_SRC, 8, 128), f32),
            pltpu.VMEM((QUAD, PER_DEV, BAND, 128), f32),
            pltpu.VMEM((QUAD, 2, 2, 8, 256), f32),
            pltpu.VMEM((QUAD, ROWS_C // 2, 128), f32),
            pltpu.VMEM((QUAD, 2, 2, ROWS_C, 256), f32),
            pltpu.VMEM((QUAD, 2, 2, ROWS_C // 2, 256), f32),
            pltpu.VMEM((TILE, TILE), f32),
            pltpu.VMEM((QUAD, 8, 128), f32),
            pltpu.VMEM((QUAD - 1, 8, 128), f32),
            pltpu.VMEM((N_TILE, 1, 128), f32),
            pltpu.VMEM((1, 128), f32),
            pltpu.SemaphoreType.DMA((7,)),
            pltpu.SemaphoreType.DMA((7,)),
            pltpu.SemaphoreType.DMA((7,)),
            pltpu.SemaphoreType.REGULAR((N_SRC,)),
            pltpu.SemaphoreType.REGULAR((2,)),
        ],
        compiler_params=pltpu.CompilerParams(
            collective_id=0, has_side_effects=True, vmem_limit_bytes=60 * 1024 * 1024
        ),
    )(mask, target, shifts.T, weights.reshape(1, PER_DEV), jnp.asarray(TABLE))
    return pl.pallas_call(
        hand_over,
        out_shape=(
            jax.ShapeDtypeStruct((ROWS, TILE), f32),
            jax.ShapeDtypeStruct((ROWS, TILE), f32),
            jax.ShapeDtypeStruct((PER_DEV,), f32),
        ),
        in_specs=[inside] * 3,
        out_specs=(anywhere,) * 3,
        scratch_shapes=[pltpu.VMEM((PER_DEV,), f32), pltpu.SemaphoreType.DMA((3,))],
    )(*[pltpu.with_memory_space_constraint(result, pltpu.VMEM) for result in results])


def solution(mesh):
    placed = (P("src", "tile"), P(None, "tile"), P("src", None), P("src"))
    return jax.shard_map(
        local,
        mesh=mesh,
        in_specs=placed,
        out_specs=(P("src", "tile"), P("src", "tile"), P("src")),
        check_vma=False,
    )
```

```python
import functools

import jax
import jax.numpy as jnp
import ml_dtypes
import numpy as np
from jax import lax
from jax.experimental import pallas as pl
from jax.experimental.pallas import tpu as pltpu
from jax.sharding import PartitionSpec as P

TILE = 256
MARGIN = 32
BAND = 64
RAD = 16
EXT = 320
STEEP = 8.0
THRESH = 0.25
LOSS_SCALE = 2.0

N_SRC = 16
N_TILE = 32
PER_DEV = 8
SOURCES = 128
ROWS = 16
HALF = 32
POINTS_R = 66
ROWS_C = 80
COLS_C = 128
QUAD = 4
GROUP = 4
DEPTH = 8
HUB = 3 * GROUP
RIDERS = (31, 63, 95)
RELAYS = (0, 8, 6, 14)

MESH = pl.DeviceIdType.MESH
BF16 = ml_dtypes.bfloat16


def halves(table):
    high = table.astype(BF16)
    low = (table - high.astype(np.float64)).astype(BF16)
    return high, low


def column_slots():
    plus = np.arange(HALF)
    return np.concatenate([plus, -plus]), np.concatenate([np.ones(HALF), [0.0], np.ones(HALF - 1)])


def waves(freq, place, period):
    phase = 2.0 * np.pi * ((freq[:, None] * place[None, :]) % period) / period
    return np.cos(phase), np.sin(phase)


def interpolation(points):
    order = np.arange(-2 * RAD, 2 * RAD + 1)
    place = np.arange(TILE) + MARGIN
    offset = place[:, None] / EXT - np.arange(points)[None, :] / points
    return np.cos(2.0 * np.pi * order[None, None, :] * offset[:, :, None]).sum(axis=2) / points


def padded(rows):
    return np.concatenate([rows, np.zeros((ROWS_C // 2 - rows.shape[0], rows.shape[1]))], axis=0)


def build_tables():
    slots, used = column_slots()
    row_freq = np.arange(BAND) - BAND // 2
    pixels = np.arange(TILE) + MARGIN
    parts = {}

    real, imag = waves(np.arange(HALF), np.arange(EXT), EXT)
    fwd = np.concatenate([real, -imag], axis=0).T
    wide = np.zeros((2 * TILE, 2 * HALF))
    wide[:TILE] = fwd[MARGIN : MARGIN + TILE]
    wide[TILE + 96 : TILE + 128] = fwd[:MARGIN]
    wide[TILE + 128 : TILE + 160] = fwd[MARGIN + TILE :]
    high, low = halves(np.concatenate([wide, wide], axis=1))
    parts["enter"] = np.concatenate([high, low], axis=1)

    rows = np.arange(TILE).reshape(N_SRC, 2, 8)
    first, second = rows[:, 0].reshape(-1), rows[:, 1].reshape(-1)
    real, imag = waves(row_freq, pixels, EXT)
    both = np.concatenate([real, -imag], axis=0)
    high, low = halves(np.concatenate([both[:, first], both[:, second]], axis=0))
    parts["spec"] = np.concatenate([high, high], axis=1)
    spec_low = low

    inter_rows, inter_cols = 2.0 * interpolation(POINTS_R), interpolation(COLS_C)
    even, odd = np.arange(0, COLS_C, 2), np.arange(1, COLS_C, 2)
    for name, order in (("even", np.concatenate([even, odd])), ("odd", np.concatenate([odd, even]))):
        real, imag = waves(slots, order, COLS_C)
        real, imag = real * used[:, None], imag * used[:, None]
        cols = np.concatenate(
            [np.concatenate([real, imag], axis=1), np.concatenate([-imag, real], axis=1)], axis=0
        )
        high, low = halves(cols)
        again = high.copy()
        again[[HALF, 3 * HALF]] = high[[0, 2 * HALF]]
        parts["cols_" + name] = np.concatenate([high, again], axis=0)
        parts["cols_low_" + name] = low
        high, low = halves(np.concatenate([cols[:, :COLS_C].T, cols[:, COLS_C:].T], axis=0))
        parts["cols_back_" + name] = np.concatenate([high, low], axis=1)

    lows = []
    for name, start in (("even", 0), ("odd", 1)):
        real, imag = waves(row_freq, np.arange(start, POINTS_R, 2), POINTS_R)
        real, imag = padded(real.T), padded(imag.T)
        high, low = halves(
            np.concatenate(
                [np.concatenate([real, -imag], axis=1), np.concatenate([imag, real], axis=1)], axis=0
            )
        )
        parts["rows_" + name] = np.concatenate([high, high], axis=1)
        lows.append(low)
        pad = np.zeros((2 * BAND, TILE - 3 * ROWS_C), BF16)
        parts["rows_back_" + name] = np.concatenate([high.T, high.T, low.T, pad], axis=1)
    rows_low = np.concatenate(lows, axis=0)

    inter_rows = np.concatenate([padded(inter_rows[:, 0::2].T), padded(inter_rows[:, 1::2].T)], axis=0).T
    inter_cols = inter_cols[:, np.concatenate([even, odd])]
    high, low = halves(inter_rows)
    pad = np.zeros((TILE, TILE - 3 * ROWS_C), BF16)
    parts["fine_rows"] = np.concatenate([high, high, low, pad], axis=1)
    high, low = halves(inter_cols.T)
    parts["fine_cols"] = np.concatenate([high, high], axis=0)
    parts["fine_cols_low"] = low
    parts["coarse_cols"] = np.concatenate([high.T, low.T], axis=1)
    high, low = halves(inter_rows.T)
    parts["coarse_rows"] = high
    parts["coarse_rows_low"] = low

    owners = [
        side * DEPTH + (quad * QUAD + k - 1) % DEPTH for side in range(2) for quad in range(2) for k in range(QUAD)
    ]
    first, second = rows[owners, 0].reshape(-1), rows[owners, 1].reshape(-1)
    high, low = halves(np.concatenate([both[:, first], both[:, second]], axis=1).T)
    parts["leave"] = np.concatenate([high, high], axis=1)
    leave_low = low
    last = fwd[MARGIN : MARGIN + TILE].T
    high, low = halves(np.concatenate([last, last], axis=0))
    parts["last"] = high
    parts["last_low"] = low

    parts["lows_a"] = np.concatenate([spec_low, np.zeros((TILE, 128), BF16)], axis=1)
    rows_low = np.concatenate([rows_low, np.zeros((TILE - 2 * ROWS_C, 128), BF16)], axis=0)
    parts["lows_b"] = np.concatenate([leave_low, rows_low], axis=1)

    order = [
        "enter",
        "spec", "lows_a", "cols_even", "cols_low_even", "cols_odd", "cols_low_odd", "rows_even", "rows_odd", "lows_b",
        "fine_rows", "fine_cols", "fine_cols_low", "coarse_cols", "coarse_rows", "coarse_rows_low",
        "rows_back_even", "rows_back_odd", "cols_back_even", "cols_back_odd", "leave", "last", "last_low",
    ]
    places, start = {}, 0
    for name in order:
        places[name] = (start, parts[name].shape[0])
        start += parts[name].shape[0]
    return np.concatenate([parts[name] for name in order], axis=0), places


TABLE, PLACES = build_tables()
CUTS = (0, PLACES["spec"][0], PLACES["fine_rows"][0], TABLE.shape[0])


def dot(left, right):
    return jnp.dot(left, right, preferred_element_type=jnp.float32)


def cut(value):
    high = value.astype(jnp.bfloat16)
    low = (value - high.astype(jnp.float32)).astype(jnp.bfloat16)
    return high, low


def lanes(shape):
    return lax.broadcasted_iota(jnp.int32, shape, 1)


def enter(value, table):
    rows = value.shape[0]
    both = dot(jnp.concatenate(cut(value), axis=0), table)
    return both[:rows, :128] + both[:rows, 128:] + both[rows:, :128]


def pack(first, second):
    return jnp.where(lanes(first.shape) < 64, first, second)


def spectrum(gathered, table, low_table, roll):
    high, low = cut(gathered)
    out = dot(table, jnp.concatenate([high, low], axis=0)) + dot(low_table, high)
    both = pack(out[:128], out[128:])
    both = both + roll(both, 64, 1)
    turned = roll(both, 32, 1)
    quarter = lanes((BAND, 128)) >> 5
    outer = (quarter == 0) | (quarter == 3)
    even = jnp.where(outer, both[:BAND], turned[:BAND])
    odd = jnp.where(outer, turned[BAND:], both[BAND:])
    return (jnp.where(quarter == 3, -even, even) + jnp.where(quarter == 0, -odd, odd)) * (1.0 / (EXT * EXT))


def pupil_of(row_shift, col_shift):
    row = (lax.broadcasted_iota(jnp.int32, (BAND, 128), 0) - BAND // 2).astype(jnp.float32) + row_shift
    slot = lanes((1, 128)) & 63
    col = jnp.where(slot < HALF, slot, HALF - slot).astype(jnp.float32) + col_shift
    room = RAD * RAD - col * col
    return jnp.where(row * row <= room, 1.0, 0.0)


def swap(first, second):
    return pack(first, second), pack(second, first)


def split_bands(spec, roll):
    spare = (lanes(spec.shape) & 63) == HALF
    high, low = cut(jnp.where(spare, 0.0, spec))
    left = spec - high.astype(jnp.float32) - low.astype(jnp.float32)
    low = jnp.where(spare, roll(left, HALF, 1), low.astype(jnp.float32)).astype(jnp.bfloat16)
    return high, low


def coarse_fields(bands, pupils, cols, rows):
    high, low = bands
    mids = []
    for which in range(2):
        band_high, band_low = [
            jnp.concatenate([part * pupil for pupil in pupils[which::2]], axis=0) for part in (high, low)
        ]
        table, low_table = cols[which]
        mids.append(
            dot(jnp.concatenate([band_high, band_low], axis=1), table) + dot(band_high, low_table)
        )
    fields = []
    for group in range(2):
        stacks = ([], [])
        for pair in (2 * group, 2 * group + 1):
            at = slice(BAND * pair, BAND * pair + BAND)
            real = swap(mids[0][at, :128], mids[1][at, :128])
            imag = swap(mids[0][at, 128:], mids[1][at, 128:])
            for parity in range(2):
                stacks[parity].append(jnp.concatenate([real[parity], imag[parity]], axis=0))
        both = []
        for parity in range(2):
            upper, lower = cut(jnp.concatenate(stacks[parity], axis=1))
            table, low_table = rows[parity]
            both.append(dot(table, jnp.concatenate([upper, lower], axis=0)) + dot(low_table, upper))
        fields.append(both)
    return fields


def power_of(field):
    half = ROWS_C // 2
    return field[:half] * field[:half] + field[half:] * field[half:]


def join_image(even, odd, roll):
    return pack(even + roll(even, 64, 1), odd + roll(odd, 64, 1))


def pixels_of(coarse, fine_rows, fine_cols, fine_cols_low):
    first = lanes(coarse.shape) < 64
    coarse = jnp.concatenate([jnp.where(first, coarse, 0.0), jnp.where(first, 0.0, coarse)], axis=0)
    high, low = cut(coarse)
    mid = dot(jnp.concatenate([high, low], axis=1), fine_cols) + dot(high, fine_cols_low)
    return dot(fine_rows, three(mid))


def three(value):
    high, low = cut(value)
    pad = jnp.zeros((TILE - 3 * value.shape[0], value.shape[1]), jnp.bfloat16)
    return jnp.concatenate([high, low, high, pad], axis=0)


def coarse_of(slope, coarse_rows, coarse_rows_low, coarse_cols):
    high, low = cut(slope)
    mid = dot(coarse_rows, high) + dot(coarse_rows, low) + dot(coarse_rows_low, high)
    high, low = cut(mid)
    both = dot(high, coarse_cols)
    return both[:, :128] + both[:, 128:] + dot(low, coarse_cols[:, :128])


def twice(coarse, roll):
    half = ROWS_C // 2
    even, odd = coarse[:half], coarse[half:]
    return pack(even, roll(even, 64, 1)), pack(roll(odd, 64, 1), odd)


def band_grad(total, adjoints, pupils, rows_back, cols_back):
    sides = ([], [])
    for group in range(2):
        even, odd = [dot(rows_back[parity], three(adjoints[group][parity])) for parity in range(2)]
        for pair in range(2):
            at = slice(128 * pair, 128 * pair + 128)
            real = swap(even[:BAND, at], odd[:BAND, at])
            imag = swap(even[BAND:, at], odd[BAND:, at])
            for which in range(2):
                sides[which].append(jnp.concatenate([real[which], imag[which]], axis=1))
    for which in range(2):
        high, low = cut(jnp.concatenate(sides[which], axis=0))
        both = dot(high, cols_back[which])
        term = both[:, :128] + both[:, 128:] + dot(low, cols_back[which][:, :128])
        for k in range(PER_DEV // 2):
            total = total + term[BAND * k : BAND * k + BAND] * pupils[2 * k + which]
    return total


def fold(grad, roll):
    r32, r64, r96 = roll(grad, 32, 1), roll(grad, 64, 1), roll(grad, 96, 1)
    quarter = lanes(grad.shape) >> 5
    upper = jnp.where(
        quarter == 0, grad + r96, jnp.where(quarter == 1, r96 - r64, jnp.where(quarter == 2, r64 + r32, r32 - grad))
    )
    lower = jnp.where(
        quarter == 0, r64 + r32, jnp.where(quarter == 1, grad - r32, jnp.where(quarter == 2, grad + r96, r64 - r96))
    )
    return jnp.concatenate([upper, lower], axis=0)


def row_grads(grad, leave, leave_low, roll):
    high, low = cut(fold(grad, roll))
    out = dot(leave, jnp.concatenate([high, low], axis=0)) + dot(leave_low, high)
    half = out.shape[0] // 2
    return pack(out[:half], out[half:])


def last_step(total, last, last_low):
    first = lanes(total.shape) < 64
    value = jnp.concatenate([jnp.where(first, total, 0.0), jnp.where(first, 0.0, total)], axis=0)
    high, low = cut(value)
    return (dot(high, last) + dot(low, last) + dot(high, last_low)) * (1.0 / (EXT * EXT))


def rank_of(side, along):
    step = jnp.where(along == 3, 4, jnp.where(along == 7, 3, 11 - along))
    return 2 * jnp.where(along < 3, along, step) + side


def src_of(rank):
    step, side = rank // 2, rank % 2
    along = jnp.where(step == 3, 7, jnp.where(step == 4, 3, 11 - step))
    return side * DEPTH + jnp.where(step < 3, step, along)


def repeat(first, last, body):
    def step(k, carry):
        body(k)
        return carry

    lax.fori_loop(first, last, step, 0)


def everything(mask, target, shifts, weights, table, resist, mask_grad, source_grad, *scratch):
    (
        mask_v, target_v, shifts_v, weights_v, table_v,
        edge_v, margin_v, spec_v, pupil_v, scale_v, term_v, field_v, power_v,
        printed_v, grad_v, part_v, sums_v, total_v, local_sem, send_sem, recv_sem, ready_sem, hub_sem,
    ) = scratch
    tile, src = lax.axis_index("tile"), lax.axis_index("src")
    n_tile = lax.axis_size("tile")
    left, right = tile - 1, tile + 1
    has_left, has_right = tile > 0, tile < n_tile - 1
    side, along = src // DEPTH, src % DEPTH
    rank = rank_of(side, along)
    place_in_quad = (along + 1) % QUAD
    quad = (along + 1) % DEPTH // QUAD
    partners = [
        (side + across) % 2 * DEPTH + (along + step) % DEPTH for across, step in ((0, QUAD), (1, 0), (1, QUAD))
    ]

    def member(k):
        return side * DEPTH + (quad * QUAD + k + DEPTH - 1) % DEPTH

    layer = tile // GROUP
    place = tile % GROUP
    is_relay = functools.reduce(jnp.logical_or, [src == relay for relay in RELAYS])
    is_hub, is_teller = tile < HUB, layer == HUB // GROUP - 1

    def get(name, start=None, stop=None):
        at, size = PLACES[name]
        if start is None:
            return table_v[at : at + size, :]
        return table_v[at : at + size, start:stop]

    def signal(sem, device):
        pl.semaphore_signal(sem, inc=1, device_id=device, device_id_type=MESH)

    def send(source, target_ref, number, device):
        copy = pltpu.make_async_remote_copy(
            src_ref=source,
            dst_ref=target_ref,
            send_sem=send_sem.at[number],
            recv_sem=recv_sem.at[number],
            device_id=device,
            device_id_type=MESH,
        )
        copy.start()

    def wait(ref, sem):
        pltpu.make_async_copy(ref, ref, sem).wait()

    barrier = pltpu.get_barrier_semaphore()
    repeat(rank + 1, N_SRC, lambda k: signal(barrier, {"src": src_of(k)}))
    local = [
        pltpu.make_async_copy(mask, mask_v, local_sem.at[0]),
        pltpu.make_async_copy(shifts, shifts_v, local_sem.at[1]),
        pltpu.make_async_copy(weights, weights_v, local_sem.at[2]),
    ]
    for k in range(3):
        rows = pl.ds(CUTS[k], CUTS[k + 1] - CUTS[k])
        local.append(pltpu.make_async_copy(table.at[rows], table_v.at[rows], local_sem.at[3 + k]))
    local.append(pltpu.make_async_copy(target, target_v, local_sem.at[6]))
    local[0].start()
    local[3].start()
    repeat(jnp.where(is_hub, tile + 1, n_tile), n_tile, lambda k: signal(barrier, {"tile": k}))


    @pl.when(is_relay)
    def _():
        pl.when(has_left)(lambda: repeat(0, N_SRC, lambda k: signal(barrier, {"tile": left, "src": k})))
        pl.when(has_right)(lambda: repeat(0, N_SRC, lambda k: signal(barrier, {"tile": right, "src": k})))

    ends = has_left.astype(jnp.int32) + has_right.astype(jnp.int32)
    pl.semaphore_wait(barrier, rank + len(RELAYS) * ends + jnp.minimum(tile, HUB))

    def send_edge(number, relay):
        here = mask.at[:, pl.ds(128 - 128 * number, 128)]
        send(here, edge_v.at[number, src], number, {"tile": (right, left)[number], "src": relay})

    for relay in RELAYS:
        pl.when(has_right)(functools.partial(send_edge, 0, relay))
        pl.when(has_left)(functools.partial(send_edge, 1, relay))
    for k in (1, 2, 4, 5, 6):
        local[k].start()
    repeat(0, rank, lambda k: signal(ready_sem.at[rank], {"src": src_of(k)}))
    term_v[:, POINTS_R // 2 :, :] = jnp.zeros((QUAD, (ROWS_C - POINTS_R) // 2, 128), jnp.float32)

    local[1].wait()
    local[2].wait()
    shape = (PER_DEV, PER_DEV)
    own_place = lanes(shape) == lax.broadcasted_iota(jnp.int32, shape, 0)

    def upright(row):
        return jnp.sum(jnp.where(own_place, row, 0.0), axis=1, keepdims=True)

    own_shifts = shifts_v[...].astype(jnp.float32)
    riders = [upright(own_shifts[0:1, :]), upright(own_shifts[1:2, :]), upright(weights_v[...])]
    local[0].wait()
    local[3].wait()
    at = PLACES["enter"][0]
    own = enter(mask_v[...], table_v[at : at + TILE, :])
    own = pack(own[:8], own[8:])
    for lane, rider in zip(RIDERS, riders):
        own = jnp.where(lanes(own.shape) == lane, rider, own)
    spec_v[src] = own

    def send_piece(k):
        send(spec_v.at[src], spec_v.at[src], 2, {"src": src_of(k)})

    def answer_piece(k):
        pl.semaphore_wait(ready_sem.at[k], 1)
        send_piece(k)

    repeat(0, (rank + 1) // 2, lambda k: send_piece(2 * k))
    repeat(0, rank // 2, lambda k: send_piece(2 * k + 1))
    repeat(rank + 1, N_SRC, answer_piece)
    repeat(0, jnp.where(is_hub, tile, 0), lambda k: signal(hub_sem.at[0], {"tile": k}))

    @pl.when(jnp.logical_not(is_hub))
    def _():
        signal(hub_sem.at[1], {"tile": HUB - GROUP + place})

    local[4].wait()
    spec_tables = (get("spec"), get("lows_a", 0, 128))

    @pl.when(is_relay)
    def _():
        for number, there in enumerate((has_left, has_right)):
            pl.when(there)(functools.partial(wait, edge_v.at[number], recv_sem.at[number]))

            @pl.when(jnp.logical_not(there))
            def _():
                edge_v[number] = jnp.zeros((N_SRC, ROWS, 128), jnp.float32)

        sides = jnp.concatenate([edge_v[number].reshape(TILE, 128) for number in range(2)], axis=1)
        margins = enter(sides, table_v[at + TILE : at + 2 * TILE, :]).reshape(N_SRC, 2, 8, 128)
        margins = pack(margins[:, 0].reshape(128, 128), margins[:, 1].reshape(128, 128))
        margin_v[...] = spectrum(margins, *spec_tables, pltpu.roll)
        for k in range(QUAD):

            @pl.when(k != place_in_quad)
            def _():
                send(margin_v, margin_v, 7, {"src": member(k)})

    wait(spec_v.at[pl.ds(0, N_SRC - 1)], recv_sem.at[2])

    gathered = spec_v[...].reshape(128, 128)
    spec = spectrum(gathered, *spec_tables, pltpu.roll)

    @pl.when(jnp.logical_not(is_relay))
    def _():
        wait(margin_v, recv_sem.at[7])

    bands = split_bands(spec + margin_v[...], pltpu.roll)
    at = PLACES["lows_b"][0]
    cols = [(get("cols_" + name), get("cols_low_" + name)) for name in ("even", "odd")]
    rows = [
        (get("rows_even"), table_v[at : at + ROWS_C, 128:256]),
        (get("rows_odd"), table_v[at + ROWS_C : at + 2 * ROWS_C, 128:256]),
    ]

    def add_fields(part, images):
        owner = src
        for k, peer in enumerate(partners):
            owner = jnp.where(part == k + 1, peer, owner)
        rows_by, cols_by, scales = [spec_v[owner, :, lane : lane + 1] for lane in RIDERS]
        for s in range(PER_DEV):
            pupil_v[part, s] = pupil_of(rows_by[s : s + 1], cols_by[s : s + 1])
        for pair in range(PER_DEV // 2):
            first, second = [jnp.broadcast_to(scales[s : s + 1], (8, 128)) for s in (2 * pair, 2 * pair + 1)]
            at = slice(128 * (pair % 2), 128 * (pair % 2) + 128)
            for parity, scale in enumerate(swap(first, second)):
                scale_v[part, pair // 2, parity, :, at] = scale
        fields = coarse_fields(
            bands, [pupil_v[part, s].astype(jnp.bfloat16) for s in range(PER_DEV)], cols, rows
        )
        images = list(images)
        for group in range(2):
            for parity in range(2):
                field_v[part, group, parity] = fields[group][parity]
                power = power_of(fields[group][parity])
                power_v[part, group, parity] = power
                power = power * scale_v[part, group, parity, 0:1, :]
                images[parity] = images[parity] + power[:, :128] + power[:, 128:]
        return tuple(images)

    none = jnp.zeros((ROWS_C // 2, 128), jnp.float32)
    image = lax.fori_loop(0, QUAD, add_fields, (none, none), unroll=True)
    term_v[place_in_quad] = join_image(*image, pltpu.roll)
    image_rows = pl.ds(0, POINTS_R // 2)
    mine = term_v.at[place_in_quad, image_rows]

    def send_image(k):
        send(mine, mine, 3, {"src": member(k)})

    for k in (1, 0, 2, 3):
        pl.when(k != place_in_quad)(functools.partial(send_image, k))
    local[5].wait()
    local[6].wait()
    wait(term_v.at[pl.ds(0, QUAD - 1), image_rows], recv_sem.at[3])

    image = pixels_of(
        term_v[0] + term_v[1] + term_v[2] + term_v[3],
        get("fine_rows"),
        get("fine_cols"),
        get("fine_cols_low"),
    )
    printed = jax.nn.sigmoid(STEEP * (image * (1.0 / SOURCES) - THRESH))
    goal = target_v[...].astype(jnp.float32)
    slope = (LOSS_SCALE * 2.0 * STEEP) * (printed - goal) * printed * (1.0 - printed)
    coarse = coarse_of(slope, get("coarse_rows"), get("coarse_rows_low"), get("coarse_cols"))

    slopes = twice(coarse, pltpu.roll)
    sums = []
    for pair in range(PER_DEV // 2):
        at = slice(128 * (pair % 2), 128 * (pair % 2) + 128)
        terms = [
            jnp.sum(slopes[parity] * power_v[0, pair // 2, parity, :, at], axis=0, keepdims=True) for parity in range(2)
        ]
        sums.extend(swap(*terms))
    sums = jnp.sum(jnp.concatenate(sums, axis=0), axis=1, keepdims=True)
    spot = (PER_DEV, 128)
    sums = jnp.where(lanes(spot) == lax.broadcasted_iota(jnp.int32, spot, 0), sums, 0.0)
    sums_v[tile] = jnp.sum(sums, axis=0, keepdims=True)

    def send_sums(k):
        pltpu.make_async_remote_copy(
            src_ref=sums_v.at[tile],
            dst_ref=sums_v.at[tile],
            send_sem=send_sem.at[5],
            recv_sem=recv_sem.at[5],
            device_id={"tile": k},
            device_id_type=MESH,
        ).start()

    for k in range(HUB):
        first = k + 1 - 2 * (k % 2)
        pl.when(first < tile)(functools.partial(send_sums, first))

    printed_v[...] = printed
    resist[...] = printed_v[pl.ds(pl.multiple_of(src * ROWS, ROWS), ROWS), :]

    wide = [jnp.concatenate([slope, slope], axis=1) * (2.0 / SOURCES) for slope in slopes]
    rows_back = [get("rows_back_even"), get("rows_back_odd")]
    cols_back = [get("cols_back_even"), get("cols_back_odd")]

    def add_part(part, total):
        adjoints = []
        for group in range(2):
            adjoints.append([])
            for parity in range(2):
                scaled = wide[parity] * scale_v[part, group, parity, 0:1, :]
                adjoints[group].append(field_v[part, group, parity] * jnp.concatenate([scaled, scaled], axis=0))
        return band_grad(total, adjoints, [pupil_v[part, s] for s in range(PER_DEV)], rows_back, cols_back)

    grad = lax.fori_loop(0, QUAD, add_part, jnp.zeros((BAND, 128), jnp.float32))
    first = PLACES["leave"][0] + 8 * QUAD * (2 * side + quad)
    low_first = PLACES["lows_b"][0] + 8 * QUAD * (2 * side + quad)

    def halves_of(start, stop, begin):
        begin = pl.multiple_of(begin, 32)
        then = pl.multiple_of(begin + 128, 32)
        return jnp.concatenate(
            [table_v[pl.ds(begin, 8 * QUAD), start:stop], table_v[pl.ds(then, 8 * QUAD), start:stop]], axis=0
        )

    rows = row_grads(grad, halves_of(0, 256, first), halves_of(0, 128, low_first), pltpu.roll)
    grad_v[...] = rows.reshape(QUAD, 8, 128)
    for k in range(1, QUAD):
        other = (place_in_quad + k) % QUAD
        send(grad_v.at[other], part_v.at[k - 1], 4, {"src": member(other)})

    @pl.when(tile < HUB - 1)
    def _():
        pl.semaphore_wait(hub_sem.at[0], HUB - 1 - tile)
        repeat(tile + 1, HUB, send_sums)

    wait(part_v, recv_sem.at[4])
    total = grad_v[place_in_quad] + part_v[0] + part_v[1] + part_v[2]
    mask_grad[...] = last_step(total, get("last"), get("last_low"))

    @pl.when(is_hub)
    def _():
        wait(sums_v.at[pl.ds(0, n_tile - 1)], recv_sem.at[5])
        total_v[...] = jnp.sum(sums_v[...], axis=0) * (1.0 / (SOURCES * n_tile * TILE * TILE))

    def tell(k):
        send(total_v, total_v, 6, {"tile": k * GROUP + place})

    @pl.when(is_teller)
    def _():
        pl.semaphore_wait(hub_sem.at[1], (n_tile - HUB) // GROUP)
        repeat(HUB // GROUP, n_tile // GROUP, tell)

    @pl.when(jnp.logical_not(is_hub))
    def _():
        wait(total_v, recv_sem.at[6])

    source_grad[...] = total_v[...]

    @pl.when(is_teller)
    def _():
        wait(sums_v.at[pl.ds(0, (n_tile - HUB) // GROUP)], send_sem.at[6])

    @pl.when(is_hub)
    def _():
        wait(sums_v.at[pl.ds(0, HUB - 1)], send_sem.at[5])

    @pl.when(jnp.logical_not(is_hub))
    def _():
        wait(sums_v.at[pl.ds(0, HUB)], send_sem.at[5])


    for number, there in enumerate((has_right, has_left)):
        pl.when(there)(functools.partial(wait, edge_v.at[number, pl.ds(0, len(RELAYS))], send_sem.at[number]))

    @pl.when(is_relay)
    def _():
        for _ in range(QUAD - 1):
            wait(margin_v, send_sem.at[7])

    wait(spec_v.at[pl.ds(0, N_SRC - 1)], send_sem.at[2])
    wait(term_v.at[pl.ds(0, QUAD - 1), image_rows], send_sem.at[3])
    wait(part_v, send_sem.at[4])


def hand_over(resist, mask_grad, source_grad, resist_out, mask_grad_out, source_grad_out, row, sem):
    row[...] = source_grad[0, :PER_DEV]
    copies = [
        pltpu.make_async_copy(resist, resist_out, sem.at[0]),
        pltpu.make_async_copy(mask_grad, mask_grad_out, sem.at[1]),
        pltpu.make_async_copy(row, source_grad_out, sem.at[2]),
    ]
    for copy in copies:
        copy.start()
    for copy in copies:
        copy.wait()


def local(mask, target, shifts, weights):
    f32 = jnp.float32
    anywhere = pl.BlockSpec(memory_space=pl.ANY)
    inside = pl.BlockSpec(memory_space=pltpu.VMEM)
    results = pl.pallas_call(
        everything,
        out_shape=(
            pltpu.VMEM((ROWS, TILE), f32),
            pltpu.VMEM((ROWS, TILE), f32),
            pltpu.VMEM((1, 128), f32),
        ),
        in_specs=[anywhere] * 5,
        out_specs=(inside, inside, inside),
        scratch_shapes=[
            pltpu.VMEM((ROWS, TILE), f32),
            pltpu.VMEM((TILE, TILE), jnp.int32),
            pltpu.VMEM((2, PER_DEV), jnp.int32),
            pltpu.VMEM((1, PER_DEV), f32),
            pltpu.VMEM(TABLE.shape, jnp.bfloat16),
            pltpu.VMEM((2, N_SRC, ROWS, 128), f32),
            pltpu.VMEM((BAND, 128), f32),
            pltpu.VMEM((N_SRC, 8, 128), f32),
            pltpu.VMEM((QUAD, PER_DEV, BAND, 128), f32),
            pltpu.VMEM((QUAD, 2, 2, 8, 256), f32),
            pltpu.VMEM((QUAD, ROWS_C // 2, 128), f32),
            pltpu.VMEM((QUAD, 2, 2, ROWS_C, 256), f32),
            pltpu.VMEM((QUAD, 2, 2, ROWS_C // 2, 256), f32),
            pltpu.VMEM((TILE, TILE), f32),
            pltpu.VMEM((QUAD, 8, 128), f32),
            pltpu.VMEM((QUAD - 1, 8, 128), f32),
            pltpu.VMEM((N_TILE, 1, 128), f32),
            pltpu.VMEM((1, 128), f32),
            pltpu.SemaphoreType.DMA((7,)),
            pltpu.SemaphoreType.DMA((8,)),
            pltpu.SemaphoreType.DMA((8,)),
            pltpu.SemaphoreType.REGULAR((N_SRC,)),
            pltpu.SemaphoreType.REGULAR((2,)),
        ],
        compiler_params=pltpu.CompilerParams(
            collective_id=0, has_side_effects=True, vmem_limit_bytes=60 * 1024 * 1024
        ),
    )(mask, target, shifts.T, weights.reshape(1, PER_DEV), jnp.asarray(TABLE))
    return pl.pallas_call(
        hand_over,
        out_shape=(
            jax.ShapeDtypeStruct((ROWS, TILE), f32),
            jax.ShapeDtypeStruct((ROWS, TILE), f32),
            jax.ShapeDtypeStruct((PER_DEV,), f32),
        ),
        in_specs=[inside] * 3,
        out_specs=(anywhere,) * 3,
        scratch_shapes=[pltpu.VMEM((PER_DEV,), f32), pltpu.SemaphoreType.DMA((3,))],
    )(*[pltpu.with_memory_space_constraint(result, pltpu.VMEM) for result in results])


def solution(mesh):
    placed = (P("src", "tile"), P(None, "tile"), P("src", None), P("src"))
    return jax.shard_map(
        local,
        mesh=mesh,
        in_specs=placed,
        out_specs=(P("src", "tile"), P("src", "tile"), P("src")),
        check_vma=False,
    )
```

```python
import functools

import jax
import jax.numpy as jnp
import ml_dtypes
import numpy as np
from jax import lax
from jax.experimental import pallas as pl
from jax.experimental.pallas import tpu as pltpu
from jax.sharding import PartitionSpec as P

TILE = 256
MARGIN = 32
BAND = 64
RAD = 16
EXT = 320
STEEP = 8.0
THRESH = 0.25
LOSS_SCALE = 2.0

N_SRC = 16
N_TILE = 32
PER_DEV = 8
SOURCES = 128
ROWS = 16
HALF = 32
POINTS_R = 66
ROWS_C = 80
COLS_C = 128
QUAD = 4
GROUP = 4
DEPTH = 8
HUB = 3 * GROUP
RIDERS = (31, 63, 95)

MESH = pl.DeviceIdType.MESH
BF16 = ml_dtypes.bfloat16


def halves(table):
    high = table.astype(BF16)
    low = (table - high.astype(np.float64)).astype(BF16)
    return high, low


def column_slots():
    plus = np.arange(HALF)
    return np.concatenate([plus, -plus]), np.concatenate([np.ones(HALF), [0.0], np.ones(HALF - 1)])


def waves(freq, place, period):
    phase = 2.0 * np.pi * ((freq[:, None] * place[None, :]) % period) / period
    return np.cos(phase), np.sin(phase)


def interpolation(points):
    order = np.arange(-2 * RAD, 2 * RAD + 1)
    place = np.arange(TILE) + MARGIN
    offset = place[:, None] / EXT - np.arange(points)[None, :] / points
    return np.cos(2.0 * np.pi * order[None, None, :] * offset[:, :, None]).sum(axis=2) / points


def padded(rows):
    return np.concatenate([rows, np.zeros((ROWS_C // 2 - rows.shape[0], rows.shape[1]))], axis=0)


def build_tables():
    slots, used = column_slots()
    row_freq = np.arange(BAND) - BAND // 2
    pixels = np.arange(TILE) + MARGIN
    parts = {}

    real, imag = waves(np.arange(HALF), np.arange(EXT), EXT)
    fwd = np.concatenate([real, -imag], axis=0).T
    wide = np.zeros((2 * TILE, 2 * HALF))
    wide[:TILE] = fwd[MARGIN : MARGIN + TILE]
    wide[TILE + 96 : TILE + 128] = fwd[:MARGIN]
    wide[TILE + 128 : TILE + 160] = fwd[MARGIN + TILE :]
    high, low = halves(np.concatenate([wide, wide], axis=1))
    parts["enter"] = np.concatenate([high, low], axis=1)

    rows = np.arange(TILE).reshape(N_SRC, 2, 8)
    first, second = rows[:, 0].reshape(-1), rows[:, 1].reshape(-1)
    real, imag = waves(row_freq, pixels, EXT)
    both = np.concatenate([real, -imag], axis=0)
    high, low = halves(np.concatenate([both[:, first], both[:, second]], axis=0))
    parts["spec"] = np.concatenate([high, high], axis=1)
    spec_low = low

    inter_rows, inter_cols = 2.0 * interpolation(POINTS_R), interpolation(COLS_C)
    even, odd = np.arange(0, COLS_C, 2), np.arange(1, COLS_C, 2)
    for name, order in (("even", np.concatenate([even, odd])), ("odd", np.concatenate([odd, even]))):
        real, imag = waves(slots, order, COLS_C)
        real, imag = real * used[:, None], imag * used[:, None]
        cols = np.concatenate(
            [np.concatenate([real, imag], axis=1), np.concatenate([-imag, real], axis=1)], axis=0
        )
        high, low = halves(cols)
        again = high.copy()
        again[[HALF, 3 * HALF]] = high[[0, 2 * HALF]]
        parts["cols_" + name] = np.concatenate([high, again], axis=0)
        parts["cols_low_" + name] = low
        high, low = halves(np.concatenate([cols[:, :COLS_C].T, cols[:, COLS_C:].T], axis=0))
        parts["cols_back_" + name] = np.concatenate([high, low], axis=1)

    lows = []
    for name, start in (("even", 0), ("odd", 1)):
        real, imag = waves(row_freq, np.arange(start, POINTS_R, 2), POINTS_R)
        real, imag = padded(real.T), padded(imag.T)
        high, low = halves(
            np.concatenate(
                [np.concatenate([real, -imag], axis=1), np.concatenate([imag, real], axis=1)], axis=0
            )
        )
        parts["rows_" + name] = np.concatenate([high, high], axis=1)
        lows.append(low)
        pad = np.zeros((2 * BAND, TILE - 3 * ROWS_C), BF16)
        parts["rows_back_" + name] = np.concatenate([high.T, high.T, low.T, pad], axis=1)
    rows_low = np.concatenate(lows, axis=0)

    inter_rows = np.concatenate([padded(inter_rows[:, 0::2].T), padded(inter_rows[:, 1::2].T)], axis=0).T
    inter_cols = inter_cols[:, np.concatenate([even, odd])]
    high, low = halves(inter_rows)
    pad = np.zeros((TILE, TILE - 3 * ROWS_C), BF16)
    parts["fine_rows"] = np.concatenate([high, high, low, pad], axis=1)
    high, low = halves(inter_cols.T)
    parts["fine_cols"] = np.concatenate([high, high], axis=0)
    parts["fine_cols_low"] = low
    parts["coarse_cols"] = np.concatenate([high.T, low.T], axis=1)
    high, low = halves(inter_rows.T)
    parts["coarse_rows"] = high
    parts["coarse_rows_low"] = low

    owners = [
        side * DEPTH + (quad * QUAD + k - 1) % DEPTH for side in range(2) for quad in range(2) for k in range(QUAD)
    ]
    first, second = rows[owners, 0].reshape(-1), rows[owners, 1].reshape(-1)
    high, low = halves(np.concatenate([both[:, first], both[:, second]], axis=1).T)
    parts["leave"] = np.concatenate([high, high], axis=1)
    leave_low = low
    last = fwd[MARGIN : MARGIN + TILE].T
    high, low = halves(np.concatenate([last, last], axis=0))
    parts["last"] = high
    parts["last_low"] = low

    parts["lows_a"] = np.concatenate([spec_low, np.zeros((TILE, 128), BF16)], axis=1)
    rows_low = np.concatenate([rows_low, np.zeros((TILE - 2 * ROWS_C, 128), BF16)], axis=0)
    parts["lows_b"] = np.concatenate([leave_low, rows_low], axis=1)

    order = [
        "enter",
        "spec", "lows_a", "cols_even", "cols_low_even", "cols_odd", "cols_low_odd", "rows_even", "rows_odd", "lows_b",
        "fine_rows", "fine_cols", "fine_cols_low", "coarse_cols", "coarse_rows", "coarse_rows_low",
        "rows_back_even", "rows_back_odd", "cols_back_even", "cols_back_odd", "leave", "last", "last_low",
    ]
    places, start = {}, 0
    for name in order:
        places[name] = (start, parts[name].shape[0])
        start += parts[name].shape[0]
    return np.concatenate([parts[name] for name in order], axis=0), places


TABLE, PLACES = build_tables()
CUTS = (0, PLACES["spec"][0], PLACES["fine_rows"][0], TABLE.shape[0])


def dot(left, right):
    return jnp.dot(left, right, preferred_element_type=jnp.float32)


def cut(value):
    high = value.astype(jnp.bfloat16)
    low = (value - high.astype(jnp.float32)).astype(jnp.bfloat16)
    return high, low


def lanes(shape):
    return lax.broadcasted_iota(jnp.int32, shape, 1)


def enter(value, table):
    rows = value.shape[0]
    both = dot(jnp.concatenate(cut(value), axis=0), table)
    return both[:rows, :128] + both[:rows, 128:] + both[rows:, :128]


def pack(first, second):
    return jnp.where(lanes(first.shape) < 64, first, second)


def spectrum(gathered, table, low_table, roll):
    high, low = cut(gathered)
    out = dot(table, jnp.concatenate([high, low], axis=0)) + dot(low_table, high)
    both = pack(out[:128], out[128:])
    both = both + roll(both, 64, 1)
    turned = roll(both, 32, 1)
    quarter = lanes((BAND, 128)) >> 5
    outer = (quarter == 0) | (quarter == 3)
    even = jnp.where(outer, both[:BAND], turned[:BAND])
    odd = jnp.where(outer, turned[BAND:], both[BAND:])
    return (jnp.where(quarter == 3, -even, even) + jnp.where(quarter == 0, -odd, odd)) * (1.0 / (EXT * EXT))


def pupil_of(row_shift, col_shift):
    row = (lax.broadcasted_iota(jnp.int32, (BAND, 128), 0) - BAND // 2).astype(jnp.float32) + row_shift
    slot = lanes((1, 128)) & 63
    col = jnp.where(slot < HALF, slot, HALF - slot).astype(jnp.float32) + col_shift
    room = RAD * RAD - col * col
    return jnp.where(row * row <= room, 1.0, 0.0)


def swap(first, second):
    return pack(first, second), pack(second, first)


def split_bands(spec, roll):
    spare = (lanes(spec.shape) & 63) == HALF
    high, low = cut(jnp.where(spare, 0.0, spec))
    left = spec - high.astype(jnp.float32) - low.astype(jnp.float32)
    low = jnp.where(spare, roll(left, HALF, 1), low.astype(jnp.float32)).astype(jnp.bfloat16)
    return high, low


def coarse_fields(bands, pupils, cols, rows):
    high, low = bands
    mids = []
    for which in range(2):
        band_high, band_low = [
            jnp.concatenate([part * pupil for pupil in pupils[which::2]], axis=0) for part in (high, low)
        ]
        table, low_table = cols[which]
        mids.append(
            dot(jnp.concatenate([band_high, band_low], axis=1), table) + dot(band_high, low_table)
        )
    fields = []
    for group in range(2):
        stacks = ([], [])
        for pair in (2 * group, 2 * group + 1):
            at = slice(BAND * pair, BAND * pair + BAND)
            real = swap(mids[0][at, :128], mids[1][at, :128])
            imag = swap(mids[0][at, 128:], mids[1][at, 128:])
            for parity in range(2):
                stacks[parity].append(jnp.concatenate([real[parity], imag[parity]], axis=0))
        both = []
        for parity in range(2):
            upper, lower = cut(jnp.concatenate(stacks[parity], axis=1))
            table, low_table = rows[parity]
            both.append(dot(table, jnp.concatenate([upper, lower], axis=0)) + dot(low_table, upper))
        fields.append(both)
    return fields


def power_of(field):
    half = ROWS_C // 2
    return field[:half] * field[:half] + field[half:] * field[half:]


def join_image(even, odd, roll):
    return pack(even + roll(even, 64, 1), odd + roll(odd, 64, 1))


def pixels_of(coarse, fine_rows, fine_cols, fine_cols_low):
    first = lanes(coarse.shape) < 64
    coarse = jnp.concatenate([jnp.where(first, coarse, 0.0), jnp.where(first, 0.0, coarse)], axis=0)
    high, low = cut(coarse)
    mid = dot(jnp.concatenate([high, low], axis=1), fine_cols) + dot(high, fine_cols_low)
    return dot(fine_rows, three(mid))


def three(value):
    high, low = cut(value)
    pad = jnp.zeros((TILE - 3 * value.shape[0], value.shape[1]), jnp.bfloat16)
    return jnp.concatenate([high, low, high, pad], axis=0)


def coarse_of(slope, coarse_rows, coarse_rows_low, coarse_cols):
    high, low = cut(slope)
    mid = dot(coarse_rows, high) + dot(coarse_rows, low) + dot(coarse_rows_low, high)
    high, low = cut(mid)
    both = dot(high, coarse_cols)
    return both[:, :128] + both[:, 128:] + dot(low, coarse_cols[:, :128])


def twice(coarse, roll):
    half = ROWS_C // 2
    even, odd = coarse[:half], coarse[half:]
    return pack(even, roll(even, 64, 1)), pack(roll(odd, 64, 1), odd)


def band_grad(total, adjoints, pupils, rows_back, cols_back):
    sides = ([], [])
    for group in range(2):
        even, odd = [dot(rows_back[parity], three(adjoints[group][parity])) for parity in range(2)]
        for pair in range(2):
            at = slice(128 * pair, 128 * pair + 128)
            real = swap(even[:BAND, at], odd[:BAND, at])
            imag = swap(even[BAND:, at], odd[BAND:, at])
            for which in range(2):
                sides[which].append(jnp.concatenate([real[which], imag[which]], axis=1))
    for which in range(2):
        high, low = cut(jnp.concatenate(sides[which], axis=0))
        both = dot(high, cols_back[which])
        term = both[:, :128] + both[:, 128:] + dot(low, cols_back[which][:, :128])
        for k in range(PER_DEV // 2):
            total = total + term[BAND * k : BAND * k + BAND] * pupils[2 * k + which]
    return total


def fold(grad, roll):
    r32, r64, r96 = roll(grad, 32, 1), roll(grad, 64, 1), roll(grad, 96, 1)
    quarter = lanes(grad.shape) >> 5
    upper = jnp.where(
        quarter == 0, grad + r96, jnp.where(quarter == 1, r96 - r64, jnp.where(quarter == 2, r64 + r32, r32 - grad))
    )
    lower = jnp.where(
        quarter == 0, r64 + r32, jnp.where(quarter == 1, grad - r32, jnp.where(quarter == 2, grad + r96, r64 - r96))
    )
    return jnp.concatenate([upper, lower], axis=0)


def row_grads(grad, leave, leave_low, roll):
    high, low = cut(fold(grad, roll))
    out = dot(leave, jnp.concatenate([high, low], axis=0)) + dot(leave_low, high)
    half = out.shape[0] // 2
    return pack(out[:half], out[half:])


def last_step(total, last, last_low):
    first = lanes(total.shape) < 64
    value = jnp.concatenate([jnp.where(first, total, 0.0), jnp.where(first, 0.0, total)], axis=0)
    high, low = cut(value)
    return (dot(high, last) + dot(low, last) + dot(high, last_low)) * (1.0 / (EXT * EXT))


def rank_of(side, along):
    step = jnp.where(along == 3, 4, jnp.where(along == 7, 3, 11 - along))
    return 2 * jnp.where(along < 3, along, step) + side


def src_of(rank):
    step, side = rank // 2, rank % 2
    along = jnp.where(step == 3, 7, jnp.where(step == 4, 3, 11 - step))
    return side * DEPTH + jnp.where(step < 3, step, along)


def repeat(first, last, body):
    def step(k, carry):
        body(k)
        return carry

    lax.fori_loop(first, last, step, 0)


def everything(mask, target, shifts, weights, table, resist, mask_grad, source_grad, *scratch):
    (
        mask_v, target_v, shifts_v, weights_v, table_v,
        left_v, right_v, spec_v, pupil_v, scale_v, term_v, field_v, power_v,
        printed_v, grad_v, part_v, sums_v, total_v, local_sem, send_sem, recv_sem, ready_sem, hub_sem,
    ) = scratch
    tile, src = lax.axis_index("tile"), lax.axis_index("src")
    n_tile = lax.axis_size("tile")
    left, right = tile - 1, tile + 1
    has_left, has_right = tile > 0, tile < n_tile - 1
    side, along = src // DEPTH, src % DEPTH
    rank = rank_of(side, along)
    place_in_quad = (along + 1) % QUAD
    quad = (along + 1) % DEPTH // QUAD
    partners = [
        (side + across) % 2 * DEPTH + (along + step) % DEPTH for across, step in ((0, QUAD), (1, 0), (1, QUAD))
    ]

    def member(k):
        return side * DEPTH + (quad * QUAD + k + DEPTH - 1) % DEPTH

    layer = tile // GROUP
    place = tile % GROUP
    is_hub, is_teller = tile < HUB, layer == HUB // GROUP - 1

    def get(name, start=None, stop=None):
        at, size = PLACES[name]
        if start is None:
            return table_v[at : at + size, :]
        return table_v[at : at + size, start:stop]

    def signal(sem, device):
        pl.semaphore_signal(sem, inc=1, device_id=device, device_id_type=MESH)

    def send(source, target_ref, number, device):
        copy = pltpu.make_async_remote_copy(
            src_ref=source,
            dst_ref=target_ref,
            send_sem=send_sem.at[number],
            recv_sem=recv_sem.at[number],
            device_id=device,
            device_id_type=MESH,
        )
        copy.start()

    def wait(ref, sem):
        pltpu.make_async_copy(ref, ref, sem).wait()

    barrier = pltpu.get_barrier_semaphore()

    @pl.when(has_left)
    def _():
        signal(barrier, {"tile": left})

    @pl.when(has_right)
    def _():
        signal(barrier, {"tile": right})

    repeat(rank + 1, N_SRC, lambda k: signal(barrier, {"src": src_of(k)}))
    local = [
        pltpu.make_async_copy(mask, mask_v, local_sem.at[0]),
        pltpu.make_async_copy(shifts, shifts_v, local_sem.at[1]),
        pltpu.make_async_copy(weights, weights_v, local_sem.at[2]),
    ]
    for k in range(3):
        rows = pl.ds(CUTS[k], CUTS[k + 1] - CUTS[k])
        local.append(pltpu.make_async_copy(table.at[rows], table_v.at[rows], local_sem.at[3 + k]))
    local.append(pltpu.make_async_copy(target, target_v, local_sem.at[6]))
    for k in (0, 3, 1, 2):
        local[k].start()
    repeat(jnp.where(is_hub, tile + 1, n_tile), n_tile, lambda k: signal(barrier, {"tile": k}))

    ends = has_left.astype(jnp.int32) + has_right.astype(jnp.int32)
    pl.semaphore_wait(barrier, rank + ends + jnp.minimum(tile, HUB))

    @pl.when(has_right)
    def _():
        send(mask.at[:, pl.ds(128, 128)], left_v, 0, {"tile": right})

    @pl.when(has_left)
    def _():
        send(mask.at[:, pl.ds(0, 128)], right_v, 1, {"tile": left})

    repeat(0, rank, lambda k: signal(ready_sem.at[rank], {"src": src_of(k)}))
    term_v[:, POINTS_R // 2 :, :] = jnp.zeros((QUAD, (ROWS_C - POINTS_R) // 2, 128), jnp.float32)

    @pl.when(jnp.logical_not(has_left))
    def _():
        left_v[...] = jnp.zeros_like(left_v)

    @pl.when(jnp.logical_not(has_right))
    def _():
        right_v[...] = jnp.zeros_like(right_v)

    local[1].wait()
    local[2].wait()
    shape = (PER_DEV, PER_DEV)
    own_place = lanes(shape) == lax.broadcasted_iota(jnp.int32, shape, 0)

    def upright(row):
        return jnp.sum(jnp.where(own_place, row, 0.0), axis=1, keepdims=True)

    own_shifts = shifts_v[...].astype(jnp.float32)
    riders = [upright(own_shifts[0:1, :]), upright(own_shifts[1:2, :]), upright(weights_v[...])]
    local[0].wait()
    local[3].wait()
    at = PLACES["enter"][0]
    own = enter(mask_v[...], table_v[at : at + TILE, :])

    @pl.when(has_left)
    def _():
        wait(left_v, recv_sem.at[0])

    @pl.when(has_right)
    def _():
        wait(right_v, recv_sem.at[1])

    margins = jnp.concatenate([left_v[...], right_v[...]], axis=1)
    own = own + enter(margins, table_v[at + TILE : at + 2 * TILE, :])
    own = pack(own[:8], own[8:])
    for lane, rider in zip(RIDERS, riders):
        own = jnp.where(lanes(own.shape) == lane, rider, own)
    spec_v[src] = own

    def send_piece(k):
        send(spec_v.at[src], spec_v.at[src], 2, {"src": src_of(k)})

    def answer_piece(k):
        pl.semaphore_wait(ready_sem.at[k], 1)
        send_piece(k)

    repeat(0, (rank + 1) // 2, lambda k: send_piece(2 * k))
    repeat(0, rank // 2, lambda k: send_piece(2 * k + 1))
    for k in (4, 5, 6):
        local[k].start()
    repeat(rank + 1, N_SRC, answer_piece)
    repeat(0, jnp.where(is_hub, tile, 0), lambda k: signal(hub_sem.at[0], {"tile": k}))

    @pl.when(jnp.logical_not(is_hub))
    def _():
        signal(hub_sem.at[1], {"tile": HUB - GROUP + place})

    local[4].wait()
    wait(spec_v.at[pl.ds(0, N_SRC - 1)], recv_sem.at[2])

    gathered = spec_v[...].reshape(128, 128)
    spec = spectrum(gathered, get("spec"), get("lows_a", 0, 128), pltpu.roll)
    bands = split_bands(spec, pltpu.roll)
    at = PLACES["lows_b"][0]
    cols = [(get("cols_" + name), get("cols_low_" + name)) for name in ("even", "odd")]
    rows = [
        (get("rows_even"), table_v[at : at + ROWS_C, 128:256]),
        (get("rows_odd"), table_v[at + ROWS_C : at + 2 * ROWS_C, 128:256]),
    ]

    def add_fields(part, images):
        owner = src
        for k, peer in enumerate(partners):
            owner = jnp.where(part == k + 1, peer, owner)
        rows_by, cols_by, scales = [spec_v[owner, :, lane : lane + 1] for lane in RIDERS]
        for s in range(PER_DEV):
            pupil_v[part, s] = pupil_of(rows_by[s : s + 1], cols_by[s : s + 1])
        for pair in range(PER_DEV // 2):
            first, second = [jnp.broadcast_to(scales[s : s + 1], (8, 128)) for s in (2 * pair, 2 * pair + 1)]
            at = slice(128 * (pair % 2), 128 * (pair % 2) + 128)
            for parity, scale in enumerate(swap(first, second)):
                scale_v[part, pair // 2, parity, :, at] = scale
        fields = coarse_fields(
            bands, [pupil_v[part, s].astype(jnp.bfloat16) for s in range(PER_DEV)], cols, rows
        )
        images = list(images)
        for group in range(2):
            for parity in range(2):
                field_v[part, group, parity] = fields[group][parity]
                power = power_of(fields[group][parity])
                power_v[part, group, parity] = power
                power = power * scale_v[part, group, parity, 0:1, :]
                images[parity] = images[parity] + power[:, :128] + power[:, 128:]
        return tuple(images)

    none = jnp.zeros((ROWS_C // 2, 128), jnp.float32)
    image = lax.fori_loop(0, QUAD, add_fields, (none, none), unroll=True)
    term_v[place_in_quad] = join_image(*image, pltpu.roll)
    image_rows = pl.ds(0, POINTS_R // 2)
    mine = term_v.at[place_in_quad, image_rows]

    def send_image(k):
        send(mine, mine, 3, {"src": member(k)})

    for k in (1, 0, 2, 3):
        pl.when(k != place_in_quad)(functools.partial(send_image, k))
    local[5].wait()
    local[6].wait()
    wait(term_v.at[pl.ds(0, QUAD - 1), image_rows], recv_sem.at[3])

    image = pixels_of(
        term_v[0] + term_v[1] + term_v[2] + term_v[3],
        get("fine_rows"),
        get("fine_cols"),
        get("fine_cols_low"),
    )
    printed = jax.nn.sigmoid(STEEP * (image * (1.0 / SOURCES) - THRESH))
    goal = target_v[...].astype(jnp.float32)
    slope = (LOSS_SCALE * 2.0 * STEEP) * (printed - goal) * printed * (1.0 - printed)
    coarse = coarse_of(slope, get("coarse_rows"), get("coarse_rows_low"), get("coarse_cols"))

    slopes = twice(coarse, pltpu.roll)
    sums = []
    for pair in range(PER_DEV // 2):
        at = slice(128 * (pair % 2), 128 * (pair % 2) + 128)
        terms = [
            jnp.sum(slopes[parity] * power_v[0, pair // 2, parity, :, at], axis=0, keepdims=True) for parity in range(2)
        ]
        sums.extend(swap(*terms))
    sums = jnp.sum(jnp.concatenate(sums, axis=0), axis=1, keepdims=True)
    spot = (PER_DEV, 128)
    sums = jnp.where(lanes(spot) == lax.broadcasted_iota(jnp.int32, spot, 0), sums, 0.0)
    sums_v[tile] = jnp.sum(sums, axis=0, keepdims=True)

    def send_sums(k):
        pltpu.make_async_remote_copy(
            src_ref=sums_v.at[tile],
            dst_ref=sums_v.at[tile],
            send_sem=send_sem.at[5],
            recv_sem=recv_sem.at[5],
            device_id={"tile": k},
            device_id_type=MESH,
        ).start()

    for k in range(HUB):
        first = k + 1 - 2 * (k % 2)
        pl.when(first < tile)(functools.partial(send_sums, first))

    printed_v[...] = printed
    resist[...] = printed_v[pl.ds(pl.multiple_of(src * ROWS, ROWS), ROWS), :]

    wide = [jnp.concatenate([slope, slope], axis=1) * (2.0 / SOURCES) for slope in slopes]
    rows_back = [get("rows_back_even"), get("rows_back_odd")]
    cols_back = [get("cols_back_even"), get("cols_back_odd")]

    def add_part(part, total):
        adjoints = []
        for group in range(2):
            adjoints.append([])
            for parity in range(2):
                scaled = wide[parity] * scale_v[part, group, parity, 0:1, :]
                adjoints[group].append(field_v[part, group, parity] * jnp.concatenate([scaled, scaled], axis=0))
        return band_grad(total, adjoints, [pupil_v[part, s] for s in range(PER_DEV)], rows_back, cols_back)

    grad = lax.fori_loop(0, QUAD, add_part, jnp.zeros((BAND, 128), jnp.float32))
    first = PLACES["leave"][0] + 8 * QUAD * (2 * side + quad)
    low_first = PLACES["lows_b"][0] + 8 * QUAD * (2 * side + quad)

    def halves_of(start, stop, begin):
        begin = pl.multiple_of(begin, 32)
        then = pl.multiple_of(begin + 128, 32)
        return jnp.concatenate(
            [table_v[pl.ds(begin, 8 * QUAD), start:stop], table_v[pl.ds(then, 8 * QUAD), start:stop]], axis=0
        )

    rows = row_grads(grad, halves_of(0, 256, first), halves_of(0, 128, low_first), pltpu.roll)
    grad_v[...] = rows.reshape(QUAD, 8, 128)
    for k in range(1, QUAD):
        other = (place_in_quad + k) % QUAD
        send(grad_v.at[other], part_v.at[k - 1], 4, {"src": member(other)})

    @pl.when(tile < HUB - 1)
    def _():
        pl.semaphore_wait(hub_sem.at[0], HUB - 1 - tile)
        repeat(tile + 1, HUB, send_sums)

    wait(part_v, recv_sem.at[4])
    total = grad_v[place_in_quad] + part_v[0] + part_v[1] + part_v[2]
    mask_grad[...] = last_step(total, get("last"), get("last_low"))

    @pl.when(is_hub)
    def _():
        wait(sums_v.at[pl.ds(0, n_tile - 1)], recv_sem.at[5])
        total_v[...] = jnp.sum(sums_v[...], axis=0) * (1.0 / (SOURCES * n_tile * TILE * TILE))

    def tell(k):
        send(total_v, total_v, 6, {"tile": k * GROUP + place})

    @pl.when(is_teller)
    def _():
        pl.semaphore_wait(hub_sem.at[1], (n_tile - HUB) // GROUP)
        repeat(HUB // GROUP, n_tile // GROUP, tell)

    @pl.when(jnp.logical_not(is_hub))
    def _():
        wait(total_v, recv_sem.at[6])

    source_grad[...] = total_v[...]

    @pl.when(is_teller)
    def _():
        wait(sums_v.at[pl.ds(0, (n_tile - HUB) // GROUP)], send_sem.at[6])

    @pl.when(is_hub)
    def _():
        wait(sums_v.at[pl.ds(0, HUB - 1)], send_sem.at[5])

    @pl.when(jnp.logical_not(is_hub))
    def _():
        wait(sums_v.at[pl.ds(0, HUB)], send_sem.at[5])


    @pl.when(has_right)
    def _():
        wait(left_v, send_sem.at[0])

    @pl.when(has_left)
    def _():
        wait(right_v, send_sem.at[1])

    wait(spec_v.at[pl.ds(0, N_SRC - 1)], send_sem.at[2])
    wait(term_v.at[pl.ds(0, QUAD - 1), image_rows], send_sem.at[3])
    wait(part_v, send_sem.at[4])


def hand_over(resist, mask_grad, source_grad, resist_out, mask_grad_out, source_grad_out, row, sem):
    row[...] = source_grad[0, :PER_DEV]
    copies = [
        pltpu.make_async_copy(resist, resist_out, sem.at[0]),
        pltpu.make_async_copy(mask_grad, mask_grad_out, sem.at[1]),
        pltpu.make_async_copy(row, source_grad_out, sem.at[2]),
    ]
    for copy in copies:
        copy.start()
    for copy in copies:
        copy.wait()


def local(mask, target, shifts, weights):
    f32 = jnp.float32
    anywhere = pl.BlockSpec(memory_space=pl.ANY)
    inside = pl.BlockSpec(memory_space=pltpu.VMEM)
    results = pl.pallas_call(
        everything,
        out_shape=(
            pltpu.VMEM((ROWS, TILE), f32),
            pltpu.VMEM((ROWS, TILE), f32),
            pltpu.VMEM((1, 128), f32),
        ),
        in_specs=[anywhere] * 5,
        out_specs=(inside, inside, inside),
        scratch_shapes=[
            pltpu.VMEM((ROWS, TILE), f32),
            pltpu.VMEM((TILE, TILE), jnp.int32),
            pltpu.VMEM((2, PER_DEV), jnp.int32),
            pltpu.VMEM((1, PER_DEV), f32),
            pltpu.VMEM(TABLE.shape, jnp.bfloat16),
            pltpu.VMEM((ROWS, 128), f32),
            pltpu.VMEM((ROWS, 128), f32),
            pltpu.VMEM((N_SRC, 8, 128), f32),
            pltpu.VMEM((QUAD, PER_DEV, BAND, 128), f32),
            pltpu.VMEM((QUAD, 2, 2, 8, 256), f32),
            pltpu.VMEM((QUAD, ROWS_C // 2, 128), f32),
            pltpu.VMEM((QUAD, 2, 2, ROWS_C, 256), f32),
            pltpu.VMEM((QUAD, 2, 2, ROWS_C // 2, 256), f32),
            pltpu.VMEM((TILE, TILE), f32),
            pltpu.VMEM((QUAD, 8, 128), f32),
            pltpu.VMEM((QUAD - 1, 8, 128), f32),
            pltpu.VMEM((N_TILE, 1, 128), f32),
            pltpu.VMEM((1, 128), f32),
            pltpu.SemaphoreType.DMA((7,)),
            pltpu.SemaphoreType.DMA((7,)),
            pltpu.SemaphoreType.DMA((7,)),
            pltpu.SemaphoreType.REGULAR((N_SRC,)),
            pltpu.SemaphoreType.REGULAR((2,)),
        ],
        compiler_params=pltpu.CompilerParams(
            collective_id=0, has_side_effects=True, vmem_limit_bytes=60 * 1024 * 1024
        ),
    )(mask, target, shifts.T, weights.reshape(1, PER_DEV), jnp.asarray(TABLE))
    return pl.pallas_call(
        hand_over,
        out_shape=(
            jax.ShapeDtypeStruct((ROWS, TILE), f32),
            jax.ShapeDtypeStruct((ROWS, TILE), f32),
            jax.ShapeDtypeStruct((PER_DEV,), f32),
        ),
        in_specs=[inside] * 3,
        out_specs=(anywhere,) * 3,
        scratch_shapes=[pltpu.VMEM((PER_DEV,), f32), pltpu.SemaphoreType.DMA((3,))],
    )(*[pltpu.with_memory_space_constraint(result, pltpu.VMEM) for result in results])


def solution(mesh):
    placed = (P("src", "tile"), P(None, "tile"), P("src", None), P("src"))
    return jax.shard_map(
        local,
        mesh=mesh,
        in_specs=placed,
        out_specs=(P("src", "tile"), P("src", "tile"), P("src")),
        check_vma=False,
    )
```

```python
import functools

import jax
import jax.numpy as jnp
import ml_dtypes
import numpy as np
from jax import lax
from jax.experimental import pallas as pl
from jax.experimental.pallas import tpu as pltpu
from jax.sharding import PartitionSpec as P

TILE = 256
MARGIN = 32
BAND = 64
RAD = 16
EXT = 320
STEEP = 8.0
THRESH = 0.25
LOSS_SCALE = 2.0

N_SRC = 16
N_TILE = 32
PER_DEV = 8
SOURCES = 128
ROWS = 16
HALF = 32
POINTS_R = 66
ROWS_C = 80
COLS_C = 128
QUAD = 4
GROUP = 4
DEPTH = 8
HUB = 3 * GROUP
RIDERS = (31, 63, 95)

MESH = pl.DeviceIdType.MESH
BF16 = ml_dtypes.bfloat16


def halves(table):
    high = table.astype(BF16)
    low = (table - high.astype(np.float64)).astype(BF16)
    return high, low


def column_slots():
    plus = np.arange(HALF)
    return np.concatenate([plus, -plus]), np.concatenate([np.ones(HALF), [0.0], np.ones(HALF - 1)])


def waves(freq, place, period):
    phase = 2.0 * np.pi * ((freq[:, None] * place[None, :]) % period) / period
    return np.cos(phase), np.sin(phase)


def interpolation(points):
    order = np.arange(-2 * RAD, 2 * RAD + 1)
    place = np.arange(TILE) + MARGIN
    offset = place[:, None] / EXT - np.arange(points)[None, :] / points
    return np.cos(2.0 * np.pi * order[None, None, :] * offset[:, :, None]).sum(axis=2) / points


def padded(rows):
    return np.concatenate([rows, np.zeros((ROWS_C // 2 - rows.shape[0], rows.shape[1]))], axis=0)


def build_tables():
    slots, used = column_slots()
    row_freq = np.arange(BAND) - BAND // 2
    pixels = np.arange(TILE) + MARGIN
    parts = {}

    real, imag = waves(np.arange(HALF), np.arange(EXT), EXT)
    fwd = np.concatenate([real, -imag], axis=0).T
    wide = np.zeros((2 * TILE, 2 * HALF))
    wide[:TILE] = fwd[MARGIN : MARGIN + TILE]
    wide[TILE + 96 : TILE + 128] = fwd[:MARGIN]
    wide[TILE + 128 : TILE + 160] = fwd[MARGIN + TILE :]
    high, low = halves(np.concatenate([wide, wide], axis=1))
    parts["enter"] = np.concatenate([high, low], axis=1)

    rows = np.arange(TILE).reshape(N_SRC, 2, 8)
    first, second = rows[:, 0].reshape(-1), rows[:, 1].reshape(-1)
    real, imag = waves(row_freq, pixels, EXT)
    both = np.concatenate([real, -imag], axis=0)
    high, low = halves(np.concatenate([both[:, first], both[:, second]], axis=0))
    parts["spec"] = np.concatenate([high, high], axis=1)
    spec_low = low

    inter_rows, inter_cols = 2.0 * interpolation(POINTS_R), interpolation(COLS_C)
    even, odd = np.arange(0, COLS_C, 2), np.arange(1, COLS_C, 2)
    for name, order in (("even", np.concatenate([even, odd])), ("odd", np.concatenate([odd, even]))):
        real, imag = waves(slots, order, COLS_C)
        real, imag = real * used[:, None], imag * used[:, None]
        cols = np.concatenate(
            [np.concatenate([real, imag], axis=1), np.concatenate([-imag, real], axis=1)], axis=0
        )
        high, low = halves(cols)
        again = high.copy()
        again[[HALF, 3 * HALF]] = high[[0, 2 * HALF]]
        parts["cols_" + name] = np.concatenate([high, again], axis=0)
        parts["cols_low_" + name] = low
        high, low = halves(np.concatenate([cols[:, :COLS_C].T, cols[:, COLS_C:].T], axis=0))
        parts["cols_back_" + name] = np.concatenate([high, low], axis=1)

    lows = []
    for name, start in (("even", 0), ("odd", 1)):
        real, imag = waves(row_freq, np.arange(start, POINTS_R, 2), POINTS_R)
        real, imag = padded(real.T), padded(imag.T)
        high, low = halves(
            np.concatenate(
                [np.concatenate([real, -imag], axis=1), np.concatenate([imag, real], axis=1)], axis=0
            )
        )
        parts["rows_" + name] = np.concatenate([high, high], axis=1)
        lows.append(low)
        pad = np.zeros((2 * BAND, TILE - 3 * ROWS_C), BF16)
        parts["rows_back_" + name] = np.concatenate([high.T, high.T, low.T, pad], axis=1)
    rows_low = np.concatenate(lows, axis=0)

    inter_rows = np.concatenate([padded(inter_rows[:, 0::2].T), padded(inter_rows[:, 1::2].T)], axis=0).T
    inter_cols = inter_cols[:, np.concatenate([even, odd])]
    high, low = halves(inter_rows)
    pad = np.zeros((TILE, TILE - 3 * ROWS_C), BF16)
    parts["fine_rows"] = np.concatenate([high, high, low, pad], axis=1)
    high, low = halves(inter_cols.T)
    parts["fine_cols"] = np.concatenate([high, high], axis=0)
    parts["fine_cols_low"] = low
    parts["coarse_cols"] = np.concatenate([high.T, low.T], axis=1)
    high, low = halves(inter_rows.T)
    parts["coarse_rows"] = high
    parts["coarse_rows_low"] = low

    owners = [
        side * DEPTH + (quad * QUAD + k - 1) % DEPTH for side in range(2) for quad in range(2) for k in range(QUAD)
    ]
    first, second = rows[owners, 0].reshape(-1), rows[owners, 1].reshape(-1)
    high, low = halves(np.concatenate([both[:, first], both[:, second]], axis=1).T)
    parts["leave"] = np.concatenate([high, high], axis=1)
    leave_low = low
    last = fwd[MARGIN : MARGIN + TILE].T
    high, low = halves(np.concatenate([last, last], axis=0))
    parts["last"] = high
    parts["last_low"] = low

    parts["lows_a"] = np.concatenate([spec_low, np.zeros((TILE, 128), BF16)], axis=1)
    rows_low = np.concatenate([rows_low, np.zeros((TILE - 2 * ROWS_C, 128), BF16)], axis=0)
    parts["lows_b"] = np.concatenate([leave_low, rows_low], axis=1)

    order = [
        "enter",
        "spec", "lows_a", "cols_even", "cols_low_even", "cols_odd", "cols_low_odd", "rows_even", "rows_odd", "lows_b",
        "fine_rows", "fine_cols", "fine_cols_low", "coarse_cols", "coarse_rows", "coarse_rows_low",
        "rows_back_even", "rows_back_odd", "cols_back_even", "cols_back_odd", "leave", "last", "last_low",
    ]
    places, start = {}, 0
    for name in order:
        places[name] = (start, parts[name].shape[0])
        start += parts[name].shape[0]
    return np.concatenate([parts[name] for name in order], axis=0), places


TABLE, PLACES = build_tables()
CUTS = (0, PLACES["spec"][0], PLACES["fine_rows"][0], TABLE.shape[0])


def dot(left, right):
    return jnp.dot(left, right, preferred_element_type=jnp.float32)


def cut(value):
    high = value.astype(jnp.bfloat16)
    low = (value - high.astype(jnp.float32)).astype(jnp.bfloat16)
    return high, low


def lanes(shape):
    return lax.broadcasted_iota(jnp.int32, shape, 1)


def enter(value, table):
    rows = value.shape[0]
    both = dot(jnp.concatenate(cut(value), axis=0), table)
    return both[:rows, :128] + both[:rows, 128:] + both[rows:, :128]


def pack(first, second):
    return jnp.where(lanes(first.shape) < 64, first, second)


def spectrum(gathered, table, low_table, roll):
    high, low = cut(gathered)
    out = dot(table, jnp.concatenate([high, low], axis=0)) + dot(low_table, high)
    both = pack(out[:128], out[128:])
    both = both + roll(both, 64, 1)
    turned = roll(both, 32, 1)
    quarter = lanes((BAND, 128)) >> 5
    outer = (quarter == 0) | (quarter == 3)
    even = jnp.where(outer, both[:BAND], turned[:BAND])
    odd = jnp.where(outer, turned[BAND:], both[BAND:])
    return (jnp.where(quarter == 3, -even, even) + jnp.where(quarter == 0, -odd, odd)) * (1.0 / (EXT * EXT))


def pupil_of(row_shift, col_shift):
    row = (lax.broadcasted_iota(jnp.int32, (BAND, 128), 0) - BAND // 2).astype(jnp.float32) + row_shift
    slot = lanes((1, 128)) & 63
    col = jnp.where(slot < HALF, slot, HALF - slot).astype(jnp.float32) + col_shift
    room = RAD * RAD - col * col
    return jnp.where(row * row <= room, 1.0, 0.0)


def swap(first, second):
    return pack(first, second), pack(second, first)


def split_bands(spec, roll):
    spare = (lanes(spec.shape) & 63) == HALF
    high, low = cut(jnp.where(spare, 0.0, spec))
    left = spec - high.astype(jnp.float32) - low.astype(jnp.float32)
    low = jnp.where(spare, roll(left, HALF, 1), low.astype(jnp.float32)).astype(jnp.bfloat16)
    return high, low


def coarse_fields(bands, pupils, cols, rows):
    high, low = bands
    mids = []
    for which in range(2):
        band_high, band_low = [
            jnp.concatenate([part * pupil for pupil in pupils[which::2]], axis=0) for part in (high, low)
        ]
        table, low_table = cols[which]
        mids.append(
            dot(jnp.concatenate([band_high, band_low], axis=1), table) + dot(band_high, low_table)
        )
    fields = []
    for group in range(2):
        stacks = ([], [])
        for pair in (2 * group, 2 * group + 1):
            at = slice(BAND * pair, BAND * pair + BAND)
            real = swap(mids[0][at, :128], mids[1][at, :128])
            imag = swap(mids[0][at, 128:], mids[1][at, 128:])
            for parity in range(2):
                stacks[parity].append(jnp.concatenate([real[parity], imag[parity]], axis=0))
        both = []
        for parity in range(2):
            upper, lower = cut(jnp.concatenate(stacks[parity], axis=1))
            table, low_table = rows[parity]
            both.append(dot(table, jnp.concatenate([upper, lower], axis=0)) + dot(low_table, upper))
        fields.append(both)
    return fields


def power_of(field):
    half = ROWS_C // 2
    return field[:half] * field[:half] + field[half:] * field[half:]


def join_image(even, odd, roll):
    return pack(even + roll(even, 64, 1), odd + roll(odd, 64, 1))


def pixels_of(coarse, fine_rows, fine_cols, fine_cols_low):
    first = lanes(coarse.shape) < 64
    coarse = jnp.concatenate([jnp.where(first, coarse, 0.0), jnp.where(first, 0.0, coarse)], axis=0)
    high, low = cut(coarse)
    mid = dot(jnp.concatenate([high, low], axis=1), fine_cols) + dot(high, fine_cols_low)
    return dot(fine_rows, three(mid))


def three(value):
    high, low = cut(value)
    pad = jnp.zeros((TILE - 3 * value.shape[0], value.shape[1]), jnp.bfloat16)
    return jnp.concatenate([high, low, high, pad], axis=0)


def coarse_of(slope, coarse_rows, coarse_rows_low, coarse_cols):
    high, low = cut(slope)
    mid = dot(coarse_rows, high) + dot(coarse_rows, low) + dot(coarse_rows_low, high)
    high, low = cut(mid)
    both = dot(high, coarse_cols)
    return both[:, :128] + both[:, 128:] + dot(low, coarse_cols[:, :128])


def twice(coarse, roll):
    half = ROWS_C // 2
    even, odd = coarse[:half], coarse[half:]
    return pack(even, roll(even, 64, 1)), pack(roll(odd, 64, 1), odd)


def band_grad(total, adjoints, pupils, rows_back, cols_back):
    sides = ([], [])
    for group in range(2):
        even, odd = [dot(rows_back[parity], three(adjoints[group][parity])) for parity in range(2)]
        for pair in range(2):
            at = slice(128 * pair, 128 * pair + 128)
            real = swap(even[:BAND, at], odd[:BAND, at])
            imag = swap(even[BAND:, at], odd[BAND:, at])
            for which in range(2):
                sides[which].append(jnp.concatenate([real[which], imag[which]], axis=1))
    for which in range(2):
        high, low = cut(jnp.concatenate(sides[which], axis=0))
        both = dot(high, cols_back[which])
        term = both[:, :128] + both[:, 128:] + dot(low, cols_back[which][:, :128])
        for k in range(PER_DEV // 2):
            total = total + term[BAND * k : BAND * k + BAND] * pupils[2 * k + which]
    return total


def fold(grad, roll):
    r32, r64, r96 = roll(grad, 32, 1), roll(grad, 64, 1), roll(grad, 96, 1)
    quarter = lanes(grad.shape) >> 5
    upper = jnp.where(
        quarter == 0, grad + r96, jnp.where(quarter == 1, r96 - r64, jnp.where(quarter == 2, r64 + r32, r32 - grad))
    )
    lower = jnp.where(
        quarter == 0, r64 + r32, jnp.where(quarter == 1, grad - r32, jnp.where(quarter == 2, grad + r96, r64 - r96))
    )
    return jnp.concatenate([upper, lower], axis=0)


def row_grads(grad, leave, leave_low, roll):
    high, low = cut(fold(grad, roll))
    out = dot(leave, jnp.concatenate([high, low], axis=0)) + dot(leave_low, high)
    half = out.shape[0] // 2
    return pack(out[:half], out[half:])


def last_step(total, last, last_low):
    first = lanes(total.shape) < 64
    value = jnp.concatenate([jnp.where(first, total, 0.0), jnp.where(first, 0.0, total)], axis=0)
    high, low = cut(value)
    return (dot(high, last) + dot(low, last) + dot(high, last_low)) * (1.0 / (EXT * EXT))


def rank_of(side, along):
    step = jnp.where(along == 3, 4, jnp.where(along == 7, 3, 11 - along))
    return 2 * jnp.where(along < 3, along, step) + side


def src_of(rank):
    step, side = rank // 2, rank % 2
    along = jnp.where(step == 3, 7, jnp.where(step == 4, 3, 11 - step))
    return side * DEPTH + jnp.where(step < 3, step, along)


def repeat(first, last, body):
    def step(k, carry):
        body(k)
        return carry

    lax.fori_loop(first, last, step, 0)


def everything(mask, target, shifts, weights, table, resist, mask_grad, source_grad, *scratch):
    (
        mask_v, target_v, shifts_v, weights_v, table_v,
        left_v, right_v, spec_v, pupil_v, scale_v, term_v, field_v, power_v,
        printed_v, grad_v, part_v, sums_v, total_v, local_sem, send_sem, recv_sem, ready_sem, hub_sem,
    ) = scratch
    tile, src = lax.axis_index("tile"), lax.axis_index("src")
    n_tile = lax.axis_size("tile")
    left, right = tile - 1, tile + 1
    has_left, has_right = tile > 0, tile < n_tile - 1
    side, along = src // DEPTH, src % DEPTH
    rank = rank_of(side, along)
    place_in_quad = (along + 1) % QUAD
    quad = (along + 1) % DEPTH // QUAD
    partners = [
        (side + across) % 2 * DEPTH + (along + step) % DEPTH for across, step in ((0, QUAD), (1, 0), (1, QUAD))
    ]

    def member(k):
        return side * DEPTH + (quad * QUAD + k + DEPTH - 1) % DEPTH

    layer = tile // GROUP
    place = tile % GROUP
    is_hub, is_teller = tile < HUB, layer == HUB // GROUP - 1

    def get(name, start=None, stop=None):
        at, size = PLACES[name]
        if start is None:
            return table_v[at : at + size, :]
        return table_v[at : at + size, start:stop]

    def signal(sem, device):
        pl.semaphore_signal(sem, inc=1, device_id=device, device_id_type=MESH)

    def send(source, target_ref, number, device):
        copy = pltpu.make_async_remote_copy(
            src_ref=source,
            dst_ref=target_ref,
            send_sem=send_sem.at[number],
            recv_sem=recv_sem.at[number],
            device_id=device,
            device_id_type=MESH,
        )
        copy.start()

    def wait(ref, sem):
        pltpu.make_async_copy(ref, ref, sem).wait()

    barrier = pltpu.get_barrier_semaphore()

    @pl.when(has_left)
    def _():
        signal(barrier, {"tile": left})

    @pl.when(has_right)
    def _():
        signal(barrier, {"tile": right})

    repeat(rank + 1, N_SRC, lambda k: signal(barrier, {"src": src_of(k)}))
    local = [
        pltpu.make_async_copy(mask, mask_v, local_sem.at[0]),
        pltpu.make_async_copy(shifts, shifts_v, local_sem.at[1]),
        pltpu.make_async_copy(weights, weights_v, local_sem.at[2]),
    ]
    for k in range(3):
        rows = pl.ds(CUTS[k], CUTS[k + 1] - CUTS[k])
        local.append(pltpu.make_async_copy(table.at[rows], table_v.at[rows], local_sem.at[3 + k]))
    local.append(pltpu.make_async_copy(target, target_v, local_sem.at[6]))
    local[0].start()
    local[3].start()
    repeat(jnp.where(is_hub, tile + 1, n_tile), n_tile, lambda k: signal(barrier, {"tile": k}))

    ends = has_left.astype(jnp.int32) + has_right.astype(jnp.int32)
    pl.semaphore_wait(barrier, rank + ends + jnp.minimum(tile, HUB))

    @pl.when(has_right)
    def _():
        send(mask.at[:, pl.ds(128, 128)], left_v, 0, {"tile": right})

    @pl.when(has_left)
    def _():
        send(mask.at[:, pl.ds(0, 128)], right_v, 1, {"tile": left})

    for k in (1, 2, 4, 5, 6):
        local[k].start()
    repeat(0, rank, lambda k: signal(ready_sem.at[rank], {"src": src_of(k)}))
    term_v[:, POINTS_R // 2 :, :] = jnp.zeros((QUAD, (ROWS_C - POINTS_R) // 2, 128), jnp.float32)

    @pl.when(jnp.logical_not(has_left))
    def _():
        left_v[...] = jnp.zeros_like(left_v)

    @pl.when(jnp.logical_not(has_right))
    def _():
        right_v[...] = jnp.zeros_like(right_v)

    local[1].wait()
    local[2].wait()
    shape = (PER_DEV, PER_DEV)
    own_place = lanes(shape) == lax.broadcasted_iota(jnp.int32, shape, 0)

    def upright(row):
        return jnp.sum(jnp.where(own_place, row, 0.0), axis=1, keepdims=True)

    own_shifts = shifts_v[...].astype(jnp.float32)
    riders = [upright(own_shifts[0:1, :]), upright(own_shifts[1:2, :]), upright(weights_v[...])]
    local[0].wait()
    local[3].wait()
    at = PLACES["enter"][0]
    own = enter(mask_v[...], table_v[at : at + TILE, :])

    @pl.when(has_left)
    def _():
        wait(left_v, recv_sem.at[0])

    @pl.when(has_right)
    def _():
        wait(right_v, recv_sem.at[1])

    margins = jnp.concatenate([left_v[...], right_v[...]], axis=1)
    own = own + enter(margins, table_v[at + TILE : at + 2 * TILE, :])
    own = pack(own[:8], own[8:])
    for lane, rider in zip(RIDERS, riders):
        own = jnp.where(lanes(own.shape) == lane, rider, own)
    spec_v[src] = own

    def send_piece(k):
        send(spec_v.at[src], spec_v.at[src], 2, {"src": src_of(k)})

    def answer_piece(k):
        pl.semaphore_wait(ready_sem.at[k], 1)
        send_piece(k)

    repeat(0, (rank + 1) // 2, lambda k: send_piece(2 * k))
    repeat(0, rank // 2, lambda k: send_piece(2 * k + 1))
    repeat(rank + 1, N_SRC, answer_piece)
    repeat(0, jnp.where(is_hub, tile, 0), lambda k: signal(hub_sem.at[0], {"tile": k}))

    @pl.when(jnp.logical_not(is_hub))
    def _():
        signal(hub_sem.at[1], {"tile": HUB - GROUP + place})

    local[4].wait()
    wait(spec_v.at[pl.ds(0, N_SRC - 1)], recv_sem.at[2])

    gathered = spec_v[...].reshape(128, 128)
    spec = spectrum(gathered, get("spec"), get("lows_a", 0, 128), pltpu.roll)
    bands = split_bands(spec, pltpu.roll)
    at = PLACES["lows_b"][0]
    cols = [(get("cols_" + name), get("cols_low_" + name)) for name in ("even", "odd")]
    rows = [
        (get("rows_even"), table_v[at : at + ROWS_C, 128:256]),
        (get("rows_odd"), table_v[at + ROWS_C : at + 2 * ROWS_C, 128:256]),
    ]

    def add_fields(part, images):
        owner = ([src] + partners)[part]
        rows_by, cols_by, scales = [spec_v[owner, :, lane : lane + 1] for lane in RIDERS]
        pupils = [pupil_of(rows_by[s : s + 1], cols_by[s : s + 1]) for s in range(PER_DEV)]
        for pair in range(PER_DEV // 2):
            first, second = [jnp.broadcast_to(scales[s : s + 1], (8, 128)) for s in (2 * pair, 2 * pair + 1)]
            at = slice(128 * (pair % 2), 128 * (pair % 2) + 128)
            for parity, scale in enumerate(swap(first, second)):
                scale_v[part, pair // 2, parity, :, at] = scale
        fields = coarse_fields(bands, [pupil.astype(jnp.bfloat16) for pupil in pupils], cols, rows)
        for s, pupil in enumerate(pupils):
            pupil_v[part, s] = pupil
        images = list(images)
        for group in range(2):
            for parity in range(2):
                field_v[part, group, parity] = fields[group][parity]
                power = power_of(fields[group][parity])
                if part == 0:
                    power_v[group, parity] = power
                power = power * scale_v[part, group, parity, 0:1, :]
                images[parity] = images[parity] + power[:, :128] + power[:, 128:]
        return tuple(images)

    none = jnp.zeros((ROWS_C // 2, 128), jnp.float32)
    image = (none, none)
    for part in range(QUAD):
        image = add_fields(part, image)
    term_v[place_in_quad] = join_image(*image, pltpu.roll)
    image_rows = pl.ds(0, POINTS_R // 2)
    mine = term_v.at[place_in_quad, image_rows]

    def send_image(k):
        send(mine, mine, 3, {"src": member(k)})

    for k in (1, 0, 2, 3):
        pl.when(k != place_in_quad)(functools.partial(send_image, k))
    local[5].wait()
    local[6].wait()
    wait(term_v.at[pl.ds(0, QUAD - 1), image_rows], recv_sem.at[3])

    image = pixels_of(
        term_v[0] + term_v[1] + term_v[2] + term_v[3],
        get("fine_rows"),
        get("fine_cols"),
        get("fine_cols_low"),
    )
    printed = jax.nn.sigmoid(STEEP * (image * (1.0 / SOURCES) - THRESH))
    goal = target_v[...].astype(jnp.float32)
    slope = (LOSS_SCALE * 2.0 * STEEP) * (printed - goal) * printed * (1.0 - printed)
    coarse = coarse_of(slope, get("coarse_rows"), get("coarse_rows_low"), get("coarse_cols"))

    slopes = twice(coarse, pltpu.roll)
    sums = []
    for pair in range(PER_DEV // 2):
        at = slice(128 * (pair % 2), 128 * (pair % 2) + 128)
        terms = [
            jnp.sum(slopes[parity] * power_v[pair // 2, parity, :, at], axis=0, keepdims=True) for parity in range(2)
        ]
        sums.extend(swap(*terms))
    sums = jnp.sum(jnp.concatenate(sums, axis=0), axis=1, keepdims=True)
    spot = (PER_DEV, 128)
    sums = jnp.where(lanes(spot) == lax.broadcasted_iota(jnp.int32, spot, 0), sums, 0.0)
    sums_v[tile] = jnp.sum(sums, axis=0, keepdims=True)

    def send_sums(k):
        pltpu.make_async_remote_copy(
            src_ref=sums_v.at[tile],
            dst_ref=sums_v.at[tile],
            send_sem=send_sem.at[5],
            recv_sem=recv_sem.at[5],
            device_id={"tile": k},
            device_id_type=MESH,
        ).start()

    for k in range(HUB):
        first = k + 1 - 2 * (k % 2)
        pl.when(first < tile)(functools.partial(send_sums, first))

    printed_v[...] = printed
    resist[...] = printed_v[pl.ds(pl.multiple_of(src * ROWS, ROWS), ROWS), :]

    wide = [jnp.concatenate([slope, slope], axis=1) * (2.0 / SOURCES) for slope in slopes]
    rows_back = [get("rows_back_even"), get("rows_back_odd")]
    cols_back = [get("cols_back_even"), get("cols_back_odd")]

    def add_part(part, total):
        adjoints = []
        for group in range(2):
            adjoints.append([])
            for parity in range(2):
                scaled = wide[parity] * scale_v[part, group, parity, 0:1, :]
                adjoints[group].append(field_v[part, group, parity] * jnp.concatenate([scaled, scaled], axis=0))
        return band_grad(total, adjoints, [pupil_v[part, s] for s in range(PER_DEV)], rows_back, cols_back)

    grad = lax.fori_loop(0, QUAD, add_part, jnp.zeros((BAND, 128), jnp.float32))
    first = PLACES["leave"][0] + 8 * QUAD * (2 * side + quad)
    low_first = PLACES["lows_b"][0] + 8 * QUAD * (2 * side + quad)

    def halves_of(start, stop, begin):
        begin = pl.multiple_of(begin, 32)
        then = pl.multiple_of(begin + 128, 32)
        return jnp.concatenate(
            [table_v[pl.ds(begin, 8 * QUAD), start:stop], table_v[pl.ds(then, 8 * QUAD), start:stop]], axis=0
        )

    rows = row_grads(grad, halves_of(0, 256, first), halves_of(0, 128, low_first), pltpu.roll)
    grad_v[...] = rows.reshape(QUAD, 8, 128)
    for k in range(1, QUAD):
        other = (place_in_quad + k) % QUAD
        send(grad_v.at[other], part_v.at[k - 1], 4, {"src": member(other)})

    @pl.when(tile < HUB - 1)
    def _():
        pl.semaphore_wait(hub_sem.at[0], HUB - 1 - tile)
        repeat(tile + 1, HUB, send_sums)

    wait(part_v, recv_sem.at[4])
    total = grad_v[place_in_quad] + part_v[0] + part_v[1] + part_v[2]
    mask_grad[...] = last_step(total, get("last"), get("last_low"))

    @pl.when(is_hub)
    def _():
        wait(sums_v.at[pl.ds(0, n_tile - 1)], recv_sem.at[5])
        total_v[...] = jnp.sum(sums_v[...], axis=0) * (1.0 / (SOURCES * n_tile * TILE * TILE))

    def tell(k):
        send(total_v, total_v, 6, {"tile": k * GROUP + place})

    @pl.when(is_teller)
    def _():
        pl.semaphore_wait(hub_sem.at[1], (n_tile - HUB) // GROUP)
        repeat(HUB // GROUP, n_tile // GROUP, tell)

    @pl.when(jnp.logical_not(is_hub))
    def _():
        wait(total_v, recv_sem.at[6])

    source_grad[...] = total_v[...]

    @pl.when(is_teller)
    def _():
        wait(sums_v.at[pl.ds(0, (n_tile - HUB) // GROUP)], send_sem.at[6])

    @pl.when(is_hub)
    def _():
        wait(sums_v.at[pl.ds(0, HUB - 1)], send_sem.at[5])

    @pl.when(jnp.logical_not(is_hub))
    def _():
        wait(sums_v.at[pl.ds(0, HUB)], send_sem.at[5])


    @pl.when(has_right)
    def _():
        wait(left_v, send_sem.at[0])

    @pl.when(has_left)
    def _():
        wait(right_v, send_sem.at[1])

    wait(spec_v.at[pl.ds(0, N_SRC - 1)], send_sem.at[2])
    wait(term_v.at[pl.ds(0, QUAD - 1), image_rows], send_sem.at[3])
    wait(part_v, send_sem.at[4])


def hand_over(resist, mask_grad, source_grad, resist_out, mask_grad_out, source_grad_out, row, sem):
    row[...] = source_grad[0, :PER_DEV]
    copies = [
        pltpu.make_async_copy(resist, resist_out, sem.at[0]),
        pltpu.make_async_copy(mask_grad, mask_grad_out, sem.at[1]),
        pltpu.make_async_copy(row, source_grad_out, sem.at[2]),
    ]
    for copy in copies:
        copy.start()
    for copy in copies:
        copy.wait()


def local(mask, target, shifts, weights):
    f32 = jnp.float32
    anywhere = pl.BlockSpec(memory_space=pl.ANY)
    inside = pl.BlockSpec(memory_space=pltpu.VMEM)
    results = pl.pallas_call(
        everything,
        out_shape=(
            pltpu.VMEM((ROWS, TILE), f32),
            pltpu.VMEM((ROWS, TILE), f32),
            pltpu.VMEM((1, 128), f32),
        ),
        in_specs=[anywhere] * 5,
        out_specs=(inside, inside, inside),
        scratch_shapes=[
            pltpu.VMEM((ROWS, TILE), f32),
            pltpu.VMEM((TILE, TILE), jnp.int32),
            pltpu.VMEM((2, PER_DEV), jnp.int32),
            pltpu.VMEM((1, PER_DEV), f32),
            pltpu.VMEM(TABLE.shape, jnp.bfloat16),
            pltpu.VMEM((ROWS, 128), f32),
            pltpu.VMEM((ROWS, 128), f32),
            pltpu.VMEM((N_SRC, 8, 128), f32),
            pltpu.VMEM((QUAD, PER_DEV, BAND, 128), f32),
            pltpu.VMEM((QUAD, 2, 2, 8, 256), f32),
            pltpu.VMEM((QUAD, ROWS_C // 2, 128), f32),
            pltpu.VMEM((QUAD, 2, 2, ROWS_C, 256), f32),
            pltpu.VMEM((2, 2, ROWS_C // 2, 256), f32),
            pltpu.VMEM((TILE, TILE), f32),
            pltpu.VMEM((QUAD, 8, 128), f32),
            pltpu.VMEM((QUAD - 1, 8, 128), f32),
            pltpu.VMEM((N_TILE, 1, 128), f32),
            pltpu.VMEM((1, 128), f32),
            pltpu.SemaphoreType.DMA((7,)),
            pltpu.SemaphoreType.DMA((7,)),
            pltpu.SemaphoreType.DMA((7,)),
            pltpu.SemaphoreType.REGULAR((N_SRC,)),
            pltpu.SemaphoreType.REGULAR((2,)),
        ],
        compiler_params=pltpu.CompilerParams(
            collective_id=0, has_side_effects=True, vmem_limit_bytes=60 * 1024 * 1024
        ),
    )(mask, target, shifts.T, weights.reshape(1, PER_DEV), jnp.asarray(TABLE))
    return pl.pallas_call(
        hand_over,
        out_shape=(
            jax.ShapeDtypeStruct((ROWS, TILE), f32),
            jax.ShapeDtypeStruct((ROWS, TILE), f32),
            jax.ShapeDtypeStruct((PER_DEV,), f32),
        ),
        in_specs=[inside] * 3,
        out_specs=(anywhere,) * 3,
        scratch_shapes=[pltpu.VMEM((PER_DEV,), f32), pltpu.SemaphoreType.DMA((3,))],
    )(*[pltpu.with_memory_space_constraint(result, pltpu.VMEM) for result in results])


def solution(mesh):
    placed = (P("src", "tile"), P(None, "tile"), P("src", None), P("src"))
    return jax.shard_map(
        local,
        mesh=mesh,
        in_specs=placed,
        out_specs=(P("src", "tile"), P("src", "tile"), P("src")),
        check_vma=False,
    )
```

```python
import functools

import jax
import jax.numpy as jnp
import ml_dtypes
import numpy as np
from jax import lax
from jax.experimental import pallas as pl
from jax.experimental.pallas import tpu as pltpu
from jax.sharding import PartitionSpec as P

TILE = 256
MARGIN = 32
BAND = 64
RAD = 16
EXT = 320
STEEP = 8.0
THRESH = 0.25
LOSS_SCALE = 2.0

N_SRC = 16
N_TILE = 32
PER_DEV = 8
SOURCES = 128
ROWS = 16
HALF = 32
POINTS_R = 66
ROWS_C = 80
COLS_C = 128
QUAD = 4
GROUP = 4
DEPTH = 8
HUB = 3 * GROUP
RIDERS = (31, 63, 95)

MESH = pl.DeviceIdType.MESH
BF16 = ml_dtypes.bfloat16


def halves(table):
    high = table.astype(BF16)
    low = (table - high.astype(np.float64)).astype(BF16)
    return high, low


def column_slots():
    plus = np.arange(HALF)
    return np.concatenate([plus, -plus]), np.concatenate([np.ones(HALF), [0.0], np.ones(HALF - 1)])


def waves(freq, place, period):
    phase = 2.0 * np.pi * ((freq[:, None] * place[None, :]) % period) / period
    return np.cos(phase), np.sin(phase)


def interpolation(points):
    order = np.arange(-2 * RAD, 2 * RAD + 1)
    place = np.arange(TILE) + MARGIN
    offset = place[:, None] / EXT - np.arange(points)[None, :] / points
    return np.cos(2.0 * np.pi * order[None, None, :] * offset[:, :, None]).sum(axis=2) / points


def padded(rows):
    return np.concatenate([rows, np.zeros((ROWS_C // 2 - rows.shape[0], rows.shape[1]))], axis=0)


def build_tables():
    slots, used = column_slots()
    row_freq = np.arange(BAND) - BAND // 2
    pixels = np.arange(TILE) + MARGIN
    parts = {}

    real, imag = waves(np.arange(HALF), np.arange(EXT), EXT)
    fwd = np.concatenate([real, -imag], axis=0).T
    wide = np.zeros((2 * TILE, 2 * HALF))
    wide[:TILE] = fwd[MARGIN : MARGIN + TILE]
    wide[TILE + 96 : TILE + 128] = fwd[:MARGIN]
    wide[TILE + 128 : TILE + 160] = fwd[MARGIN + TILE :]
    high, low = halves(np.concatenate([wide, wide], axis=1))
    parts["enter"] = np.concatenate([high, low], axis=1)

    rows = np.arange(TILE).reshape(N_SRC, 2, 8)
    first, second = rows[:, 0].reshape(-1), rows[:, 1].reshape(-1)
    real, imag = waves(row_freq, pixels, EXT)
    both = np.concatenate([real, -imag], axis=0)
    high, low = halves(np.concatenate([both[:, first], both[:, second]], axis=0))
    parts["spec"] = np.concatenate([high, high], axis=1)
    spec_low = low

    inter_rows, inter_cols = 2.0 * interpolation(POINTS_R), interpolation(COLS_C)
    even, odd = np.arange(0, COLS_C, 2), np.arange(1, COLS_C, 2)
    for name, order in (("even", np.concatenate([even, odd])), ("odd", np.concatenate([odd, even]))):
        real, imag = waves(slots, order, COLS_C)
        real, imag = real * used[:, None], imag * used[:, None]
        cols = np.concatenate(
            [np.concatenate([real, imag], axis=1), np.concatenate([-imag, real], axis=1)], axis=0
        )
        high, low = halves(cols)
        again = high.copy()
        again[[HALF, 3 * HALF]] = high[[0, 2 * HALF]]
        parts["cols_" + name] = np.concatenate([high, again], axis=0)
        parts["cols_low_" + name] = low
        high, low = halves(np.concatenate([cols[:, :COLS_C].T, cols[:, COLS_C:].T], axis=0))
        parts["cols_back_" + name] = np.concatenate([high, low], axis=1)

    lows = []
    for name, start in (("even", 0), ("odd", 1)):
        real, imag = waves(row_freq, np.arange(start, POINTS_R, 2), POINTS_R)
        real, imag = padded(real.T), padded(imag.T)
        high, low = halves(
            np.concatenate(
                [np.concatenate([real, -imag], axis=1), np.concatenate([imag, real], axis=1)], axis=0
            )
        )
        parts["rows_" + name] = np.concatenate([high, high], axis=1)
        lows.append(low)
        pad = np.zeros((2 * BAND, TILE - 3 * ROWS_C), BF16)
        parts["rows_back_" + name] = np.concatenate([high.T, high.T, low.T, pad], axis=1)
    rows_low = np.concatenate(lows, axis=0)

    inter_rows = np.concatenate([padded(inter_rows[:, 0::2].T), padded(inter_rows[:, 1::2].T)], axis=0).T
    inter_cols = inter_cols[:, np.concatenate([even, odd])]
    high, low = halves(inter_rows)
    pad = np.zeros((TILE, TILE - 3 * ROWS_C), BF16)
    parts["fine_rows"] = np.concatenate([high, high, low, pad], axis=1)
    high, low = halves(inter_cols.T)
    parts["fine_cols"] = np.concatenate([high, high], axis=0)
    parts["fine_cols_low"] = low
    parts["coarse_cols"] = np.concatenate([high.T, low.T], axis=1)
    high, low = halves(inter_rows.T)
    parts["coarse_rows"] = high
    parts["coarse_rows_low"] = low

    owners = [
        side * DEPTH + (quad * QUAD + k - 1) % DEPTH for side in range(2) for quad in range(2) for k in range(QUAD)
    ]
    first, second = rows[owners, 0].reshape(-1), rows[owners, 1].reshape(-1)
    high, low = halves(np.concatenate([both[:, first], both[:, second]], axis=1).T)
    parts["leave"] = np.concatenate([high, high], axis=1)
    leave_low = low
    last = fwd[MARGIN : MARGIN + TILE].T
    high, low = halves(np.concatenate([last, last], axis=0))
    parts["last"] = high
    parts["last_low"] = low

    parts["lows_a"] = np.concatenate([spec_low, np.zeros((TILE, 128), BF16)], axis=1)
    rows_low = np.concatenate([rows_low, np.zeros((TILE - 2 * ROWS_C, 128), BF16)], axis=0)
    parts["lows_b"] = np.concatenate([leave_low, rows_low], axis=1)

    order = [
        "enter",
        "spec", "lows_a", "cols_even", "cols_low_even", "cols_odd", "cols_low_odd", "rows_even", "rows_odd", "lows_b",
        "fine_rows", "fine_cols", "fine_cols_low", "coarse_cols", "coarse_rows", "coarse_rows_low",
        "rows_back_even", "rows_back_odd", "cols_back_even", "cols_back_odd", "leave", "last", "last_low",
    ]
    places, start = {}, 0
    for name in order:
        places[name] = (start, parts[name].shape[0])
        start += parts[name].shape[0]
    return np.concatenate([parts[name] for name in order], axis=0), places


TABLE, PLACES = build_tables()
CUTS = (0, PLACES["spec"][0], PLACES["fine_rows"][0], TABLE.shape[0])


def dot(left, right):
    return jnp.dot(left, right, preferred_element_type=jnp.float32)


def cut(value):
    high = value.astype(jnp.bfloat16)
    low = (value - high.astype(jnp.float32)).astype(jnp.bfloat16)
    return high, low


def lanes(shape):
    return lax.broadcasted_iota(jnp.int32, shape, 1)


def enter(value, table):
    rows = value.shape[0]
    both = dot(jnp.concatenate(cut(value), axis=0), table)
    return both[:rows, :128] + both[:rows, 128:] + both[rows:, :128]


def pack(first, second):
    return jnp.where(lanes(first.shape) < 64, first, second)


def spectrum(gathered, table, low_table, roll):
    high, low = cut(gathered)
    out = dot(table, jnp.concatenate([high, low], axis=0)) + dot(low_table, high)
    both = pack(out[:128], out[128:])
    both = both + roll(both, 64, 1)
    turned = roll(both, 32, 1)
    quarter = lanes((BAND, 128)) >> 5
    outer = (quarter == 0) | (quarter == 3)
    even = jnp.where(outer, both[:BAND], turned[:BAND])
    odd = jnp.where(outer, turned[BAND:], both[BAND:])
    return (jnp.where(quarter == 3, -even, even) + jnp.where(quarter == 0, -odd, odd)) * (1.0 / (EXT * EXT))


def pupil_of(row_shift, col_shift):
    row = (lax.broadcasted_iota(jnp.int32, (BAND, 128), 0) - BAND // 2).astype(jnp.float32) + row_shift
    slot = lanes((1, 128)) & 63
    col = jnp.where(slot < HALF, slot, HALF - slot).astype(jnp.float32) + col_shift
    room = RAD * RAD - col * col
    return jnp.where(row * row <= room, 1.0, 0.0)


def swap(first, second):
    return pack(first, second), pack(second, first)


def split_bands(spec, roll):
    spare = (lanes(spec.shape) & 63) == HALF
    high, low = cut(jnp.where(spare, 0.0, spec))
    left = spec - high.astype(jnp.float32) - low.astype(jnp.float32)
    low = jnp.where(spare, roll(left, HALF, 1), low.astype(jnp.float32)).astype(jnp.bfloat16)
    return high, low


def coarse_fields(bands, pupils, cols, rows):
    high, low = bands
    mids = []
    for which in range(2):
        band_high, band_low = [
            jnp.concatenate([part * pupil for pupil in pupils[which::2]], axis=0) for part in (high, low)
        ]
        table, low_table = cols[which]
        mids.append(
            dot(jnp.concatenate([band_high, band_low], axis=1), table) + dot(band_high, low_table)
        )
    fields = []
    for group in range(2):
        stacks = ([], [])
        for pair in (2 * group, 2 * group + 1):
            at = slice(BAND * pair, BAND * pair + BAND)
            real = swap(mids[0][at, :128], mids[1][at, :128])
            imag = swap(mids[0][at, 128:], mids[1][at, 128:])
            for parity in range(2):
                stacks[parity].append(jnp.concatenate([real[parity], imag[parity]], axis=0))
        both = []
        for parity in range(2):
            upper, lower = cut(jnp.concatenate(stacks[parity], axis=1))
            table, low_table = rows[parity]
            both.append(dot(table, jnp.concatenate([upper, lower], axis=0)) + dot(low_table, upper))
        fields.append(both)
    return fields


def power_of(field):
    half = ROWS_C // 2
    return field[:half] * field[:half] + field[half:] * field[half:]


def join_image(even, odd, roll):
    return pack(even + roll(even, 64, 1), odd + roll(odd, 64, 1))


def pixels_of(coarse, fine_rows, fine_cols, fine_cols_low):
    first = lanes(coarse.shape) < 64
    coarse = jnp.concatenate([jnp.where(first, coarse, 0.0), jnp.where(first, 0.0, coarse)], axis=0)
    high, low = cut(coarse)
    mid = dot(jnp.concatenate([high, low], axis=1), fine_cols) + dot(high, fine_cols_low)
    return dot(fine_rows, three(mid))


def three(value):
    high, low = cut(value)
    pad = jnp.zeros((TILE - 3 * value.shape[0], value.shape[1]), jnp.bfloat16)
    return jnp.concatenate([high, low, high, pad], axis=0)


def coarse_of(slope, coarse_rows, coarse_rows_low, coarse_cols):
    high, low = cut(slope)
    mid = dot(coarse_rows, high) + dot(coarse_rows, low) + dot(coarse_rows_low, high)
    high, low = cut(mid)
    both = dot(high, coarse_cols)
    return both[:, :128] + both[:, 128:] + dot(low, coarse_cols[:, :128])


def twice(coarse, roll):
    half = ROWS_C // 2
    even, odd = coarse[:half], coarse[half:]
    return pack(even, roll(even, 64, 1)), pack(roll(odd, 64, 1), odd)


def band_grad(total, adjoints, pupils, rows_back, cols_back):
    sides = ([], [])
    for group in range(2):
        even, odd = [dot(rows_back[parity], three(adjoints[group][parity])) for parity in range(2)]
        for pair in range(2):
            at = slice(128 * pair, 128 * pair + 128)
            real = swap(even[:BAND, at], odd[:BAND, at])
            imag = swap(even[BAND:, at], odd[BAND:, at])
            for which in range(2):
                sides[which].append(jnp.concatenate([real[which], imag[which]], axis=1))
    for which in range(2):
        high, low = cut(jnp.concatenate(sides[which], axis=0))
        both = dot(high, cols_back[which])
        term = both[:, :128] + both[:, 128:] + dot(low, cols_back[which][:, :128])
        for k in range(PER_DEV // 2):
            total = total + term[BAND * k : BAND * k + BAND] * pupils[2 * k + which]
    return total


def fold(grad, roll):
    r32, r64, r96 = roll(grad, 32, 1), roll(grad, 64, 1), roll(grad, 96, 1)
    quarter = lanes(grad.shape) >> 5
    upper = jnp.where(
        quarter == 0, grad + r96, jnp.where(quarter == 1, r96 - r64, jnp.where(quarter == 2, r64 + r32, r32 - grad))
    )
    lower = jnp.where(
        quarter == 0, r64 + r32, jnp.where(quarter == 1, grad - r32, jnp.where(quarter == 2, grad + r96, r64 - r96))
    )
    return jnp.concatenate([upper, lower], axis=0)


def row_grads(grad, leave, leave_low, roll):
    high, low = cut(fold(grad, roll))
    out = dot(leave, jnp.concatenate([high, low], axis=0)) + dot(leave_low, high)
    half = out.shape[0] // 2
    return pack(out[:half], out[half:])


def last_step(total, last, last_low):
    first = lanes(total.shape) < 64
    value = jnp.concatenate([jnp.where(first, total, 0.0), jnp.where(first, 0.0, total)], axis=0)
    high, low = cut(value)
    return (dot(high, last) + dot(low, last) + dot(high, last_low)) * (1.0 / (EXT * EXT))


def rank_of(side, along):
    step = jnp.where(along == 3, 4, jnp.where(along == 7, 3, 11 - along))
    return 2 * jnp.where(along < 3, along, step) + side


def src_of(rank):
    step, side = rank // 2, rank % 2
    along = jnp.where(step == 3, 7, jnp.where(step == 4, 3, 11 - step))
    return side * DEPTH + jnp.where(step < 3, step, along)


def repeat(first, last, body):
    def step(k, carry):
        body(k)
        return carry

    lax.fori_loop(first, last, step, 0)


def everything(mask, target, shifts, weights, table, resist, mask_grad, source_grad, *scratch):
    (
        mask_v, target_v, shifts_v, weights_v, table_v,
        left_v, right_v, spec_v, pupil_v, scale_v, term_v, field_v, power_v,
        printed_v, grad_v, part_v, sums_v, total_v, local_sem, send_sem, recv_sem, ready_sem, hub_sem,
    ) = scratch
    tile, src = lax.axis_index("tile"), lax.axis_index("src")
    n_tile = lax.axis_size("tile")
    left, right = tile - 1, tile + 1
    has_left, has_right = tile > 0, tile < n_tile - 1
    side, along = src // DEPTH, src % DEPTH
    rank = rank_of(side, along)
    place_in_quad = (along + 1) % QUAD
    quad = (along + 1) % DEPTH // QUAD
    partners = [
        (side + across) % 2 * DEPTH + (along + step) % DEPTH for across, step in ((0, QUAD), (1, 0), (1, QUAD))
    ]

    def member(k, group=quad):
        return side * DEPTH + (group * QUAD + k + DEPTH - 1) % DEPTH

    layer = tile // GROUP
    place = tile % GROUP
    is_hub, is_teller = tile < HUB, layer == HUB // GROUP - 1

    def get(name, start=None, stop=None):
        at, size = PLACES[name]
        if start is None:
            return table_v[at : at + size, :]
        return table_v[at : at + size, start:stop]

    def signal(sem, device):
        pl.semaphore_signal(sem, inc=1, device_id=device, device_id_type=MESH)

    def send(source, target_ref, number, device):
        copy = pltpu.make_async_remote_copy(
            src_ref=source,
            dst_ref=target_ref,
            send_sem=send_sem.at[number],
            recv_sem=recv_sem.at[number],
            device_id=device,
            device_id_type=MESH,
        )
        copy.start()

    def wait(ref, sem):
        pltpu.make_async_copy(ref, ref, sem).wait()

    barrier = pltpu.get_barrier_semaphore()

    @pl.when(has_left)
    def _():
        signal(barrier, {"tile": left})

    @pl.when(has_right)
    def _():
        signal(barrier, {"tile": right})

    repeat(rank + 1, N_SRC, lambda k: signal(barrier, {"src": src_of(k)}))
    local = [
        pltpu.make_async_copy(mask, mask_v, local_sem.at[0]),
        pltpu.make_async_copy(shifts, shifts_v, local_sem.at[1]),
        pltpu.make_async_copy(weights, weights_v, local_sem.at[2]),
    ]
    for k in range(3):
        rows = pl.ds(CUTS[k], CUTS[k + 1] - CUTS[k])
        local.append(pltpu.make_async_copy(table.at[rows], table_v.at[rows], local_sem.at[3 + k]))
    local.append(pltpu.make_async_copy(target, target_v, local_sem.at[6]))
    local[0].start()
    local[3].start()
    repeat(jnp.where(is_hub, tile + 1, n_tile), n_tile, lambda k: signal(barrier, {"tile": k}))

    ends = has_left.astype(jnp.int32) + has_right.astype(jnp.int32)
    pl.semaphore_wait(barrier, rank + ends + jnp.minimum(tile, HUB))

    @pl.when(has_right)
    def _():
        send(mask.at[:, pl.ds(128, 128)], left_v, 0, {"tile": right})

    @pl.when(has_left)
    def _():
        send(mask.at[:, pl.ds(0, 128)], right_v, 1, {"tile": left})

    for k in (1, 2, 4, 5, 6):
        local[k].start()
    repeat(0, rank, lambda k: signal(ready_sem.at[rank], {"src": src_of(k)}))
    term_v[:, POINTS_R // 2 :, :] = jnp.zeros((QUAD, (ROWS_C - POINTS_R) // 2, 128), jnp.float32)

    @pl.when(jnp.logical_not(has_left))
    def _():
        left_v[...] = jnp.zeros_like(left_v)

    @pl.when(jnp.logical_not(has_right))
    def _():
        right_v[...] = jnp.zeros_like(right_v)

    local[1].wait()
    local[2].wait()
    shape = (PER_DEV, PER_DEV)
    own_place = lanes(shape) == lax.broadcasted_iota(jnp.int32, shape, 0)

    def upright(row):
        return jnp.sum(jnp.where(own_place, row, 0.0), axis=1, keepdims=True)

    own_shifts = shifts_v[...].astype(jnp.float32)
    riders = [upright(own_shifts[0:1, :]), upright(own_shifts[1:2, :]), upright(weights_v[...])]
    local[0].wait()
    local[3].wait()
    at = PLACES["enter"][0]
    own = enter(mask_v[...], table_v[at : at + TILE, :])

    @pl.when(has_left)
    def _():
        wait(left_v, recv_sem.at[0])

    @pl.when(has_right)
    def _():
        wait(right_v, recv_sem.at[1])

    margins = jnp.concatenate([left_v[...], right_v[...]], axis=1)
    own = own + enter(margins, table_v[at + TILE : at + 2 * TILE, :])
    own = pack(own[:8], own[8:])
    for lane, rider in zip(RIDERS, riders):
        own = jnp.where(lanes(own.shape) == lane, rider, own)
    spec_v[src] = own

    def send_piece(k):
        send(spec_v.at[src], spec_v.at[src], 2, {"src": src_of(k)})

    def answer_piece(k):
        pl.semaphore_wait(ready_sem.at[k], 1)
        send_piece(k)

    def send_even(k):
        send_piece(2 * jnp.where((rank >= N_SRC // 2) & (k < QUAD), (k + 1) % QUAD, k))

    repeat(0, (rank + 1) // 2, send_even)
    repeat(0, rank // 2, lambda k: send_piece(2 * k + 1))
    repeat(rank + 1, N_SRC, answer_piece)
    repeat(0, jnp.where(is_hub, tile, 0), lambda k: signal(hub_sem.at[0], {"tile": k}))

    @pl.when(jnp.logical_not(is_hub))
    def _():
        signal(hub_sem.at[1], {"tile": HUB - GROUP + place})

    local[4].wait()
    wait(spec_v.at[pl.ds(0, N_SRC - 1)], recv_sem.at[2])

    gathered = spec_v[...].reshape(128, 128)
    spec = spectrum(gathered, get("spec"), get("lows_a", 0, 128), pltpu.roll)
    bands = split_bands(spec, pltpu.roll)
    at = PLACES["lows_b"][0]
    cols = [(get("cols_" + name), get("cols_low_" + name)) for name in ("even", "odd")]
    rows = [
        (get("rows_even"), table_v[at : at + ROWS_C, 128:256]),
        (get("rows_odd"), table_v[at + ROWS_C : at + 2 * ROWS_C, 128:256]),
    ]

    def add_fields(part, images):
        owner = src
        for k, peer in enumerate(partners):
            owner = jnp.where(part == k + 1, peer, owner)
        rows_by, cols_by, scales = [spec_v[owner, :, lane : lane + 1] for lane in RIDERS]
        for s in range(PER_DEV):
            pupil_v[part, s] = pupil_of(rows_by[s : s + 1], cols_by[s : s + 1])
        for pair in range(PER_DEV // 2):
            first, second = [jnp.broadcast_to(scales[s : s + 1], (8, 128)) for s in (2 * pair, 2 * pair + 1)]
            at = slice(128 * (pair % 2), 128 * (pair % 2) + 128)
            for parity, scale in enumerate(swap(first, second)):
                scale_v[part, pair // 2, parity, :, at] = scale
        fields = coarse_fields(
            bands, [pupil_v[part, s].astype(jnp.bfloat16) for s in range(PER_DEV)], cols, rows
        )
        images = list(images)
        for group in range(2):
            for parity in range(2):
                field_v[part, group, parity] = fields[group][parity]
                power = power_of(fields[group][parity])
                power_v[part, group, parity] = power
                power = power * scale_v[part, group, parity, 0:1, :]
                images[parity] = images[parity] + power[:, :128] + power[:, 128:]
        return tuple(images)

    none = jnp.zeros((ROWS_C // 2, 128), jnp.float32)
    image = lax.fori_loop(0, QUAD, add_fields, (none, none), unroll=True)
    term_v[place_in_quad] = join_image(*image, pltpu.roll)
    image_rows = pl.ds(0, POINTS_R // 2)
    mine = term_v.at[place_in_quad, image_rows]

    middle = (place_in_quad == 1) | (place_in_quad == 2)
    tells_own, tells_other = jnp.logical_not(middle & (quad == 1)), middle & (quad == 0)

    def send_image(k, group):
        send(mine, mine, 3, {"src": member(k, group)})

    for k in (1, 0, 2, 3):
        pl.when(tells_own & (k != place_in_quad))(functools.partial(send_image, k, quad))
    for k in (3, 0, 1, 2):
        pl.when(tells_other & (k != place_in_quad))(functools.partial(send_image, k, 1))
    local[5].wait()
    local[6].wait()
    wait(term_v.at[pl.ds(0, QUAD - 1), image_rows], recv_sem.at[3])

    image = pixels_of(
        term_v[0] + term_v[1] + term_v[2] + term_v[3],
        get("fine_rows"),
        get("fine_cols"),
        get("fine_cols_low"),
    )
    printed = jax.nn.sigmoid(STEEP * (image * (1.0 / SOURCES) - THRESH))
    goal = target_v[...].astype(jnp.float32)
    slope = (LOSS_SCALE * 2.0 * STEEP) * (printed - goal) * printed * (1.0 - printed)
    coarse = coarse_of(slope, get("coarse_rows"), get("coarse_rows_low"), get("coarse_cols"))

    slopes = twice(coarse, pltpu.roll)
    sums = []
    for pair in range(PER_DEV // 2):
        at = slice(128 * (pair % 2), 128 * (pair % 2) + 128)
        terms = [
            jnp.sum(slopes[parity] * power_v[0, pair // 2, parity, :, at], axis=0, keepdims=True) for parity in range(2)
        ]
        sums.extend(swap(*terms))
    sums = jnp.sum(jnp.concatenate(sums, axis=0), axis=1, keepdims=True)
    spot = (PER_DEV, 128)
    sums = jnp.where(lanes(spot) == lax.broadcasted_iota(jnp.int32, spot, 0), sums, 0.0)
    sums_v[tile] = jnp.sum(sums, axis=0, keepdims=True)

    def send_sums(k):
        pltpu.make_async_remote_copy(
            src_ref=sums_v.at[tile],
            dst_ref=sums_v.at[tile],
            send_sem=send_sem.at[5],
            recv_sem=recv_sem.at[5],
            device_id={"tile": k},
            device_id_type=MESH,
        ).start()

    for k in range(HUB):
        first = k + 1 - 2 * (k % 2)
        pl.when(first < tile)(functools.partial(send_sums, first))

    printed_v[...] = printed
    resist[...] = printed_v[pl.ds(pl.multiple_of(src * ROWS, ROWS), ROWS), :]

    wide = [jnp.concatenate([slope, slope], axis=1) * (2.0 / SOURCES) for slope in slopes]
    rows_back = [get("rows_back_even"), get("rows_back_odd")]
    cols_back = [get("cols_back_even"), get("cols_back_odd")]

    def add_part(part, total):
        adjoints = []
        for group in range(2):
            adjoints.append([])
            for parity in range(2):
                scaled = wide[parity] * scale_v[part, group, parity, 0:1, :]
                adjoints[group].append(field_v[part, group, parity] * jnp.concatenate([scaled, scaled], axis=0))
        return band_grad(total, adjoints, [pupil_v[part, s] for s in range(PER_DEV)], rows_back, cols_back)

    grad = lax.fori_loop(0, QUAD, add_part, jnp.zeros((BAND, 128), jnp.float32))
    first = PLACES["leave"][0] + 8 * QUAD * (2 * side + quad)
    low_first = PLACES["lows_b"][0] + 8 * QUAD * (2 * side + quad)

    def halves_of(start, stop, begin):
        begin = pl.multiple_of(begin, 32)
        then = pl.multiple_of(begin + 128, 32)
        return jnp.concatenate(
            [table_v[pl.ds(begin, 8 * QUAD), start:stop], table_v[pl.ds(then, 8 * QUAD), start:stop]], axis=0
        )

    rows = row_grads(grad, halves_of(0, 256, first), halves_of(0, 128, low_first), pltpu.roll)
    grad_v[...] = rows.reshape(QUAD, 8, 128)
    for k in range(1, QUAD):
        other = (place_in_quad + k) % QUAD
        send(grad_v.at[other], part_v.at[k - 1], 4, {"src": member(other)})

    @pl.when(tile < HUB - 1)
    def _():
        pl.semaphore_wait(hub_sem.at[0], HUB - 1 - tile)
        repeat(tile + 1, HUB, send_sums)

    wait(part_v, recv_sem.at[4])
    total = grad_v[place_in_quad] + part_v[0] + part_v[1] + part_v[2]
    mask_grad[...] = last_step(total, get("last"), get("last_low"))

    @pl.when(is_hub)
    def _():
        wait(sums_v.at[pl.ds(0, n_tile - 1)], recv_sem.at[5])
        total_v[...] = jnp.sum(sums_v[...], axis=0) * (1.0 / (SOURCES * n_tile * TILE * TILE))

    def tell(k):
        send(total_v, total_v, 6, {"tile": k * GROUP + place})

    @pl.when(is_teller)
    def _():
        pl.semaphore_wait(hub_sem.at[1], (n_tile - HUB) // GROUP)
        repeat(HUB // GROUP, n_tile // GROUP, tell)

    @pl.when(jnp.logical_not(is_hub))
    def _():
        wait(total_v, recv_sem.at[6])

    source_grad[...] = total_v[...]

    @pl.when(is_teller)
    def _():
        wait(sums_v.at[pl.ds(0, (n_tile - HUB) // GROUP)], send_sem.at[6])

    @pl.when(is_hub)
    def _():
        wait(sums_v.at[pl.ds(0, HUB - 1)], send_sem.at[5])

    @pl.when(jnp.logical_not(is_hub))
    def _():
        wait(sums_v.at[pl.ds(0, HUB)], send_sem.at[5])


    @pl.when(has_right)
    def _():
        wait(left_v, send_sem.at[0])

    @pl.when(has_left)
    def _():
        wait(right_v, send_sem.at[1])

    wait(spec_v.at[pl.ds(0, N_SRC - 1)], send_sem.at[2])
    for told in (tells_own, tells_other):
        pl.when(told)(lambda: wait(term_v.at[pl.ds(0, QUAD - 1), image_rows], send_sem.at[3]))
    wait(part_v, send_sem.at[4])


def hand_over(resist, mask_grad, source_grad, resist_out, mask_grad_out, source_grad_out, row, sem):
    row[...] = source_grad[0, :PER_DEV]
    copies = [
        pltpu.make_async_copy(resist, resist_out, sem.at[0]),
        pltpu.make_async_copy(mask_grad, mask_grad_out, sem.at[1]),
        pltpu.make_async_copy(row, source_grad_out, sem.at[2]),
    ]
    for copy in copies:
        copy.start()
    for copy in copies:
        copy.wait()


def local(mask, target, shifts, weights):
    f32 = jnp.float32
    anywhere = pl.BlockSpec(memory_space=pl.ANY)
    inside = pl.BlockSpec(memory_space=pltpu.VMEM)
    results = pl.pallas_call(
        everything,
        out_shape=(
            pltpu.VMEM((ROWS, TILE), f32),
            pltpu.VMEM((ROWS, TILE), f32),
            pltpu.VMEM((1, 128), f32),
        ),
        in_specs=[anywhere] * 5,
        out_specs=(inside, inside, inside),
        scratch_shapes=[
            pltpu.VMEM((ROWS, TILE), f32),
            pltpu.VMEM((TILE, TILE), jnp.int32),
            pltpu.VMEM((2, PER_DEV), jnp.int32),
            pltpu.VMEM((1, PER_DEV), f32),
            pltpu.VMEM(TABLE.shape, jnp.bfloat16),
            pltpu.VMEM((ROWS, 128), f32),
            pltpu.VMEM((ROWS, 128), f32),
            pltpu.VMEM((N_SRC, 8, 128), f32),
            pltpu.VMEM((QUAD, PER_DEV, BAND, 128), f32),
            pltpu.VMEM((QUAD, 2, 2, 8, 256), f32),
            pltpu.VMEM((QUAD, ROWS_C // 2, 128), f32),
            pltpu.VMEM((QUAD, 2, 2, ROWS_C, 256), f32),
            pltpu.VMEM((QUAD, 2, 2, ROWS_C // 2, 256), f32),
            pltpu.VMEM((TILE, TILE), f32),
            pltpu.VMEM((QUAD, 8, 128), f32),
            pltpu.VMEM((QUAD - 1, 8, 128), f32),
            pltpu.VMEM((N_TILE, 1, 128), f32),
            pltpu.VMEM((1, 128), f32),
            pltpu.SemaphoreType.DMA((7,)),
            pltpu.SemaphoreType.DMA((7,)),
            pltpu.SemaphoreType.DMA((7,)),
            pltpu.SemaphoreType.REGULAR((N_SRC,)),
            pltpu.SemaphoreType.REGULAR((2,)),
        ],
        compiler_params=pltpu.CompilerParams(
            collective_id=0, has_side_effects=True, vmem_limit_bytes=60 * 1024 * 1024
        ),
    )(mask, target, shifts.T, weights.reshape(1, PER_DEV), jnp.asarray(TABLE))
    return pl.pallas_call(
        hand_over,
        out_shape=(
            jax.ShapeDtypeStruct((ROWS, TILE), f32),
            jax.ShapeDtypeStruct((ROWS, TILE), f32),
            jax.ShapeDtypeStruct((PER_DEV,), f32),
        ),
        in_specs=[inside] * 3,
        out_specs=(anywhere,) * 3,
        scratch_shapes=[pltpu.VMEM((PER_DEV,), f32), pltpu.SemaphoreType.DMA((3,))],
    )(*[pltpu.with_memory_space_constraint(result, pltpu.VMEM) for result in results])


def solution(mesh):
    placed = (P("src", "tile"), P(None, "tile"), P("src", None), P("src"))
    return jax.shard_map(
        local,
        mesh=mesh,
        in_specs=placed,
        out_specs=(P("src", "tile"), P("src", "tile"), P("src")),
        check_vma=False,
    )
```

```python
import functools

import jax
import jax.numpy as jnp
import ml_dtypes
import numpy as np
from jax import lax
from jax.experimental import pallas as pl
from jax.experimental.pallas import tpu as pltpu
from jax.sharding import PartitionSpec as P

TILE = 256
MARGIN = 32
BAND = 64
RAD = 16
EXT = 320
STEEP = 8.0
THRESH = 0.25
LOSS_SCALE = 2.0

N_SRC = 16
N_TILE = 32
PER_DEV = 8
SOURCES = 128
ROWS = 16
HALF = 32
POINTS_R = 66
ROWS_C = 80
COLS_C = 128
QUAD = 4
GROUP = 4
DEPTH = 8
HUB = 3 * GROUP
RIDERS = (31, 63, 95)

MESH = pl.DeviceIdType.MESH
BF16 = ml_dtypes.bfloat16


def halves(table):
    high = table.astype(BF16)
    low = (table - high.astype(np.float64)).astype(BF16)
    return high, low


def column_slots():
    plus = np.arange(HALF)
    return np.concatenate([plus, -plus]), np.concatenate([np.ones(HALF), [0.0], np.ones(HALF - 1)])


def waves(freq, place, period):
    phase = 2.0 * np.pi * ((freq[:, None] * place[None, :]) % period) / period
    return np.cos(phase), np.sin(phase)


def interpolation(points):
    order = np.arange(-2 * RAD, 2 * RAD + 1)
    place = np.arange(TILE) + MARGIN
    offset = place[:, None] / EXT - np.arange(points)[None, :] / points
    return np.cos(2.0 * np.pi * order[None, None, :] * offset[:, :, None]).sum(axis=2) / points


def padded(rows):
    return np.concatenate([rows, np.zeros((ROWS_C // 2 - rows.shape[0], rows.shape[1]))], axis=0)


def build_tables():
    slots, used = column_slots()
    row_freq = np.arange(BAND) - BAND // 2
    pixels = np.arange(TILE) + MARGIN
    parts = {}

    real, imag = waves(np.arange(HALF), np.arange(EXT), EXT)
    fwd = np.concatenate([real, -imag], axis=0).T
    wide = np.zeros((2 * TILE, 2 * HALF))
    wide[:TILE] = fwd[MARGIN : MARGIN + TILE]
    wide[TILE + 96 : TILE + 128] = fwd[:MARGIN]
    wide[TILE + 128 : TILE + 160] = fwd[MARGIN + TILE :]
    high, low = halves(np.concatenate([wide, wide], axis=1))
    parts["enter"] = np.concatenate([high, low], axis=1)

    rows = np.arange(TILE).reshape(N_SRC, 2, 8)
    first, second = rows[:, 0].reshape(-1), rows[:, 1].reshape(-1)
    real, imag = waves(row_freq, pixels, EXT)
    both = np.concatenate([real, -imag], axis=0)
    high, low = halves(np.concatenate([both[:, first], both[:, second]], axis=0))
    parts["spec"] = np.concatenate([high, high], axis=1)
    spec_low = low

    inter_rows, inter_cols = 2.0 * interpolation(POINTS_R), interpolation(COLS_C)
    even, odd = np.arange(0, COLS_C, 2), np.arange(1, COLS_C, 2)
    for name, order in (("even", np.concatenate([even, odd])), ("odd", np.concatenate([odd, even]))):
        real, imag = waves(slots, order, COLS_C)
        real, imag = real * used[:, None], imag * used[:, None]
        cols = np.concatenate(
            [np.concatenate([real, imag], axis=1), np.concatenate([-imag, real], axis=1)], axis=0
        )
        high, low = halves(cols)
        again = high.copy()
        again[[HALF, 3 * HALF]] = high[[0, 2 * HALF]]
        parts["cols_" + name] = np.concatenate([high, again], axis=0)
        parts["cols_low_" + name] = low
        high, low = halves(np.concatenate([cols[:, :COLS_C].T, cols[:, COLS_C:].T], axis=0))
        parts["cols_back_" + name] = np.concatenate([high, low], axis=1)

    lows = []
    for name, start in (("even", 0), ("odd", 1)):
        real, imag = waves(row_freq, np.arange(start, POINTS_R, 2), POINTS_R)
        real, imag = padded(real.T), padded(imag.T)
        high, low = halves(
            np.concatenate(
                [np.concatenate([real, -imag], axis=1), np.concatenate([imag, real], axis=1)], axis=0
            )
        )
        parts["rows_" + name] = np.concatenate([high, high], axis=1)
        lows.append(low)
        pad = np.zeros((2 * BAND, TILE - 3 * ROWS_C), BF16)
        parts["rows_back_" + name] = np.concatenate([high.T, high.T, low.T, pad], axis=1)
    rows_low = np.concatenate(lows, axis=0)

    inter_rows = np.concatenate([padded(inter_rows[:, 0::2].T), padded(inter_rows[:, 1::2].T)], axis=0).T
    inter_cols = inter_cols[:, np.concatenate([even, odd])]
    high, low = halves(inter_rows)
    pad = np.zeros((TILE, TILE - 3 * ROWS_C), BF16)
    parts["fine_rows"] = np.concatenate([high, high, low, pad], axis=1)
    high, low = halves(inter_cols.T)
    parts["fine_cols"] = np.concatenate([high, high], axis=0)
    parts["fine_cols_low"] = low
    parts["coarse_cols"] = np.concatenate([high.T, low.T], axis=1)
    high, low = halves(inter_rows.T)
    parts["coarse_rows"] = high
    parts["coarse_rows_low"] = low

    owners = [
        side * DEPTH + (quad * QUAD + k - 1) % DEPTH for side in range(2) for quad in range(2) for k in range(QUAD)
    ]
    first, second = rows[owners, 0].reshape(-1), rows[owners, 1].reshape(-1)
    high, low = halves(np.concatenate([both[:, first], both[:, second]], axis=1).T)
    parts["leave"] = np.concatenate([high, high], axis=1)
    leave_low = low
    last = fwd[MARGIN : MARGIN + TILE].T
    high, low = halves(np.concatenate([last, last], axis=0))
    parts["last"] = high
    parts["last_low"] = low

    parts["lows_a"] = np.concatenate([spec_low, np.zeros((TILE, 128), BF16)], axis=1)
    rows_low = np.concatenate([rows_low, np.zeros((TILE - 2 * ROWS_C, 128), BF16)], axis=0)
    parts["lows_b"] = np.concatenate([leave_low, rows_low], axis=1)

    order = [
        "enter",
        "spec", "lows_a", "cols_even", "cols_low_even", "cols_odd", "cols_low_odd", "rows_even", "rows_odd", "lows_b",
        "fine_rows", "fine_cols", "fine_cols_low", "coarse_cols", "coarse_rows", "coarse_rows_low",
        "rows_back_even", "rows_back_odd", "cols_back_even", "cols_back_odd", "leave", "last", "last_low",
    ]
    places, start = {}, 0
    for name in order:
        places[name] = (start, parts[name].shape[0])
        start += parts[name].shape[0]
    return np.concatenate([parts[name] for name in order], axis=0), places


TABLE, PLACES = build_tables()
CUTS = (0, PLACES["spec"][0], PLACES["fine_rows"][0], TABLE.shape[0])


def dot(left, right):
    return jnp.dot(left, right, preferred_element_type=jnp.float32)


def cut(value):
    high = value.astype(jnp.bfloat16)
    low = (value - high.astype(jnp.float32)).astype(jnp.bfloat16)
    return high, low


def lanes(shape):
    return lax.broadcasted_iota(jnp.int32, shape, 1)


def enter(value, table):
    rows = value.shape[0]
    both = dot(jnp.concatenate(cut(value), axis=0), table)
    return both[:rows, :128] + both[:rows, 128:] + both[rows:, :128]


def pack(first, second):
    return jnp.where(lanes(first.shape) < 64, first, second)


def spectrum(gathered, table, low_table, roll):
    high, low = cut(gathered)
    out = dot(table, jnp.concatenate([high, low], axis=0)) + dot(low_table, high)
    both = pack(out[:128], out[128:])
    both = both + roll(both, 64, 1)
    turned = roll(both, 32, 1)
    quarter = lanes((BAND, 128)) >> 5
    outer = (quarter == 0) | (quarter == 3)
    even = jnp.where(outer, both[:BAND], turned[:BAND])
    odd = jnp.where(outer, turned[BAND:], both[BAND:])
    return (jnp.where(quarter == 3, -even, even) + jnp.where(quarter == 0, -odd, odd)) * (1.0 / (EXT * EXT))


def pupil_of(row_shift, col_shift):
    row = (lax.broadcasted_iota(jnp.int32, (BAND, 128), 0) - BAND // 2).astype(jnp.float32) + row_shift
    slot = lanes((1, 128)) & 63
    col = jnp.where(slot < HALF, slot, HALF - slot).astype(jnp.float32) + col_shift
    room = RAD * RAD - col * col
    return jnp.where(row * row <= room, 1.0, 0.0)


def swap(first, second):
    return pack(first, second), pack(second, first)


def split_bands(spec, roll):
    spare = (lanes(spec.shape) & 63) == HALF
    high, low = cut(jnp.where(spare, 0.0, spec))
    left = spec - high.astype(jnp.float32) - low.astype(jnp.float32)
    low = jnp.where(spare, roll(left, HALF, 1), low.astype(jnp.float32)).astype(jnp.bfloat16)
    return high, low


def coarse_fields(bands, pupils, cols, rows):
    high, low = bands
    mids = []
    for which in range(2):
        band_high, band_low = [
            jnp.concatenate([part * pupil for pupil in pupils[which::2]], axis=0) for part in (high, low)
        ]
        table, low_table = cols[which]
        mids.append(
            dot(jnp.concatenate([band_high, band_low], axis=1), table) + dot(band_high, low_table)
        )
    fields = []
    for group in range(2):
        stacks = ([], [])
        for pair in (2 * group, 2 * group + 1):
            at = slice(BAND * pair, BAND * pair + BAND)
            real = swap(mids[0][at, :128], mids[1][at, :128])
            imag = swap(mids[0][at, 128:], mids[1][at, 128:])
            for parity in range(2):
                stacks[parity].append(jnp.concatenate([real[parity], imag[parity]], axis=0))
        both = []
        for parity in range(2):
            upper, lower = cut(jnp.concatenate(stacks[parity], axis=1))
            table, low_table = rows[parity]
            both.append(dot(table, jnp.concatenate([upper, lower], axis=0)) + dot(low_table, upper))
        fields.append(both)
    return fields


def power_of(field):
    half = ROWS_C // 2
    return field[:half] * field[:half] + field[half:] * field[half:]


def join_image(even, odd, roll):
    return pack(even + roll(even, 64, 1), odd + roll(odd, 64, 1))


def pixels_of(coarse, fine_rows, fine_cols, fine_cols_low):
    first = lanes(coarse.shape) < 64
    coarse = jnp.concatenate([jnp.where(first, coarse, 0.0), jnp.where(first, 0.0, coarse)], axis=0)
    high, low = cut(coarse)
    mid = dot(jnp.concatenate([high, low], axis=1), fine_cols) + dot(high, fine_cols_low)
    return dot(fine_rows, three(mid))


def three(value):
    high, low = cut(value)
    pad = jnp.zeros((TILE - 3 * value.shape[0], value.shape[1]), jnp.bfloat16)
    return jnp.concatenate([high, low, high, pad], axis=0)


def coarse_of(slope, coarse_rows, coarse_rows_low, coarse_cols):
    high, low = cut(slope)
    mid = dot(coarse_rows, high) + dot(coarse_rows, low) + dot(coarse_rows_low, high)
    high, low = cut(mid)
    both = dot(high, coarse_cols)
    return both[:, :128] + both[:, 128:] + dot(low, coarse_cols[:, :128])


def twice(coarse, roll):
    half = ROWS_C // 2
    even, odd = coarse[:half], coarse[half:]
    return pack(even, roll(even, 64, 1)), pack(roll(odd, 64, 1), odd)


def band_grad(total, adjoints, pupils, rows_back, cols_back):
    sides = ([], [])
    for group in range(2):
        even, odd = [dot(rows_back[parity], three(adjoints[group][parity])) for parity in range(2)]
        for pair in range(2):
            at = slice(128 * pair, 128 * pair + 128)
            real = swap(even[:BAND, at], odd[:BAND, at])
            imag = swap(even[BAND:, at], odd[BAND:, at])
            for which in range(2):
                sides[which].append(jnp.concatenate([real[which], imag[which]], axis=1))
    for which in range(2):
        high, low = cut(jnp.concatenate(sides[which], axis=0))
        both = dot(high, cols_back[which])
        term = both[:, :128] + both[:, 128:] + dot(low, cols_back[which][:, :128])
        for k in range(PER_DEV // 2):
            total = total + term[BAND * k : BAND * k + BAND] * pupils[2 * k + which]
    return total


def fold(grad, roll):
    r32, r64, r96 = roll(grad, 32, 1), roll(grad, 64, 1), roll(grad, 96, 1)
    quarter = lanes(grad.shape) >> 5
    upper = jnp.where(
        quarter == 0, grad + r96, jnp.where(quarter == 1, r96 - r64, jnp.where(quarter == 2, r64 + r32, r32 - grad))
    )
    lower = jnp.where(
        quarter == 0, r64 + r32, jnp.where(quarter == 1, grad - r32, jnp.where(quarter == 2, grad + r96, r64 - r96))
    )
    return jnp.concatenate([upper, lower], axis=0)


def row_grads(grad, leave, leave_low, roll):
    high, low = cut(fold(grad, roll))
    out = dot(leave, jnp.concatenate([high, low], axis=0)) + dot(leave_low, high)
    half = out.shape[0] // 2
    return pack(out[:half], out[half:])


def last_step(total, last, last_low):
    first = lanes(total.shape) < 64
    value = jnp.concatenate([jnp.where(first, total, 0.0), jnp.where(first, 0.0, total)], axis=0)
    high, low = cut(value)
    return (dot(high, last) + dot(low, last) + dot(high, last_low)) * (1.0 / (EXT * EXT))


def rank_of(side, along):
    step = jnp.where(along == 3, 4, jnp.where(along == 7, 3, 11 - along))
    return 2 * jnp.where(along < 3, along, step) + side


def src_of(rank):
    step, side = rank // 2, rank % 2
    along = jnp.where(step == 3, 7, jnp.where(step == 4, 3, 11 - step))
    return side * DEPTH + jnp.where(step < 3, step, along)


def repeat(first, last, body):
    def step(k, carry):
        body(k)
        return carry

    lax.fori_loop(first, last, step, 0)


def everything(mask, target, shifts, weights, table, resist, mask_grad, source_grad, *scratch):
    (
        mask_v, target_v, shifts_v, weights_v, table_v,
        left_v, right_v, spec_v, pupil_v, scale_v, term_v, field_v, power_v,
        printed_v, grad_v, part_v, sums_v, total_v, local_sem, send_sem, recv_sem, ready_sem, hub_sem,
    ) = scratch
    tile, src = lax.axis_index("tile"), lax.axis_index("src")
    n_tile = lax.axis_size("tile")
    left, right = tile - 1, tile + 1
    has_left, has_right = tile > 0, tile < n_tile - 1
    side, along = src // DEPTH, src % DEPTH
    rank = rank_of(side, along)
    place_in_quad = (along + 1) % QUAD
    quad = (along + 1) % DEPTH // QUAD
    partners = [
        (side + across) % 2 * DEPTH + (along + step) % DEPTH for across, step in ((0, QUAD), (1, 0), (1, QUAD))
    ]

    def member(k):
        return side * DEPTH + (quad * QUAD + k + DEPTH - 1) % DEPTH

    layer = tile // GROUP
    place = tile % GROUP
    is_hub, is_teller = tile < HUB, layer == HUB // GROUP - 1

    def get(name, start=None, stop=None):
        at, size = PLACES[name]
        if start is None:
            return table_v[at : at + size, :]
        return table_v[at : at + size, start:stop]

    def signal(sem, device):
        pl.semaphore_signal(sem, inc=1, device_id=device, device_id_type=MESH)

    def send(source, target_ref, number, device):
        copy = pltpu.make_async_remote_copy(
            src_ref=source,
            dst_ref=target_ref,
            send_sem=send_sem.at[number],
            recv_sem=recv_sem.at[number],
            device_id=device,
            device_id_type=MESH,
        )
        copy.start()

    def wait(ref, sem):
        pltpu.make_async_copy(ref, ref, sem).wait()

    barrier = pltpu.get_barrier_semaphore()

    @pl.when(has_left)
    def _():
        signal(barrier, {"tile": left})

    @pl.when(has_right)
    def _():
        signal(barrier, {"tile": right})

    repeat(rank + 1, N_SRC, lambda k: signal(barrier, {"src": src_of(k)}))
    local = [
        pltpu.make_async_copy(mask, mask_v, local_sem.at[0]),
        pltpu.make_async_copy(shifts, shifts_v, local_sem.at[1]),
        pltpu.make_async_copy(weights, weights_v, local_sem.at[2]),
    ]
    for k in range(3):
        rows = pl.ds(CUTS[k], CUTS[k + 1] - CUTS[k])
        local.append(pltpu.make_async_copy(table.at[rows], table_v.at[rows], local_sem.at[3 + k]))
    local.append(pltpu.make_async_copy(target, target_v, local_sem.at[6]))
    local[0].start()
    local[3].start()
    repeat(jnp.where(is_hub, tile + 1, n_tile), n_tile, lambda k: signal(barrier, {"tile": k}))

    ends = has_left.astype(jnp.int32) + has_right.astype(jnp.int32)
    pl.semaphore_wait(barrier, rank + ends + jnp.minimum(tile, HUB))

    @pl.when(has_right)
    def _():
        send(mask.at[:, pl.ds(128, 128)], left_v, 0, {"tile": right})

    @pl.when(has_left)
    def _():
        send(mask.at[:, pl.ds(0, 128)], right_v, 1, {"tile": left})

    for k in (1, 2, 4, 5, 6):
        local[k].start()
    repeat(0, rank, lambda k: signal(ready_sem.at[rank], {"src": src_of(k)}))
    term_v[:, POINTS_R // 2 :, :] = jnp.zeros((QUAD, (ROWS_C - POINTS_R) // 2, 128), jnp.float32)

    @pl.when(jnp.logical_not(has_left))
    def _():
        left_v[...] = jnp.zeros_like(left_v)

    @pl.when(jnp.logical_not(has_right))
    def _():
        right_v[...] = jnp.zeros_like(right_v)

    local[1].wait()
    local[2].wait()
    shape = (PER_DEV, PER_DEV)
    own_place = lanes(shape) == lax.broadcasted_iota(jnp.int32, shape, 0)

    def upright(row):
        return jnp.sum(jnp.where(own_place, row, 0.0), axis=1, keepdims=True)

    own_shifts = shifts_v[...].astype(jnp.float32)
    riders = [upright(own_shifts[0:1, :]), upright(own_shifts[1:2, :]), upright(weights_v[...])]
    local[0].wait()
    local[3].wait()
    at = PLACES["enter"][0]
    own = enter(mask_v[...], table_v[at : at + TILE, :])

    @pl.when(has_left)
    def _():
        wait(left_v, recv_sem.at[0])

    @pl.when(has_right)
    def _():
        wait(right_v, recv_sem.at[1])

    margins = jnp.concatenate([left_v[...], right_v[...]], axis=1)
    own = own + enter(margins, table_v[at + TILE : at + 2 * TILE, :])
    own = pack(own[:8], own[8:])
    for lane, rider in zip(RIDERS, riders):
        own = jnp.where(lanes(own.shape) == lane, rider, own)
    spec_v[src] = own

    def send_piece(k):
        send(spec_v.at[src], spec_v.at[src], 2, {"src": src_of(k)})

    def answer_piece(k):
        pl.semaphore_wait(ready_sem.at[k], 1)
        send_piece(k)

    def send_even(k):
        served = k
        for place_in_row, turn in enumerate((1, 2, 3, 5, 4, 0)):
            served = jnp.where((k == place_in_row) & (rank >= 11), turn, served)
        send_piece(2 * served)

    repeat(0, (rank + 1) // 2, send_even)
    repeat(0, rank // 2, lambda k: send_piece(2 * k + 1))
    repeat(rank + 1, N_SRC, answer_piece)
    repeat(0, jnp.where(is_hub, tile, 0), lambda k: signal(hub_sem.at[0], {"tile": k}))

    @pl.when(jnp.logical_not(is_hub))
    def _():
        signal(hub_sem.at[1], {"tile": HUB - GROUP + place})

    local[4].wait()
    wait(spec_v.at[pl.ds(0, N_SRC - 1)], recv_sem.at[2])

    gathered = spec_v[...].reshape(128, 128)
    spec = spectrum(gathered, get("spec"), get("lows_a", 0, 128), pltpu.roll)
    bands = split_bands(spec, pltpu.roll)
    at = PLACES["lows_b"][0]
    cols = [(get("cols_" + name), get("cols_low_" + name)) for name in ("even", "odd")]
    rows = [
        (get("rows_even"), table_v[at : at + ROWS_C, 128:256]),
        (get("rows_odd"), table_v[at + ROWS_C : at + 2 * ROWS_C, 128:256]),
    ]

    def add_fields(part, images):
        owner = src
        for k, peer in enumerate(partners):
            owner = jnp.where(part == k + 1, peer, owner)
        rows_by, cols_by, scales = [spec_v[owner, :, lane : lane + 1] for lane in RIDERS]
        for s in range(PER_DEV):
            pupil_v[part, s] = pupil_of(rows_by[s : s + 1], cols_by[s : s + 1])
        for pair in range(PER_DEV // 2):
            first, second = [jnp.broadcast_to(scales[s : s + 1], (8, 128)) for s in (2 * pair, 2 * pair + 1)]
            at = slice(128 * (pair % 2), 128 * (pair % 2) + 128)
            for parity, scale in enumerate(swap(first, second)):
                scale_v[part, pair // 2, parity, :, at] = scale
        fields = coarse_fields(
            bands, [pupil_v[part, s].astype(jnp.bfloat16) for s in range(PER_DEV)], cols, rows
        )
        images = list(images)
        for group in range(2):
            for parity in range(2):
                field_v[part, group, parity] = fields[group][parity]
                power = power_of(fields[group][parity])
                power_v[part, group, parity] = power
                power = power * scale_v[part, group, parity, 0:1, :]
                images[parity] = images[parity] + power[:, :128] + power[:, 128:]
        return tuple(images)

    none = jnp.zeros((ROWS_C // 2, 128), jnp.float32)
    image = lax.fori_loop(0, QUAD, add_fields, (none, none), unroll=True)
    term_v[place_in_quad] = join_image(*image, pltpu.roll)
    image_rows = pl.ds(0, POINTS_R // 2)
    mine = term_v.at[place_in_quad, image_rows]

    def send_image(k):
        send(mine, mine, 3, {"src": member(k)})

    for k in (1, 0, 2, 3):
        pl.when(k != place_in_quad)(functools.partial(send_image, k))
    local[5].wait()
    local[6].wait()
    wait(term_v.at[pl.ds(0, QUAD - 1), image_rows], recv_sem.at[3])

    image = pixels_of(
        term_v[0] + term_v[1] + term_v[2] + term_v[3],
        get("fine_rows"),
        get("fine_cols"),
        get("fine_cols_low"),
    )
    printed = jax.nn.sigmoid(STEEP * (image * (1.0 / SOURCES) - THRESH))
    goal = target_v[...].astype(jnp.float32)
    slope = (LOSS_SCALE * 2.0 * STEEP) * (printed - goal) * printed * (1.0 - printed)
    coarse = coarse_of(slope, get("coarse_rows"), get("coarse_rows_low"), get("coarse_cols"))

    slopes = twice(coarse, pltpu.roll)
    sums = []
    for pair in range(PER_DEV // 2):
        at = slice(128 * (pair % 2), 128 * (pair % 2) + 128)
        terms = [
            jnp.sum(slopes[parity] * power_v[0, pair // 2, parity, :, at], axis=0, keepdims=True) for parity in range(2)
        ]
        sums.extend(swap(*terms))
    sums = jnp.sum(jnp.concatenate(sums, axis=0), axis=1, keepdims=True)
    spot = (PER_DEV, 128)
    sums = jnp.where(lanes(spot) == lax.broadcasted_iota(jnp.int32, spot, 0), sums, 0.0)
    sums_v[tile] = jnp.sum(sums, axis=0, keepdims=True)

    def send_sums(k):
        pltpu.make_async_remote_copy(
            src_ref=sums_v.at[tile],
            dst_ref=sums_v.at[tile],
            send_sem=send_sem.at[5],
            recv_sem=recv_sem.at[5],
            device_id={"tile": k},
            device_id_type=MESH,
        ).start()

    for k in range(HUB):
        first = k + 1 - 2 * (k % 2)
        pl.when(first < tile)(functools.partial(send_sums, first))

    printed_v[...] = printed
    resist[...] = printed_v[pl.ds(pl.multiple_of(src * ROWS, ROWS), ROWS), :]

    wide = [jnp.concatenate([slope, slope], axis=1) * (2.0 / SOURCES) for slope in slopes]
    rows_back = [get("rows_back_even"), get("rows_back_odd")]
    cols_back = [get("cols_back_even"), get("cols_back_odd")]

    def add_part(part, total):
        adjoints = []
        for group in range(2):
            adjoints.append([])
            for parity in range(2):
                scaled = wide[parity] * scale_v[part, group, parity, 0:1, :]
                adjoints[group].append(field_v[part, group, parity] * jnp.concatenate([scaled, scaled], axis=0))
        return band_grad(total, adjoints, [pupil_v[part, s] for s in range(PER_DEV)], rows_back, cols_back)

    grad = lax.fori_loop(0, QUAD, add_part, jnp.zeros((BAND, 128), jnp.float32))
    first = PLACES["leave"][0] + 8 * QUAD * (2 * side + quad)
    low_first = PLACES["lows_b"][0] + 8 * QUAD * (2 * side + quad)

    def halves_of(start, stop, begin):
        begin = pl.multiple_of(begin, 32)
        then = pl.multiple_of(begin + 128, 32)
        return jnp.concatenate(
            [table_v[pl.ds(begin, 8 * QUAD), start:stop], table_v[pl.ds(then, 8 * QUAD), start:stop]], axis=0
        )

    rows = row_grads(grad, halves_of(0, 256, first), halves_of(0, 128, low_first), pltpu.roll)
    grad_v[...] = rows.reshape(QUAD, 8, 128)
    for k in range(1, QUAD):
        other = (place_in_quad + k) % QUAD
        send(grad_v.at[other], part_v.at[k - 1], 4, {"src": member(other)})

    @pl.when(tile < HUB - 1)
    def _():
        pl.semaphore_wait(hub_sem.at[0], HUB - 1 - tile)
        repeat(tile + 1, HUB, send_sums)

    wait(part_v, recv_sem.at[4])
    total = grad_v[place_in_quad] + part_v[0] + part_v[1] + part_v[2]
    mask_grad[...] = last_step(total, get("last"), get("last_low"))

    @pl.when(is_hub)
    def _():
        wait(sums_v.at[pl.ds(0, n_tile - 1)], recv_sem.at[5])
        total_v[...] = jnp.sum(sums_v[...], axis=0) * (1.0 / (SOURCES * n_tile * TILE * TILE))

    def tell(k):
        send(total_v, total_v, 6, {"tile": k * GROUP + place})

    @pl.when(is_teller)
    def _():
        pl.semaphore_wait(hub_sem.at[1], (n_tile - HUB) // GROUP)
        repeat(HUB // GROUP, n_tile // GROUP, tell)

    @pl.when(jnp.logical_not(is_hub))
    def _():
        wait(total_v, recv_sem.at[6])

    source_grad[...] = total_v[...]

    @pl.when(is_teller)
    def _():
        wait(sums_v.at[pl.ds(0, (n_tile - HUB) // GROUP)], send_sem.at[6])

    @pl.when(is_hub)
    def _():
        wait(sums_v.at[pl.ds(0, HUB - 1)], send_sem.at[5])

    @pl.when(jnp.logical_not(is_hub))
    def _():
        wait(sums_v.at[pl.ds(0, HUB)], send_sem.at[5])


    @pl.when(has_right)
    def _():
        wait(left_v, send_sem.at[0])

    @pl.when(has_left)
    def _():
        wait(right_v, send_sem.at[1])

    wait(spec_v.at[pl.ds(0, N_SRC - 1)], send_sem.at[2])
    wait(term_v.at[pl.ds(0, QUAD - 1), image_rows], send_sem.at[3])
    wait(part_v, send_sem.at[4])


def hand_over(resist, mask_grad, source_grad, resist_out, mask_grad_out, source_grad_out, row, sem):
    row[...] = source_grad[0, :PER_DEV]
    copies = [
        pltpu.make_async_copy(resist, resist_out, sem.at[0]),
        pltpu.make_async_copy(mask_grad, mask_grad_out, sem.at[1]),
        pltpu.make_async_copy(row, source_grad_out, sem.at[2]),
    ]
    for copy in copies:
        copy.start()
    for copy in copies:
        copy.wait()


def local(mask, target, shifts, weights):
    f32 = jnp.float32
    anywhere = pl.BlockSpec(memory_space=pl.ANY)
    inside = pl.BlockSpec(memory_space=pltpu.VMEM)
    results = pl.pallas_call(
        everything,
        out_shape=(
            pltpu.VMEM((ROWS, TILE), f32),
            pltpu.VMEM((ROWS, TILE), f32),
            pltpu.VMEM((1, 128), f32),
        ),
        in_specs=[anywhere] * 5,
        out_specs=(inside, inside, inside),
        scratch_shapes=[
            pltpu.VMEM((ROWS, TILE), f32),
            pltpu.VMEM((TILE, TILE), jnp.int32),
            pltpu.VMEM((2, PER_DEV), jnp.int32),
            pltpu.VMEM((1, PER_DEV), f32),
            pltpu.VMEM(TABLE.shape, jnp.bfloat16),
            pltpu.VMEM((ROWS, 128), f32),
            pltpu.VMEM((ROWS, 128), f32),
            pltpu.VMEM((N_SRC, 8, 128), f32),
            pltpu.VMEM((QUAD, PER_DEV, BAND, 128), f32),
            pltpu.VMEM((QUAD, 2, 2, 8, 256), f32),
            pltpu.VMEM((QUAD, ROWS_C // 2, 128), f32),
            pltpu.VMEM((QUAD, 2, 2, ROWS_C, 256), f32),
            pltpu.VMEM((QUAD, 2, 2, ROWS_C // 2, 256), f32),
            pltpu.VMEM((TILE, TILE), f32),
            pltpu.VMEM((QUAD, 8, 128), f32),
            pltpu.VMEM((QUAD - 1, 8, 128), f32),
            pltpu.VMEM((N_TILE, 1, 128), f32),
            pltpu.VMEM((1, 128), f32),
            pltpu.SemaphoreType.DMA((7,)),
            pltpu.SemaphoreType.DMA((7,)),
            pltpu.SemaphoreType.DMA((7,)),
            pltpu.SemaphoreType.REGULAR((N_SRC,)),
            pltpu.SemaphoreType.REGULAR((2,)),
        ],
        compiler_params=pltpu.CompilerParams(
            collective_id=0, has_side_effects=True, vmem_limit_bytes=60 * 1024 * 1024
        ),
    )(mask, target, shifts.T, weights.reshape(1, PER_DEV), jnp.asarray(TABLE))
    return pl.pallas_call(
        hand_over,
        out_shape=(
            jax.ShapeDtypeStruct((ROWS, TILE), f32),
            jax.ShapeDtypeStruct((ROWS, TILE), f32),
            jax.ShapeDtypeStruct((PER_DEV,), f32),
        ),
        in_specs=[inside] * 3,
        out_specs=(anywhere,) * 3,
        scratch_shapes=[pltpu.VMEM((PER_DEV,), f32), pltpu.SemaphoreType.DMA((3,))],
    )(*[pltpu.with_memory_space_constraint(result, pltpu.VMEM) for result in results])


def solution(mesh):
    placed = (P("src", "tile"), P(None, "tile"), P("src", None), P("src"))
    return jax.shard_map(
        local,
        mesh=mesh,
        in_specs=placed,
        out_specs=(P("src", "tile"), P("src", "tile"), P("src")),
        check_vma=False,
    )
```

```python
import functools

import jax
import jax.numpy as jnp
import ml_dtypes
import numpy as np
from jax import lax
from jax.experimental import pallas as pl
from jax.experimental.pallas import tpu as pltpu
from jax.sharding import PartitionSpec as P

TILE = 256
MARGIN = 32
BAND = 64
RAD = 16
EXT = 320
STEEP = 8.0
THRESH = 0.25
LOSS_SCALE = 2.0

N_SRC = 16
N_TILE = 32
PER_DEV = 8
SOURCES = 128
ROWS = 16
HALF = 32
POINTS_R = 66
ROWS_C = 80
COLS_C = 128
QUAD = 4
GROUP = 4
DEPTH = 8
HUB = 3 * GROUP
RIDERS = (31, 63, 95)

MESH = pl.DeviceIdType.MESH
BF16 = ml_dtypes.bfloat16


def halves(table):
    high = table.astype(BF16)
    low = (table - high.astype(np.float64)).astype(BF16)
    return high, low


def column_slots():
    plus = np.arange(HALF)
    return np.concatenate([plus, -plus]), np.concatenate([np.ones(HALF), [0.0], np.ones(HALF - 1)])


def waves(freq, place, period):
    phase = 2.0 * np.pi * ((freq[:, None] * place[None, :]) % period) / period
    return np.cos(phase), np.sin(phase)


def interpolation(points):
    order = np.arange(-2 * RAD, 2 * RAD + 1)
    place = np.arange(TILE) + MARGIN
    offset = place[:, None] / EXT - np.arange(points)[None, :] / points
    return np.cos(2.0 * np.pi * order[None, None, :] * offset[:, :, None]).sum(axis=2) / points


def padded(rows):
    return np.concatenate([rows, np.zeros((ROWS_C // 2 - rows.shape[0], rows.shape[1]))], axis=0)


def build_tables():
    slots, used = column_slots()
    row_freq = np.arange(BAND) - BAND // 2
    pixels = np.arange(TILE) + MARGIN
    parts = {}

    real, imag = waves(np.arange(HALF), np.arange(EXT), EXT)
    fwd = np.concatenate([real, -imag], axis=0).T
    wide = np.zeros((2 * TILE, 2 * HALF))
    wide[:TILE] = fwd[MARGIN : MARGIN + TILE]
    wide[TILE + 96 : TILE + 128] = fwd[:MARGIN]
    wide[TILE + 128 : TILE + 160] = fwd[MARGIN + TILE :]
    high, low = halves(np.concatenate([wide, wide], axis=1))
    parts["enter"] = np.concatenate([high, low], axis=1)

    rows = np.arange(TILE).reshape(N_SRC, 2, 8)
    first, second = rows[:, 0].reshape(-1), rows[:, 1].reshape(-1)
    real, imag = waves(row_freq, pixels, EXT)
    both = np.concatenate([real, -imag], axis=0)
    high, low = halves(np.concatenate([both[:, first], both[:, second]], axis=0))
    parts["spec"] = np.concatenate([high, high], axis=1)
    spec_low = low

    inter_rows, inter_cols = 2.0 * interpolation(POINTS_R), interpolation(COLS_C)
    even, odd = np.arange(0, COLS_C, 2), np.arange(1, COLS_C, 2)
    for name, order in (("even", np.concatenate([even, odd])), ("odd", np.concatenate([odd, even]))):
        real, imag = waves(slots, order, COLS_C)
        real, imag = real * used[:, None], imag * used[:, None]
        cols = np.concatenate(
            [np.concatenate([real, imag], axis=1), np.concatenate([-imag, real], axis=1)], axis=0
        )
        high, low = halves(cols)
        again = high.copy()
        again[[HALF, 3 * HALF]] = high[[0, 2 * HALF]]
        parts["cols_" + name] = np.concatenate([high, again], axis=0)
        parts["cols_low_" + name] = low
        high, low = halves(np.concatenate([cols[:, :COLS_C].T, cols[:, COLS_C:].T], axis=0))
        parts["cols_back_" + name] = np.concatenate([high, low], axis=1)

    lows = []
    for name, start in (("even", 0), ("odd", 1)):
        real, imag = waves(row_freq, np.arange(start, POINTS_R, 2), POINTS_R)
        real, imag = padded(real.T), padded(imag.T)
        high, low = halves(
            np.concatenate(
                [np.concatenate([real, -imag], axis=1), np.concatenate([imag, real], axis=1)], axis=0
            )
        )
        parts["rows_" + name] = np.concatenate([high, high], axis=1)
        lows.append(low)
        pad = np.zeros((2 * BAND, TILE - 3 * ROWS_C), BF16)
        parts["rows_back_" + name] = np.concatenate([high.T, high.T, low.T, pad], axis=1)
    rows_low = np.concatenate(lows, axis=0)

    inter_rows = np.concatenate([padded(inter_rows[:, 0::2].T), padded(inter_rows[:, 1::2].T)], axis=0).T
    inter_cols = inter_cols[:, np.concatenate([even, odd])]
    high, low = halves(inter_rows)
    pad = np.zeros((TILE, TILE - 3 * ROWS_C), BF16)
    parts["fine_rows"] = np.concatenate([high, high, low, pad], axis=1)
    high, low = halves(inter_cols.T)
    parts["fine_cols"] = np.concatenate([high, high], axis=0)
    parts["fine_cols_low"] = low
    parts["coarse_cols"] = np.concatenate([high.T, low.T], axis=1)
    high, low = halves(inter_rows.T)
    parts["coarse_rows"] = high
    parts["coarse_rows_low"] = low

    owners = [
        side * DEPTH + (quad * QUAD + k - 1) % DEPTH for side in range(2) for quad in range(2) for k in range(QUAD)
    ]
    first, second = rows[owners, 0].reshape(-1), rows[owners, 1].reshape(-1)
    high, low = halves(np.concatenate([both[:, first], both[:, second]], axis=1).T)
    parts["leave"] = np.concatenate([high, high], axis=1)
    leave_low = low
    last = fwd[MARGIN : MARGIN + TILE].T
    high, low = halves(np.concatenate([last, last], axis=0))
    parts["last"] = high
    parts["last_low"] = low

    parts["lows_a"] = np.concatenate([spec_low, np.zeros((TILE, 128), BF16)], axis=1)
    rows_low = np.concatenate([rows_low, np.zeros((TILE - 2 * ROWS_C, 128), BF16)], axis=0)
    parts["lows_b"] = np.concatenate([leave_low, rows_low], axis=1)

    order = [
        "enter",
        "spec", "lows_a", "cols_even", "cols_low_even", "cols_odd", "cols_low_odd", "rows_even", "rows_odd", "lows_b",
        "fine_rows", "fine_cols", "fine_cols_low", "coarse_cols", "coarse_rows", "coarse_rows_low",
        "rows_back_even", "rows_back_odd", "cols_back_even", "cols_back_odd", "leave", "last", "last_low",
    ]
    places, start = {}, 0
    for name in order:
        places[name] = (start, parts[name].shape[0])
        start += parts[name].shape[0]
    return np.concatenate([parts[name] for name in order], axis=0), places


TABLE, PLACES = build_tables()
CUTS = (0, PLACES["spec"][0], PLACES["fine_rows"][0], TABLE.shape[0])


def dot(left, right):
    return jnp.dot(left, right, preferred_element_type=jnp.float32)


def cut(value):
    high = value.astype(jnp.bfloat16)
    low = (value - high.astype(jnp.float32)).astype(jnp.bfloat16)
    return high, low


def lanes(shape):
    return lax.broadcasted_iota(jnp.int32, shape, 1)


def enter(value, table):
    rows = value.shape[0]
    both = dot(jnp.concatenate(cut(value), axis=0), table)
    return both[:rows, :128] + both[:rows, 128:] + both[rows:, :128]


def pack(first, second):
    return jnp.where(lanes(first.shape) < 64, first, second)


def spectrum(gathered, table, low_table, roll):
    high, low = cut(gathered)
    out = dot(table, jnp.concatenate([high, low], axis=0)) + dot(low_table, high)
    both = pack(out[:128], out[128:])
    both = both + roll(both, 64, 1)
    turned = roll(both, 32, 1)
    quarter = lanes((BAND, 128)) >> 5
    outer = (quarter == 0) | (quarter == 3)
    even = jnp.where(outer, both[:BAND], turned[:BAND])
    odd = jnp.where(outer, turned[BAND:], both[BAND:])
    return (jnp.where(quarter == 3, -even, even) + jnp.where(quarter == 0, -odd, odd)) * (1.0 / (EXT * EXT))


def pupil_of(row_shift, col_shift):
    row = (lax.broadcasted_iota(jnp.int32, (BAND, 128), 0) - BAND // 2).astype(jnp.float32) + row_shift
    slot = lanes((1, 128)) & 63
    col = jnp.where(slot < HALF, slot, HALF - slot).astype(jnp.float32) + col_shift
    room = RAD * RAD - col * col
    return jnp.where(row * row <= room, 1.0, 0.0)


def swap(first, second):
    return pack(first, second), pack(second, first)


def split_bands(spec, roll):
    spare = (lanes(spec.shape) & 63) == HALF
    high, low = cut(jnp.where(spare, 0.0, spec))
    left = spec - high.astype(jnp.float32) - low.astype(jnp.float32)
    low = jnp.where(spare, roll(left, HALF, 1), low.astype(jnp.float32)).astype(jnp.bfloat16)
    return high, low


def coarse_fields(bands, pupils, cols, rows):
    high, low = bands
    mids = []
    for which in range(2):
        band_high, band_low = [
            jnp.concatenate([part * pupil for pupil in pupils[which::2]], axis=0) for part in (high, low)
        ]
        table, low_table = cols[which]
        mids.append(
            dot(jnp.concatenate([band_high, band_low], axis=1), table) + dot(band_high, low_table)
        )
    fields = []
    for group in range(2):
        stacks = ([], [])
        for pair in (2 * group, 2 * group + 1):
            at = slice(BAND * pair, BAND * pair + BAND)
            real = swap(mids[0][at, :128], mids[1][at, :128])
            imag = swap(mids[0][at, 128:], mids[1][at, 128:])
            for parity in range(2):
                stacks[parity].append(jnp.concatenate([real[parity], imag[parity]], axis=0))
        both = []
        for parity in range(2):
            upper, lower = cut(jnp.concatenate(stacks[parity], axis=1))
            table, low_table = rows[parity]
            both.append(dot(table, jnp.concatenate([upper, lower], axis=0)) + dot(low_table, upper))
        fields.append(both)
    return fields


def power_of(field):
    half = ROWS_C // 2
    return field[:half] * field[:half] + field[half:] * field[half:]


def join_image(even, odd, roll):
    return pack(even + roll(even, 64, 1), odd + roll(odd, 64, 1))


def pixels_of(coarse, fine_rows, fine_cols, fine_cols_low):
    first = lanes(coarse.shape) < 64
    coarse = jnp.concatenate([jnp.where(first, coarse, 0.0), jnp.where(first, 0.0, coarse)], axis=0)
    high, low = cut(coarse)
    mid = dot(jnp.concatenate([high, low], axis=1), fine_cols) + dot(high, fine_cols_low)
    return dot(fine_rows, three(mid))


def three(value):
    high, low = cut(value)
    pad = jnp.zeros((TILE - 3 * value.shape[0], value.shape[1]), jnp.bfloat16)
    return jnp.concatenate([high, low, high, pad], axis=0)


def coarse_of(slope, coarse_rows, coarse_rows_low, coarse_cols):
    high, low = cut(slope)
    mid = dot(coarse_rows, high) + dot(coarse_rows, low) + dot(coarse_rows_low, high)
    high, low = cut(mid)
    both = dot(high, coarse_cols)
    return both[:, :128] + both[:, 128:] + dot(low, coarse_cols[:, :128])


def twice(coarse, roll):
    half = ROWS_C // 2
    even, odd = coarse[:half], coarse[half:]
    return pack(even, roll(even, 64, 1)), pack(roll(odd, 64, 1), odd)


def band_grad(total, adjoints, pupils, rows_back, cols_back):
    sides = ([], [])
    for group in range(2):
        even, odd = [dot(rows_back[parity], three(adjoints[group][parity])) for parity in range(2)]
        for pair in range(2):
            at = slice(128 * pair, 128 * pair + 128)
            real = swap(even[:BAND, at], odd[:BAND, at])
            imag = swap(even[BAND:, at], odd[BAND:, at])
            for which in range(2):
                sides[which].append(jnp.concatenate([real[which], imag[which]], axis=1))
    for which in range(2):
        high, low = cut(jnp.concatenate(sides[which], axis=0))
        both = dot(high, cols_back[which])
        term = both[:, :128] + both[:, 128:] + dot(low, cols_back[which][:, :128])
        for k in range(PER_DEV // 2):
            total = total + term[BAND * k : BAND * k + BAND] * pupils[2 * k + which]
    return total


def fold(grad, roll):
    r32, r64, r96 = roll(grad, 32, 1), roll(grad, 64, 1), roll(grad, 96, 1)
    quarter = lanes(grad.shape) >> 5
    upper = jnp.where(
        quarter == 0, grad + r96, jnp.where(quarter == 1, r96 - r64, jnp.where(quarter == 2, r64 + r32, r32 - grad))
    )
    lower = jnp.where(
        quarter == 0, r64 + r32, jnp.where(quarter == 1, grad - r32, jnp.where(quarter == 2, grad + r96, r64 - r96))
    )
    return jnp.concatenate([upper, lower], axis=0)


def row_grads(grad, leave, leave_low, roll):
    high, low = cut(fold(grad, roll))
    out = dot(leave, jnp.concatenate([high, low], axis=0)) + dot(leave_low, high)
    half = out.shape[0] // 2
    return pack(out[:half], out[half:])


def last_step(total, last, last_low):
    first = lanes(total.shape) < 64
    value = jnp.concatenate([jnp.where(first, total, 0.0), jnp.where(first, 0.0, total)], axis=0)
    high, low = cut(value)
    return (dot(high, last) + dot(low, last) + dot(high, last_low)) * (1.0 / (EXT * EXT))


def rank_of(side, along):
    step = jnp.where(along == 3, 4, jnp.where(along == 7, 3, 11 - along))
    return 2 * jnp.where(along < 3, along, step) + side


def src_of(rank):
    step, side = rank // 2, rank % 2
    along = jnp.where(step == 3, 7, jnp.where(step == 4, 3, 11 - step))
    return side * DEPTH + jnp.where(step < 3, step, along)


def repeat(first, last, body):
    def step(k, carry):
        body(k)
        return carry

    lax.fori_loop(first, last, step, 0)


def everything(mask, target, shifts, weights, table, resist, mask_grad, source_grad, *scratch):
    (
        mask_v, target_v, shifts_v, weights_v, table_v,
        left_v, right_v, spec_v, pupil_v, scale_v, term_v, field_v, power_v,
        printed_v, grad_v, part_v, sums_v, total_v, local_sem, send_sem, recv_sem, ready_sem, hub_sem,
    ) = scratch
    tile, src = lax.axis_index("tile"), lax.axis_index("src")
    n_tile = lax.axis_size("tile")
    left, right = tile - 1, tile + 1
    has_left, has_right = tile > 0, tile < n_tile - 1
    side, along = src // DEPTH, src % DEPTH
    rank = rank_of(side, along)
    place_in_quad = (along + 1) % QUAD
    quad = (along + 1) % DEPTH // QUAD
    partners = [
        (side + across) % 2 * DEPTH + (along + step) % DEPTH for across, step in ((0, QUAD), (1, 0), (1, QUAD))
    ]

    def member(k, group=quad):
        return side * DEPTH + (group * QUAD + k + DEPTH - 1) % DEPTH

    layer = tile // GROUP
    place = tile % GROUP
    is_hub, is_teller = tile < HUB, layer == HUB // GROUP - 1

    def get(name, start=None, stop=None):
        at, size = PLACES[name]
        if start is None:
            return table_v[at : at + size, :]
        return table_v[at : at + size, start:stop]

    def signal(sem, device):
        pl.semaphore_signal(sem, inc=1, device_id=device, device_id_type=MESH)

    def send(source, target_ref, number, device):
        copy = pltpu.make_async_remote_copy(
            src_ref=source,
            dst_ref=target_ref,
            send_sem=send_sem.at[number],
            recv_sem=recv_sem.at[number],
            device_id=device,
            device_id_type=MESH,
        )
        copy.start()

    def wait(ref, sem):
        pltpu.make_async_copy(ref, ref, sem).wait()

    barrier = pltpu.get_barrier_semaphore()

    @pl.when(has_left)
    def _():
        signal(barrier, {"tile": left})

    @pl.when(has_right)
    def _():
        signal(barrier, {"tile": right})

    repeat(rank + 1, N_SRC, lambda k: signal(barrier, {"src": src_of(k)}))
    local = [
        pltpu.make_async_copy(mask, mask_v, local_sem.at[0]),
        pltpu.make_async_copy(shifts, shifts_v, local_sem.at[1]),
        pltpu.make_async_copy(weights, weights_v, local_sem.at[2]),
    ]
    for k in range(3):
        rows = pl.ds(CUTS[k], CUTS[k + 1] - CUTS[k])
        local.append(pltpu.make_async_copy(table.at[rows], table_v.at[rows], local_sem.at[3 + k]))
    local.append(pltpu.make_async_copy(target, target_v, local_sem.at[6]))
    for k in (0, 3, 1, 2):
        local[k].start()
    repeat(jnp.where(is_hub, tile + 1, n_tile), n_tile, lambda k: signal(barrier, {"tile": k}))

    ends = has_left.astype(jnp.int32) + has_right.astype(jnp.int32)
    pl.semaphore_wait(barrier, rank + ends + jnp.minimum(tile, HUB))

    @pl.when(has_right)
    def _():
        send(mask.at[:, pl.ds(128, 128)], left_v, 0, {"tile": right})

    @pl.when(has_left)
    def _():
        send(mask.at[:, pl.ds(0, 128)], right_v, 1, {"tile": left})

    repeat(0, rank, lambda k: signal(ready_sem.at[rank], {"src": src_of(k)}))
    term_v[:, POINTS_R // 2 :, :] = jnp.zeros((QUAD, (ROWS_C - POINTS_R) // 2, 128), jnp.float32)

    @pl.when(jnp.logical_not(has_left))
    def _():
        left_v[...] = jnp.zeros_like(left_v)

    @pl.when(jnp.logical_not(has_right))
    def _():
        right_v[...] = jnp.zeros_like(right_v)

    local[1].wait()
    local[2].wait()
    shape = (PER_DEV, PER_DEV)
    own_place = lanes(shape) == lax.broadcasted_iota(jnp.int32, shape, 0)

    def upright(row):
        return jnp.sum(jnp.where(own_place, row, 0.0), axis=1, keepdims=True)

    own_shifts = shifts_v[...].astype(jnp.float32)
    riders = [upright(own_shifts[0:1, :]), upright(own_shifts[1:2, :]), upright(weights_v[...])]
    local[0].wait()
    local[3].wait()
    at = PLACES["enter"][0]
    own = enter(mask_v[...], table_v[at : at + TILE, :])

    @pl.when(has_left)
    def _():
        wait(left_v, recv_sem.at[0])

    @pl.when(has_right)
    def _():
        wait(right_v, recv_sem.at[1])

    margins = jnp.concatenate([left_v[...], right_v[...]], axis=1)
    own = own + enter(margins, table_v[at + TILE : at + 2 * TILE, :])
    own = pack(own[:8], own[8:])
    for lane, rider in zip(RIDERS, riders):
        own = jnp.where(lanes(own.shape) == lane, rider, own)
    spec_v[src] = own

    def send_piece(k):
        send(spec_v.at[src], spec_v.at[src], 2, {"src": src_of(k)})

    def answer_piece(k):
        pl.semaphore_wait(ready_sem.at[k], 1)
        send_piece(k)

    def send_even(k):
        send_piece(2 * jnp.where((rank >= N_SRC // 2) & (k < QUAD), (k + 1) % QUAD, k))

    repeat(0, (rank + 1) // 2, send_even)
    repeat(0, rank // 2, lambda k: send_piece(2 * k + 1))
    for k in (4, 5, 6):
        local[k].start()
    repeat(rank + 1, N_SRC, answer_piece)
    repeat(0, jnp.where(is_hub, tile, 0), lambda k: signal(hub_sem.at[0], {"tile": k}))

    @pl.when(jnp.logical_not(is_hub))
    def _():
        signal(hub_sem.at[1], {"tile": HUB - GROUP + place})

    local[4].wait()
    wait(spec_v.at[pl.ds(0, N_SRC - 1)], recv_sem.at[2])

    gathered = spec_v[...].reshape(128, 128)
    spec = spectrum(gathered, get("spec"), get("lows_a", 0, 128), pltpu.roll)
    bands = split_bands(spec, pltpu.roll)
    at = PLACES["lows_b"][0]
    cols = [(get("cols_" + name), get("cols_low_" + name)) for name in ("even", "odd")]
    rows = [
        (get("rows_even"), table_v[at : at + ROWS_C, 128:256]),
        (get("rows_odd"), table_v[at + ROWS_C : at + 2 * ROWS_C, 128:256]),
    ]

    def add_fields(part, images):
        owner = src
        for k, peer in enumerate(partners):
            owner = jnp.where(part == k + 1, peer, owner)
        rows_by, cols_by, scales = [spec_v[owner, :, lane : lane + 1] for lane in RIDERS]
        for s in range(PER_DEV):
            pupil_v[part, s] = pupil_of(rows_by[s : s + 1], cols_by[s : s + 1])
        for pair in range(PER_DEV // 2):
            first, second = [jnp.broadcast_to(scales[s : s + 1], (8, 128)) for s in (2 * pair, 2 * pair + 1)]
            at = slice(128 * (pair % 2), 128 * (pair % 2) + 128)
            for parity, scale in enumerate(swap(first, second)):
                scale_v[part, pair // 2, parity, :, at] = scale
        fields = coarse_fields(
            bands, [pupil_v[part, s].astype(jnp.bfloat16) for s in range(PER_DEV)], cols, rows
        )
        images = list(images)
        for group in range(2):
            for parity in range(2):
                field_v[part, group, parity] = fields[group][parity]
                power = power_of(fields[group][parity])
                power_v[part, group, parity] = power
                power = power * scale_v[part, group, parity, 0:1, :]
                images[parity] = images[parity] + power[:, :128] + power[:, 128:]
        return tuple(images)

    none = jnp.zeros((ROWS_C // 2, 128), jnp.float32)
    image = lax.fori_loop(0, QUAD, add_fields, (none, none), unroll=True)
    term_v[place_in_quad] = join_image(*image, pltpu.roll)
    image_rows = pl.ds(0, POINTS_R // 2)
    mine = term_v.at[place_in_quad, image_rows]

    middle = (place_in_quad == 1) | (place_in_quad == 2)
    tells_own, tells_other = jnp.logical_not(middle & (quad == 1)), middle & (quad == 0)

    def send_image(k, group):
        send(mine, mine, 3, {"src": member(k, group)})

    for k in (1, 0, 2, 3):
        pl.when(tells_own & (k != place_in_quad))(functools.partial(send_image, k, quad))
    for k in (3, 0, 1, 2):
        pl.when(tells_other & (k != place_in_quad))(functools.partial(send_image, k, 1))
    local[5].wait()
    local[6].wait()
    wait(term_v.at[pl.ds(0, QUAD - 1), image_rows], recv_sem.at[3])

    image = pixels_of(
        term_v[0] + term_v[1] + term_v[2] + term_v[3],
        get("fine_rows"),
        get("fine_cols"),
        get("fine_cols_low"),
    )
    printed = jax.nn.sigmoid(STEEP * (image * (1.0 / SOURCES) - THRESH))
    goal = target_v[...].astype(jnp.float32)
    slope = (LOSS_SCALE * 2.0 * STEEP) * (printed - goal) * printed * (1.0 - printed)
    coarse = coarse_of(slope, get("coarse_rows"), get("coarse_rows_low"), get("coarse_cols"))

    slopes = twice(coarse, pltpu.roll)
    sums = []
    for pair in range(PER_DEV // 2):
        at = slice(128 * (pair % 2), 128 * (pair % 2) + 128)
        terms = [
            jnp.sum(slopes[parity] * power_v[0, pair // 2, parity, :, at], axis=0, keepdims=True) for parity in range(2)
        ]
        sums.extend(swap(*terms))
    sums = jnp.sum(jnp.concatenate(sums, axis=0), axis=1, keepdims=True)
    spot = (PER_DEV, 128)
    sums = jnp.where(lanes(spot) == lax.broadcasted_iota(jnp.int32, spot, 0), sums, 0.0)
    sums_v[tile] = jnp.sum(sums, axis=0, keepdims=True)

    def send_sums(k):
        pltpu.make_async_remote_copy(
            src_ref=sums_v.at[tile],
            dst_ref=sums_v.at[tile],
            send_sem=send_sem.at[5],
            recv_sem=recv_sem.at[5],
            device_id={"tile": k},
            device_id_type=MESH,
        ).start()

    for k in range(HUB):
        first = k + 1 - 2 * (k % 2)
        pl.when(first < tile)(functools.partial(send_sums, first))

    printed_v[...] = printed
    resist[...] = printed_v[pl.ds(pl.multiple_of(src * ROWS, ROWS), ROWS), :]

    wide = [jnp.concatenate([slope, slope], axis=1) * (2.0 / SOURCES) for slope in slopes]
    rows_back = [get("rows_back_even"), get("rows_back_odd")]
    cols_back = [get("cols_back_even"), get("cols_back_odd")]

    def add_part(part, total):
        adjoints = []
        for group in range(2):
            adjoints.append([])
            for parity in range(2):
                scaled = wide[parity] * scale_v[part, group, parity, 0:1, :]
                adjoints[group].append(field_v[part, group, parity] * jnp.concatenate([scaled, scaled], axis=0))
        return band_grad(total, adjoints, [pupil_v[part, s] for s in range(PER_DEV)], rows_back, cols_back)

    grad = lax.fori_loop(0, QUAD, add_part, jnp.zeros((BAND, 128), jnp.float32))
    first = PLACES["leave"][0] + 8 * QUAD * (2 * side + quad)
    low_first = PLACES["lows_b"][0] + 8 * QUAD * (2 * side + quad)

    def halves_of(start, stop, begin):
        begin = pl.multiple_of(begin, 32)
        then = pl.multiple_of(begin + 128, 32)
        return jnp.concatenate(
            [table_v[pl.ds(begin, 8 * QUAD), start:stop], table_v[pl.ds(then, 8 * QUAD), start:stop]], axis=0
        )

    rows = row_grads(grad, halves_of(0, 256, first), halves_of(0, 128, low_first), pltpu.roll)
    grad_v[...] = rows.reshape(QUAD, 8, 128)
    for k in range(1, QUAD):
        other = (place_in_quad + k) % QUAD
        send(grad_v.at[other], part_v.at[k - 1], 4, {"src": member(other)})

    @pl.when(tile < HUB - 1)
    def _():
        pl.semaphore_wait(hub_sem.at[0], HUB - 1 - tile)
        repeat(tile + 1, HUB, send_sums)

    wait(part_v, recv_sem.at[4])
    total = grad_v[place_in_quad] + part_v[0] + part_v[1] + part_v[2]
    mask_grad[...] = last_step(total, get("last"), get("last_low"))

    @pl.when(is_hub)
    def _():
        wait(sums_v.at[pl.ds(0, n_tile - 1)], recv_sem.at[5])
        total_v[...] = jnp.sum(sums_v[...], axis=0) * (1.0 / (SOURCES * n_tile * TILE * TILE))

    def tell(k):
        send(total_v, total_v, 6, {"tile": k * GROUP + place})

    @pl.when(is_teller)
    def _():
        pl.semaphore_wait(hub_sem.at[1], (n_tile - HUB) // GROUP)
        repeat(HUB // GROUP, n_tile // GROUP, tell)

    @pl.when(jnp.logical_not(is_hub))
    def _():
        wait(total_v, recv_sem.at[6])

    source_grad[...] = total_v[...]

    @pl.when(is_teller)
    def _():
        wait(sums_v.at[pl.ds(0, (n_tile - HUB) // GROUP)], send_sem.at[6])

    @pl.when(is_hub)
    def _():
        wait(sums_v.at[pl.ds(0, HUB - 1)], send_sem.at[5])

    @pl.when(jnp.logical_not(is_hub))
    def _():
        wait(sums_v.at[pl.ds(0, HUB)], send_sem.at[5])


    @pl.when(has_right)
    def _():
        wait(left_v, send_sem.at[0])

    @pl.when(has_left)
    def _():
        wait(right_v, send_sem.at[1])

    wait(spec_v.at[pl.ds(0, N_SRC - 1)], send_sem.at[2])
    for told in (tells_own, tells_other):
        pl.when(told)(lambda: wait(term_v.at[pl.ds(0, QUAD - 1), image_rows], send_sem.at[3]))
    wait(part_v, send_sem.at[4])


def hand_over(resist, mask_grad, source_grad, resist_out, mask_grad_out, source_grad_out, row, sem):
    row[...] = source_grad[0, :PER_DEV]
    copies = [
        pltpu.make_async_copy(resist, resist_out, sem.at[0]),
        pltpu.make_async_copy(mask_grad, mask_grad_out, sem.at[1]),
        pltpu.make_async_copy(row, source_grad_out, sem.at[2]),
    ]
    for copy in copies:
        copy.start()
    for copy in copies:
        copy.wait()


def local(mask, target, shifts, weights):
    f32 = jnp.float32
    anywhere = pl.BlockSpec(memory_space=pl.ANY)
    inside = pl.BlockSpec(memory_space=pltpu.VMEM)
    results = pl.pallas_call(
        everything,
        out_shape=(
            pltpu.VMEM((ROWS, TILE), f32),
            pltpu.VMEM((ROWS, TILE), f32),
            pltpu.VMEM((1, 128), f32),
        ),
        in_specs=[anywhere] * 5,
        out_specs=(inside, inside, inside),
        scratch_shapes=[
            pltpu.VMEM((ROWS, TILE), f32),
            pltpu.VMEM((TILE, TILE), jnp.int32),
            pltpu.VMEM((2, PER_DEV), jnp.int32),
            pltpu.VMEM((1, PER_DEV), f32),
            pltpu.VMEM(TABLE.shape, jnp.bfloat16),
            pltpu.VMEM((ROWS, 128), f32),
            pltpu.VMEM((ROWS, 128), f32),
            pltpu.VMEM((N_SRC, 8, 128), f32),
            pltpu.VMEM((QUAD, PER_DEV, BAND, 128), f32),
            pltpu.VMEM((QUAD, 2, 2, 8, 256), f32),
            pltpu.VMEM((QUAD, ROWS_C // 2, 128), f32),
            pltpu.VMEM((QUAD, 2, 2, ROWS_C, 256), f32),
            pltpu.VMEM((QUAD, 2, 2, ROWS_C // 2, 256), f32),
            pltpu.VMEM((TILE, TILE), f32),
            pltpu.VMEM((QUAD, 8, 128), f32),
            pltpu.VMEM((QUAD - 1, 8, 128), f32),
            pltpu.VMEM((N_TILE, 1, 128), f32),
            pltpu.VMEM((1, 128), f32),
            pltpu.SemaphoreType.DMA((7,)),
            pltpu.SemaphoreType.DMA((7,)),
            pltpu.SemaphoreType.DMA((7,)),
            pltpu.SemaphoreType.REGULAR((N_SRC,)),
            pltpu.SemaphoreType.REGULAR((2,)),
        ],
        compiler_params=pltpu.CompilerParams(
            collective_id=0, has_side_effects=True, vmem_limit_bytes=60 * 1024 * 1024
        ),
    )(mask, target, shifts.T, weights.reshape(1, PER_DEV), jnp.asarray(TABLE))
    return pl.pallas_call(
        hand_over,
        out_shape=(
            jax.ShapeDtypeStruct((ROWS, TILE), f32),
            jax.ShapeDtypeStruct((ROWS, TILE), f32),
            jax.ShapeDtypeStruct((PER_DEV,), f32),
        ),
        in_specs=[inside] * 3,
        out_specs=(anywhere,) * 3,
        scratch_shapes=[pltpu.VMEM((PER_DEV,), f32), pltpu.SemaphoreType.DMA((3,))],
    )(*[pltpu.with_memory_space_constraint(result, pltpu.VMEM) for result in results])


def solution(mesh):
    placed = (P("src", "tile"), P(None, "tile"), P("src", None), P("src"))
    return jax.shard_map(
        local,
        mesh=mesh,
        in_specs=placed,
        out_specs=(P("src", "tile"), P("src", "tile"), P("src")),
        check_vma=False,
    )
```

```python
import functools

import jax
import jax.numpy as jnp
import ml_dtypes
import numpy as np
from jax import lax
from jax.experimental import pallas as pl
from jax.experimental.pallas import tpu as pltpu
from jax.sharding import PartitionSpec as P

TILE = 256
MARGIN = 32
BAND = 64
RAD = 16
EXT = 320
STEEP = 8.0
THRESH = 0.25
LOSS_SCALE = 2.0

N_SRC = 16
N_TILE = 32
PER_DEV = 8
SOURCES = 128
ROWS = 16
HALF = 32
POINTS_R = 66
ROWS_C = 80
COLS_C = 128
QUAD = 4
GROUP = 4
DEPTH = 8
HUB = 3 * GROUP
RIDERS = (31, 63, 95)

MESH = pl.DeviceIdType.MESH
BF16 = ml_dtypes.bfloat16


def halves(table):
    high = table.astype(BF16)
    low = (table - high.astype(np.float64)).astype(BF16)
    return high, low


def column_slots():
    plus = np.arange(HALF)
    return np.concatenate([plus, -plus]), np.concatenate([np.ones(HALF), [0.0], np.ones(HALF - 1)])


def waves(freq, place, period):
    phase = 2.0 * np.pi * ((freq[:, None] * place[None, :]) % period) / period
    return np.cos(phase), np.sin(phase)


def interpolation(points):
    order = np.arange(-2 * RAD, 2 * RAD + 1)
    place = np.arange(TILE) + MARGIN
    offset = place[:, None] / EXT - np.arange(points)[None, :] / points
    return np.cos(2.0 * np.pi * order[None, None, :] * offset[:, :, None]).sum(axis=2) / points


def padded(rows):
    return np.concatenate([rows, np.zeros((ROWS_C // 2 - rows.shape[0], rows.shape[1]))], axis=0)


def build_tables():
    slots, used = column_slots()
    row_freq = np.arange(BAND) - BAND // 2
    pixels = np.arange(TILE) + MARGIN
    parts = {}

    real, imag = waves(np.arange(HALF), np.arange(EXT), EXT)
    fwd = np.concatenate([real, -imag], axis=0).T
    wide = np.zeros((2 * TILE, 2 * HALF))
    wide[:TILE] = fwd[MARGIN : MARGIN + TILE]
    wide[TILE + 96 : TILE + 128] = fwd[:MARGIN]
    wide[TILE + 128 : TILE + 160] = fwd[MARGIN + TILE :]
    high, low = halves(np.concatenate([wide, wide], axis=1))
    parts["enter"] = np.concatenate([high, low], axis=1)

    rows = np.arange(TILE).reshape(N_SRC, 2, 8)
    first, second = rows[:, 0].reshape(-1), rows[:, 1].reshape(-1)
    real, imag = waves(row_freq, pixels, EXT)
    both = np.concatenate([real, -imag], axis=0)
    high, low = halves(np.concatenate([both[:, first], both[:, second]], axis=0))
    parts["spec"] = np.concatenate([high, high], axis=1)
    spec_low = low

    inter_rows, inter_cols = 2.0 * interpolation(POINTS_R), interpolation(COLS_C)
    even, odd = np.arange(0, COLS_C, 2), np.arange(1, COLS_C, 2)
    for name, order in (("even", np.concatenate([even, odd])), ("odd", np.concatenate([odd, even]))):
        real, imag = waves(slots, order, COLS_C)
        real, imag = real * used[:, None], imag * used[:, None]
        cols = np.concatenate(
            [np.concatenate([real, imag], axis=1), np.concatenate([-imag, real], axis=1)], axis=0
        )
        high, low = halves(cols)
        again = high.copy()
        again[[HALF, 3 * HALF]] = high[[0, 2 * HALF]]
        parts["cols_" + name] = np.concatenate([high, again], axis=0)
        parts["cols_low_" + name] = low
        high, low = halves(np.concatenate([cols[:, :COLS_C].T, cols[:, COLS_C:].T], axis=0))
        parts["cols_back_" + name] = np.concatenate([high, low], axis=1)

    lows = []
    for name, start in (("even", 0), ("odd", 1)):
        real, imag = waves(row_freq, np.arange(start, POINTS_R, 2), POINTS_R)
        real, imag = padded(real.T), padded(imag.T)
        high, low = halves(
            np.concatenate(
                [np.concatenate([real, -imag], axis=1), np.concatenate([imag, real], axis=1)], axis=0
            )
        )
        parts["rows_" + name] = np.concatenate([high, high], axis=1)
        lows.append(low)
        pad = np.zeros((2 * BAND, TILE - 3 * ROWS_C), BF16)
        parts["rows_back_" + name] = np.concatenate([high.T, high.T, low.T, pad], axis=1)
    rows_low = np.concatenate(lows, axis=0)

    inter_rows = np.concatenate([padded(inter_rows[:, 0::2].T), padded(inter_rows[:, 1::2].T)], axis=0).T
    inter_cols = inter_cols[:, np.concatenate([even, odd])]
    high, low = halves(inter_rows)
    pad = np.zeros((TILE, TILE - 3 * ROWS_C), BF16)
    parts["fine_rows"] = np.concatenate([high, high, low, pad], axis=1)
    high, low = halves(inter_cols.T)
    parts["fine_cols"] = np.concatenate([high, high], axis=0)
    parts["fine_cols_low"] = low
    parts["coarse_cols"] = np.concatenate([high.T, low.T], axis=1)
    high, low = halves(inter_rows.T)
    parts["coarse_rows"] = high
    parts["coarse_rows_low"] = low

    owners = [
        side * DEPTH + (quad * QUAD + k - 1) % DEPTH for side in range(2) for quad in range(2) for k in range(QUAD)
    ]
    first, second = rows[owners, 0].reshape(-1), rows[owners, 1].reshape(-1)
    high, low = halves(np.concatenate([both[:, first], both[:, second]], axis=1).T)
    parts["leave"] = np.concatenate([high, high], axis=1)
    leave_low = low
    last = fwd[MARGIN : MARGIN + TILE].T
    high, low = halves(np.concatenate([last, last], axis=0))
    parts["last"] = high
    parts["last_low"] = low

    parts["lows_a"] = np.concatenate([spec_low, np.zeros((TILE, 128), BF16)], axis=1)
    rows_low = np.concatenate([rows_low, np.zeros((TILE - 2 * ROWS_C, 128), BF16)], axis=0)
    parts["lows_b"] = np.concatenate([leave_low, rows_low], axis=1)

    order = [
        "enter",
        "spec", "lows_a", "cols_even", "cols_low_even", "cols_odd", "cols_low_odd", "rows_even", "rows_odd", "lows_b",
        "fine_rows", "fine_cols", "fine_cols_low", "coarse_cols", "coarse_rows", "coarse_rows_low",
        "rows_back_even", "rows_back_odd", "cols_back_even", "cols_back_odd", "leave", "last", "last_low",
    ]
    places, start = {}, 0
    for name in order:
        places[name] = (start, parts[name].shape[0])
        start += parts[name].shape[0]
    return np.concatenate([parts[name] for name in order], axis=0), places


TABLE, PLACES = build_tables()
CUTS = (0, PLACES["spec"][0], PLACES["fine_rows"][0], TABLE.shape[0])


def dot(left, right):
    return jnp.dot(left, right, preferred_element_type=jnp.float32)


def cut(value):
    high = value.astype(jnp.bfloat16)
    low = (value - high.astype(jnp.float32)).astype(jnp.bfloat16)
    return high, low


def lanes(shape):
    return lax.broadcasted_iota(jnp.int32, shape, 1)


def enter(value, table):
    rows = value.shape[0]
    both = dot(jnp.concatenate(cut(value), axis=0), table)
    return both[:rows, :128] + both[:rows, 128:] + both[rows:, :128]


def pack(first, second):
    return jnp.where(lanes(first.shape) < 64, first, second)


def spectrum(gathered, table, low_table, roll):
    high, low = cut(gathered)
    out = dot(table, jnp.concatenate([high, low], axis=0)) + dot(low_table, high)
    both = pack(out[:128], out[128:])
    both = both + roll(both, 64, 1)
    turned = roll(both, 32, 1)
    quarter = lanes((BAND, 128)) >> 5
    outer = (quarter == 0) | (quarter == 3)
    even = jnp.where(outer, both[:BAND], turned[:BAND])
    odd = jnp.where(outer, turned[BAND:], both[BAND:])
    return (jnp.where(quarter == 3, -even, even) + jnp.where(quarter == 0, -odd, odd)) * (1.0 / (EXT * EXT))


def pupil_of(row_shift, col_shift):
    row = (lax.broadcasted_iota(jnp.int32, (BAND, 128), 0) - BAND // 2).astype(jnp.float32) + row_shift
    slot = lanes((1, 128)) & 63
    col = jnp.where(slot < HALF, slot, HALF - slot).astype(jnp.float32) + col_shift
    room = RAD * RAD - col * col
    return jnp.where(row * row <= room, 1.0, 0.0)


def swap(first, second):
    return pack(first, second), pack(second, first)


def split_bands(spec, roll):
    spare = (lanes(spec.shape) & 63) == HALF
    high, low = cut(jnp.where(spare, 0.0, spec))
    left = spec - high.astype(jnp.float32) - low.astype(jnp.float32)
    low = jnp.where(spare, roll(left, HALF, 1), low.astype(jnp.float32)).astype(jnp.bfloat16)
    return high, low


def coarse_fields(bands, pupils, cols, rows):
    high, low = bands
    mids = []
    for which in range(2):
        band_high, band_low = [
            jnp.concatenate([part * pupil for pupil in pupils[which::2]], axis=0) for part in (high, low)
        ]
        table, low_table = cols[which]
        mids.append(
            dot(jnp.concatenate([band_high, band_low], axis=1), table) + dot(band_high, low_table)
        )
    fields = []
    for group in range(2):
        stacks = ([], [])
        for pair in (2 * group, 2 * group + 1):
            at = slice(BAND * pair, BAND * pair + BAND)
            real = swap(mids[0][at, :128], mids[1][at, :128])
            imag = swap(mids[0][at, 128:], mids[1][at, 128:])
            for parity in range(2):
                stacks[parity].append(jnp.concatenate([real[parity], imag[parity]], axis=0))
        both = []
        for parity in range(2):
            upper, lower = cut(jnp.concatenate(stacks[parity], axis=1))
            table, low_table = rows[parity]
            both.append(dot(table, jnp.concatenate([upper, lower], axis=0)) + dot(low_table, upper))
        fields.append(both)
    return fields


def power_of(field):
    half = ROWS_C // 2
    return field[:half] * field[:half] + field[half:] * field[half:]


def join_image(even, odd, roll):
    return pack(even + roll(even, 64, 1), odd + roll(odd, 64, 1))


def pixels_of(coarse, fine_rows, fine_cols, fine_cols_low):
    first = lanes(coarse.shape) < 64
    coarse = jnp.concatenate([jnp.where(first, coarse, 0.0), jnp.where(first, 0.0, coarse)], axis=0)
    high, low = cut(coarse)
    mid = dot(jnp.concatenate([high, low], axis=1), fine_cols) + dot(high, fine_cols_low)
    return dot(fine_rows, three(mid))


def three(value):
    high, low = cut(value)
    pad = jnp.zeros((TILE - 3 * value.shape[0], value.shape[1]), jnp.bfloat16)
    return jnp.concatenate([high, low, high, pad], axis=0)


def coarse_of(slope, coarse_rows, coarse_rows_low, coarse_cols):
    high, low = cut(slope)
    mid = dot(coarse_rows, high) + dot(coarse_rows, low) + dot(coarse_rows_low, high)
    high, low = cut(mid)
    both = dot(high, coarse_cols)
    return both[:, :128] + both[:, 128:] + dot(low, coarse_cols[:, :128])


def twice(coarse, roll):
    half = ROWS_C // 2
    even, odd = coarse[:half], coarse[half:]
    return pack(even, roll(even, 64, 1)), pack(roll(odd, 64, 1), odd)


def band_grad(total, adjoints, pupils, rows_back, cols_back):
    sides = ([], [])
    for group in range(2):
        even, odd = [dot(rows_back[parity], three(adjoints[group][parity])) for parity in range(2)]
        for pair in range(2):
            at = slice(128 * pair, 128 * pair + 128)
            real = swap(even[:BAND, at], odd[:BAND, at])
            imag = swap(even[BAND:, at], odd[BAND:, at])
            for which in range(2):
                sides[which].append(jnp.concatenate([real[which], imag[which]], axis=1))
    for which in range(2):
        high, low = cut(jnp.concatenate(sides[which], axis=0))
        both = dot(high, cols_back[which])
        term = both[:, :128] + both[:, 128:] + dot(low, cols_back[which][:, :128])
        for k in range(PER_DEV // 2):
            total = total + term[BAND * k : BAND * k + BAND] * pupils[2 * k + which]
    return total


def fold(grad, roll):
    r32, r64, r96 = roll(grad, 32, 1), roll(grad, 64, 1), roll(grad, 96, 1)
    quarter = lanes(grad.shape) >> 5
    upper = jnp.where(
        quarter == 0, grad + r96, jnp.where(quarter == 1, r96 - r64, jnp.where(quarter == 2, r64 + r32, r32 - grad))
    )
    lower = jnp.where(
        quarter == 0, r64 + r32, jnp.where(quarter == 1, grad - r32, jnp.where(quarter == 2, grad + r96, r64 - r96))
    )
    return jnp.concatenate([upper, lower], axis=0)


def row_grads(grad, leave, leave_low, roll):
    high, low = cut(fold(grad, roll))
    out = dot(leave, jnp.concatenate([high, low], axis=0)) + dot(leave_low, high)
    half = out.shape[0] // 2
    return pack(out[:half], out[half:])


def last_step(total, last, last_low):
    first = lanes(total.shape) < 64
    value = jnp.concatenate([jnp.where(first, total, 0.0), jnp.where(first, 0.0, total)], axis=0)
    high, low = cut(value)
    return (dot(high, last) + dot(low, last) + dot(high, last_low)) * (1.0 / (EXT * EXT))


def rank_of(side, along):
    step = jnp.where(along == 3, 4, jnp.where(along == 7, 3, 11 - along))
    return 2 * jnp.where(along < 3, along, step) + side


def src_of(rank):
    step, side = rank // 2, rank % 2
    along = jnp.where(step == 3, 7, jnp.where(step == 4, 3, 11 - step))
    return side * DEPTH + jnp.where(step < 3, step, along)


def repeat(first, last, body):
    def step(k, carry):
        body(k)
        return carry

    lax.fori_loop(first, last, step, 0)


def everything(mask, target, shifts, weights, table, resist, mask_grad, source_grad, *scratch):
    (
        mask_v, target_v, shifts_v, weights_v, table_v,
        left_v, right_v, spec_v, pupil_v, scale_v, term_v, field_v, power_v,
        printed_v, grad_v, part_v, sums_v, total_v, local_sem, send_sem, recv_sem, ready_sem, hub_sem,
    ) = scratch
    tile, src = lax.axis_index("tile"), lax.axis_index("src")
    n_tile = lax.axis_size("tile")
    left, right = tile - 1, tile + 1
    has_left, has_right = tile > 0, tile < n_tile - 1
    side, along = src // DEPTH, src % DEPTH
    rank = rank_of(side, along)
    place_in_quad = (along + 1) % QUAD
    quad = (along + 1) % DEPTH // QUAD
    partners = [
        (side + across) % 2 * DEPTH + (along + step) % DEPTH for across, step in ((0, QUAD), (1, 0), (1, QUAD))
    ]

    def member(k):
        return side * DEPTH + (quad * QUAD + k + DEPTH - 1) % DEPTH

    layer = tile // GROUP
    place = tile % GROUP
    is_hub, is_teller = tile < HUB, layer == HUB // GROUP - 1

    def get(name, start=None, stop=None):
        at, size = PLACES[name]
        if start is None:
            return table_v[at : at + size, :]
        return table_v[at : at + size, start:stop]

    def signal(sem, device):
        pl.semaphore_signal(sem, inc=1, device_id=device, device_id_type=MESH)

    def send(source, target_ref, number, device):
        copy = pltpu.make_async_remote_copy(
            src_ref=source,
            dst_ref=target_ref,
            send_sem=send_sem.at[number],
            recv_sem=recv_sem.at[number],
            device_id=device,
            device_id_type=MESH,
        )
        copy.start()

    def wait(ref, sem):
        pltpu.make_async_copy(ref, ref, sem).wait()

    barrier = pltpu.get_barrier_semaphore()

    @pl.when(has_left)
    def _():
        signal(barrier, {"tile": left})

    @pl.when(has_right)
    def _():
        signal(barrier, {"tile": right})

    repeat(rank + 1, N_SRC, lambda k: signal(barrier, {"src": src_of(k)}))
    local = [
        pltpu.make_async_copy(mask, mask_v, local_sem.at[0]),
        pltpu.make_async_copy(shifts, shifts_v, local_sem.at[1]),
        pltpu.make_async_copy(weights, weights_v, local_sem.at[2]),
    ]
    for k in range(3):
        rows = pl.ds(CUTS[k], CUTS[k + 1] - CUTS[k])
        local.append(pltpu.make_async_copy(table.at[rows], table_v.at[rows], local_sem.at[3 + k]))
    local.append(pltpu.make_async_copy(target, target_v, local_sem.at[6]))
    local[0].start()
    local[3].start()
    repeat(jnp.where(is_hub, tile + 1, n_tile), n_tile, lambda k: signal(barrier, {"tile": k}))

    ends = has_left.astype(jnp.int32) + has_right.astype(jnp.int32)
    pl.semaphore_wait(barrier, rank + ends + jnp.minimum(tile, HUB))

    @pl.when(has_right)
    def _():
        send(mask.at[:, pl.ds(128, 128)], left_v, 0, {"tile": right})

    @pl.when(has_left)
    def _():
        send(mask.at[:, pl.ds(0, 128)], right_v, 1, {"tile": left})

    for k in (1, 2, 4, 5, 6):
        local[k].start()
    repeat(0, rank, lambda k: signal(ready_sem.at[rank], {"src": src_of(k)}))
    term_v[:, POINTS_R // 2 :, :] = jnp.zeros((QUAD, (ROWS_C - POINTS_R) // 2, 128), jnp.float32)

    @pl.when(jnp.logical_not(has_left))
    def _():
        left_v[...] = jnp.zeros_like(left_v)

    @pl.when(jnp.logical_not(has_right))
    def _():
        right_v[...] = jnp.zeros_like(right_v)

    local[1].wait()
    local[2].wait()
    shape = (PER_DEV, PER_DEV)
    own_place = lanes(shape) == lax.broadcasted_iota(jnp.int32, shape, 0)

    def upright(row):
        return jnp.sum(jnp.where(own_place, row, 0.0), axis=1, keepdims=True)

    own_shifts = shifts_v[...].astype(jnp.float32)
    riders = [upright(own_shifts[0:1, :]), upright(own_shifts[1:2, :]), upright(weights_v[...])]
    local[0].wait()
    local[3].wait()
    at = PLACES["enter"][0]
    own = enter(mask_v[...], table_v[at : at + TILE, :])

    @pl.when(has_left)
    def _():
        wait(left_v, recv_sem.at[0])

    @pl.when(has_right)
    def _():
        wait(right_v, recv_sem.at[1])

    margins = jnp.concatenate([left_v[...], right_v[...]], axis=1)
    own = own + enter(margins, table_v[at + TILE : at + 2 * TILE, :])
    own = pack(own[:8], own[8:])
    for lane, rider in zip(RIDERS, riders):
        own = jnp.where(lanes(own.shape) == lane, rider, own)
    spec_v[src] = own

    def send_piece(k):
        send(spec_v.at[src], spec_v.at[src], 2, {"src": src_of(k)})

    def answer_piece(k):
        pl.semaphore_wait(ready_sem.at[k], 1)
        send_piece(k)

    repeat(0, (rank + 1) // 2, lambda k: send_piece(2 * k))
    repeat(0, rank // 2, lambda k: send_piece(2 * k + 1))
    repeat(rank + 1, N_SRC, answer_piece)
    repeat(0, jnp.where(is_hub, tile, 0), lambda k: signal(hub_sem.at[0], {"tile": k}))

    @pl.when(jnp.logical_not(is_hub))
    def _():
        signal(hub_sem.at[1], {"tile": HUB - GROUP + place})

    local[4].wait()
    wait(spec_v.at[pl.ds(0, N_SRC - 1)], recv_sem.at[2])

    gathered = spec_v[...].reshape(128, 128)
    spec = spectrum(gathered, get("spec"), get("lows_a", 0, 128), pltpu.roll)
    bands = split_bands(spec, pltpu.roll)
    at = PLACES["lows_b"][0]
    cols = [(get("cols_" + name), get("cols_low_" + name)) for name in ("even", "odd")]
    rows = [
        (get("rows_even"), table_v[at : at + ROWS_C, 128:256]),
        (get("rows_odd"), table_v[at + ROWS_C : at + 2 * ROWS_C, 128:256]),
    ]

    def add_fields(part, images):
        owner = src
        for k, peer in enumerate(partners):
            owner = jnp.where(part == k + 1, peer, owner)
        rows_by, cols_by, scales = [spec_v[owner, :, lane : lane + 1] for lane in RIDERS]
        for s in range(PER_DEV):
            pupil_v[part, s] = pupil_of(rows_by[s : s + 1], cols_by[s : s + 1])
        for pair in range(PER_DEV // 2):
            first, second = [jnp.broadcast_to(scales[s : s + 1], (8, 128)) for s in (2 * pair, 2 * pair + 1)]
            at = slice(128 * (pair % 2), 128 * (pair % 2) + 128)
            for parity, scale in enumerate(swap(first, second)):
                scale_v[part, pair // 2, parity, :, at] = scale
        fields = coarse_fields(
            bands, [pupil_v[part, s].astype(jnp.bfloat16) for s in range(PER_DEV)], cols, rows
        )
        images = list(images)
        for group in range(2):
            for parity in range(2):
                field_v[part, group, parity] = fields[group][parity]
                power = power_of(fields[group][parity])
                power_v[part, group, parity] = power
                power = power * scale_v[part, group, parity, 0:1, :]
                images[parity] = images[parity] + power[:, :128] + power[:, 128:]
        return tuple(images)

    none = jnp.zeros((ROWS_C // 2, 128), jnp.float32)
    image = lax.fori_loop(0, QUAD, add_fields, (none, none), unroll=True)
    term_v[place_in_quad] = join_image(*image, pltpu.roll)
    image_rows = pl.ds(0, POINTS_R // 2)
    mine = term_v.at[place_in_quad, image_rows]

    def send_image(k):
        send(mine, mine, 3, {"src": member(k)})

    for group, order in enumerate(((1, 0, 2, 3), (3, 0, 1, 2))):
        for k in order:
            pl.when((quad == group) & (k != place_in_quad))(functools.partial(send_image, k))
    local[5].wait()
    local[6].wait()
    wait(term_v.at[pl.ds(0, QUAD - 1), image_rows], recv_sem.at[3])

    image = pixels_of(
        term_v[0] + term_v[1] + term_v[2] + term_v[3],
        get("fine_rows"),
        get("fine_cols"),
        get("fine_cols_low"),
    )
    printed = jax.nn.sigmoid(STEEP * (image * (1.0 / SOURCES) - THRESH))
    goal = target_v[...].astype(jnp.float32)
    slope = (LOSS_SCALE * 2.0 * STEEP) * (printed - goal) * printed * (1.0 - printed)
    coarse = coarse_of(slope, get("coarse_rows"), get("coarse_rows_low"), get("coarse_cols"))

    slopes = twice(coarse, pltpu.roll)
    sums = []
    for pair in range(PER_DEV // 2):
        at = slice(128 * (pair % 2), 128 * (pair % 2) + 128)
        terms = [
            jnp.sum(slopes[parity] * power_v[0, pair // 2, parity, :, at], axis=0, keepdims=True) for parity in range(2)
        ]
        sums.extend(swap(*terms))
    sums = jnp.sum(jnp.concatenate(sums, axis=0), axis=1, keepdims=True)
    spot = (PER_DEV, 128)
    sums = jnp.where(lanes(spot) == lax.broadcasted_iota(jnp.int32, spot, 0), sums, 0.0)
    sums_v[tile] = jnp.sum(sums, axis=0, keepdims=True)

    def send_sums(k):
        pltpu.make_async_remote_copy(
            src_ref=sums_v.at[tile],
            dst_ref=sums_v.at[tile],
            send_sem=send_sem.at[5],
            recv_sem=recv_sem.at[5],
            device_id={"tile": k},
            device_id_type=MESH,
        ).start()

    for k in range(HUB):
        first = k + 1 - 2 * (k % 2)
        pl.when(first < tile)(functools.partial(send_sums, first))

    printed_v[...] = printed
    resist[...] = printed_v[pl.ds(pl.multiple_of(src * ROWS, ROWS), ROWS), :]

    wide = [jnp.concatenate([slope, slope], axis=1) * (2.0 / SOURCES) for slope in slopes]
    rows_back = [get("rows_back_even"), get("rows_back_odd")]
    cols_back = [get("cols_back_even"), get("cols_back_odd")]

    def add_part(part, total):
        adjoints = []
        for group in range(2):
            adjoints.append([])
            for parity in range(2):
                scaled = wide[parity] * scale_v[part, group, parity, 0:1, :]
                adjoints[group].append(field_v[part, group, parity] * jnp.concatenate([scaled, scaled], axis=0))
        return band_grad(total, adjoints, [pupil_v[part, s] for s in range(PER_DEV)], rows_back, cols_back)

    grad = lax.fori_loop(0, QUAD, add_part, jnp.zeros((BAND, 128), jnp.float32))
    first = PLACES["leave"][0] + 8 * QUAD * (2 * side + quad)
    low_first = PLACES["lows_b"][0] + 8 * QUAD * (2 * side + quad)

    def halves_of(start, stop, begin):
        begin = pl.multiple_of(begin, 32)
        then = pl.multiple_of(begin + 128, 32)
        return jnp.concatenate(
            [table_v[pl.ds(begin, 8 * QUAD), start:stop], table_v[pl.ds(then, 8 * QUAD), start:stop]], axis=0
        )

    rows = row_grads(grad, halves_of(0, 256, first), halves_of(0, 128, low_first), pltpu.roll)
    grad_v[...] = rows.reshape(QUAD, 8, 128)
    for k in range(1, QUAD):
        other = (place_in_quad + k) % QUAD
        send(grad_v.at[other], part_v.at[k - 1], 4, {"src": member(other)})

    @pl.when(tile < HUB - 1)
    def _():
        pl.semaphore_wait(hub_sem.at[0], HUB - 1 - tile)
        repeat(tile + 1, HUB, send_sums)

    wait(part_v, recv_sem.at[4])
    total = grad_v[place_in_quad] + part_v[0] + part_v[1] + part_v[2]
    mask_grad[...] = last_step(total, get("last"), get("last_low"))

    @pl.when(is_hub)
    def _():
        wait(sums_v.at[pl.ds(0, n_tile - 1)], recv_sem.at[5])
        total_v[...] = jnp.sum(sums_v[...], axis=0) * (1.0 / (SOURCES * n_tile * TILE * TILE))

    def tell(k):
        send(total_v, total_v, 6, {"tile": k * GROUP + place})

    @pl.when(is_teller)
    def _():
        pl.semaphore_wait(hub_sem.at[1], (n_tile - HUB) // GROUP)
        repeat(HUB // GROUP, n_tile // GROUP, tell)

    @pl.when(jnp.logical_not(is_hub))
    def _():
        wait(total_v, recv_sem.at[6])

    source_grad[...] = total_v[...]

    @pl.when(is_teller)
    def _():
        wait(sums_v.at[pl.ds(0, (n_tile - HUB) // GROUP)], send_sem.at[6])

    @pl.when(is_hub)
    def _():
        wait(sums_v.at[pl.ds(0, HUB - 1)], send_sem.at[5])

    @pl.when(jnp.logical_not(is_hub))
    def _():
        wait(sums_v.at[pl.ds(0, HUB)], send_sem.at[5])


    @pl.when(has_right)
    def _():
        wait(left_v, send_sem.at[0])

    @pl.when(has_left)
    def _():
        wait(right_v, send_sem.at[1])

    wait(spec_v.at[pl.ds(0, N_SRC - 1)], send_sem.at[2])
    wait(term_v.at[pl.ds(0, QUAD - 1), image_rows], send_sem.at[3])
    wait(part_v, send_sem.at[4])


def hand_over(resist, mask_grad, source_grad, resist_out, mask_grad_out, source_grad_out, row, sem):
    row[...] = source_grad[0, :PER_DEV]
    copies = [
        pltpu.make_async_copy(resist, resist_out, sem.at[0]),
        pltpu.make_async_copy(mask_grad, mask_grad_out, sem.at[1]),
        pltpu.make_async_copy(row, source_grad_out, sem.at[2]),
    ]
    for copy in copies:
        copy.start()
    for copy in copies:
        copy.wait()


def local(mask, target, shifts, weights):
    f32 = jnp.float32
    anywhere = pl.BlockSpec(memory_space=pl.ANY)
    inside = pl.BlockSpec(memory_space=pltpu.VMEM)
    results = pl.pallas_call(
        everything,
        out_shape=(
            pltpu.VMEM((ROWS, TILE), f32),
            pltpu.VMEM((ROWS, TILE), f32),
            pltpu.VMEM((1, 128), f32),
        ),
        in_specs=[anywhere] * 5,
        out_specs=(inside, inside, inside),
        scratch_shapes=[
            pltpu.VMEM((ROWS, TILE), f32),
            pltpu.VMEM((TILE, TILE), jnp.int32),
            pltpu.VMEM((2, PER_DEV), jnp.int32),
            pltpu.VMEM((1, PER_DEV), f32),
            pltpu.VMEM(TABLE.shape, jnp.bfloat16),
            pltpu.VMEM((ROWS, 128), f32),
            pltpu.VMEM((ROWS, 128), f32),
            pltpu.VMEM((N_SRC, 8, 128), f32),
            pltpu.VMEM((QUAD, PER_DEV, BAND, 128), f32),
            pltpu.VMEM((QUAD, 2, 2, 8, 256), f32),
            pltpu.VMEM((QUAD, ROWS_C // 2, 128), f32),
            pltpu.VMEM((QUAD, 2, 2, ROWS_C, 256), f32),
            pltpu.VMEM((QUAD, 2, 2, ROWS_C // 2, 256), f32),
            pltpu.VMEM((TILE, TILE), f32),
            pltpu.VMEM((QUAD, 8, 128), f32),
            pltpu.VMEM((QUAD - 1, 8, 128), f32),
            pltpu.VMEM((N_TILE, 1, 128), f32),
            pltpu.VMEM((1, 128), f32),
            pltpu.SemaphoreType.DMA((7,)),
            pltpu.SemaphoreType.DMA((7,)),
            pltpu.SemaphoreType.DMA((7,)),
            pltpu.SemaphoreType.REGULAR((N_SRC,)),
            pltpu.SemaphoreType.REGULAR((2,)),
        ],
        compiler_params=pltpu.CompilerParams(
            collective_id=0, has_side_effects=True, vmem_limit_bytes=60 * 1024 * 1024
        ),
    )(mask, target, shifts.T, weights.reshape(1, PER_DEV), jnp.asarray(TABLE))
    return pl.pallas_call(
        hand_over,
        out_shape=(
            jax.ShapeDtypeStruct((ROWS, TILE), f32),
            jax.ShapeDtypeStruct((ROWS, TILE), f32),
            jax.ShapeDtypeStruct((PER_DEV,), f32),
        ),
        in_specs=[inside] * 3,
        out_specs=(anywhere,) * 3,
        scratch_shapes=[pltpu.VMEM((PER_DEV,), f32), pltpu.SemaphoreType.DMA((3,))],
    )(*[pltpu.with_memory_space_constraint(result, pltpu.VMEM) for result in results])


def solution(mesh):
    placed = (P("src", "tile"), P(None, "tile"), P("src", None), P("src"))
    return jax.shard_map(
        local,
        mesh=mesh,
        in_specs=placed,
        out_specs=(P("src", "tile"), P("src", "tile"), P("src")),
        check_vma=False,
    )
```
